32 devices in a mesh: parts: 2 (over y), gx: 4 (over x, core), gy: 4 (over z).
Axes of the slice: x: 2, y: 2, z: 4, core: 2. Of those that a mesh axis runs over, the one named last changes fastest.
Arguments:
- adj_fields: float32 [3, 2, 1024, 1024], P(None, None, ('parts', 'gx'), 'gy'), parts along dimension 2, may hold values from -6 to 6
- inv_eps: float32 [2, 1024, 1024], P(None, ('parts', 'gx'), 'gy'), parts along dimension 1, may hold values from 0.0833 to 1
- fwd_diff: float32 [4, 2, 1024, 1024], P(None, None, ('parts', 'gx'), 'gy'), parts along dimension 2, may hold values from -6 to 6
- mon_x: int32 [128], P('parts'), parts along dimension 0, may hold values from 0 to 511
- mon_y: int32 [128], P('parts'), parts along dimension 0, may hold values from 0 to 1023
- mon_amp: float32 [4, 128], P(None, 'parts'), parts along dimension 1, may hold values from -16 to 16
- design_mask: int32 [8, 4, 128], P(('parts', 'gx'), 'gy'), parts along dimension 0, may hold values 0 or 1
- tile_owner: int32 [8, 4, 128, 1], P(('parts', 'gx'), 'gy'), parts along dimension 0, may hold values from 0 to 15; in each aligned block of 128 rows (0 to 127, 128 to 255, ..., all dimensions but the last counted through in order) at most 16 rows name the same one
Outputs:
- adj_final: float32 [3, 2, 1024, 1024], P(None, None, ('parts', 'gx'), 'gy'), parts along dimension 2
- grad_slots: float32 [32, 16, 16, 128], P(('parts', 'gx', 'gy')), parts along dimension 0
The draws below stay inside these ranges and needn't reach their ends.
There are 2 independent parts, one for each index of `parts`. The reference program is written for one: setup_inputs(seed, part) draws one part's arguments, and reference() takes and returns one part's arrays. A program takes and returns all parts, laid end to end along the dimension named above; each array names one. Nothing has to cross between parts.
Inputs may be any that keep to these rules, and one draw needn't show every extreme that they name: `tile_owner`: among the tiles of one device no owner is named more than 16 times, and in every draw some owner is named exactly 16 times there.
All inputs are finite; a program needn't handle non-finite values. No bound on the sum of `design_mask` on one device may be relied on, other than what follows from the above.
Results may differ from the reference program's by a relative error of at most 0.0003.
Values sent between devices are 32-bit elements; how exact they have to be, the bound alone decides.
No kernel may reach another device: no remote copies, remote signals or barrier semaphores. Data moves between devices by JAX's collectives and lax.ppermute only.
A program may use at most 64 MiB of HBM per device.

```python
import math
import jax
import jax.numpy as jnp
import numpy as np
from jax import lax

CX = 128
CY = 256
STEPS = 4
CHANNELS = 64
PIX = 2
TS = 16
RADIUS = 4
NX = 512
NY = 1024
OWNERS = 16
TP = 8
TV = 128
TILES_DEV = 128
MOST = 16
N_GX = 4
N_GY = 4


def touch_ends(result, rng, low, top_value):
    longest = result.shape.index(max(result.shape))
    spots = []
    for shift in (0, 1):
        where = [jax.random.randint(jax.random.fold_in(rng, axis), (), 0, length) for axis, length in enumerate(result.shape)]
        where[longest] = (where[longest] + shift) % result.shape[longest]
        spots.append(tuple(where))
    return result.at[spots[0]].set(low).at[spots[1]].set(top_value)


def levels(key, dims, cuts, smallest, largest):
    gain, own = 1.0, jax.random.fold_in(key, 6)
    for dim, parts in cuts:
        heights = jnp.exp(jax.random.uniform(jax.random.fold_in(own, dim), (parts,), jnp.float32, smallest / len(cuts), largest / len(cuts)))
        gain = gain * jnp.repeat(heights, dims[dim] // parts).reshape([-1 if axis == dim else 1 for axis in range(len(dims))])
    return gain


def routed_block(rng, own, number, rows, amount, top, bound, skew):
    ranking = jax.random.permutation(rng, amount)
    crowded, ordinary = load_shares(amount, rows * top, bound, skew, True), load_shares(amount, rows * top, bound, skew, False)
    places = jnp.arange(amount)

    def named(lengths, rotation):
        used = int((lengths > 0).sum())
        fixed = max(1, used // 4)
        moved = fixed + (places - fixed + rotation * (used - fixed)) % max(1, amount - fixed)
        return jnp.zeros((amount,), jnp.int32).at[ranking[jnp.where(places < fixed, places, moved)]].set(jnp.asarray(lengths, jnp.int32))

    lengths = jnp.where(number % 4 == 0, named(crowded, number // 4), named(ordinary, number - number // 4 - 1))
    mixed = jax.random.permutation(jax.random.fold_in(own, 3), amount)
    source_of, sink = mixed[0:amount // 2 * 2:2], mixed[1:amount // 2 * 2:2]
    margin = jnp.minimum(lengths[source_of] - 1, bound - lengths[sink]) // 2
    margin = jnp.where((source_of == ranking[0]) | (sink == ranking[0]) | (lengths[sink] == 0), 0, jnp.maximum(margin, 0))
    moved = jax.random.randint(jax.random.fold_in(own, 4), (amount // 2,), 0, 1 << 20) % (margin + 1)
    lengths = lengths.at[source_of].add(-moved).at[sink].add(moved)
    labels = jnp.searchsorted(jnp.cumsum(lengths), jnp.arange(rows * top), side="right").astype(jnp.int32)
    grid = labels.reshape(top, rows).T
    grid = grid[jax.random.permutation(jax.random.fold_in(own, 1), rows)]
    rotation = jax.random.randint(jax.random.fold_in(own, 2), (rows, 1), 0, top)
    return jnp.take_along_axis(grid, (jnp.arange(top)[None, :] + rotation) % top, axis=1)


def load_shares(number_of, total, limit, skew, full):
    portions = [(1 << 20) // math.isqrt(rank ** skew) + 1 for rank in range(1, number_of + 1)]
    largest = limit if full else min(limit, max(-(-total // number_of), total * portions[0] // sum(portions)))
    least = 1 if total - largest >= number_of - 1 else 0
    counts, rest = [largest] + [least] * (number_of - 1), total - largest - least * (number_of - 1)
    while rest > 0:
        free = [i for i in range(1, number_of) if counts[i] < largest] or [i for i in range(1, number_of) if counts[i] < limit]
        pool, budget = sum([portions[i] for i in free]), rest
        for i in free:
            addition = min(limit - counts[i], max(1, budget * portions[i] // pool), rest)
            counts[i] = counts[i] + addition
            rest = rest - addition
    return np.array(counts)


def scatter_about(stream_key, extent, width, most, cuts=(), kind=jnp.bfloat16):
    result = width * jax.random.normal(stream_key, extent, jnp.float32)
    if cuts:
        result = result * levels(stream_key, extent, cuts, -0.22, 0.18)
    return jnp.clip(result, -most, most).astype(kind)


def setup_inputs(seed: int = 0, part: int = 0) -> dict:
    key_list = jax.random.split(jax.random.key(seed), 9)
    part_keys = jax.random.split(jax.random.fold_in(key_list[8], part), 9)
    adj_fields = scatter_about(part_keys[0], (3, 2, NX, NY), 1.0, 6.0, ((2, 4), (3, 4)), jnp.float32)
    inv_eps = jnp.clip(jnp.exp(math.log(1.0) - 2.4853067 * jax.random.uniform(part_keys[1], (2, NX, NY), jnp.float32) ** levels(part_keys[1], (2, NX, NY), ((1, 4), (2, 4)), -0.2, 0.2)), 0.0833, 1.0)
    fwd_diff = scatter_about(part_keys[2], (STEPS, 2, NX, NY), 1.0, 6.0, ((2, 4), (3, 4)), jnp.float32)
    mon_x = touch_ends(jax.random.randint(part_keys[3], (CHANNELS,), 0, NX), jax.random.fold_in(part_keys[3], 1), 0, NX - 1).astype(jnp.int32)
    mon_y = touch_ends(jax.random.randint(part_keys[4], (CHANNELS,), 0, NY), jax.random.fold_in(part_keys[4], 1), 0, NY - 1).astype(jnp.int32)
    mon_amp = scatter_about(part_keys[5], (STEPS, CHANNELS), 4.0, 16.0, (), jnp.float32)
    design_mask = touch_ends((jax.random.randint(part_keys[6], (N_GX, N_GY, TILES_DEV), 0, 4) < 3).astype(jnp.int32), jax.random.fold_in(part_keys[6], 1), 0, 1)
    tile_owner_keys = jax.random.split(jax.random.fold_in(part_keys[7], 1), N_GX * N_GY * TILES_DEV // TILES_DEV)
    tile_owner_turns = jax.random.permutation(jax.random.fold_in(part_keys[7], 3), N_GX * N_GY * TILES_DEV // TILES_DEV)
    tile_owner = jax.vmap(lambda own, number: routed_block(jax.random.fold_in(part_keys[7], 2), own, number, TILES_DEV, OWNERS, 1, MOST, 2))(tile_owner_keys, tile_owner_turns).reshape((N_GX, N_GY, TILES_DEV, 1))
    return dict(adj_fields=adj_fields, inv_eps=inv_eps, fwd_diff=fwd_diff, mon_x=mon_x, mon_y=mon_y, mon_amp=mon_amp, design_mask=design_mask, tile_owner=tile_owner)


COURANT = 0.6
COUPLING = 0.25

def cone_weights(radius):
    reach_cells = radius - 1
    offsets = np.arange(-reach_cells, reach_cells + 1)
    distance = np.sqrt(offsets[:, None] * offsets[:, None] + offsets[None, :] * offsets[None, :])
    weights = np.maximum(radius - distance, 0.0)
    return weights / weights.sum()

def yee_step(fields, inv_eps, source, inside_mask):
    electric, magnet_x, magnet_y = (fields[0], fields[1], fields[2])
    electric_next_x = jnp.concatenate([electric[:, 1:, :], jnp.zeros_like(electric[:, :1, :])], axis=1)
    electric_next_y = jnp.concatenate([electric[:, :, 1:], jnp.zeros_like(electric[:, :, :1])], axis=2)
    magnet_x = (magnet_x + COURANT * (electric_next_y - electric)) * inside_mask
    magnet_y = (magnet_y - COURANT * (electric_next_x - electric)) * inside_mask
    magnet_y_prev = jnp.concatenate([jnp.zeros_like(magnet_y[:, :1, :]), magnet_y[:, :-1, :]], axis=1)
    magnet_x_prev = jnp.concatenate([jnp.zeros_like(magnet_x[:, :, :1]), magnet_x[:, :, :-1]], axis=2)
    curl_sum = magnet_y - magnet_y_prev - (magnet_x - magnet_x_prev)
    electric = electric - COURANT * inv_eps * (curl_sum + COUPLING * (electric[::-1] - electric)) + source
    electric = electric * inside_mask
    return jnp.stack([electric, magnet_x, magnet_y])

def cone_filter(padded, out_rows, out_cols):
    weights = cone_weights(RADIUS)
    reach_cells = RADIUS - 1
    total = jnp.zeros((padded.shape[0], out_rows, out_cols), jnp.float32)
    for offset_x in range(2 * reach_cells + 1):
        for offset_y in range(2 * reach_cells + 1):
            weight_here = float(weights[offset_x, offset_y])
            if weight_here > 0.0:
                total = total + weight_here * padded[:, offset_x:offset_x + out_rows, offset_y:offset_y + out_cols]
    return total

def slots_of(tile_dest):
    position = jnp.arange(tile_dest.shape[0], dtype=jnp.int32)
    earlier = (position[None, :] < position[:, None]) & (tile_dest[None, :] == tile_dest[:, None])
    return lax.optimization_barrier(jnp.sum(earlier.astype(jnp.int32), axis=1))

def reference(adj_fields, inv_eps, fwd_diff, mon_x, mon_y, mon_amp, design_mask, tile_owner):
    layer_of = jnp.arange(CHANNELS, dtype=jnp.int32) % 2
    fields = adj_fields
    gradient = jnp.zeros((2, NX, NY), jnp.float32)
    for step_at in range(STEPS):
        source = jnp.zeros((2, NX, NY), jnp.float32).at[layer_of, mon_x, mon_y].add(mon_amp[step_at])
        fields = yee_step(fields, inv_eps, source, 1.0)
        gradient = gradient - fields[0] * fwd_diff[step_at]
    pooled = gradient.reshape(2, NX // PIX, PIX, NY // PIX, PIX).sum(axis=(2, 4))
    reach_cells = RADIUS - 1
    padded = jnp.pad(pooled, ((0, 0), (reach_cells, reach_cells), (reach_cells, reach_cells)))
    filtered = cone_filter(padded, NX // PIX, NY // PIX)
    tile_rows = CX // TS
    tile_cols = CY // TS
    blocks = filtered.reshape(2, N_GX, tile_rows, TP, N_GY, tile_cols, TP)
    blocks = blocks.transpose(1, 4, 2, 5, 0, 3, 6).reshape(N_GX, N_GY, TILES_DEV, TV)
    tile_vals = blocks * design_mask.astype(jnp.float32)[..., None]
    tile_dest = tile_owner[..., 0].reshape(OWNERS, TILES_DEV)
    tile_slot = jax.vmap(slots_of)(tile_dest)
    source_id = jnp.broadcast_to(jnp.arange(OWNERS, dtype=jnp.int32)[:, None], (OWNERS, TILES_DEV))
    grad_slots = jnp.zeros((OWNERS, OWNERS, MOST, TV), jnp.float32)
    grad_slots = grad_slots.at[tile_dest.reshape(-1), source_id.reshape(-1), tile_slot.reshape(-1)].set(tile_vals.reshape(-1, TV))
    return (fields, grad_slots)
```

```python
import jax
import jax.numpy as jnp
import numpy as np
from jax import lax
from jax.experimental import pallas as pl
from jax.experimental.pallas import tpu as pltpu
from jax.sharding import PartitionSpec as P

STEPS = 4
PIX = 2
TS = 16
RADIUS = 4
COURANT = 0.6
COUPLING = 0.25

LANES = 128
SUB = 8
FAR = STEPS + PIX * (RADIUS - 1)
NEAR = PIX * (RADIUS - 1)
PAD = 16
PADF = 8
F32 = jnp.float32
BF16 = jnp.bfloat16


def cone_weights(radius):
    reach_cells = radius - 1
    offsets = np.arange(-reach_cells, reach_cells + 1)
    distance = np.sqrt(offsets[:, None] * offsets[:, None] + offsets[None, :] * offsets[None, :])
    weights = np.maximum(radius - distance, 0.0)
    return weights / weights.sum()


def lane_plan():
    plan, at = [], 0
    for kind, count, width in (("f", 6, FAR), ("e", 2, FAR), ("d", 2 * STEPS, NEAR)):
        for index in range(count):
            plan.append((kind, index, at, width))
            at += width
    assert at <= LANES
    return plan


def split2(value):
    high = value.astype(BF16)
    return high, (value - high.astype(F32)).astype(BF16)


def split3(value):
    high, rest = value.astype(BF16), None
    rest = value - high.astype(F32)
    mid = rest.astype(BF16)
    return high, mid, (rest - mid.astype(F32)).astype(BF16)


def dot(a, b):
    return jnp.dot(a, b, preferred_element_type=F32)


def rows_kernel(fields, eps, fwd, first, last, sems):
    rows = fields.shape[2]
    copies = []
    for n, (out, at, at_fwd) in enumerate(((first, 0, 0), (last, rows - PAD, rows - PADF))):
        pairs = (
            (fields.at[:, :, pl.ds(at, PAD), :], out.at[pl.ds(0, 3)]),
            (eps.at[:, pl.ds(at, PAD), :], out.at[3]),
            (fwd.at[pl.ds(0, 2), :, pl.ds(at_fwd, PADF), :], out.at[pl.ds(4, 2), :, pl.ds(0, PADF), :]),
            (fwd.at[pl.ds(2, 2), :, pl.ds(at_fwd, PADF), :], out.at[pl.ds(4, 2), :, pl.ds(PADF, PADF), :]),
        )
        for m, (src, dst) in enumerate(pairs):
            copies.append(pltpu.make_async_copy(src, dst, sems.at[4 * n + m]))
    for copy in copies:
        copy.start()
    for copy in copies:
        copy.wait()


def pack_rows(load, plan, lane, right):
    total = jnp.zeros((SUB, LANES), F32)
    for kind, index, at, width in plan:
        value = load(kind, index)
        if value is None:
            continue
        shift = (at - (LANES - width)) % LANES if right else at
        if shift:
            value = pltpu.roll(value, shift, 1)
        total = jnp.where((lane >= at) & (lane < at + width), value, total)
    return total


def cols_kernel(fields, eps, fwd, left, right):
    rows, cols = fields.shape[2], fields.shape[3]
    plan = lane_plan()
    lane = lax.broadcasted_iota(jnp.int32, (SUB, LANES), 1)

    def tile(t, carry):
        at = pl.multiple_of(t * SUB, SUB)
        for out, lo, is_right in ((left, 0, False), (right, cols - LANES, True)):

            def load(kind, index):
                where = (pl.ds(at, SUB), pl.ds(lo, LANES))
                if kind == "f":
                    return fields[(index // 2, index % 2) + where]
                if kind == "e":
                    return eps[(index,) + where]
                return fwd[(index // 2, index % 2) + where]

            out[pl.ds(pl.multiple_of(at + PAD, SUB), SUB), :] = pack_rows(load, plan, lane, is_right)
        return carry

    lax.fori_loop(0, rows // SUB, tile, 0)
    zero = jnp.zeros((PAD, LANES), F32)
    for out in (left, right):
        out[pl.ds(0, PAD), :] = zero
        out[pl.ds(PAD + rows, PAD), :] = zero


def strip_tile(strip, which, kind, index, lo):
    cols = pl.ds(lo, LANES)
    if kind == "f":
        return strip[index // 2, index % 2, pl.ds(which * SUB, SUB), cols]
    return strip[3, index, pl.ds(which * SUB, SUB), cols]


def strip_fwd(strip, index, lo):
    step, layer = index // 2, index % 2
    return strip[4 + step % 2, layer, pl.ds((step // 2) * PADF, PADF), pl.ds(lo, LANES)]


def corners_kernel(left_in, right_in, above, below, left, right):
    total_rows = left.shape[0]
    cols = above.shape[3]
    plan = lane_plan()
    lane = lax.broadcasted_iota(jnp.int32, (SUB, LANES), 1)
    for out, core, lo, is_right in ((left, left_in, 0, False), (right, right_in, cols - LANES, True)):
        out[pl.ds(PAD, total_rows - 2 * PAD), :] = core[pl.ds(PAD, total_rows - 2 * PAD), :]
        for strip, base, fwd_tile in ((above, 0, 1), (below, total_rows - PAD, 0)):
            for which in range(2):

                def load(kind, index):
                    if kind != "d":
                        return strip_tile(strip, which, kind, index, lo)
                    return strip_fwd(strip, index, lo) if which == fwd_tile else None

                out[pl.ds(base + which * SUB, SUB), :] = pack_rows(load, plan, lane, is_right)


def side_kernel(capacity, mon_x, mon_y, amp, mask, owner, src, place):
    _, _, ext_rows, ext_cols = src.shape
    rows, cols = ext_rows - 2 * PAD, ext_cols - LANES
    channels = mon_x.shape[1]
    local_x = mon_x[...] - lax.axis_index("gx") * rows + PAD
    local_y = mon_y[...] - lax.axis_index("gy") * cols
    lane_y = jnp.where((local_y < 0) & (local_y >= -PAD), local_y + ext_cols, local_y)
    lane_y = jnp.where((local_y >= -PAD) & (local_y < cols + PAD), lane_y, -1)
    at_y = lax.broadcasted_iota(jnp.int32, (ext_cols, channels), 0) == lane_y
    one_y = jnp.where(at_y, 1.0, 0.0).astype(BF16)
    one_y = jnp.concatenate([one_y] * 3, axis=1)
    at_x = lax.broadcasted_iota(jnp.int32, (ext_rows, channels), 0) == local_x
    one_x = jnp.where(at_x, 1.0, 0.0).astype(F32)
    layer = lax.broadcasted_iota(jnp.int32, (1, channels), 1) & 1
    for step in range(STEPS):
        for which in range(2):
            strength = jnp.where(layer == which, amp[pl.ds(step, 1), :], 0.0)
            parts = [part.astype(F32) for part in split3(strength)]
            lhs = jnp.concatenate([one_x * part for part in parts], axis=1).astype(BF16)
            src[step, which] = lax.dot_general(
                lhs, one_y, (((1,), (1,)), ((), ())), preferred_element_type=F32
            )
    tiles = owner.shape[1]
    own = owner[...].astype(F32)
    own_wide = jnp.broadcast_to(own, (tiles, tiles))
    earlier = lax.broadcasted_iota(jnp.int32, (tiles, tiles), 0) < lax.broadcasted_iota(
        jnp.int32, (tiles, tiles), 1
    )
    same = (own_wide.T == own_wide) & earlier
    slot = jnp.sum(jnp.where(same, 1.0, 0.0), axis=0, keepdims=True)
    dest = owner[...] * capacity + slot.astype(jnp.int32)
    dest = jnp.where(mask[...] != 0, dest, -1)
    hit = lax.broadcasted_iota(jnp.int32, place.shape, 0) == dest
    place[...] = jnp.where(hit, 1.0, 0.0).astype(BF16)


def main_kernel(
    fields, eps, fwd, above, below, from_left, from_right, src, place, out_fields, out_slots,
    f, e, d, g, pooled, sem,
):
    rows, cols = fields.shape[2], fields.shape[3]
    ext_rows, ext_cols = rows + 2 * PAD, cols + LANES
    n_tiles, n_lanes = ext_rows // SUB, ext_cols // LANES
    halo = pl.ds(cols, LANES)
    plan = lane_plan()
    lane = lax.broadcasted_iota(jnp.int32, (SUB, LANES), 1)
    sub = lax.broadcasted_iota(jnp.int32, (SUB, LANES), 0)
    is_low = lane < LANES // 2

    core, wide = pl.ds(PAD, rows), pl.ds(0, cols)
    for index in range(6):
        f[index, core, wide] = fields[index // 2, index % 2]
        f[index, pl.ds(0, PAD), wide] = above[index // 2, index % 2]
        f[index, pl.ds(PAD + rows, PAD), wide] = below[index // 2, index % 2]
    for index in range(2):
        e[index, core, wide] = COURANT * eps[index]
        e[index, pl.ds(0, PAD), wide] = COURANT * above[3, index]
        e[index, pl.ds(PAD + rows, PAD), wide] = COURANT * below[3, index]
    for index in range(2 * STEPS):
        step, layer = index // 2, index % 2
        strip_rows = pl.ds((step // 2) * PADF, PADF)
        d[index, core, wide] = fwd[step, layer]
        d[index, pl.ds(PAD - PADF, PADF), wide] = above[4 + step % 2, layer, strip_rows, :]
        d[index, pl.ds(PAD + rows, PADF), wide] = below[4 + step % 2, layer, strip_rows, :]

    def unpack(t, carry):
        at = pl.ds(pl.multiple_of(t * SUB, SUB), SUB)
        low, high = from_right[at, :], from_left[at, :]
        for kind, index, first, width in plan:
            down, up = (-first) % LANES, (LANES - width - first) % LANES
            a = pltpu.roll(low, down, 1) if down else low
            b = pltpu.roll(high, up, 1) if up else high
            value = jnp.where(is_low, a, b)
            if kind == "f":
                f[index, at, halo] = value
            elif kind == "e":
                e[index, at, halo] = COURANT * value
            else:
                d[index, at, halo] = value
        return carry

    lax.fori_loop(0, n_tiles, unpack, 0)

    coef_first = jnp.where(lax.axis_index("gx") > 0, COURANT, 0.0).astype(F32)
    coef_left = jnp.where(lax.axis_index("gy") > 0, COURANT, 0.0).astype(F32)
    coef_halo = jnp.where(is_low, COURANT, coef_left)
    at_end, at_start = lane == LANES - 1, lane == 0
    bottom, top = sub == SUB - 1, sub == 0
    keys = [(l, k) for l in range(2) for k in range(n_lanes)]

    def lane_of(k):
        return pl.ds(k * LANES, LANES)

    for step in range(STEPS):

        def tile(t, carry, step=step):
            e_now, e_rot, hy_rot = carry
            at = pl.ds(pl.multiple_of(t * SUB, SUB), SUB)
            nxt = pl.ds(pl.multiple_of(jnp.minimum(t + 1, n_tiles - 1) * SUB, SUB), SUB)
            coef_y = jnp.where(t < PAD // SUB, coef_first, COURANT)
            e_next = {key: f[key[0], nxt, lane_of(key[1])] for key in keys}
            e_next_rot = {key: pltpu.roll(e_next[key], SUB - 1, 0) for key in keys}
            e_side = {key: pltpu.roll(e_now[key], LANES - 1, 1) for key in keys}
            hx, hy, hy_rot_new, hx_side = {}, {}, {}, {}
            for key in keys:
                l, k = key
                right = jnp.where(at_end, e_side[l, (k + 1) % n_lanes], e_side[key])
                coef = coef_halo if k == n_lanes - 1 else COURANT
                hx[key] = f[2 + l, at, lane_of(k)] + coef * (right - e_now[key])
                under = jnp.where(bottom, e_next_rot[key], e_rot[key])
                hy[key] = f[4 + l, at, lane_of(k)] - coef_y * (under - e_now[key])
                hy_rot_new[key] = pltpu.roll(hy[key], 1, 0)
                hx_side[key] = pltpu.roll(hx[key], 1, 1)
            for key in keys:
                l, k = key
                over = jnp.where(top, hy_rot[key], hy_rot_new[key])
                left = jnp.where(at_start, hx_side[l, (k - 1) % n_lanes], hx_side[key])
                curl = (hy[key] - over) - (hx[key] - left)
                curl = curl + COUPLING * (e_now[1 - l, k] - e_now[key])
                new = e_now[key] - e[l, at, lane_of(k)] * curl + src[step, l, at, lane_of(k)]
                f[l, at, lane_of(k)] = new
                f[2 + l, at, lane_of(k)] = hx[key]
                f[4 + l, at, lane_of(k)] = hy[key]
                change = new * d[2 * step + l, at, lane_of(k)]
                if step == 0:
                    g[l, k, at, :] = -change
                else:
                    g[l, k, at, :] = g[l, k, at, :] - change
            return e_next, e_next_rot, hy_rot_new

        first = {key: f[key[0], pl.ds(0, SUB), lane_of(key[1])] for key in keys}
        carry = (
            first,
            {key: pltpu.roll(first[key], SUB - 1, 0) for key in keys},
            {key: jnp.zeros((SUB, LANES), F32) for key in keys},
        )
        lax.fori_loop(0, n_tiles, tile, carry)

    copies = [
        pltpu.make_async_copy(
            f.at[pl.ds(2 * c, 2), core, wide], out_fields.at[c], sem.at[c]
        )
        for c in range(3)
    ]
    for copy in copies:
        copy.start()

    pix_rows = ext_rows // PIX
    j_in = lax.broadcasted_iota(jnp.int32, (LANES, LANES), 0)
    q_out = lax.broadcasted_iota(jnp.int32, (LANES, LANES), 1)
    half = j_in // PIX
    mats = [
        (half == q_out),
        (half + LANES // PIX == q_out),
        (jnp.where(j_in < LANES // 2, half, half + LANES // PIX) == q_out),
    ]
    mats = [jnp.where(m, 1.0, 0.0).astype(BF16) for m in mats]
    for l in range(2):
        halves = []
        for k in range(n_lanes):
            even = g[l, k, pl.ds(0, pix_rows, stride=PIX), :]
            odd = g[l, k, pl.ds(1, pix_rows, stride=PIX), :]
            high, low = split2(even + odd)
            halves.append(dot(high, mats[k]) + dot(low, mats[k]))
        pooled[l, 0] = halves[0] + halves[1]
        pooled[l, 1] = halves[2]

    weights = cone_weights(RADIUS)
    reach = RADIUS - 1
    out_pix = rows // PIX
    base = PAD // PIX
    lane_wide = lax.broadcasted_iota(jnp.int32, (out_pix, LANES), 1)
    blocks = []
    for l in range(2):
        sums = []
        for part in range(2):
            at = [pooled[l, part, pl.ds(base + a, out_pix), :] for a in range(-reach, reach + 1)]
            sums.append([at[reach]] + [at[reach + a] + at[reach - a] for a in range(1, reach + 1)])
        total = None
        for b in range(reach + 1):
            mixed = []
            for part in range(2):
                value = None
                for a in range(reach + 1):
                    weight = float(weights[reach + a, reach + b])
                    if weight > 0.0:
                        term = weight * sums[part][a]
                        value = term if value is None else value + term
                mixed.append(value)
            if b == 0:
                total = mixed[0]
            else:
                total = total + pltpu.roll(jnp.where(lane_wide < b, mixed[1], mixed[0]), LANES - b, 1)
                total = total + pltpu.roll(
                    jnp.where(lane_wide >= LANES - b, mixed[1], mixed[0]), b, 1
                )
        blocks.append(total)

    span = TS // PIX
    tile_rows = out_pix // span
    x = jnp.stack([b.reshape(tile_rows, span, LANES) for b in blocks], axis=1)
    x = x.reshape(tile_rows * 2, span, LANES)
    group = lax.broadcasted_iota(jnp.int32, x.shape, 2) // span
    row = (lax.broadcasted_iota(jnp.int32, x.shape, 0) & 1) * span + lax.broadcasted_iota(
        jnp.int32, x.shape, 1
    )
    for bit in (1, 2, 4):
        row_on, lane_on = (row & bit) != 0, (group & bit) != 0
        a = pltpu.roll(pltpu.roll(x, span - bit, 1), bit * span, 2)
        b = pltpu.roll(pltpu.roll(x, bit, 1), LANES - bit * span, 2)
        x = jnp.where(row_on == lane_on, x, jnp.where(lane_on, a, b))
    x = x.reshape(tile_rows, 2, span, LANES)
    even, odd = x[:, 0], x[:, 1]
    upper = (lax.broadcasted_iota(jnp.int32, even.shape, 2) // span) >= span
    new_even = jnp.where(upper, pltpu.roll(odd, LANES // 2, 2), even)
    new_odd = jnp.where(upper, odd, pltpu.roll(even, LANES // 2, 2))
    vals = jnp.stack([new_even, new_odd], axis=1).reshape(tile_rows * 2 * span, LANES)
    high, low = split2(vals)
    out_slots[...] = dot(place[...], high) + dot(place[...], low)
    for copy in copies:
        copy.wait()


def vmem():
    return pl.BlockSpec(memory_space=pltpu.VMEM)


def anywhere():
    return pl.BlockSpec(memory_space=pl.ANY)


def shape(*dims, dtype=F32):
    return jax.ShapeDtypeStruct(dims, dtype)


def cost(flops, size):
    return pl.CostEstimate(flops=flops, bytes_accessed=size, transcendentals=0)


def params():
    return pltpu.CompilerParams(vmem_limit_bytes=40 * 1024 * 1024)


def on_device(adj_fields, inv_eps, fwd_diff, mon_x, mon_y, mon_amp, design_mask, tile_owner):
    rows, cols = adj_fields.shape[2], adj_fields.shape[3]
    gx_count, gy_count = lax.axis_size("gx"), lax.axis_size("gy")
    owners = gx_count * gy_count
    tiles = (rows // TS) * (cols // TS)
    width = 2 * (TS // PIX) ** 2
    capacity = max(8, 2 * tiles // owners)
    ext_rows, ext_cols = rows + 2 * PAD, cols + LANES

    strip = shape(6, 2, PAD, cols)
    first, last = pl.pallas_call(
        rows_kernel,
        out_shape=(strip, strip),
        in_specs=[anywhere()] * 3,
        out_specs=(vmem(), vmem()),
        scratch_shapes=[pltpu.SemaphoreType.DMA((8,))],
        compiler_params=params(),
        cost_estimate=cost(0, 4 * 2 * 12 * PAD * cols),
    )(adj_fields, inv_eps, fwd_diff)
    up = [(i, i + 1) for i in range(gx_count - 1)]
    down = [(i + 1, i) for i in range(gx_count - 1)]
    above = lax.ppermute(last, "gx", up)
    below = lax.ppermute(first, "gx", down)

    packed = shape(ext_rows, LANES)
    left, right = pl.pallas_call(
        cols_kernel,
        out_shape=(packed, packed),
        in_specs=[vmem()] * 3,
        out_specs=(vmem(), vmem()),
        compiler_params=params(),
        cost_estimate=cost(16 * rows * cols, 64 * rows * cols),
    )(adj_fields, inv_eps, fwd_diff)
    left, right = pl.pallas_call(
        corners_kernel,
        out_shape=(packed, packed),
        in_specs=[vmem()] * 4,
        out_specs=(vmem(), vmem()),
        compiler_params=params(),
        cost_estimate=cost(16 * 2 * PAD * cols, 8 * ext_rows * LANES),
    )(left, right, above, below)
    up = [(i, i + 1) for i in range(gy_count - 1)]
    down = [(i + 1, i) for i in range(gy_count - 1)]
    from_left = lax.ppermute(right, "gy", up)
    from_right = lax.ppermute(left, "gy", down)

    channels = mon_x.shape[0]
    src, place = pl.pallas_call(
        lambda *refs: side_kernel(capacity, *refs),
        out_shape=(shape(STEPS, 2, ext_rows, ext_cols), shape(owners * capacity, tiles, dtype=BF16)),
        in_specs=[vmem()] * 5,
        out_specs=(vmem(), vmem()),
        compiler_params=params(),
        cost_estimate=cost(16 * ext_rows * ext_cols * 3 * channels, 32 * ext_rows * ext_cols),
    )(
        mon_x.reshape(1, channels),
        mon_y.reshape(1, channels),
        mon_amp,
        design_mask.reshape(1, tiles),
        tile_owner.reshape(1, tiles),
    )

    fields, outgoing = pl.pallas_call(
        main_kernel,
        out_shape=(shape(3, 2, rows, cols), shape(owners * capacity, width)),
        in_specs=[vmem()] * 9,
        out_specs=(anywhere(), vmem()),
        scratch_shapes=[
            pltpu.VMEM((6, ext_rows, ext_cols), F32),
            pltpu.VMEM((2, ext_rows, ext_cols), F32),
            pltpu.VMEM((2 * STEPS, ext_rows, ext_cols), F32),
            pltpu.VMEM((2, ext_cols // LANES, ext_rows, LANES), F32),
            pltpu.VMEM((2, 2, ext_rows // PIX, LANES), F32),
            pltpu.SemaphoreType.DMA((3,)),
        ],
        compiler_params=params(),
        cost_estimate=cost(200 * ext_rows * ext_cols, 96 * rows * cols),
    )(adj_fields, inv_eps, fwd_diff, above, below, from_left, from_right, src, place)

    outgoing = outgoing.reshape(owners, capacity, width)
    incoming = lax.all_to_all(outgoing, ("gx", "gy"), split_axis=0, concat_axis=0, tiled=True)
    return fields, incoming[None]


def solution(mesh):
    placed = (
        P(None, None, ("parts", "gx"), "gy"),
        P(None, ("parts", "gx"), "gy"),
        P(None, None, ("parts", "gx"), "gy"),
        P("parts"),
        P("parts"),
        P(None, "parts"),
        P(("parts", "gx"), "gy", None),
        P(("parts", "gx"), "gy", None, None),
    )
    return jax.shard_map(
        on_device,
        mesh=mesh,
        in_specs=placed,
        out_specs=(
            P(None, None, ("parts", "gx"), "gy"),
            P(("parts", "gx", "gy"), None, None, None),
        ),
        check_vma=False,
    )
```

```python
import jax
import jax.numpy as jnp
import ml_dtypes
import numpy as np
from jax import lax
from jax.experimental import pallas as pl
from jax.experimental.pallas import tpu as pltpu
from jax.sharding import PartitionSpec as P

STEPS = 4
PIX = 2
TS = 16
RADIUS = 4
COURANT = 0.6
COUPLING = 0.25

LANES = 128
SUB = 8
FAR = STEPS + PIX * (RADIUS - 1)
NEAR = PIX * (RADIUS - 1)
LEFT_OVER = FAR - SUB
PAD = 2 * SUB
HALF = LANES // 2
SIDE = HALF // 2
OUT = SIDE // 2
KEEP = 8
F32 = jnp.float32
BF16 = jnp.bfloat16
WIDTHS = (FAR,) * 4 + (NEAR,) * STEPS
FIRST = tuple(sum(WIDTHS[:k]) for k in range(len(WIDTHS)))
assert sum(WIDTHS) <= HALF and FAR <= OUT and STEPS + KEEP <= OUT


def cone_weights(radius):
    reach_cells = radius - 1
    offsets = np.arange(-reach_cells, reach_cells + 1)
    distance = np.sqrt(offsets[:, None] * offsets[:, None] + offsets[None, :] * offsets[None, :])
    weights = np.maximum(radius - distance, 0.0)
    return weights / weights.sum()


def pool_matrices():
    inner = np.zeros((2, LANES, LANES), np.float32)
    for j in range(2 * LANES):
        if KEEP <= j < 2 * LANES - KEEP:
            inner[j // LANES, j % LANES, j // PIX] = 1.0
    edge = np.zeros((LANES, 4 * LANES), np.float32)
    for lane in range(LANES):
        layer, at = lane // HALF, lane % HALF
        col = at - OUT if at < SIDE else at - SIDE + 2 * LANES - OUT
        pixel = col // PIX
        if 0 <= col < KEEP or 2 * LANES - KEEP <= col < 2 * LANES:
            edge[lane, 2 * layer * LANES + pixel] = 1.0
        elif -NEAR <= col < 0 or 2 * LANES <= col < 2 * LANES + NEAR:
            edge[lane, (2 * layer + 1) * LANES + pixel % LANES] = 1.0
    return inner.astype(ml_dtypes.bfloat16), edge.astype(ml_dtypes.bfloat16)


def split2(value):
    high = value.astype(BF16)
    return high, (value - high.astype(F32)).astype(BF16)


def split3(value):
    high = value.astype(BF16)
    rest = value - high.astype(F32)
    mid = rest.astype(BF16)
    return high, mid, (rest - mid.astype(F32)).astype(BF16)


def dot(a, b):
    return jnp.dot(a, b, preferred_element_type=F32)


def turn(value, shift, axis):
    size = value.shape[axis]
    return pltpu.roll(value, shift % size, axis) if shift % size else value


def lanes():
    return lax.broadcasted_iota(jnp.int32, (SUB, LANES), 1)


def subs():
    return lax.broadcasted_iota(jnp.int32, (SUB, LANES), 0)


def lane_tile(k):
    return pl.ds(k * LANES, LANES)


def is_odd():
    return ((subs() * 0 + lax.axis_index("gx")) & 1) == 1


def rows_kernel(fields, eps, fwd, cross, near, hold, hold_fwd, sems):
    rows, cols = fields.shape[2], fields.shape[3]
    copies = []
    for n, at in enumerate((0, rows - PAD)):
        at_fwd = 0 if n == 0 else rows - SUB
        pairs = (
            (fields.at[:, :, pl.ds(at, PAD), :], hold.at[n, pl.ds(0, 3)]),
            (eps.at[:, pl.ds(at, PAD), :], hold.at[n, 3]),
            (fwd.at[:, :, pl.ds(at_fwd, SUB), :], hold_fwd.at[n]),
        )
        for m, (src, dst) in enumerate(pairs):
            copies.append(pltpu.make_async_copy(src, dst, sems.at[3 * n + m]))
    for copy in copies:
        copy.start()
    for copy in copies:
        copy.wait()
    odd, sub = is_odd(), subs()
    for kind in range(4):
        for layer in range(2):
            plane = 2 * kind + layer
            for k in range(cols // LANES):
                at = lane_tile(k)
                low = hold[0, kind, layer, pl.ds(0, SUB), at]
                high = hold[1, kind, layer, pl.ds(SUB, SUB), at]
                cross[plane, :, at] = jnp.where(odd, high, low)
                near[plane, :, at] = jnp.where(odd, low, high)
                rest_low = turn(hold[0, kind, layer, pl.ds(SUB, SUB), at], -LEFT_OVER, 0)
                rest_high = turn(hold[1, kind, layer, pl.ds(0, SUB), at], LEFT_OVER, 0)
                low = jnp.where(sub >= NEAR, rest_low, hold_fwd[0, kind, layer, :, at])
                high = jnp.where(sub < SUB - NEAR, rest_high, hold_fwd[1, kind, layer, :, at])
                cross[8 + plane, :, at] = jnp.where(odd, high, low)
                near[8 + plane, :, at] = jnp.where(odd, low, high)


def halo_tile(cross, near, odd, tile, kind, layer, at):
    is_above = tile < 2
    outer = tile in (0, 3)
    if outer and kind >= 4:
        return None
    plane = 2 * kind + layer + (8 if outer else 0)
    a, b = near[plane, :, at], cross[plane, :, at]
    value = jnp.where(odd, a, b) if is_above else jnp.where(odd, b, a)
    if outer:
        value = turn(value, -LEFT_OVER if is_above else LEFT_OVER, 0)
    return value


def core_tile(fields, eps, fwd, at, kind, layer, cols):
    if kind < 3:
        return fields[kind, layer, at, cols]
    if kind == 3:
        return eps[layer, at, cols]
    return fwd[kind - 4, layer, at, cols]


def pack_tile(load, lane, right):
    total = jnp.zeros((SUB, LANES), F32)
    for kind, width in enumerate(WIDTHS):
        for layer in range(2):
            value = load(kind, layer)
            if value is None:
                continue
            first = FIRST[kind] + HALF * layer
            value = turn(value, first + width if right else first, 1)
            total = jnp.where((lane >= first) & (lane < first + width), value, total)
    return total


def cols_kernel(fields, eps, fwd, left, right):
    rows, cols = fields.shape[2], fields.shape[3]
    lane = lanes()

    def tile(t, carry):
        at = pl.ds(pl.multiple_of(t * SUB, SUB), SUB)
        out_at = pl.ds(pl.multiple_of(t * SUB + PAD, SUB), SUB)
        for out, lo, is_right in ((left, 0, False), (right, cols - LANES, True)):
            out[out_at, :] = pack_tile(
                lambda kind, layer: core_tile(fields, eps, fwd, at, kind, layer, pl.ds(lo, LANES)),
                lane, is_right,
            )
        return carry

    lax.fori_loop(0, rows // SUB, tile, 0, unroll=4)
    zero = jnp.zeros((PAD, LANES), F32)
    for out in (left, right):
        out[pl.ds(0, PAD), :] = zero
        out[pl.ds(PAD + rows, PAD), :] = zero


def corners_kernel(left_in, right_in, cross, near, left, right):
    rows, cols = left.shape[0] - 2 * PAD, cross.shape[2]
    lane, odd = lanes(), is_odd()
    for out, core, lo, is_right in ((left, left_in, 0, False), (right, right_in, cols - LANES, True)):
        out[pl.ds(PAD, rows), :] = core[pl.ds(PAD, rows), :]
        for tile in range(4):
            base = tile * SUB if tile < 2 else PAD + rows + (tile - 2) * SUB
            out[pl.ds(base, SUB), :] = pack_tile(
                lambda kind, layer: halo_tile(cross, near, odd, tile, kind, layer, pl.ds(lo, LANES)),
                lane, is_right,
            )


def side_kernel(capacity, mon_x, mon_y, amp, mask, owner, src, src_edge, place):
    _, _, ext_rows, cols = src.shape
    rows = ext_rows - 2 * PAD
    channels = mon_x.shape[1]
    row = mon_x[...] - lax.axis_index("gx") * rows + PAD
    col = mon_y[...] - lax.axis_index("gy") * cols
    in_left = (col >= -OUT) & (col < OUT)
    in_right = (col >= cols - OUT) & (col < cols + OUT)
    edge = jnp.where(in_left, col + OUT, jnp.where(in_right, col - cols + OUT + SIDE, -LANES))
    layer = lax.broadcasted_iota(jnp.int32, (1, channels), 1) & 1
    edge = edge + HALF * layer
    inside = jnp.where((col >= 0) & (col < cols), col, -1)
    one_y = lax.broadcasted_iota(jnp.int32, (cols, channels), 0) == inside
    one_e = lax.broadcasted_iota(jnp.int32, (LANES, channels), 0) == edge
    one_y = jnp.where(one_y, 1.0, 0.0).astype(BF16)
    one_e = jnp.where(one_e, 1.0, 0.0).astype(BF16)
    one_y = jnp.concatenate([one_y] * 3, axis=1)
    one_e = jnp.concatenate([one_e] * 3, axis=1)
    one_x = lax.broadcasted_iota(jnp.int32, (ext_rows, channels), 0) == row
    one_x = jnp.where(one_x, 1.0, 0.0).astype(F32)
    nt = (((1,), (1,)), ((), ()))
    for step in range(STEPS):
        parts = [part.astype(F32) for part in split3(amp[pl.ds(step, 1), :])]
        lhs = jnp.concatenate([one_x * part for part in parts], axis=1)
        src_edge[step] = lax.dot_general(lhs.astype(BF16), one_e, nt, preferred_element_type=F32)
        layer_wide = jnp.concatenate([layer] * 3, axis=1)
        for which in range(2):
            some = jnp.where(layer_wide == which, lhs, 0.0).astype(BF16)
            src[step, which] = lax.dot_general(some, one_y, nt, preferred_element_type=F32)
    tiles = owner.shape[1]
    own = owner[...].astype(F32)
    own_wide = jnp.broadcast_to(own, (tiles, tiles))
    earlier = lax.broadcasted_iota(jnp.int32, (tiles, tiles), 0) < lax.broadcasted_iota(
        jnp.int32, (tiles, tiles), 1
    )
    same = (own_wide.T == own_wide) & earlier
    slot = jnp.sum(jnp.where(same, 1.0, 0.0), axis=0, keepdims=True)
    dest = owner[...] * capacity + slot.astype(jnp.int32)
    dest = jnp.where(mask[...] != 0, dest, -1)
    hit = lax.broadcasted_iota(jnp.int32, place.shape, 0) == dest
    place[...] = jnp.where(hit, 1.0, 0.0).astype(BF16)


def yee(bufs, keys, eps_of, change_of, src_of, grad, coef_x, coef_first, next_col, prev_col, other):
    n_tiles = (bufs[0].shape[-2] - 2 * SUB) // SUB
    for step in range(STEPS):
        old, new = ((0, 1), (1, 0), (0, 1), (1, 2))[step]
        old, new = bufs[old], bufs[new]
        low = 0 if step < 2 else 1
        high = n_tiles if step == 0 else n_tiles - 1
        for t in range(low, high):
            at = pl.ds(SUB + t * SUB, SUB)
            under = pl.ds(SUB + t * SUB + 1, SUB)
            over = pl.ds(SUB + t * SUB - 1, SUB)
            coef_y = coef_first if t < PAD // SUB else COURANT
            e = {key: old[(0,) + key + (at, slice(None))] for key in keys}
            e_right = next_col(e)
            hx, hy = {}, {}
            for key in keys:
                hx[key] = old[(1,) + key + (at, slice(None))] + coef_x * (e_right[key] - e[key])
                below = old[(0,) + key + (under, slice(None))]
                hy[key] = old[(2,) + key + (at, slice(None))] - coef_y * (below - e[key])
                new[(1,) + key + (at, slice(None))] = hx[key]
                new[(2,) + key + (at, slice(None))] = hy[key]
            hx_left = prev_col(hx)
            for key in keys:
                hy_above = new[(2,) + key + (over, slice(None))]
                curl = (hy[key] - hy_above) - (hx[key] - hx_left[key])
                curl = curl + COUPLING * (other(e, key) - e[key])
                value = e[key] - eps_of(key, t) * curl + src_of(step, key, t)
                new[(0,) + key + (at, slice(None))] = value
                if 1 <= t < n_tiles - 1:
                    change = value * change_of(step, key, t)
                    where = key + (pl.ds(t * SUB, SUB), slice(None))
                    grad[where] = -change if step == 0 else grad[where] - change


def coef_above():
    return jnp.where((subs() * 0 + lax.axis_index("gx")) > 0, COURANT, 0.0).astype(F32)


def clear_rims(buf):
    size = buf.shape[-2]
    zero = jnp.zeros(buf.shape[:-2] + (SUB, LANES), F32)
    lead = (slice(None),) * (len(buf.shape) - 2)
    buf[lead + (pl.ds(0, SUB), slice(None))] = zero
    buf[lead + (pl.ds(size - SUB, SUB), slice(None))] = zero


def row_pairs(ref, lead, count):
    even = ref[lead + (pl.ds(0, count, stride=PIX), slice(None))]
    return even + ref[lead + (pl.ds(1, count, stride=PIX), slice(None))]


def inner_kernel(fields, eps, fwd, cross, near, src, mats, last, pooled, base, a, b, e, g):
    rows, cols = fields.shape[2], fields.shape[3]
    n_tiles = (rows + 2 * PAD) // SUB
    n_lanes = cols // LANES
    lane, odd = lanes(), is_odd()
    halo_of = {0: 0, 1: 1, n_tiles - 2: 2, n_tiles - 1: 3}

    def load(kind, layer, t, k):
        if t in halo_of:
            return halo_tile(cross, near, odd, halo_of[t], kind, layer, lane_tile(k))
        return core_tile(fields, eps, fwd, pl.ds(t * SUB - PAD, SUB), kind, layer, lane_tile(k))

    for buf in (a, b, last):
        clear_rims(buf)
    for t in range(n_tiles):
        for layer in range(2):
            for k in range(n_lanes):
                for kind in range(3):
                    a[kind, layer, k, pl.ds(SUB + t * SUB, SUB), :] = load(kind, layer, t, k)
                e[layer, k, pl.ds(t * SUB, SUB), :] = COURANT * load(3, layer, t, k)

    at_end, at_start = lane == LANES - 1, lane == 0
    keys = [(layer, k) for layer in range(2) for k in range(n_lanes)]

    def next_col(values):
        moved = {key: turn(value, -1, 1) for key, value in values.items()}
        return {
            (l, k): jnp.where(at_end, moved[l, (k + 1) % n_lanes], moved[l, k]) for l, k in keys
        }

    def prev_col(values):
        moved = {key: turn(value, 1, 1) for key, value in values.items()}
        return {
            (l, k): jnp.where(at_start, moved[l, (k - 1) % n_lanes], moved[l, k]) for l, k in keys
        }

    yee(
        (a, b, last), keys,
        lambda key, t: e[key + (pl.ds(t * SUB, SUB), slice(None))],
        lambda step, key, t: load(4 + step, key[0], t, key[1]),
        lambda step, key, t: src[step, key[0], pl.ds(t * SUB, SUB), lane_tile(key[1])],
        g, COURANT, coef_above(), next_col, prev_col,
        lambda values, key: values[1 - key[0], key[1]],
    )
    for layer in range(2):
        total = None
        for k in range(n_lanes):
            for part in split2(row_pairs(g, (layer, k), n_tiles * SUB // PIX)):
                term = dot(part, mats[k])
                total = term if total is None else total + term
        pooled[layer] = total

    spot = lane & (HALF - 1)
    for t in range(n_tiles):
        for kind in range(4 + STEPS):
            if kind >= 4 and t in (0, n_tiles - 1):
                continue
            total = jnp.zeros((SUB, LANES), F32)
            for layer in range(2):
                mine = (lane >= HALF * layer) & (lane < HALF * (layer + 1))
                low = turn(load(kind, layer, t, 0), HALF * layer + OUT, 1)
                high = turn(load(kind, layer, t, n_lanes - 1), HALF * layer + SIDE + OUT, 1)
                total = jnp.where(mine & (spot < SIDE), low, total)
                total = jnp.where(mine & (spot >= SIDE), high, total)
            base[kind, pl.ds(t * SUB, SUB), :] = total


def edge_kernel(
    last, pooled_in, base, from_left, from_right, src, place, mats, out_fields, out_slots,
    a, b, c, e, d, g, pooled, merged, sem,
):
    rows, cols = merged.shape[2], merged.shape[3]
    n_tiles = (rows + 2 * PAD) // SUB
    n_lanes = cols // LANES
    lane = lanes()
    spot = lane & (HALF - 1)
    is_left, is_right = spot < OUT, spot >= HALF - OUT

    for buf in (a, b, c):
        clear_rims(buf)
    for t in range(n_tiles):
        at = pl.ds(t * SUB, SUB)
        high, low = from_left[at, :], from_right[at, :]
        for kind, width in enumerate(WIDTHS):
            if kind >= 4 and t in (0, n_tiles - 1):
                continue
            value = jnp.where(is_left, turn(high, OUT - width - FIRST[kind], 1), base[kind, at, :])
            value = jnp.where(is_right, turn(low, HALF - OUT - FIRST[kind], 1), value)
            if kind < 3:
                a[kind, pl.ds(SUB + t * SUB, SUB), :] = value
            elif kind == 3:
                e[at, :] = COURANT * value
            else:
                d[kind - 4, at, :] = value

    before = (lax.axis_index("gy") + lane * 0) > 0
    coef_x = jnp.where(before | (spot >= OUT), COURANT, 0.0).astype(F32)
    yee(
        (a, b, c), [()],
        lambda key, t: e[pl.ds(t * SUB, SUB), :],
        lambda step, key, t: d[step, pl.ds(t * SUB, SUB), :],
        lambda step, key, t: src[step, pl.ds(t * SUB, SUB), :],
        g, coef_x, coef_above(),
        lambda values: {(): turn(values[()], -1, 1)},
        lambda values: {(): turn(values[()], 1, 1)},
        lambda values, key: turn(values[()], HALF, 1),
    )

    for t in range(PAD // SUB, n_tiles - PAD // SUB):
        at, out_at = pl.ds(SUB + t * SUB, SUB), pl.ds(t * SUB - PAD, SUB)
        for kind in range(3):
            edge = c[kind, at, :]
            for layer in range(2):
                for k in range(n_lanes):
                    value = last[kind, layer, k, at, :]
                    if k == 0:
                        value = jnp.where(lane < KEEP, turn(edge, -HALF * layer - OUT, 1), value)
                    if k == n_lanes - 1:
                        value = jnp.where(
                            lane >= LANES - KEEP, turn(edge, -HALF * layer - SIDE - OUT, 1), value
                        )
                    merged[kind, layer, out_at, lane_tile(k)] = value
    copy = pltpu.make_async_copy(merged, out_fields, sem)
    copy.start()

    high, low = split2(row_pairs(g, (), n_tiles * SUB // PIX))
    edge = dot(high, mats[...]) + dot(low, mats[...])
    for layer in range(2):
        pooled[layer, 0] = pooled_in[layer] + edge[:, 2 * layer * LANES : (2 * layer + 1) * LANES]
        pooled[layer, 1] = edge[:, (2 * layer + 1) * LANES : (2 * layer + 2) * LANES]

    weights = cone_weights(RADIUS)
    reach = RADIUS - 1
    out_pix = rows // PIX
    first = PAD // PIX
    lane_wide = lax.broadcasted_iota(jnp.int32, (out_pix, LANES), 1)
    blocks = []
    for layer in range(2):
        sums = []
        for part in range(2):
            at = [pooled[layer, part, pl.ds(first + s, out_pix), :] for s in range(-reach, reach + 1)]
            sums.append([at[reach]] + [at[reach + s] + at[reach - s] for s in range(1, reach + 1)])
        total = None
        for shift in range(reach + 1):
            mixed = []
            for part in range(2):
                value = None
                for s in range(reach + 1):
                    weight = float(weights[reach + s, reach + shift])
                    if weight > 0.0:
                        term = weight * sums[part][s]
                        value = term if value is None else value + term
                mixed.append(value)
            if shift == 0:
                total = mixed[0]
            else:
                total = total + turn(jnp.where(lane_wide < shift, mixed[1], mixed[0]), -shift, 1)
                total = total + turn(
                    jnp.where(lane_wide >= LANES - shift, mixed[1], mixed[0]), shift, 1
                )
        blocks.append(total)

    span = TS // PIX
    tile_rows = out_pix // span
    x = jnp.stack([block.reshape(tile_rows, span, LANES) for block in blocks], axis=1)
    x = x.reshape(tile_rows * 2, span, LANES)
    group = lax.broadcasted_iota(jnp.int32, x.shape, 2) // span
    row = lax.broadcasted_iota(jnp.int32, x.shape, 1)
    for bit in (1, 2, 4):
        row_on, lane_on = (row & bit) != 0, (group & bit) != 0
        ahead = turn(turn(x, -bit, 1), bit * span, 2)
        behind = turn(turn(x, bit, 1), -bit * span, 2)
        x = jnp.where(row_on == lane_on, x, jnp.where(lane_on, ahead, behind))
    x = x.reshape(tile_rows, 2, span, LANES)
    even, odd = x[:, 0], x[:, 1]
    upper = lax.broadcasted_iota(jnp.int32, even.shape, 2) >= HALF
    new_even = jnp.where(upper, turn(odd, HALF, 2), even)
    new_odd = jnp.where(upper, odd, turn(even, HALF, 2))
    vals = jnp.stack([new_even, new_odd], axis=1).reshape(tile_rows * 2 * span, LANES)
    high, low = split2(vals)
    out_slots[...] = dot(place[...], high) + dot(place[...], low)
    copy.wait()


def vmem():
    return pl.BlockSpec(memory_space=pltpu.VMEM)


def shape(*dims, dtype=F32):
    return jax.ShapeDtypeStruct(dims, dtype)


def call(kernel, outs, n_in, *, in_space=pltpu.VMEM, out_specs=None, scratch=(), flops=0, size=0):
    return pl.pallas_call(
        kernel,
        out_shape=outs,
        in_specs=[pl.BlockSpec(memory_space=in_space)] * n_in,
        out_specs=out_specs or tuple(vmem() for _ in outs),
        scratch_shapes=list(scratch),
        compiler_params=pltpu.CompilerParams(vmem_limit_bytes=40 * 1024 * 1024),
        cost_estimate=pl.CostEstimate(flops=flops, bytes_accessed=size, transcendentals=0),
    )


def on_device(adj_fields, inv_eps, fwd_diff, mon_x, mon_y, mon_amp, design_mask, tile_owner):
    rows, cols = adj_fields.shape[2], adj_fields.shape[3]
    assert cols == 2 * LANES and rows % TS == 0
    gx_count, gy_count = lax.axis_size("gx"), lax.axis_size("gy")
    owners = gx_count * gy_count
    tiles = (rows // TS) * (cols // TS)
    width = 2 * (TS // PIX) ** 2
    assert width == LANES
    capacity = max(8, 2 * tiles // owners)
    ext_rows = rows + 2 * PAD
    n_lanes = cols // LANES
    cells = rows * cols
    blocks = (adj_fields, inv_eps, fwd_diff)
    inner_mats, edge_mats = pool_matrices()

    strip = shape(16, SUB, cols)
    cross, near = call(
        rows_kernel, (strip, strip), 3, in_space=pltpu.HBM,
        scratch=(
            pltpu.VMEM((2, 4, 2, PAD, cols), F32),
            pltpu.VMEM((2, STEPS, 2, SUB, cols), F32),
            pltpu.SemaphoreType.DMA((6,)),
        ),
        size=2**20,
    )(*blocks)

    def pairs(start):
        some = [(i, i + 1) for i in range(start, gx_count - 1, 2)]
        return some + [(j, i) for i, j in some]

    cross = lax.ppermute(cross, "gx", pairs(1))
    near = lax.ppermute(near, "gx", pairs(0))

    packed = shape(ext_rows, LANES)
    left, right = call(cols_kernel, (packed, packed), 3, flops=16 * cells, size=64 * cells)(*blocks)

    channels = mon_x.shape[0]
    src, src_edge, place = call(
        lambda *refs: side_kernel(capacity, *refs),
        (
            shape(STEPS, 2, ext_rows, cols),
            shape(STEPS, ext_rows, LANES),
            shape(owners * capacity, tiles, dtype=BF16),
        ),
        5,
        flops=16 * ext_rows * (cols + LANES) * 3 * channels,
        size=32 * cells,
    )(
        mon_x.reshape(1, channels),
        mon_y.reshape(1, channels),
        mon_amp,
        design_mask.reshape(1, tiles),
        tile_owner.reshape(1, tiles),
    )

    left, right = call(corners_kernel, (packed, packed), 4, flops=cells, size=8 * ext_rows * LANES)(
        left, right, cross, near
    )
    up = [(i, i + 1) for i in range(gy_count - 1)]
    from_left = lax.ppermute(right, "gy", up)
    from_right = lax.ppermute(left, "gy", [(j, i) for i, j in up])

    state = (3, 2, n_lanes, ext_rows + 2 * SUB, LANES)
    last, pooled, base = call(
        inner_kernel,
        (shape(*state), shape(2, ext_rows // PIX, LANES), shape(4 + STEPS, ext_rows, LANES)),
        7,
        scratch=(
            pltpu.VMEM(state, F32),
            pltpu.VMEM(state, F32),
            pltpu.VMEM((2, n_lanes, ext_rows, LANES), F32),
            pltpu.VMEM((2, n_lanes, ext_rows, LANES), F32),
        ),
        flops=200 * cells,
        size=96 * cells,
    )(*blocks, cross, near, src, inner_mats)

    edge_state = (3, ext_rows + 2 * SUB, LANES)
    fields, outgoing = call(
        edge_kernel,
        (shape(3, 2, rows, cols), shape(owners * capacity, width)),
        8,
        out_specs=(pl.BlockSpec(memory_space=pl.ANY), vmem()),
        scratch=(
            pltpu.VMEM(edge_state, F32),
            pltpu.VMEM(edge_state, F32),
            pltpu.VMEM(edge_state, F32),
            pltpu.VMEM((ext_rows, LANES), F32),
            pltpu.VMEM((STEPS, ext_rows, LANES), F32),
            pltpu.VMEM((ext_rows, LANES), F32),
            pltpu.VMEM((2, 2, ext_rows // PIX, LANES), F32),
            pltpu.VMEM((3, 2, rows, cols), F32),
            pltpu.SemaphoreType.DMA,
        ),
        flops=100 * cells,
        size=32 * cells,
    )(last, pooled, base, from_left, from_right, src_edge, place, edge_mats)

    outgoing = outgoing.reshape(owners, capacity, width)
    incoming = lax.all_to_all(outgoing, ("gx", "gy"), split_axis=0, concat_axis=0, tiled=True)
    return fields, incoming[None]


def solution(mesh):
    placed = (
        P(None, None, ("parts", "gx"), "gy"),
        P(None, ("parts", "gx"), "gy"),
        P(None, None, ("parts", "gx"), "gy"),
        P("parts"),
        P("parts"),
        P(None, "parts"),
        P(("parts", "gx"), "gy", None),
        P(("parts", "gx"), "gy", None, None),
    )
    return jax.shard_map(
        on_device,
        mesh=mesh,
        in_specs=placed,
        out_specs=(
            P(None, None, ("parts", "gx"), "gy"),
            P(("parts", "gx", "gy"), None, None, None),
        ),
        check_vma=False,
    )
```

```python
import jax
import jax.numpy as jnp
import ml_dtypes
import numpy as np
from jax import lax
from jax.experimental import pallas as pl
from jax.experimental.pallas import tpu as pltpu
from jax.sharding import PartitionSpec as P

STEPS = 4
PIX = 2
TS = 16
RADIUS = 4
COURANT = 0.6
COUPLING = 0.25

LANES = 128
SUB = 8
FAR = STEPS + PIX * (RADIUS - 1)
NEAR = PIX * (RADIUS - 1)
LEFT_OVER = FAR - SUB
PAD = 2 * SUB
HALF = LANES // 2
SIDE = HALF // 2
OUT = SIDE // 2
KEEP = 8
F32 = jnp.float32
BF16 = jnp.bfloat16
WIDTHS = (FAR,) * 4 + (NEAR,) * STEPS
FIRST = tuple(sum(WIDTHS[:k]) for k in range(len(WIDTHS)))
assert sum(WIDTHS) <= HALF and FAR <= OUT and STEPS + KEEP <= OUT


def cone_weights(radius):
    reach_cells = radius - 1
    offsets = np.arange(-reach_cells, reach_cells + 1)
    distance = np.sqrt(offsets[:, None] * offsets[:, None] + offsets[None, :] * offsets[None, :])
    weights = np.maximum(radius - distance, 0.0)
    return weights / weights.sum()


def pool_matrices():
    inner = np.zeros((2, LANES, LANES), np.float32)
    for j in range(2 * LANES):
        if KEEP <= j < 2 * LANES - KEEP:
            inner[j // LANES, j % LANES, j // PIX] = 1.0
    edge = np.zeros((LANES, 4 * LANES), np.float32)
    for lane in range(LANES):
        layer, at = lane // HALF, lane % HALF
        col = at - OUT if at < SIDE else at - SIDE + 2 * LANES - OUT
        pixel = col // PIX
        if 0 <= col < KEEP or 2 * LANES - KEEP <= col < 2 * LANES:
            edge[lane, 2 * layer * LANES + pixel] = 1.0
        elif -NEAR <= col < 0 or 2 * LANES <= col < 2 * LANES + NEAR:
            edge[lane, (2 * layer + 1) * LANES + pixel % LANES] = 1.0
    return inner.astype(ml_dtypes.bfloat16), edge.astype(ml_dtypes.bfloat16)


def split2(value):
    high = value.astype(BF16)
    return high, (value - high.astype(F32)).astype(BF16)


def split3(value):
    high = value.astype(BF16)
    rest = value - high.astype(F32)
    mid = rest.astype(BF16)
    return high, mid, (rest - mid.astype(F32)).astype(BF16)


def dot(a, b):
    return jnp.dot(a, b, preferred_element_type=F32)


def turn(value, shift, axis):
    size = value.shape[axis]
    return pltpu.roll(value, shift % size, axis) if shift % size else value


def lanes():
    return lax.broadcasted_iota(jnp.int32, (SUB, LANES), 1)


def subs():
    return lax.broadcasted_iota(jnp.int32, (SUB, LANES), 0)


def lane_tile(k):
    return pl.ds(k * LANES, LANES)


def is_odd(axis):
    return ((subs() * 0 + lax.axis_index(axis)) & 1) == 1


def rows_kernel(fields, eps, fwd, cross, near, hold, hold_fwd, sems):
    rows, cols = fields.shape[2], fields.shape[3]
    copies = []
    for n, at in enumerate((0, rows - PAD)):
        at_fwd = 0 if n == 0 else rows - SUB
        pairs = (
            (fields.at[:, :, pl.ds(at, PAD), :], hold.at[n, pl.ds(0, 3)]),
            (eps.at[:, pl.ds(at, PAD), :], hold.at[n, 3]),
            (fwd.at[:, :, pl.ds(at_fwd, SUB), :], hold_fwd.at[n]),
        )
        for m, (src, dst) in enumerate(pairs):
            copies.append(pltpu.make_async_copy(src, dst, sems.at[3 * n + m]))
    for copy in copies:
        copy.start()
    for copy in copies:
        copy.wait()
    odd, sub = is_odd("gx"), subs()
    for kind in range(4):
        for layer in range(2):
            plane = 2 * kind + layer
            for k in range(cols // LANES):
                at = lane_tile(k)
                low = hold[0, kind, layer, pl.ds(0, SUB), at]
                high = hold[1, kind, layer, pl.ds(SUB, SUB), at]
                cross[plane, :, at] = jnp.where(odd, high, low)
                near[plane, :, at] = jnp.where(odd, low, high)
                rest_low = turn(hold[0, kind, layer, pl.ds(SUB, SUB), at], -LEFT_OVER, 0)
                rest_high = turn(hold[1, kind, layer, pl.ds(0, SUB), at], LEFT_OVER, 0)
                low = jnp.where(sub >= NEAR, rest_low, hold_fwd[0, kind, layer, :, at])
                high = jnp.where(sub < SUB - NEAR, rest_high, hold_fwd[1, kind, layer, :, at])
                cross[8 + plane, :, at] = jnp.where(odd, high, low)
                near[8 + plane, :, at] = jnp.where(odd, low, high)


def halo_tile(cross, near, odd, tile, kind, layer, at):
    is_above = tile < 2
    outer = tile in (0, 3)
    if outer and kind >= 4:
        return None
    plane = 2 * kind + layer + (8 if outer else 0)
    a, b = near[plane, :, at], cross[plane, :, at]
    value = jnp.where(odd, a, b) if is_above else jnp.where(odd, b, a)
    if outer:
        value = turn(value, -LEFT_OVER if is_above else LEFT_OVER, 0)
    return value


def core_tile(fields, eps, fwd, at, kind, layer, cols):
    if kind < 3:
        return fields[kind, layer, at, cols]
    if kind == 3:
        return eps[layer, at, cols]
    return fwd[kind - 4, layer, at, cols]


def pack_tile(load, lane, right):
    total = jnp.zeros((SUB, LANES), F32)
    for kind, width in enumerate(WIDTHS):
        for layer in range(2):
            value = load(kind, layer)
            if value is None:
                continue
            first = FIRST[kind] + HALF * layer
            value = turn(value, first + width if right else first, 1)
            total = jnp.where((lane >= first) & (lane < first + width), value, total)
    return total


def edge_tile(load, kind, lane, n_lanes):
    spot = lane & (HALF - 1)
    total = None
    for layer in range(2):
        low = turn(load(kind, layer, 0), HALF * layer + OUT, 1)
        high = turn(load(kind, layer, n_lanes - 1), HALF * layer + SIDE + OUT, 1)
        value = jnp.where(spot < SIDE, low, high)
        total = value if total is None else jnp.where(lane < HALF, total, value)
    return total


def cols_kernel(fields, eps, fwd, cross, near, base):
    rows, cols = fields.shape[2], fields.shape[3]
    n_lanes = cols // LANES
    lane, odd = lanes(), is_odd("gy")

    def tile(t, carry):
        at = pl.ds(pl.multiple_of(t * SUB, SUB), SUB)
        out_at = pl.ds(pl.multiple_of(t * SUB + PAD, SUB), SUB)

        def load(kind, layer, k):
            return core_tile(fields, eps, fwd, at, kind, layer, lane_tile(k))

        left = pack_tile(lambda kind, layer: load(kind, layer, 0), lane, False)
        right = pack_tile(lambda kind, layer: load(kind, layer, n_lanes - 1), lane, True)
        cross[out_at, :] = jnp.where(odd, right, left)
        near[out_at, :] = jnp.where(odd, left, right)
        for kind in range(4 + STEPS):
            base[kind, out_at, :] = edge_tile(load, kind, lane, n_lanes)
        return carry

    lax.fori_loop(0, rows // SUB, tile, 0, unroll=4)
    zero = jnp.zeros((PAD, LANES), F32)
    for out in (cross, near) + tuple(base.at[kind] for kind in range(4 + STEPS)):
        out[pl.ds(0, PAD), :] = zero
        out[pl.ds(PAD + rows, PAD), :] = zero


def corners_kernel(cross_in, near_in, cross_rows, near_rows, cross, near):
    rows, cols = cross.shape[0] - 2 * PAD, cross_rows.shape[2]
    lane, odd, odd_col = lanes(), is_odd("gx"), is_odd("gy")
    core = pl.ds(PAD, rows)
    cross[core, :] = cross_in[core, :]
    near[core, :] = near_in[core, :]
    for tile in range(4):
        at = pl.ds(tile * SUB if tile < 2 else PAD + rows + (tile - 2) * SUB, SUB)
        left, right = (
            pack_tile(
                lambda kind, layer: halo_tile(
                    cross_rows, near_rows, odd, tile, kind, layer, pl.ds(lo, LANES)
                ),
                lane, is_right,
            )
            for lo, is_right in ((0, False), (cols - LANES, True))
        )
        cross[at, :] = jnp.where(odd_col, right, left)
        near[at, :] = jnp.where(odd_col, left, right)


def prep_kernel(
    capacity, fields, eps, fwd, mon_x, mon_y, amp, mask, owner, cross, near, base, src, src_edge, place
):
    cols_kernel(fields, eps, fwd, cross, near, base)
    side_kernel(capacity, mon_x, mon_y, amp, mask, owner, src, src_edge, place)


def side_kernel(capacity, mon_x, mon_y, amp, mask, owner, src, src_edge, place):
    _, _, ext_rows, cols = src.shape
    rows = ext_rows - 2 * PAD
    channels = mon_x.shape[1]
    row = mon_x[...] - lax.axis_index("gx") * rows + PAD
    col = mon_y[...] - lax.axis_index("gy") * cols
    in_left = (col >= -OUT) & (col < OUT)
    in_right = (col >= cols - OUT) & (col < cols + OUT)
    edge = jnp.where(in_left, col + OUT, jnp.where(in_right, col - cols + OUT + SIDE, -LANES))
    layer = lax.broadcasted_iota(jnp.int32, (1, channels), 1) & 1
    edge = edge + HALF * layer
    inside = jnp.where((col >= 0) & (col < cols), col, -1)
    one_y = lax.broadcasted_iota(jnp.int32, (cols, channels), 0) == inside
    one_e = lax.broadcasted_iota(jnp.int32, (LANES, channels), 0) == edge
    one_y = jnp.where(one_y, 1.0, 0.0).astype(BF16)
    one_e = jnp.where(one_e, 1.0, 0.0).astype(BF16)
    one_y = jnp.concatenate([one_y] * 3, axis=1)
    one_e = jnp.concatenate([one_e] * 3, axis=1)
    one_x = lax.broadcasted_iota(jnp.int32, (ext_rows, channels), 0) == row
    one_x = jnp.where(one_x, 1.0, 0.0).astype(F32)
    nt = (((1,), (1,)), ((), ()))
    for step in range(STEPS):
        parts = [part.astype(F32) for part in split3(amp[pl.ds(step, 1), :])]
        lhs = jnp.concatenate([one_x * part for part in parts], axis=1)
        src_edge[step] = lax.dot_general(lhs.astype(BF16), one_e, nt, preferred_element_type=F32)
        layer_wide = jnp.concatenate([layer] * 3, axis=1)
        for which in range(2):
            some = jnp.where(layer_wide == which, lhs, 0.0).astype(BF16)
            src[step, which] = lax.dot_general(some, one_y, nt, preferred_element_type=F32)
    tiles = owner.shape[1]
    own = owner[...].astype(F32)
    own_wide = jnp.broadcast_to(own, (tiles, tiles))
    earlier = lax.broadcasted_iota(jnp.int32, (tiles, tiles), 0) < lax.broadcasted_iota(
        jnp.int32, (tiles, tiles), 1
    )
    same = (own_wide.T == own_wide) & earlier
    slot = jnp.sum(jnp.where(same, 1.0, 0.0), axis=0, keepdims=True)
    dest = owner[...] * capacity + slot.astype(jnp.int32)
    dest = jnp.where(mask[...] != 0, dest, -1)
    hit = lax.broadcasted_iota(jnp.int32, place.shape, 0) == dest
    place[...] = jnp.where(hit, 1.0, 0.0).astype(BF16)


def yee(bufs, keys, eps_of, change_of, src_of, grad, coef_x, coef_first, next_col, prev_col, other):
    n_tiles = (bufs[0].shape[-2] - 2 * SUB) // SUB
    for step in range(STEPS):
        old, new = ((0, 1), (1, 0), (0, 1), (1, 2))[step]
        old, new = bufs[old], bufs[new]
        low = 0 if step < 2 else 1
        high = n_tiles if step == 0 else n_tiles - 1
        for t in range(low, high):
            at = pl.ds(SUB + t * SUB, SUB)
            under = pl.ds(SUB + t * SUB + 1, SUB)
            over = pl.ds(SUB + t * SUB - 1, SUB)
            coef_y = coef_first if t < PAD // SUB else COURANT
            e = {key: old[(0,) + key + (at, slice(None))] for key in keys}
            e_right = next_col(e)
            hx, hy = {}, {}
            for key in keys:
                hx[key] = old[(1,) + key + (at, slice(None))] + coef_x * (e_right[key] - e[key])
                below = old[(0,) + key + (under, slice(None))]
                hy[key] = old[(2,) + key + (at, slice(None))] - coef_y * (below - e[key])
                new[(1,) + key + (at, slice(None))] = hx[key]
                new[(2,) + key + (at, slice(None))] = hy[key]
            hx_left = prev_col(hx)
            for key in keys:
                hy_above = new[(2,) + key + (over, slice(None))]
                curl = (hy[key] - hy_above) - (hx[key] - hx_left[key])
                curl = curl + COUPLING * (other(e, key) - e[key])
                value = e[key] - eps_of(key, t) * curl + src_of(step, key, t)
                new[(0,) + key + (at, slice(None))] = value
                if 1 <= t < n_tiles - 1:
                    change = value * change_of(step, key, t)
                    where = key + (pl.ds(t * SUB, SUB), slice(None))
                    grad[where] = -change if step == 0 else grad[where] - change


def coef_above():
    return jnp.where((subs() * 0 + lax.axis_index("gx")) > 0, COURANT, 0.0).astype(F32)


def clear_rims(buf):
    size = buf.shape[-2]
    zero = jnp.zeros(buf.shape[:-2] + (SUB, LANES), F32)
    lead = (slice(None),) * (len(buf.shape) - 2)
    buf[lead + (pl.ds(0, SUB), slice(None))] = zero
    buf[lead + (pl.ds(size - SUB, SUB), slice(None))] = zero


def row_pairs(ref, lead, count):
    even = ref[lead + (pl.ds(0, count, stride=PIX), slice(None))]
    return even + ref[lead + (pl.ds(1, count, stride=PIX), slice(None))]


def inner_kernel(fields, eps, fwd, cross, near, src, mats, base_in, last, pooled, base, a, b, e, g):
    rows, cols = fields.shape[2], fields.shape[3]
    n_tiles = (rows + 2 * PAD) // SUB
    n_lanes = cols // LANES
    lane, odd = lanes(), is_odd("gx")
    halo_of = {0: 0, 1: 1, n_tiles - 2: 2, n_tiles - 1: 3}

    def load(kind, layer, t, k):
        if t in halo_of:
            return halo_tile(cross, near, odd, halo_of[t], kind, layer, lane_tile(k))
        return core_tile(fields, eps, fwd, pl.ds(t * SUB - PAD, SUB), kind, layer, lane_tile(k))

    for buf in (a, b, last):
        clear_rims(buf)
    for t in range(n_tiles):
        for layer in range(2):
            for k in range(n_lanes):
                for kind in range(3):
                    a[kind, layer, k, pl.ds(SUB + t * SUB, SUB), :] = load(kind, layer, t, k)
                e[layer, k, pl.ds(t * SUB, SUB), :] = COURANT * load(3, layer, t, k)

    at_end, at_start = lane == LANES - 1, lane == 0
    keys = [(layer, k) for layer in range(2) for k in range(n_lanes)]

    def next_col(values):
        moved = {key: turn(value, -1, 1) for key, value in values.items()}
        return {
            (l, k): jnp.where(at_end, moved[l, (k + 1) % n_lanes], moved[l, k]) for l, k in keys
        }

    def prev_col(values):
        moved = {key: turn(value, 1, 1) for key, value in values.items()}
        return {
            (l, k): jnp.where(at_start, moved[l, (k - 1) % n_lanes], moved[l, k]) for l, k in keys
        }

    yee(
        (a, b, last), keys,
        lambda key, t: e[key + (pl.ds(t * SUB, SUB), slice(None))],
        lambda step, key, t: load(4 + step, key[0], t, key[1]),
        lambda step, key, t: src[step, key[0], pl.ds(t * SUB, SUB), lane_tile(key[1])],
        g, COURANT, coef_above(), next_col, prev_col,
        lambda values, key: values[1 - key[0], key[1]],
    )
    for layer in range(2):
        total = None
        for k in range(n_lanes):
            for part in split2(row_pairs(g, (layer, k), n_tiles * SUB // PIX)):
                term = dot(part, mats[k])
                total = term if total is None else total + term
        pooled[layer] = total

    for t in range(n_tiles):
        for kind in range(4 + STEPS):
            at = pl.ds(t * SUB, SUB)
            if t not in halo_of:
                base[kind, at, :] = base_in[kind, at, :]
            elif kind < 4 or t not in (0, n_tiles - 1):
                base[kind, at, :] = edge_tile(
                    lambda kind, layer, k: load(kind, layer, t, k), kind, lane, n_lanes
                )


def edge_kernel(
    last, pooled_in, base, cross, near, src, place, mats, out_fields, out_slots,
    a, b, c, e, d, g, pooled, merged, sem,
):
    rows, cols = merged.shape[2], merged.shape[3]
    n_tiles = (rows + 2 * PAD) // SUB
    n_lanes = cols // LANES
    lane, odd = lanes(), is_odd("gy")
    spot = lane & (HALF - 1)
    is_left, is_right = spot < OUT, spot >= HALF - OUT

    for buf in (a, b, c):
        clear_rims(buf)
    for t in range(n_tiles):
        at = pl.ds(t * SUB, SUB)
        far, close = cross[at, :], near[at, :]
        high, low = jnp.where(odd, close, far), jnp.where(odd, far, close)
        for kind, width in enumerate(WIDTHS):
            if kind >= 4 and t in (0, n_tiles - 1):
                continue
            value = jnp.where(is_left, turn(high, OUT - width - FIRST[kind], 1), base[kind, at, :])
            value = jnp.where(is_right, turn(low, HALF - OUT - FIRST[kind], 1), value)
            if kind < 3:
                a[kind, pl.ds(SUB + t * SUB, SUB), :] = value
            elif kind == 3:
                e[at, :] = COURANT * value
            else:
                d[kind - 4, at, :] = value

    before = (lax.axis_index("gy") + lane * 0) > 0
    coef_x = jnp.where(before | (spot >= OUT), COURANT, 0.0).astype(F32)
    yee(
        (a, b, c), [()],
        lambda key, t: e[pl.ds(t * SUB, SUB), :],
        lambda step, key, t: d[step, pl.ds(t * SUB, SUB), :],
        lambda step, key, t: src[step, pl.ds(t * SUB, SUB), :],
        g, coef_x, coef_above(),
        lambda values: {(): turn(values[()], -1, 1)},
        lambda values: {(): turn(values[()], 1, 1)},
        lambda values, key: turn(values[()], HALF, 1),
    )

    for t in range(PAD // SUB, n_tiles - PAD // SUB):
        at, out_at = pl.ds(SUB + t * SUB, SUB), pl.ds(t * SUB - PAD, SUB)
        for kind in range(3):
            edge = c[kind, at, :]
            for layer in range(2):
                for k in range(n_lanes):
                    value = last[kind, layer, k, at, :]
                    if k == 0:
                        value = jnp.where(lane < KEEP, turn(edge, -HALF * layer - OUT, 1), value)
                    if k == n_lanes - 1:
                        value = jnp.where(
                            lane >= LANES - KEEP, turn(edge, -HALF * layer - SIDE - OUT, 1), value
                        )
                    merged[kind, layer, out_at, lane_tile(k)] = value
    copy = pltpu.make_async_copy(merged, out_fields, sem)
    copy.start()

    high, low = split2(row_pairs(g, (), n_tiles * SUB // PIX))
    edge = dot(high, mats[...]) + dot(low, mats[...])
    for layer in range(2):
        pooled[layer, 0] = pooled_in[layer] + edge[:, 2 * layer * LANES : (2 * layer + 1) * LANES]
        pooled[layer, 1] = edge[:, (2 * layer + 1) * LANES : (2 * layer + 2) * LANES]

    weights = cone_weights(RADIUS)
    reach = RADIUS - 1
    out_pix = rows // PIX
    first = PAD // PIX
    lane_wide = lax.broadcasted_iota(jnp.int32, (out_pix, LANES), 1)
    blocks = []
    for layer in range(2):
        sums = []
        for part in range(2):
            at = [pooled[layer, part, pl.ds(first + s, out_pix), :] for s in range(-reach, reach + 1)]
            sums.append([at[reach]] + [at[reach + s] + at[reach - s] for s in range(1, reach + 1)])
        total = None
        for shift in range(reach + 1):
            mixed = []
            for part in range(2):
                value = None
                for s in range(reach + 1):
                    weight = float(weights[reach + s, reach + shift])
                    if weight > 0.0:
                        term = weight * sums[part][s]
                        value = term if value is None else value + term
                mixed.append(value)
            if shift == 0:
                total = mixed[0]
            else:
                total = total + turn(jnp.where(lane_wide < shift, mixed[1], mixed[0]), -shift, 1)
                total = total + turn(
                    jnp.where(lane_wide >= LANES - shift, mixed[1], mixed[0]), shift, 1
                )
        blocks.append(total)

    span = TS // PIX
    tile_rows = out_pix // span
    x = jnp.stack([block.reshape(tile_rows, span, LANES) for block in blocks], axis=1)
    x = x.reshape(tile_rows * 2, span, LANES)
    group = lax.broadcasted_iota(jnp.int32, x.shape, 2) // span
    row = lax.broadcasted_iota(jnp.int32, x.shape, 1)
    for bit in (1, 2, 4):
        row_on, lane_on = (row & bit) != 0, (group & bit) != 0
        ahead = turn(turn(x, -bit, 1), bit * span, 2)
        behind = turn(turn(x, bit, 1), -bit * span, 2)
        x = jnp.where(row_on == lane_on, x, jnp.where(lane_on, ahead, behind))
    x = x.reshape(tile_rows, 2, span, LANES)
    even, odd = x[:, 0], x[:, 1]
    upper = lax.broadcasted_iota(jnp.int32, even.shape, 2) >= HALF
    new_even = jnp.where(upper, turn(odd, HALF, 2), even)
    new_odd = jnp.where(upper, odd, turn(even, HALF, 2))
    vals = jnp.stack([new_even, new_odd], axis=1).reshape(tile_rows * 2 * span, LANES)
    high, low = split2(vals)
    out_slots[...] = dot(place[...], high) + dot(place[...], low)
    copy.wait()


def vmem():
    return pl.BlockSpec(memory_space=pltpu.VMEM)


def shape(*dims, dtype=F32):
    return jax.ShapeDtypeStruct(dims, dtype)


def call(kernel, outs, n_in, *, in_space=pltpu.VMEM, out_specs=None, scratch=(), flops=0, size=0):
    return pl.pallas_call(
        kernel,
        out_shape=outs,
        in_specs=[pl.BlockSpec(memory_space=in_space)] * n_in,
        out_specs=out_specs or tuple(vmem() for _ in outs),
        scratch_shapes=list(scratch),
        compiler_params=pltpu.CompilerParams(vmem_limit_bytes=40 * 1024 * 1024),
        cost_estimate=pl.CostEstimate(flops=flops, bytes_accessed=size, transcendentals=0),
    )


def on_device(adj_fields, inv_eps, fwd_diff, mon_x, mon_y, mon_amp, design_mask, tile_owner):
    rows, cols = adj_fields.shape[2], adj_fields.shape[3]
    assert cols == 2 * LANES and rows % TS == 0
    gx_count, gy_count = lax.axis_size("gx"), lax.axis_size("gy")
    owners = gx_count * gy_count
    tiles = (rows // TS) * (cols // TS)
    width = 2 * (TS // PIX) ** 2
    assert width == LANES
    capacity = max(8, 2 * tiles // owners)
    ext_rows = rows + 2 * PAD
    n_lanes = cols // LANES
    cells = rows * cols
    blocks = (adj_fields, inv_eps, fwd_diff)
    inner_mats, edge_mats = pool_matrices()

    strip = shape(16, SUB, cols)
    cross, near = call(
        rows_kernel, (strip, strip), 3, in_space=pltpu.HBM,
        scratch=(
            pltpu.VMEM((2, 4, 2, PAD, cols), F32),
            pltpu.VMEM((2, STEPS, 2, SUB, cols), F32),
            pltpu.SemaphoreType.DMA((6,)),
        ),
        size=2**20,
    )(*(pltpu.with_memory_space_constraint(block, pltpu.HBM) for block in blocks))

    def pairs(count, start):
        some = [(i, i + 1) for i in range(start, count - 1, 2)]
        return some + [(j, i) for i, j in some]

    cross = lax.ppermute(cross, "gx", pairs(gx_count, 1))
    near = lax.ppermute(near, "gx", pairs(gx_count, 0))

    packed = shape(ext_rows, LANES)
    channels = mon_x.shape[0]
    cross_cols, near_cols, base, src, src_edge, place = call(
        lambda *refs: prep_kernel(capacity, *refs),
        (
            packed,
            packed,
            shape(4 + STEPS, ext_rows, LANES),
            shape(STEPS, 2, ext_rows, cols),
            shape(STEPS, ext_rows, LANES),
            shape(owners * capacity, tiles, dtype=BF16),
        ),
        8,
        flops=16 * ext_rows * (cols + LANES) * 3 * channels,
        size=64 * cells,
    )(
        *blocks,
        mon_x.reshape(1, channels),
        mon_y.reshape(1, channels),
        mon_amp,
        design_mask.reshape(1, tiles),
        tile_owner.reshape(1, tiles),
    )
    cross_cols, near_cols = call(
        corners_kernel, (packed, packed), 4, flops=cells, size=8 * ext_rows * LANES
    )(cross_cols, near_cols, cross, near)
    cross_cols = lax.ppermute(cross_cols, "gy", pairs(gy_count, 1))
    near_cols = lax.ppermute(near_cols, "gy", pairs(gy_count, 0))

    state = (3, 2, n_lanes, ext_rows + 2 * SUB, LANES)
    last, pooled, base = call(
        inner_kernel,
        (shape(*state), shape(2, ext_rows // PIX, LANES), shape(4 + STEPS, ext_rows, LANES)),
        8,
        scratch=(
            pltpu.VMEM(state, F32),
            pltpu.VMEM(state, F32),
            pltpu.VMEM((2, n_lanes, ext_rows, LANES), F32),
            pltpu.VMEM((2, n_lanes, ext_rows, LANES), F32),
        ),
        flops=200 * cells,
        size=96 * cells,
    )(*blocks, cross, near, src, inner_mats, base)

    edge_state = (3, ext_rows + 2 * SUB, LANES)
    fields, outgoing = call(
        edge_kernel,
        (shape(3, 2, rows, cols), shape(owners * capacity, width)),
        8,
        out_specs=(pl.BlockSpec(memory_space=pl.ANY), vmem()),
        scratch=(
            pltpu.VMEM(edge_state, F32),
            pltpu.VMEM(edge_state, F32),
            pltpu.VMEM(edge_state, F32),
            pltpu.VMEM((ext_rows, LANES), F32),
            pltpu.VMEM((STEPS, ext_rows, LANES), F32),
            pltpu.VMEM((ext_rows, LANES), F32),
            pltpu.VMEM((2, 2, ext_rows // PIX, LANES), F32),
            pltpu.VMEM((3, 2, rows, cols), F32),
            pltpu.SemaphoreType.DMA,
        ),
        flops=100 * cells,
        size=32 * cells,
    )(last, pooled, base, cross_cols, near_cols, src_edge, place, edge_mats)

    outgoing = outgoing.reshape(owners, capacity, width)
    incoming = lax.all_to_all(outgoing, ("gx", "gy"), split_axis=0, concat_axis=0, tiled=True)
    return fields, incoming[None]


def solution(mesh):
    placed = (
        P(None, None, ("parts", "gx"), "gy"),
        P(None, ("parts", "gx"), "gy"),
        P(None, None, ("parts", "gx"), "gy"),
        P("parts"),
        P("parts"),
        P(None, "parts"),
        P(("parts", "gx"), "gy", None),
        P(("parts", "gx"), "gy", None, None),
    )
    return jax.shard_map(
        on_device,
        mesh=mesh,
        in_specs=placed,
        out_specs=(
            P(None, None, ("parts", "gx"), "gy"),
            P(("parts", "gx", "gy"), None, None, None),
        ),
        check_vma=False,
    )
```

```python
import jax
import jax.numpy as jnp
import ml_dtypes
import numpy as np
from jax import lax
from jax.experimental import pallas as pl
from jax.experimental.pallas import tpu as pltpu
from jax.sharding import PartitionSpec as P

STEPS = 4
PIX = 2
TS = 16
RADIUS = 4
COURANT = 0.6
COUPLING = 0.25

LANES = 128
SUB = 8
FAR = STEPS + PIX * (RADIUS - 1)
NEAR = PIX * (RADIUS - 1)
LEFT_OVER = FAR - SUB
PAD = 2 * SUB
HALF = LANES // 2
SIDE = HALF // 2
OUT = SIDE // 2
KEEP = 8
F32 = jnp.float32
BF16 = jnp.bfloat16
WIDTHS = (FAR,) * 4 + (NEAR,) * STEPS
FIRST = tuple(sum(WIDTHS[:k]) for k in range(len(WIDTHS)))
assert sum(WIDTHS) <= HALF and FAR <= OUT and STEPS + KEEP <= OUT


def cone_weights(radius):
    reach_cells = radius - 1
    offsets = np.arange(-reach_cells, reach_cells + 1)
    distance = np.sqrt(offsets[:, None] * offsets[:, None] + offsets[None, :] * offsets[None, :])
    weights = np.maximum(radius - distance, 0.0)
    return weights / weights.sum()


def pool_matrices():
    inner = np.zeros((2, LANES, LANES), np.float32)
    for j in range(KEEP, 2 * LANES - KEEP):
        inner[j // LANES, j % LANES, j // PIX] = 1.0
    return inner.astype(ml_dtypes.bfloat16)


def edge_matrices():
    weights = cone_weights(RADIUS)
    reach = RADIUS - 1
    result = np.zeros((RADIUS, LANES, 2, LANES), np.float32)
    for lane in range(LANES):
        layer, at = lane // HALF, lane % HALF
        col = at - OUT if at < SIDE else at - SIDE + 2 * LANES - OUT
        if not (-NEAR <= col < KEEP or 2 * LANES - KEEP <= col < 2 * LANES + NEAR):
            continue
        for row in range(RADIUS):
            for shift in range(-reach, reach + 1):
                pixel = col // PIX + shift
                if 0 <= pixel < LANES:
                    result[row, lane, layer, pixel] = weights[reach + row, reach + shift]
    result = result.reshape(RADIUS * LANES, 2 * LANES)
    high = result.astype(ml_dtypes.bfloat16)
    low = (result - high.astype(np.float32)).astype(ml_dtypes.bfloat16)
    return high, low


def split2(value):
    high = value.astype(BF16)
    return high, (value - high.astype(F32)).astype(BF16)


def split3(value):
    high = value.astype(BF16)
    rest = value - high.astype(F32)
    mid = rest.astype(BF16)
    return high, mid, (rest - mid.astype(F32)).astype(BF16)


def dot(a, b):
    return jnp.dot(a, b, preferred_element_type=F32)


def turn(value, shift, axis):
    size = value.shape[axis]
    return pltpu.roll(value, shift % size, axis) if shift % size else value


def lanes():
    return lax.broadcasted_iota(jnp.int32, (SUB, LANES), 1)


def subs():
    return lax.broadcasted_iota(jnp.int32, (SUB, LANES), 0)


def lane_tile(k):
    return pl.ds(k * LANES, LANES)


def is_odd(axis):
    return ((subs() * 0 + lax.axis_index(axis)) & 1) == 1


def rows_kernel(fields, eps, fwd, cross, near, hold, hold_fwd, sems):
    rows, cols = fields.shape[2], fields.shape[3]
    copies = []
    for n, at in enumerate((0, rows - PAD)):
        at_fwd = 0 if n == 0 else rows - SUB
        pairs = (
            (fields.at[:, :, pl.ds(at, PAD), :], hold.at[n, pl.ds(0, 3)]),
            (eps.at[:, pl.ds(at, PAD), :], hold.at[n, 3]),
            (fwd.at[:, :, pl.ds(at_fwd, SUB), :], hold_fwd.at[n]),
        )
        for m, (src, dst) in enumerate(pairs):
            copies.append(pltpu.make_async_copy(src, dst, sems.at[3 * n + m]))
    for copy in copies:
        copy.start()
    for copy in copies:
        copy.wait()
    odd, sub = is_odd("gx"), subs()
    for kind in range(4):
        for layer in range(2):
            plane = 2 * kind + layer
            for k in range(cols // LANES):
                at = lane_tile(k)
                low = hold[0, kind, layer, pl.ds(0, SUB), at]
                high = hold[1, kind, layer, pl.ds(SUB, SUB), at]
                cross[plane, :, at] = jnp.where(odd, high, low)
                near[plane, :, at] = jnp.where(odd, low, high)
                rest_low = turn(hold[0, kind, layer, pl.ds(SUB, SUB), at], -LEFT_OVER, 0)
                rest_high = turn(hold[1, kind, layer, pl.ds(0, SUB), at], LEFT_OVER, 0)
                low = jnp.where(sub >= NEAR, rest_low, hold_fwd[0, kind, layer, :, at])
                high = jnp.where(sub < SUB - NEAR, rest_high, hold_fwd[1, kind, layer, :, at])
                cross[8 + plane, :, at] = jnp.where(odd, high, low)
                near[8 + plane, :, at] = jnp.where(odd, low, high)


def halo_tile(cross, near, odd, tile, kind, layer, at):
    is_above = tile < 2
    outer = tile in (0, 3)
    if outer and kind >= 4:
        return None
    plane = 2 * kind + layer + (8 if outer else 0)
    a, b = near[plane, :, at], cross[plane, :, at]
    value = jnp.where(odd, a, b) if is_above else jnp.where(odd, b, a)
    if outer:
        value = turn(value, -LEFT_OVER if is_above else LEFT_OVER, 0)
    return value


def core_tile(fields, eps, fwd, at, kind, layer, cols):
    if kind < 3:
        return fields[kind, layer, at, cols]
    if kind == 3:
        return eps[layer, at, cols]
    return fwd[kind - 4, layer, at, cols]


def pack_tile(load, lane, right):
    total = jnp.zeros((SUB, LANES), F32)
    for kind, width in enumerate(WIDTHS):
        for layer in range(2):
            value = load(kind, layer)
            if value is None:
                continue
            first = FIRST[kind] + HALF * layer
            value = turn(value, first + width if right else first, 1)
            total = jnp.where((lane >= first) & (lane < first + width), value, total)
    return total


def edge_tile(load, kind, lane, n_lanes):
    spot = lane & (HALF - 1)
    total = None
    for layer in range(2):
        low = turn(load(kind, layer, 0), HALF * layer + OUT, 1)
        high = turn(load(kind, layer, n_lanes - 1), HALF * layer + SIDE + OUT, 1)
        value = jnp.where(spot < SIDE, low, high)
        total = value if total is None else jnp.where(lane < HALF, total, value)
    return total


def cols_kernel(fields, eps, fwd, cross, near, base):
    rows, cols = fields.shape[2], fields.shape[3]
    n_lanes = cols // LANES
    lane, odd = lanes(), is_odd("gy")

    def tile(t, carry):
        at = pl.ds(pl.multiple_of(t * SUB, SUB), SUB)
        out_at = pl.ds(pl.multiple_of(t * SUB + PAD, SUB), SUB)

        def load(kind, layer, k):
            return core_tile(fields, eps, fwd, at, kind, layer, lane_tile(k))

        left = pack_tile(lambda kind, layer: load(kind, layer, 0), lane, False)
        right = pack_tile(lambda kind, layer: load(kind, layer, n_lanes - 1), lane, True)
        cross[out_at, :] = jnp.where(odd, right, left)
        near[out_at, :] = jnp.where(odd, left, right)
        for kind in range(4 + STEPS):
            base[kind, out_at, :] = edge_tile(load, kind, lane, n_lanes)
        return carry

    lax.fori_loop(0, rows // SUB, tile, 0, unroll=4)
    zero = jnp.zeros((PAD, LANES), F32)
    for out in (cross, near) + tuple(base.at[kind] for kind in range(4 + STEPS)):
        out[pl.ds(0, PAD), :] = zero
        out[pl.ds(PAD + rows, PAD), :] = zero


def corners_kernel(cross_in, near_in, cross_rows, near_rows, cross, near):
    rows, cols = cross.shape[0] - 2 * PAD, cross_rows.shape[2]
    lane, odd, odd_col = lanes(), is_odd("gx"), is_odd("gy")
    core = pl.ds(PAD, rows)
    cross[core, :] = cross_in[core, :]
    near[core, :] = near_in[core, :]
    for tile in range(4):
        at = pl.ds(tile * SUB if tile < 2 else PAD + rows + (tile - 2) * SUB, SUB)
        left, right = (
            pack_tile(
                lambda kind, layer: halo_tile(
                    cross_rows, near_rows, odd, tile, kind, layer, pl.ds(lo, LANES)
                ),
                lane, is_right,
            )
            for lo, is_right in ((0, False), (cols - LANES, True))
        )
        cross[at, :] = jnp.where(odd_col, right, left)
        near[at, :] = jnp.where(odd_col, left, right)


def prep_kernel(
    capacity, fields, eps, fwd, mon_x, mon_y, amp, mask, owner, cross, near, base, src, src_edge, place
):
    cols_kernel(fields, eps, fwd, cross, near, base)
    side_kernel(capacity, mon_x, mon_y, amp, mask, owner, src, src_edge, place)


def side_kernel(capacity, mon_x, mon_y, amp, mask, owner, src, src_edge, place):
    _, _, ext_rows, cols = src.shape
    rows = ext_rows - 2 * PAD
    channels = mon_x.shape[1]
    row = mon_x[...] - lax.axis_index("gx") * rows + PAD
    col = mon_y[...] - lax.axis_index("gy") * cols
    in_left = (col >= -OUT) & (col < OUT)
    in_right = (col >= cols - OUT) & (col < cols + OUT)
    edge = jnp.where(in_left, col + OUT, jnp.where(in_right, col - cols + OUT + SIDE, -LANES))
    layer = lax.broadcasted_iota(jnp.int32, (1, channels), 1) & 1
    edge = edge + HALF * layer
    inside = jnp.where((col >= 0) & (col < cols), col, -1)
    one_y = lax.broadcasted_iota(jnp.int32, (cols, channels), 0) == inside
    one_e = lax.broadcasted_iota(jnp.int32, (LANES, channels), 0) == edge
    one_y = jnp.where(one_y, 1.0, 0.0).astype(BF16)
    one_e = jnp.where(one_e, 1.0, 0.0).astype(BF16)
    one_y = jnp.concatenate([one_y] * 3, axis=1)
    one_e = jnp.concatenate([one_e] * 3, axis=1)
    one_x = lax.broadcasted_iota(jnp.int32, (ext_rows, channels), 0) == row
    one_x = jnp.where(one_x, 1.0, 0.0).astype(F32)
    nt = (((1,), (1,)), ((), ()))
    for step in range(STEPS):
        parts = [part.astype(F32) for part in split3(amp[pl.ds(step, 1), :])]
        lhs = jnp.concatenate([one_x * part for part in parts], axis=1)
        src_edge[step] = lax.dot_general(lhs.astype(BF16), one_e, nt, preferred_element_type=F32)
        layer_wide = jnp.concatenate([layer] * 3, axis=1)
        for which in range(2):
            some = jnp.where(layer_wide == which, lhs, 0.0).astype(BF16)
            src[step, which] = lax.dot_general(some, one_y, nt, preferred_element_type=F32)
    tiles = owner.shape[1]
    own = owner[...].astype(F32)
    own_wide = jnp.broadcast_to(own, (tiles, tiles))
    earlier = lax.broadcasted_iota(jnp.int32, (tiles, tiles), 0) < lax.broadcasted_iota(
        jnp.int32, (tiles, tiles), 1
    )
    same = (own_wide.T == own_wide) & earlier
    slot = jnp.sum(jnp.where(same, 1.0, 0.0), axis=0, keepdims=True)
    dest = owner[...] * capacity + slot.astype(jnp.int32)
    dest = jnp.where(mask[...] != 0, dest, -1)
    hit = lax.broadcasted_iota(jnp.int32, place.shape, 0) == dest
    place[...] = jnp.where(hit, 1.0, 0.0).astype(BF16)


def yee(bufs, keys, eps_of, change_of, src_of, grad, coef_x, coef_first, next_col, prev_col, other):
    n_tiles = (bufs[0].shape[-2] - 2 * SUB) // SUB
    for step in range(STEPS):
        old, new = ((0, 1), (1, 0), (0, 1), (1, 2))[step]
        old, new = bufs[old], bufs[new]
        low = 0 if step < 2 else 1
        high = n_tiles if step == 0 else n_tiles - 1
        for t in range(low, high):
            at = pl.ds(SUB + t * SUB, SUB)
            under = pl.ds(SUB + t * SUB + 1, SUB)
            over = pl.ds(SUB + t * SUB - 1, SUB)
            coef_y = coef_first if t < PAD // SUB else COURANT
            e = {key: old[(0,) + key + (at, slice(None))] for key in keys}
            e_right = next_col(e)
            hx, hy = {}, {}
            for key in keys:
                hx[key] = old[(1,) + key + (at, slice(None))] + coef_x * (e_right[key] - e[key])
                below = old[(0,) + key + (under, slice(None))]
                hy[key] = old[(2,) + key + (at, slice(None))] - coef_y * (below - e[key])
                new[(1,) + key + (at, slice(None))] = hx[key]
                new[(2,) + key + (at, slice(None))] = hy[key]
            hx_left = prev_col(hx)
            for key in keys:
                hy_above = new[(2,) + key + (over, slice(None))]
                curl = (hy[key] - hy_above) - (hx[key] - hx_left[key])
                curl = curl + COUPLING * (other(e, key) - e[key])
                value = e[key] - eps_of(key, t) * curl + src_of(step, key, t)
                new[(0,) + key + (at, slice(None))] = value
                if 1 <= t < n_tiles - 1:
                    change = value * change_of(step, key, t)
                    where = key + (pl.ds(t * SUB, SUB), slice(None))
                    grad[where] = -change if step == 0 else grad[where] - change


def coef_above():
    return jnp.where((subs() * 0 + lax.axis_index("gx")) > 0, COURANT, 0.0).astype(F32)


def clear_rims(buf):
    size = buf.shape[-2]
    zero = jnp.zeros(buf.shape[:-2] + (SUB, LANES), F32)
    lead = (slice(None),) * (len(buf.shape) - 2)
    buf[lead + (pl.ds(0, SUB), slice(None))] = zero
    buf[lead + (pl.ds(size - SUB, SUB), slice(None))] = zero


def row_pairs(ref, lead, count):
    even = ref[lead + (pl.ds(0, count, stride=PIX), slice(None))]
    return even + ref[lead + (pl.ds(1, count, stride=PIX), slice(None))]


def inner_kernel(fields, eps, fwd, cross, near, src, mats, base_in, last, filtered, base, a, b, e, g, pooled):
    rows, cols = fields.shape[2], fields.shape[3]
    n_tiles = (rows + 2 * PAD) // SUB
    n_lanes = cols // LANES
    lane, odd = lanes(), is_odd("gx")
    halo_of = {0: 0, 1: 1, n_tiles - 2: 2, n_tiles - 1: 3}

    def load(kind, layer, t, k):
        if t in halo_of:
            return halo_tile(cross, near, odd, halo_of[t], kind, layer, lane_tile(k))
        return core_tile(fields, eps, fwd, pl.ds(t * SUB - PAD, SUB), kind, layer, lane_tile(k))

    for buf in (a, b, last):
        clear_rims(buf)
    for t in range(n_tiles):
        for layer in range(2):
            for k in range(n_lanes):
                for kind in range(3):
                    a[kind, layer, k, pl.ds(SUB + t * SUB, SUB), :] = load(kind, layer, t, k)
                e[layer, k, pl.ds(t * SUB, SUB), :] = COURANT * load(3, layer, t, k)

    at_end, at_start = lane == LANES - 1, lane == 0
    keys = [(layer, k) for layer in range(2) for k in range(n_lanes)]

    def next_col(values):
        moved = {key: turn(value, -1, 1) for key, value in values.items()}
        return {
            (l, k): jnp.where(at_end, moved[l, (k + 1) % n_lanes], moved[l, k]) for l, k in keys
        }

    def prev_col(values):
        moved = {key: turn(value, 1, 1) for key, value in values.items()}
        return {
            (l, k): jnp.where(at_start, moved[l, (k - 1) % n_lanes], moved[l, k]) for l, k in keys
        }

    yee(
        (a, b, last), keys,
        lambda key, t: e[key + (pl.ds(t * SUB, SUB), slice(None))],
        lambda step, key, t: load(4 + step, key[0], t, key[1]),
        lambda step, key, t: src[step, key[0], pl.ds(t * SUB, SUB), lane_tile(key[1])],
        g, COURANT, coef_above(), next_col, prev_col,
        lambda values, key: values[1 - key[0], key[1]],
    )
    for layer in range(2):
        total = None
        for k in range(n_lanes):
            for part in split2(row_pairs(g, (layer, k), n_tiles * SUB // PIX)):
                term = dot(part, mats[k])
                total = term if total is None else total + term
        pooled[layer] = total

    for layer in range(2):
        filtered[layer] = cone_filter(pooled.at[layer], rows // PIX, PAD // PIX)

    for t in range(n_tiles):
        for kind in range(4 + STEPS):
            at = pl.ds(t * SUB, SUB)
            if t not in halo_of:
                base[kind, at, :] = base_in[kind, at, :]
            elif kind < 4 or t not in (0, n_tiles - 1):
                base[kind, at, :] = edge_tile(
                    lambda kind, layer, k: load(kind, layer, t, k), kind, lane, n_lanes
                )


def cone_filter(pooled, out_pix, first):
    weights = cone_weights(RADIUS)
    reach = RADIUS - 1
    lane = lax.broadcasted_iota(jnp.int32, (out_pix, LANES), 1)
    at = [pooled[pl.ds(first + s, out_pix), :] for s in range(-reach, reach + 1)]
    sums = [at[reach]] + [at[reach + s] + at[reach - s] for s in range(1, reach + 1)]
    total = None
    for shift in range(reach + 1):
        mixed = None
        for s in range(reach + 1):
            weight = float(weights[reach + s, reach + shift])
            if weight > 0.0:
                term = weight * sums[s]
                mixed = term if mixed is None else mixed + term
        if shift == 0:
            total = mixed
        else:
            total = total + turn(jnp.where(lane < shift, 0.0, mixed), -shift, 1)
            total = total + turn(jnp.where(lane >= LANES - shift, 0.0, mixed), shift, 1)
    return total


def edge_kernel(
    filtered, base, cross, near, src, place, high_mat, low_mat, c, out_slots, a, b, e, d, g, pooled
):
    ext_rows = base.shape[1]
    rows = ext_rows - 2 * PAD
    n_tiles = ext_rows // SUB
    lane, odd = lanes(), is_odd("gy")
    spot = lane & (HALF - 1)
    is_left, is_right = spot < OUT, spot >= HALF - OUT

    for buf in (a, b, c):
        clear_rims(buf)
    for t in range(n_tiles):
        at = pl.ds(t * SUB, SUB)
        far, close = cross[at, :], near[at, :]
        high, low = jnp.where(odd, close, far), jnp.where(odd, far, close)
        for kind, width in enumerate(WIDTHS):
            if kind >= 4 and t in (0, n_tiles - 1):
                continue
            value = jnp.where(is_left, turn(high, OUT - width - FIRST[kind], 1), base[kind, at, :])
            value = jnp.where(is_right, turn(low, HALF - OUT - FIRST[kind], 1), value)
            if kind < 3:
                a[kind, pl.ds(SUB + t * SUB, SUB), :] = value
            elif kind == 3:
                e[at, :] = COURANT * value
            else:
                d[kind - 4, at, :] = value

    before = (lax.axis_index("gy") + lane * 0) > 0
    coef_x = jnp.where(before | (spot >= OUT), COURANT, 0.0).astype(F32)
    yee(
        (a, b, c), [()],
        lambda key, t: e[pl.ds(t * SUB, SUB), :],
        lambda step, key, t: d[step, pl.ds(t * SUB, SUB), :],
        lambda step, key, t: src[step, pl.ds(t * SUB, SUB), :],
        g, coef_x, coef_above(),
        lambda values: {(): turn(values[()], -1, 1)},
        lambda values: {(): turn(values[()], 1, 1)},
        lambda values, key: turn(values[()], HALF, 1),
    )

    pooled[...] = row_pairs(g, (), ext_rows // PIX)
    reach = RADIUS - 1
    out_pix = rows // PIX
    first = PAD // PIX
    at = [pooled[pl.ds(first + s, out_pix), :] for s in range(-reach, reach + 1)]
    sums = [at[reach]] + [at[reach + s] + at[reach - s] for s in range(1, reach + 1)]
    high, low = split2(jnp.concatenate(sums, axis=1))
    edge = dot(high, high_mat[...]) + (dot(low, high_mat[...]) + dot(high, low_mat[...]))
    blocks = [filtered[l] + edge[:, l * LANES : (l + 1) * LANES] for l in range(2)]

    span = TS // PIX
    tile_rows = out_pix // span
    x = jnp.stack([block.reshape(tile_rows, span, LANES) for block in blocks], axis=1)
    x = x.reshape(tile_rows * 2, span, LANES)
    group = lax.broadcasted_iota(jnp.int32, x.shape, 2) // span
    row = lax.broadcasted_iota(jnp.int32, x.shape, 1)
    for bit in (1, 2, 4):
        row_on, lane_on = (row & bit) != 0, (group & bit) != 0
        ahead = turn(turn(x, -bit, 1), bit * span, 2)
        behind = turn(turn(x, bit, 1), -bit * span, 2)
        x = jnp.where(row_on == lane_on, x, jnp.where(lane_on, ahead, behind))
    x = x.reshape(tile_rows, 2, span, LANES)
    even, odd = x[:, 0], x[:, 1]
    upper = lax.broadcasted_iota(jnp.int32, even.shape, 2) >= HALF
    new_even = jnp.where(upper, turn(odd, HALF, 2), even)
    new_odd = jnp.where(upper, odd, turn(even, HALF, 2))
    vals = jnp.stack([new_even, new_odd], axis=1).reshape(tile_rows * 2 * span, LANES)
    high, low = split2(vals)
    out_slots[...] = dot(place[...], high) + dot(place[...], low)


def merge_kernel(last, edge_last, out_fields, merged, sem):
    rows, cols = merged.shape[2], merged.shape[3]
    n_lanes = cols // LANES
    lane = lanes()
    for t in range(rows // SUB):
        at, out_at = pl.ds(SUB + PAD + t * SUB, SUB), pl.ds(t * SUB, SUB)
        for kind in range(3):
            edge = edge_last[kind, at, :]
            for layer in range(2):
                for k in range(n_lanes):
                    value = last[kind, layer, k, at, :]
                    if k == 0:
                        value = jnp.where(lane < KEEP, turn(edge, -HALF * layer - OUT, 1), value)
                    if k == n_lanes - 1:
                        value = jnp.where(
                            lane >= LANES - KEEP, turn(edge, -HALF * layer - SIDE - OUT, 1), value
                        )
                    merged[kind, layer, out_at, lane_tile(k)] = value
    copy = pltpu.make_async_copy(merged, out_fields, sem)
    copy.start()
    copy.wait()


def vmem():
    return pl.BlockSpec(memory_space=pltpu.VMEM)


def shape(*dims, dtype=F32):
    return jax.ShapeDtypeStruct(dims, dtype)


def call(kernel, outs, n_in, *, in_space=pltpu.VMEM, out_specs=None, scratch=(), flops=0, size=0):
    return pl.pallas_call(
        kernel,
        out_shape=outs,
        in_specs=[pl.BlockSpec(memory_space=in_space)] * n_in,
        out_specs=out_specs or tuple(vmem() for _ in outs),
        scratch_shapes=list(scratch),
        compiler_params=pltpu.CompilerParams(vmem_limit_bytes=40 * 1024 * 1024),
        cost_estimate=pl.CostEstimate(flops=flops, bytes_accessed=size, transcendentals=0),
    )


def on_device(adj_fields, inv_eps, fwd_diff, mon_x, mon_y, mon_amp, design_mask, tile_owner):
    rows, cols = adj_fields.shape[2], adj_fields.shape[3]
    assert cols == 2 * LANES and rows % TS == 0
    gx_count, gy_count = lax.axis_size("gx"), lax.axis_size("gy")
    owners = gx_count * gy_count
    tiles = (rows // TS) * (cols // TS)
    width = 2 * (TS // PIX) ** 2
    assert width == LANES
    capacity = max(8, 2 * tiles // owners)
    ext_rows = rows + 2 * PAD
    n_lanes = cols // LANES
    cells = rows * cols
    blocks = (adj_fields, inv_eps, fwd_diff)


    strip = shape(16, SUB, cols)
    cross, near = call(
        rows_kernel, (strip, strip), 3, in_space=pltpu.HBM,
        scratch=(
            pltpu.VMEM((2, 4, 2, PAD, cols), F32),
            pltpu.VMEM((2, STEPS, 2, SUB, cols), F32),
            pltpu.SemaphoreType.DMA((6,)),
        ),
        size=2**20,
    )(*(pltpu.with_memory_space_constraint(block, pltpu.HBM) for block in blocks))

    def pairs(count, start):
        some = [(i, i + 1) for i in range(start, count - 1, 2)]
        return some + [(j, i) for i, j in some]

    cross = lax.ppermute(cross, "gx", pairs(gx_count, 1))
    near = lax.ppermute(near, "gx", pairs(gx_count, 0))

    packed = shape(ext_rows, LANES)
    channels = mon_x.shape[0]
    cross_cols, near_cols, base, src, src_edge, place = call(
        lambda *refs: prep_kernel(capacity, *refs),
        (
            packed,
            packed,
            shape(4 + STEPS, ext_rows, LANES),
            shape(STEPS, 2, ext_rows, cols),
            shape(STEPS, ext_rows, LANES),
            shape(owners * capacity, tiles, dtype=BF16),
        ),
        8,
        flops=16 * ext_rows * (cols + LANES) * 3 * channels,
        size=64 * cells,
    )(
        *blocks,
        mon_x.reshape(1, channels),
        mon_y.reshape(1, channels),
        mon_amp,
        design_mask.reshape(1, tiles),
        tile_owner.reshape(1, tiles),
    )
    cross_cols, near_cols = call(
        corners_kernel, (packed, packed), 4, flops=cells, size=8 * ext_rows * LANES
    )(cross_cols, near_cols, cross, near)
    cross_cols = lax.ppermute(cross_cols, "gy", pairs(gy_count, 1))
    near_cols = lax.ppermute(near_cols, "gy", pairs(gy_count, 0))

    state = (3, 2, n_lanes, ext_rows + 2 * SUB, LANES)
    last, filtered, base = call(
        inner_kernel,
        (shape(*state), shape(2, rows // PIX, LANES), shape(4 + STEPS, ext_rows, LANES)),
        8,
        scratch=(
            pltpu.VMEM(state, F32),
            pltpu.VMEM(state, F32),
            pltpu.VMEM((2, n_lanes, ext_rows, LANES), F32),
            pltpu.VMEM((2, n_lanes, ext_rows, LANES), F32),
            pltpu.VMEM((2, ext_rows // PIX, LANES), F32),
        ),
        flops=200 * cells,
        size=96 * cells,
    )(*blocks, cross, near, src, pool_matrices(), base)

    edge_state = (3, ext_rows + 2 * SUB, LANES)
    edge_last, outgoing = call(
        edge_kernel,
        (shape(*edge_state), shape(owners * capacity, width)),
        8,
        scratch=(
            pltpu.VMEM(edge_state, F32),
            pltpu.VMEM(edge_state, F32),
            pltpu.VMEM((ext_rows, LANES), F32),
            pltpu.VMEM((STEPS, ext_rows, LANES), F32),
            pltpu.VMEM((ext_rows, LANES), F32),
            pltpu.VMEM((ext_rows // PIX, LANES), F32),
        ),
        flops=100 * cells,
        size=32 * cells,
    )(filtered, base, cross_cols, near_cols, src_edge, place, *edge_matrices())
    (fields,) = call(
        merge_kernel,
        (shape(3, 2, rows, cols),),
        2,
        out_specs=(pl.BlockSpec(memory_space=pl.ANY),),
        scratch=(pltpu.VMEM((3, 2, rows, cols), F32), pltpu.SemaphoreType.DMA),
        flops=20 * cells,
        size=48 * cells,
    )(last, edge_last)

    outgoing = outgoing.reshape(owners, capacity, width)
    incoming = lax.all_to_all(outgoing, ("gx", "gy"), split_axis=0, concat_axis=0, tiled=True)
    return fields, incoming[None]


def solution(mesh):
    placed = (
        P(None, None, ("parts", "gx"), "gy"),
        P(None, ("parts", "gx"), "gy"),
        P(None, None, ("parts", "gx"), "gy"),
        P("parts"),
        P("parts"),
        P(None, "parts"),
        P(("parts", "gx"), "gy", None),
        P(("parts", "gx"), "gy", None, None),
    )
    return jax.shard_map(
        on_device,
        mesh=mesh,
        in_specs=placed,
        out_specs=(
            P(None, None, ("parts", "gx"), "gy"),
            P(("parts", "gx", "gy"), None, None, None),
        ),
        check_vma=False,
    )
```

```python
import jax
import jax.numpy as jnp
import ml_dtypes
import numpy as np
from jax import lax
from jax.experimental import pallas as pl
from jax.experimental.pallas import tpu as pltpu
from jax.sharding import PartitionSpec as P

STEPS = 4
PIX = 2
TS = 16
RADIUS = 4
COURANT = 0.6
COUPLING = 0.25

LANES = 128
SUB = 8
FAR = STEPS + PIX * (RADIUS - 1)
NEAR = PIX * (RADIUS - 1)
LEFT_OVER = FAR - SUB
PAD = 2 * SUB
HALF = LANES // 2
SIDE = HALF // 2
OUT = SIDE // 2
KEEP = 8
F32 = jnp.float32
BF16 = jnp.bfloat16
WIDTHS = (FAR,) * 4 + (NEAR,) * STEPS
FIRST = tuple(sum(WIDTHS[:k]) for k in range(len(WIDTHS)))
assert sum(WIDTHS) <= HALF and FAR <= OUT and STEPS + KEEP <= OUT


def cone_weights(radius):
    reach_cells = radius - 1
    offsets = np.arange(-reach_cells, reach_cells + 1)
    distance = np.sqrt(offsets[:, None] * offsets[:, None] + offsets[None, :] * offsets[None, :])
    weights = np.maximum(radius - distance, 0.0)
    return weights / weights.sum()


def pool_matrices():
    inner = np.zeros((2, LANES, LANES), np.float32)
    for j in range(KEEP, 2 * LANES - KEEP):
        inner[j // LANES, j % LANES, j // PIX] = 1.0
    return inner.astype(ml_dtypes.bfloat16)


def spread_matrix():
    span = TS // PIX
    result = np.zeros((2, LANES, 2, 2, span, span), np.float32)
    for e in range(span):
        move = (e % 2) + SIDE * (e % 4 // 2)
        for layer in range(2):
            for side in range(2):
                for f in range(span):
                    lane = (HALF * layer + OUT + OUT * side + PIX * f + move) % LANES
                    result[e // 4, lane, side, layer, e, f] = 1.0
    return result.reshape(2 * LANES, 2 * LANES).astype(ml_dtypes.bfloat16)


def split2(value):
    high = value.astype(BF16)
    return high, (value - high.astype(F32)).astype(BF16)


def split3(value):
    high = value.astype(BF16)
    rest = value - high.astype(F32)
    mid = rest.astype(BF16)
    return high, mid, (rest - mid.astype(F32)).astype(BF16)


def dot(a, b):
    return jnp.dot(a, b, preferred_element_type=F32)


def turn(value, shift, axis):
    size = value.shape[axis]
    return pltpu.roll(value, shift % size, axis) if shift % size else value


def lanes():
    return lax.broadcasted_iota(jnp.int32, (SUB, LANES), 1)


def subs():
    return lax.broadcasted_iota(jnp.int32, (SUB, LANES), 0)


def lane_tile(k):
    return pl.ds(k * LANES, LANES)


def spread_rows(ext_rows):
    return (ext_rows // SUB) | 1


def nth(r, n):
    return pl.ds(r, SUB, stride=n)


def is_odd(axis):
    return ((subs() * 0 + lax.axis_index(axis)) & 1) == 1


def rows_kernel(fields, eps, fwd, cross, near, hold, hold_fwd, sems):
    rows, cols = fields.shape[2], fields.shape[3]
    copies = []
    for n, at in enumerate((0, rows - PAD)):
        at_fwd = 0 if n == 0 else rows - SUB
        pairs = (
            (fields.at[:, :, pl.ds(at, PAD), :], hold.at[n, pl.ds(0, 3)]),
            (eps.at[:, pl.ds(at, PAD), :], hold.at[n, 3]),
            (fwd.at[:, :, pl.ds(at_fwd, SUB), :], hold_fwd.at[n]),
        )
        for m, (src, dst) in enumerate(pairs):
            copies.append(pltpu.make_async_copy(src, dst, sems.at[3 * n + m]))
    for copy in copies:
        copy.start()
    for copy in copies:
        copy.wait()
    odd, sub = is_odd("gx"), subs()
    for kind in range(4):
        for layer in range(2):
            plane = 2 * kind + layer
            for k in range(cols // LANES):
                at = lane_tile(k)
                low = hold[0, kind, layer, pl.ds(0, SUB), at]
                high = hold[1, kind, layer, pl.ds(SUB, SUB), at]
                cross[plane, :, at] = jnp.where(odd, high, low)
                near[plane, :, at] = jnp.where(odd, low, high)
                rest_low = turn(hold[0, kind, layer, pl.ds(SUB, SUB), at], -LEFT_OVER, 0)
                rest_high = turn(hold[1, kind, layer, pl.ds(0, SUB), at], LEFT_OVER, 0)
                low = jnp.where(sub >= NEAR, rest_low, hold_fwd[0, kind, layer, :, at])
                high = jnp.where(sub < SUB - NEAR, rest_high, hold_fwd[1, kind, layer, :, at])
                cross[8 + plane, :, at] = jnp.where(odd, high, low)
                near[8 + plane, :, at] = jnp.where(odd, low, high)


def halo_tile(cross, near, odd, tile, kind, layer, at):
    is_above = tile < 2
    outer = tile in (0, 3)
    if outer and kind >= 4:
        return None
    plane = 2 * kind + layer + (8 if outer else 0)
    a, b = near[plane, :, at], cross[plane, :, at]
    value = jnp.where(odd, a, b) if is_above else jnp.where(odd, b, a)
    if outer:
        value = turn(value, -LEFT_OVER if is_above else LEFT_OVER, 0)
    return value


def core_tile(fields, eps, fwd, at, kind, layer, cols):
    if kind < 3:
        return fields[kind, layer, at, cols]
    if kind == 3:
        return eps[layer, at, cols]
    return fwd[kind - 4, layer, at, cols]


def pack_tile(load, lane, right):
    total = jnp.zeros((SUB, LANES), F32)
    for kind, width in enumerate(WIDTHS):
        for layer in range(2):
            value = load(kind, layer)
            if value is None:
                continue
            first = FIRST[kind] + HALF * layer
            value = turn(value, first + width if right else first, 1)
            total = jnp.where((lane >= first) & (lane < first + width), value, total)
    return total


def edge_tile(load, kind, lane, n_lanes):
    spot = lane & (HALF - 1)
    total = None
    for layer in range(2):
        low = turn(load(kind, layer, 0), HALF * layer + OUT, 1)
        high = turn(load(kind, layer, n_lanes - 1), HALF * layer + SIDE + OUT, 1)
        value = jnp.where(spot < SIDE, low, high)
        total = value if total is None else jnp.where(lane < HALF, total, value)
    return total


def cols_kernel(fields, eps, fwd, cross, near, base):
    rows, cols = fields.shape[2], fields.shape[3]
    n_lanes = cols // LANES
    lane, odd = lanes(), is_odd("gy")

    def tile(t, carry):
        at = pl.ds(pl.multiple_of(t * SUB, SUB), SUB)
        out_at = pl.ds(pl.multiple_of(t * SUB + PAD, SUB), SUB)

        def load(kind, layer, k):
            return core_tile(fields, eps, fwd, at, kind, layer, lane_tile(k))

        left = pack_tile(lambda kind, layer: load(kind, layer, 0), lane, False)
        right = pack_tile(lambda kind, layer: load(kind, layer, n_lanes - 1), lane, True)
        cross[out_at, :] = jnp.where(odd, right, left)
        near[out_at, :] = jnp.where(odd, left, right)
        for kind in range(4 + STEPS):
            base[kind, out_at, :] = edge_tile(load, kind, lane, n_lanes)
        return carry

    lax.fori_loop(0, rows // SUB, tile, 0, unroll=4)
    zero = jnp.zeros((PAD, LANES), F32)
    for out in (cross, near) + tuple(base.at[kind] for kind in range(4 + STEPS)):
        out[pl.ds(0, PAD), :] = zero
        out[pl.ds(PAD + rows, PAD), :] = zero


def corners_kernel(cross_in, near_in, cross_rows, near_rows, cross, near):
    rows, cols = cross.shape[0] - 2 * PAD, cross_rows.shape[2]
    lane, odd, odd_col = lanes(), is_odd("gx"), is_odd("gy")
    core = pl.ds(PAD, rows)
    cross[core, :] = cross_in[core, :]
    near[core, :] = near_in[core, :]
    for tile in range(4):
        at = pl.ds(tile * SUB if tile < 2 else PAD + rows + (tile - 2) * SUB, SUB)
        left, right = (
            pack_tile(
                lambda kind, layer: halo_tile(
                    cross_rows, near_rows, odd, tile, kind, layer, pl.ds(lo, LANES)
                ),
                lane, is_right,
            )
            for lo, is_right in ((0, False), (cols - LANES, True))
        )
        cross[at, :] = jnp.where(odd_col, right, left)
        near[at, :] = jnp.where(odd_col, left, right)


def prep_kernel(
    capacity, fields, eps, fwd, mon_x, mon_y, amp, mask, owner, cross, near, base, src, src_edge, place
):
    cols_kernel(fields, eps, fwd, cross, near, base)
    side_kernel(capacity, fields.shape[2], mon_x, mon_y, amp, mask, owner, src, src_edge, place)


def side_kernel(capacity, rows, mon_x, mon_y, amp, mask, owner, src, src_edge, place):
    _, _, long_rows, cols = src.shape
    n = long_rows // SUB
    channels = mon_x.shape[1]
    row = mon_x[...] - lax.axis_index("gx") * rows + PAD
    col = mon_y[...] - lax.axis_index("gy") * cols
    in_left = (col >= -OUT) & (col < OUT)
    in_right = (col >= cols - OUT) & (col < cols + OUT)
    edge = jnp.where(in_left, col + OUT, jnp.where(in_right, col - cols + OUT + SIDE, -LANES))
    layer = lax.broadcasted_iota(jnp.int32, (1, channels), 1) & 1
    edge = edge + HALF * layer
    inside = jnp.where((col >= 0) & (col < cols), col, -1)
    one_y = lax.broadcasted_iota(jnp.int32, (cols, channels), 0) == inside
    one_e = lax.broadcasted_iota(jnp.int32, (LANES, channels), 0) == edge
    one_y = jnp.where(one_y, 1.0, 0.0).astype(BF16)
    one_e = jnp.where(one_e, 1.0, 0.0).astype(BF16)
    one_y = jnp.concatenate([one_y] * 3, axis=1)
    one_e = jnp.concatenate([one_e] * 3, axis=1)
    place_of = lax.broadcasted_iota(jnp.int32, (long_rows, channels), 0)
    one_x = (place_of >> 3) + n * (place_of & (SUB - 1)) == row
    one_x = jnp.where(one_x, 1.0, 0.0).astype(F32)
    nt = (((1,), (1,)), ((), ()))
    for step in range(STEPS):
        parts = [part.astype(F32) for part in split3(amp[pl.ds(step, 1), :])]
        lhs = jnp.concatenate([one_x * part for part in parts], axis=1)
        src_edge[step] = lax.dot_general(lhs.astype(BF16), one_e, nt, preferred_element_type=F32)
        layer_wide = jnp.concatenate([layer] * 3, axis=1)
        for which in range(2):
            some = jnp.where(layer_wide == which, lhs, 0.0).astype(BF16)
            src[step, which] = lax.dot_general(some, one_y, nt, preferred_element_type=F32)
    tiles = owner.shape[1]
    own = owner[...].astype(F32)
    own_wide = jnp.broadcast_to(own, (tiles, tiles))
    earlier = lax.broadcasted_iota(jnp.int32, (tiles, tiles), 0) < lax.broadcasted_iota(
        jnp.int32, (tiles, tiles), 1
    )
    same = (own_wide.T == own_wide) & earlier
    slot = jnp.sum(jnp.where(same, 1.0, 0.0), axis=0, keepdims=True)
    dest = owner[...] * capacity + slot.astype(jnp.int32)
    dest = jnp.where(mask[...] != 0, dest, -1)
    hit = lax.broadcasted_iota(jnp.int32, place.shape, 0) == dest
    place[...] = jnp.where(hit, 1.0, 0.0).astype(BF16)


def yee(n, keys, start, state, eps_of, src_of, keep, finish, coef_x, next_col, prev_col, other):
    coef_first = jnp.where(subs() == 0, coef_above(), COURANT)

    def coef_y(r):
        return coef_first if r < PAD else COURANT

    for step in range(STEPS):

        def load(kind, key, r):
            if step == 0:
                return start(kind, key, r)
            return state[(kind,) + key + (pl.ds(r * SUB, SUB), slice(None))]

        e = {key: load(0, key, 0) for key in keys}
        e_wrap = {key: turn(e[key], -1, 0) for key in keys}
        hy_end = {
            key: load(2, key, n - 1) - coef_y(n - 1) * (e_wrap[key] - load(0, key, n - 1))
            for key in keys
        }
        hy_above = {key: turn(hy_end[key], 1, 0) for key in keys}
        for r in range(n):
            e_below = {key: load(0, key, r + 1) for key in keys} if r < n - 1 else e_wrap
            e_right = next_col(e)
            hx = {key: load(1, key, r) + coef_x * (e_right[key] - e[key]) for key in keys}
            if r < n - 1:
                hy = {key: load(2, key, r) - coef_y(r) * (e_below[key] - e[key]) for key in keys}
            else:
                hy = hy_end
            hx_left = prev_col(hx)
            for key in keys:
                curl = (hy[key] - hy_above[key]) - (hx[key] - hx_left[key])
                curl = curl + COUPLING * (other(e, key) - e[key])
                new = e[key] - eps_of(key, r) * curl + src_of(step, key, r)
                keep(step, key, r, new)
                for kind, value in enumerate((new, hx[key], hy[key])):
                    if step < STEPS - 1:
                        state[(kind,) + key + (pl.ds(r * SUB, SUB), slice(None))] = value
                    else:
                        finish(kind, key, r, value)
            e, hy_above = e_below, hy


def coef_above():
    return jnp.where((subs() * 0 + lax.axis_index("gx")) > 0, COURANT, 0.0).astype(F32)


def row_pairs(ref, lead, count):
    even = ref[lead + (pl.ds(0, count, stride=PIX), slice(None))]
    return even + ref[lead + (pl.ds(1, count, stride=PIX), slice(None))]


def inner_kernel(
    fields, eps, fwd, cross, near, src, mats, base_in, last, vals, base, first, state, e, kept, g, pooled
):
    rows, cols = fields.shape[2], fields.shape[3]
    ext_rows = rows + 2 * PAD
    n_tiles, n = ext_rows // SUB, spread_rows(ext_rows)
    n_lanes = cols // LANES
    lane, odd = lanes(), is_odd("gx")
    halo_of = {0: 0, 1: 1, n_tiles - 2: 2, n_tiles - 1: 3}

    def load(kind, layer, t, k):
        if t in halo_of:
            return halo_tile(cross, near, odd, halo_of[t], kind, layer, lane_tile(k))
        return core_tile(fields, eps, fwd, pl.ds(t * SUB - PAD, SUB), kind, layer, lane_tile(k))

    zero = jnp.zeros((SUB, LANES), F32)
    for t in range(n):
        at = pl.ds(t * SUB, SUB)
        for layer in range(2):
            for k in range(n_lanes):
                for kind in range(3):
                    first[kind, layer, k, at, :] = load(kind, layer, t, k) if t < n_tiles else zero
                e[layer, k, at, :] = COURANT * load(3, layer, t, k) if t < n_tiles else zero

    at_end, at_start = lane == LANES - 1, lane == 0
    keys = [(layer, k) for layer in range(2) for k in range(n_lanes)]

    def next_col(values):
        moved = {key: turn(value, -1, 1) for key, value in values.items()}
        return {
            (l, k): jnp.where(at_end, moved[l, (k + 1) % n_lanes], moved[l, k]) for l, k in keys
        }

    def prev_col(values):
        moved = {key: turn(value, 1, 1) for key, value in values.items()}
        return {
            (l, k): jnp.where(at_start, moved[l, (k - 1) % n_lanes], moved[l, k]) for l, k in keys
        }

    def start(kind, key, r):
        return first[(kind,) + key + (nth(r, n), slice(None))]

    def keep(step, key, r, value):
        kept[(step,) + key + (nth(r, n), slice(None))] = value

    def finish(kind, key, r, value):
        last[(kind,) + key + (nth(r, n), slice(None))] = value

    yee(
        n, keys, start, state,
        lambda key, r: e[key + (nth(r, n), slice(None))],
        lambda step, key, r: src[step, key[0], pl.ds(r * SUB, SUB), lane_tile(key[1])],
        keep, finish, COURANT, next_col, prev_col,
        lambda values, key: values[1 - key[0], key[1]],
    )
    for t in range(1, n_tiles - 1):
        at = pl.ds(t * SUB, SUB)
        for layer, k in keys:
            total = None
            for step in range(STEPS):
                term = kept[step, layer, k, at, :] * load(4 + step, layer, t, k)
                total = term if total is None else total + term
            g[layer, k, at, :] = -total
    for layer in range(2):
        total = None
        for k in range(n_lanes):
            for part in split2(row_pairs(g, (layer, k), n_tiles * SUB // PIX)):
                term = dot(part, mats[k])
                total = term if total is None else total + term
        pooled[layer] = total

    vals[...] = by_tile([cone_filter(pooled.at[layer], rows // PIX, PAD // PIX) for layer in range(2)])

    for t in range(n_tiles):
        for kind in range(4 + STEPS):
            at = pl.ds(t * SUB, SUB)
            if t not in halo_of:
                base[kind, at, :] = base_in[kind, at, :]
            elif kind < 4 or t not in (0, n_tiles - 1):
                base[kind, at, :] = edge_tile(
                    lambda kind, layer, k: load(kind, layer, t, k), kind, lane, n_lanes
                )


def cone_filter(pooled, out_pix, first):
    weights = cone_weights(RADIUS)
    reach = RADIUS - 1
    lane = lax.broadcasted_iota(jnp.int32, (out_pix, LANES), 1)
    at = [pooled[pl.ds(first + s, out_pix), :] for s in range(-reach, reach + 1)]
    sums = [at[reach]] + [at[reach + s] + at[reach - s] for s in range(1, reach + 1)]
    total = None
    for shift in range(reach + 1):
        mixed = None
        for s in range(reach + 1):
            weight = float(weights[reach + s, reach + shift])
            if weight > 0.0:
                term = weight * sums[s]
                mixed = term if mixed is None else mixed + term
        if shift == 0:
            total = mixed
        else:
            total = total + turn(jnp.where(lane < shift, 0.0, mixed), -shift, 1)
            total = total + turn(jnp.where(lane >= LANES - shift, 0.0, mixed), shift, 1)
    return total


def by_tile(blocks):
    span = TS // PIX
    tile_rows = blocks[0].shape[0] // span
    x = jnp.stack([block.reshape(tile_rows, span, LANES) for block in blocks], axis=1)
    x = x.reshape(tile_rows * 2, span, LANES)
    group = lax.broadcasted_iota(jnp.int32, x.shape, 2) // span
    row = lax.broadcasted_iota(jnp.int32, x.shape, 1)
    for bit in (1, 2, 4):
        row_on, lane_on = (row & bit) != 0, (group & bit) != 0
        ahead = turn(turn(x, -bit, 1), bit * span, 2)
        behind = turn(turn(x, bit, 1), -bit * span, 2)
        x = jnp.where(row_on == lane_on, x, jnp.where(lane_on, ahead, behind))
    x = x.reshape(tile_rows, 2, span, LANES)
    even, odd = x[:, 0], x[:, 1]
    upper = lax.broadcasted_iota(jnp.int32, even.shape, 2) >= HALF
    new_even = jnp.where(upper, turn(odd, HALF, 2), even)
    new_odd = jnp.where(upper, odd, turn(even, HALF, 2))
    return jnp.stack([new_even, new_odd], axis=1).reshape(tile_rows * 2 * span, LANES)


def merge_spans(rows_of, lane):
    even = (lane & 1) == 0
    window = ((lane - OUT) & (HALF - 1)) < SIDE
    merged = []
    for e in (0, 4):
        low = jnp.where(even, rows_of(e), turn(rows_of(e + 1), 1, 1))
        high = jnp.where(even, turn(rows_of(e + 2), SIDE, 1), turn(rows_of(e + 3), SIDE + 1, 1))
        merged.append(jnp.where(window, low, high))
    return jnp.concatenate(merged, axis=1)


def edge_kernel(
    vals_in, base, cross, near, src, place, spread, last, out_slots,
    first, state, e, kept, g, pooled, pixels, vals,
):
    ext_rows = base.shape[1]
    rows = ext_rows - 2 * PAD
    n_tiles, n = ext_rows // SUB, spread_rows(ext_rows)
    lane, odd = lanes(), is_odd("gy")
    spot = lane & (HALF - 1)
    is_left, is_right = spot < OUT, spot >= HALF - OUT

    def load(kind, t):
        at = pl.ds(t * SUB, SUB)
        far, close = cross[at, :], near[at, :]
        high, low = jnp.where(odd, close, far), jnp.where(odd, far, close)
        value = jnp.where(is_left, turn(high, OUT - WIDTHS[kind] - FIRST[kind], 1), base[kind, at, :])
        return jnp.where(is_right, turn(low, HALF - OUT - FIRST[kind], 1), value)

    zero = jnp.zeros((SUB, LANES), F32)
    for t in range(n):
        at = pl.ds(t * SUB, SUB)
        for kind in range(3):
            first[kind, at, :] = load(kind, t) if t < n_tiles else zero
        e[at, :] = COURANT * load(3, t) if t < n_tiles else zero

    before = (lax.axis_index("gy") + lane * 0) > 0
    coef_x = jnp.where(before | (spot >= OUT), COURANT, 0.0).astype(F32)

    def keep(step, key, r, value):
        kept[step, nth(r, n), :] = value

    def finish(kind, key, r, value):
        last[kind, nth(r, n), :] = value

    yee(
        n, [()],
        lambda kind, key, r: first[kind, nth(r, n), :],
        state,
        lambda key, r: e[nth(r, n), :],
        lambda step, key, r: src[step, pl.ds(r * SUB, SUB), :],
        keep, finish, coef_x,
        lambda values: {(): turn(values[()], -1, 1)},
        lambda values: {(): turn(values[()], 1, 1)},
        lambda values, key: turn(values[()], HALF, 1),
    )

    inside = (spot >= OUT - NEAR) & (spot < OUT + KEEP)
    inside = inside | ((spot >= HALF - OUT - KEEP) & (spot < HALF - OUT + NEAR))
    for t in range(1, n_tiles - 1):
        at = pl.ds(t * SUB, SUB)
        total = None
        for step in range(STEPS):
            term = kept[step, at, :] * load(4 + step, t)
            total = term if total is None else total + term
        g[at, :] = jnp.where(inside, -total, 0.0)

    summed = row_pairs(g, (), ext_rows // PIX)
    pooled[...] = summed + turn(summed, -1, 1)
    weights = cone_weights(RADIUS)
    reach = RADIUS - 1
    out_pix, top = rows // PIX, PAD // PIX
    at = [pooled[pl.ds(top + s, out_pix), :] for s in range(-reach, reach + 1)]
    sums = [at[reach]] + [at[reach + s] + at[reach - s] for s in range(1, reach + 1)]
    total = None
    for shift in range(reach + 1):
        mixed = None
        for s in range(reach + 1):
            weight = float(weights[reach + s, reach + shift])
            if weight > 0.0:
                term = weight * sums[s]
                mixed = term if mixed is None else mixed + term
        if shift:
            mixed = turn(mixed, -PIX * shift, 1) + turn(mixed, PIX * shift, 1)
        total = mixed if total is None else total + mixed
    pixels[...] = total

    span = TS // PIX
    tile_rows, tile_cols = rows // TS, vals.shape[0] // (rows // TS)
    merged = merge_spans(lambda row: pixels[pl.ds(row, tile_rows, stride=span), :], lane)
    high, low = split2(merged)
    edge = dot(high, spread[...]) + dot(low, spread[...])
    vals[...] = vals_in[...]
    for side, row in enumerate((0, tile_cols - 1)):
        spots = pl.ds(row, tile_rows, stride=tile_cols)
        vals[spots, :] = vals[spots, :] + edge[:, side * LANES : (side + 1) * LANES]
    high, low = split2(vals[...])
    out_slots[...] = dot(place[...], high) + dot(place[...], low)


def merge_kernel(last, edge_last, out_fields, merged, sem):
    rows, cols = merged.shape[2], merged.shape[3]
    n_lanes = cols // LANES
    lane = lanes()
    for t in range(rows // SUB):
        at, out_at = pl.ds(PAD + t * SUB, SUB), pl.ds(t * SUB, SUB)
        for kind in range(3):
            edge = edge_last[kind, at, :]
            for layer in range(2):
                for k in range(n_lanes):
                    value = last[kind, layer, k, at, :]
                    if k == 0:
                        value = jnp.where(lane < KEEP, turn(edge, -HALF * layer - OUT, 1), value)
                    if k == n_lanes - 1:
                        value = jnp.where(
                            lane >= LANES - KEEP, turn(edge, -HALF * layer - SIDE - OUT, 1), value
                        )
                    merged[kind, layer, out_at, lane_tile(k)] = value
    copy = pltpu.make_async_copy(merged, out_fields, sem)
    copy.start()
    copy.wait()


def deliver_kernel(array, out, sems):
    parts = sems.shape[0]
    size = array.shape[0] // parts
    copies = [
        pltpu.make_async_copy(
            array.at[pl.ds(i * size, size)], out.at[0, pl.ds(i * size, size)], sems.at[i]
        )
        for i in range(parts)
    ]
    for copy in copies:
        copy.start()
    for copy in copies:
        copy.wait()


def vmem():
    return pl.BlockSpec(memory_space=pltpu.VMEM)


def shape(*dims, dtype=F32):
    return jax.ShapeDtypeStruct(dims, dtype)


def call(kernel, outs, n_in, *, in_space=pltpu.VMEM, out_specs=None, scratch=(), flops=0, size=0):
    return pl.pallas_call(
        kernel,
        out_shape=outs,
        in_specs=[pl.BlockSpec(memory_space=in_space)] * n_in,
        out_specs=out_specs or tuple(vmem() for _ in outs),
        scratch_shapes=list(scratch),
        compiler_params=pltpu.CompilerParams(vmem_limit_bytes=40 * 1024 * 1024),
        cost_estimate=pl.CostEstimate(flops=flops, bytes_accessed=size, transcendentals=0),
    )


def on_device(adj_fields, inv_eps, fwd_diff, mon_x, mon_y, mon_amp, design_mask, tile_owner):
    rows, cols = adj_fields.shape[2], adj_fields.shape[3]
    assert cols == 2 * LANES and rows % TS == 0
    gx_count, gy_count = lax.axis_size("gx"), lax.axis_size("gy")
    owners = gx_count * gy_count
    tiles = (rows // TS) * (cols // TS)
    width = 2 * (TS // PIX) ** 2
    assert width == LANES
    capacity = max(8, 2 * tiles // owners)
    assert rows == TS * SUB and cols == 2 * TS * SUB
    ext_rows = rows + 2 * PAD
    long_rows = SUB * spread_rows(ext_rows)
    n_lanes = cols // LANES
    cells = rows * cols
    blocks = (adj_fields, inv_eps, fwd_diff)


    strip = shape(16, SUB, cols)
    cross, near = call(
        rows_kernel, (strip, strip), 3, in_space=pltpu.HBM,
        scratch=(
            pltpu.VMEM((2, 4, 2, PAD, cols), F32),
            pltpu.VMEM((2, STEPS, 2, SUB, cols), F32),
            pltpu.SemaphoreType.DMA((6,)),
        ),
        size=2**20,
    )(*(pltpu.with_memory_space_constraint(block, pltpu.HBM) for block in blocks))

    def pairs(count, start):
        some = [(i, i + 1) for i in range(start, count - 1, 2)]
        return some + [(j, i) for i, j in some]

    cross = lax.ppermute(cross, "gx", pairs(gx_count, 1))
    near = lax.ppermute(near, "gx", pairs(gx_count, 0))

    packed = shape(ext_rows, LANES)
    channels = mon_x.shape[0]
    cross_cols, near_cols, base, src, src_edge, place = call(
        lambda *refs: prep_kernel(capacity, *refs),
        (
            packed,
            packed,
            shape(4 + STEPS, ext_rows, LANES),
            shape(STEPS, 2, long_rows, cols),
            shape(STEPS, long_rows, LANES),
            shape(owners * capacity, tiles, dtype=BF16),
        ),
        8,
        flops=16 * ext_rows * (cols + LANES) * 3 * channels,
        size=64 * cells,
    )(
        *blocks,
        mon_x.reshape(1, channels),
        mon_y.reshape(1, channels),
        mon_amp,
        design_mask.reshape(1, tiles),
        tile_owner.reshape(1, tiles),
    )
    cross_cols, near_cols = call(
        corners_kernel, (packed, packed), 4, flops=cells, size=8 * ext_rows * LANES
    )(cross_cols, near_cols, cross, near)
    cross_cols = lax.ppermute(cross_cols, "gy", pairs(gy_count, 1))
    near_cols = lax.ppermute(near_cols, "gy", pairs(gy_count, 0))

    state = (3, 2, n_lanes, long_rows, LANES)
    last, vals, base = call(
        inner_kernel,
        (shape(*state), shape(tiles, LANES), shape(4 + STEPS, ext_rows, LANES)),
        8,
        scratch=(
            pltpu.VMEM(state, F32),
            pltpu.VMEM(state, F32),
            pltpu.VMEM((2, n_lanes, long_rows, LANES), F32),
            pltpu.VMEM((STEPS, 2, n_lanes, long_rows, LANES), F32),
            pltpu.VMEM((2, n_lanes, ext_rows, LANES), F32),
            pltpu.VMEM((2, ext_rows // PIX, LANES), F32),
        ),
        flops=200 * cells,
        size=96 * cells,
    )(*blocks, cross, near, src, pool_matrices(), base)

    edge_state = (3, long_rows, LANES)
    edge_last, outgoing = call(
        edge_kernel,
        (shape(*edge_state), shape(owners * capacity, width)),
        7,
        scratch=(
            pltpu.VMEM(edge_state, F32),
            pltpu.VMEM(edge_state, F32),
            pltpu.VMEM((long_rows, LANES), F32),
            pltpu.VMEM((STEPS, long_rows, LANES), F32),
            pltpu.VMEM((ext_rows, LANES), F32),
            pltpu.VMEM((ext_rows // PIX, LANES), F32),
            pltpu.VMEM((rows // PIX, LANES), F32),
            pltpu.VMEM((tiles, LANES), F32),
        ),
        flops=100 * cells,
        size=32 * cells,
    )(vals, base, cross_cols, near_cols, src_edge, place, spread_matrix())
    (fields,) = call(
        merge_kernel,
        (shape(3, 2, rows, cols),),
        2,
        out_specs=(pl.BlockSpec(memory_space=pl.ANY),),
        scratch=(pltpu.VMEM((3, 2, rows, cols), F32), pltpu.SemaphoreType.DMA),
        flops=20 * cells,
        size=48 * cells,
    )(last, edge_last)

    outgoing = outgoing.reshape(owners, capacity, width)
    incoming = lax.all_to_all(outgoing, ("gx", "gy"), split_axis=0, concat_axis=0, tiled=True)
    (incoming,) = call(
        deliver_kernel,
        (shape(1, *incoming.shape),),
        1,
        out_specs=(pl.BlockSpec(memory_space=pl.ANY),),
        scratch=(pltpu.SemaphoreType.DMA((4,)),),
        size=8 * owners * capacity * width,
    )(pltpu.with_memory_space_constraint(incoming, pltpu.VMEM))
    return fields, incoming


def solution(mesh):
    placed = (
        P(None, None, ("parts", "gx"), "gy"),
        P(None, ("parts", "gx"), "gy"),
        P(None, None, ("parts", "gx"), "gy"),
        P("parts"),
        P("parts"),
        P(None, "parts"),
        P(("parts", "gx"), "gy", None),
        P(("parts", "gx"), "gy", None, None),
    )
    return jax.shard_map(
        on_device,
        mesh=mesh,
        in_specs=placed,
        out_specs=(
            P(None, None, ("parts", "gx"), "gy"),
            P(("parts", "gx", "gy"), None, None, None),
        ),
        check_vma=False,
    )
```

```python
import jax
import jax.numpy as jnp
import ml_dtypes
import numpy as np
from jax import lax
from jax.experimental import pallas as pl
from jax.experimental.pallas import tpu as pltpu
from jax.sharding import PartitionSpec as P

STEPS = 4
PIX = 2
TS = 16
RADIUS = 4
COURANT = 0.6
COUPLING = 0.25

LANES = 128
SUB = 8
FAR = STEPS + PIX * (RADIUS - 1)
NEAR = PIX * (RADIUS - 1)
LEFT_OVER = FAR - SUB
PAD = 2 * SUB
HALF = LANES // 2
SIDE = HALF // 2
OUT = SIDE // 2
KEEP = 8
F32 = jnp.float32
BF16 = jnp.bfloat16
WIDTHS = (FAR,) * 4 + (NEAR,) * STEPS
FIRST = tuple(sum(WIDTHS[:k]) for k in range(len(WIDTHS)))
assert sum(WIDTHS) <= HALF and FAR <= OUT and STEPS + KEEP <= OUT


def cone_weights(radius):
    reach_cells = radius - 1
    offsets = np.arange(-reach_cells, reach_cells + 1)
    distance = np.sqrt(offsets[:, None] * offsets[:, None] + offsets[None, :] * offsets[None, :])
    weights = np.maximum(radius - distance, 0.0)
    return weights / weights.sum()


def pool_matrices():
    inner = np.zeros((2, LANES, LANES), np.float32)
    for j in range(KEEP, 2 * LANES - KEEP):
        inner[j // LANES, j % LANES, j // PIX] = 1.0
    return inner.astype(ml_dtypes.bfloat16)


def spread_matrix():
    span = TS // PIX
    result = np.zeros((2, LANES, 2, 2, span, span), np.float32)
    for e in range(span):
        move = (e % 2) + SIDE * (e % 4 // 2)
        for layer in range(2):
            for side in range(2):
                for f in range(span):
                    lane = (HALF * layer + OUT + OUT * side + PIX * f + move) % LANES
                    result[e // 4, lane, side, layer, e, f] = 1.0
    return result.reshape(2 * LANES, 2 * LANES).astype(ml_dtypes.bfloat16)


def split2(value):
    high = value.astype(BF16)
    return high, (value - high.astype(F32)).astype(BF16)


def split3(value):
    high = value.astype(BF16)
    rest = value - high.astype(F32)
    mid = rest.astype(BF16)
    return high, mid, (rest - mid.astype(F32)).astype(BF16)


def dot(a, b):
    return jnp.dot(a, b, preferred_element_type=F32)


def turn(value, shift, axis):
    size = value.shape[axis]
    return pltpu.roll(value, shift % size, axis) if shift % size else value


def lanes():
    return lax.broadcasted_iota(jnp.int32, (SUB, LANES), 1)


def subs():
    return lax.broadcasted_iota(jnp.int32, (SUB, LANES), 0)


def lane_tile(k):
    return pl.ds(k * LANES, LANES)


def is_odd(axis):
    return ((subs() * 0 + lax.axis_index(axis)) & 1) == 1


def rows_kernel(fields, eps, fwd, cross, near, hold, hold_fwd, sems):
    rows, cols = fields.shape[2], fields.shape[3]
    copies = []
    for n, at in enumerate((0, rows - PAD)):
        at_fwd = 0 if n == 0 else rows - SUB
        pairs = (
            (fields.at[:, :, pl.ds(at, PAD), :], hold.at[n, pl.ds(0, 3)]),
            (eps.at[:, pl.ds(at, PAD), :], hold.at[n, 3]),
            (fwd.at[:, :, pl.ds(at_fwd, SUB), :], hold_fwd.at[n]),
        )
        for m, (src, dst) in enumerate(pairs):
            copies.append(pltpu.make_async_copy(src, dst, sems.at[3 * n + m]))
    for copy in copies:
        copy.start()
    for copy in copies:
        copy.wait()
    odd, sub = is_odd("gx"), subs()
    for kind in range(4):
        for layer in range(2):
            plane = 2 * kind + layer
            for k in range(cols // LANES):
                at = lane_tile(k)
                low = hold[0, kind, layer, pl.ds(0, SUB), at]
                high = hold[1, kind, layer, pl.ds(SUB, SUB), at]
                cross[plane, :, at] = jnp.where(odd, high, low)
                near[plane, :, at] = jnp.where(odd, low, high)
                rest_low = turn(hold[0, kind, layer, pl.ds(SUB, SUB), at], -LEFT_OVER, 0)
                rest_high = turn(hold[1, kind, layer, pl.ds(0, SUB), at], LEFT_OVER, 0)
                low = jnp.where(sub >= NEAR, rest_low, hold_fwd[0, kind, layer, :, at])
                high = jnp.where(sub < SUB - NEAR, rest_high, hold_fwd[1, kind, layer, :, at])
                cross[8 + plane, :, at] = jnp.where(odd, high, low)
                near[8 + plane, :, at] = jnp.where(odd, low, high)


def halo_tile(cross, near, odd, tile, kind, layer, at):
    is_above = tile < 2
    outer = tile in (0, 3)
    if outer and kind >= 4:
        return None
    plane = 2 * kind + layer + (8 if outer else 0)
    a, b = near[plane, :, at], cross[plane, :, at]
    value = jnp.where(odd, a, b) if is_above else jnp.where(odd, b, a)
    if outer:
        value = turn(value, -LEFT_OVER if is_above else LEFT_OVER, 0)
    return value


def core_tile(fields, eps, fwd, at, kind, layer, cols):
    if kind < 3:
        return fields[kind, layer, at, cols]
    if kind == 3:
        return eps[layer, at, cols]
    return fwd[kind - 4, layer, at, cols]


def pack_tile(load, lane, right):
    total = jnp.zeros((SUB, LANES), F32)
    for kind, width in enumerate(WIDTHS):
        for layer in range(2):
            value = load(kind, layer)
            if value is None:
                continue
            first = FIRST[kind] + HALF * layer
            value = turn(value, first + width if right else first, 1)
            total = jnp.where((lane >= first) & (lane < first + width), value, total)
    return total


def edge_tile(load, kind, lane, n_lanes):
    spot = lane & (HALF - 1)
    total = None
    for layer in range(2):
        low = turn(load(kind, layer, 0), HALF * layer + OUT, 1)
        high = turn(load(kind, layer, n_lanes - 1), HALF * layer + SIDE + OUT, 1)
        value = jnp.where(spot < SIDE, low, high)
        total = value if total is None else jnp.where(lane < HALF, total, value)
    return total


def cols_kernel(fields, eps, fwd, cross, near, base):
    rows, cols = fields.shape[2], fields.shape[3]
    n_lanes = cols // LANES
    lane, odd = lanes(), is_odd("gy")

    def tile(t, carry):
        at = pl.ds(pl.multiple_of(t * SUB, SUB), SUB)
        out_at = pl.ds(pl.multiple_of(t * SUB + PAD, SUB), SUB)

        def load(kind, layer, k):
            return core_tile(fields, eps, fwd, at, kind, layer, lane_tile(k))

        left = pack_tile(lambda kind, layer: load(kind, layer, 0), lane, False)
        right = pack_tile(lambda kind, layer: load(kind, layer, n_lanes - 1), lane, True)
        cross[out_at, :] = jnp.where(odd, right, left)
        near[out_at, :] = jnp.where(odd, left, right)
        for kind in range(4 + STEPS):
            base[kind, out_at, :] = edge_tile(load, kind, lane, n_lanes)
        return carry

    lax.fori_loop(0, rows // SUB, tile, 0, unroll=4)
    zero = jnp.zeros((PAD, LANES), F32)
    for out in (cross, near) + tuple(base.at[kind] for kind in range(4 + STEPS)):
        out[pl.ds(0, PAD), :] = zero
        out[pl.ds(PAD + rows, PAD), :] = zero


def corners_kernel(cross_in, near_in, cross_rows, near_rows, cross, near):
    rows, cols = cross.shape[0] - 2 * PAD, cross_rows.shape[2]
    lane, odd, odd_col = lanes(), is_odd("gx"), is_odd("gy")
    core = pl.ds(PAD, rows)
    cross[core, :] = cross_in[core, :]
    near[core, :] = near_in[core, :]
    for tile in range(4):
        at = pl.ds(tile * SUB if tile < 2 else PAD + rows + (tile - 2) * SUB, SUB)
        left, right = (
            pack_tile(
                lambda kind, layer: halo_tile(
                    cross_rows, near_rows, odd, tile, kind, layer, pl.ds(lo, LANES)
                ),
                lane, is_right,
            )
            for lo, is_right in ((0, False), (cols - LANES, True))
        )
        cross[at, :] = jnp.where(odd_col, right, left)
        near[at, :] = jnp.where(odd_col, left, right)


def prep_kernel(
    capacity, fields, eps, fwd, mon_x, mon_y, amp, mask, owner, cross, near, base, src, src_edge, place
):
    cols_kernel(fields, eps, fwd, cross, near, base)
    side_kernel(capacity, fields.shape[2], mon_x, mon_y, amp, mask, owner, src, src_edge, place)


def side_kernel(capacity, rows, mon_x, mon_y, amp, mask, owner, src, src_edge, place):
    _, _, ext_rows, cols = src.shape
    channels = mon_x.shape[1]
    row = mon_x[...] - lax.axis_index("gx") * rows + PAD
    col = mon_y[...] - lax.axis_index("gy") * cols
    in_left = (col >= -OUT) & (col < OUT)
    in_right = (col >= cols - OUT) & (col < cols + OUT)
    edge = jnp.where(in_left, col + OUT, jnp.where(in_right, col - cols + OUT + SIDE, -LANES))
    layer = lax.broadcasted_iota(jnp.int32, (1, channels), 1) & 1
    edge = edge + HALF * layer
    inside = jnp.where((col >= 0) & (col < cols), col, -1)
    one_y = lax.broadcasted_iota(jnp.int32, (cols, channels), 0) == inside
    one_e = lax.broadcasted_iota(jnp.int32, (LANES, channels), 0) == edge
    one_y = jnp.where(one_y, 1.0, 0.0).astype(BF16)
    one_e = jnp.where(one_e, 1.0, 0.0).astype(BF16)
    one_y = jnp.concatenate([one_y] * 3, axis=1)
    one_e = jnp.concatenate([one_e] * 3, axis=1)
    one_x = lax.broadcasted_iota(jnp.int32, (ext_rows, channels), 0) == row
    one_x = jnp.where(one_x, 1.0, 0.0).astype(F32)
    nt = (((1,), (1,)), ((), ()))
    for step in range(STEPS):
        parts = [part.astype(F32) for part in split3(amp[pl.ds(step, 1), :])]
        lhs = jnp.concatenate([one_x * part for part in parts], axis=1)
        src_edge[step] = lax.dot_general(lhs.astype(BF16), one_e, nt, preferred_element_type=F32)
        layer_wide = jnp.concatenate([layer] * 3, axis=1)
        for which in range(2):
            some = jnp.where(layer_wide == which, lhs, 0.0).astype(BF16)
            src[step, which] = lax.dot_general(some, one_y, nt, preferred_element_type=F32)
    tiles = owner.shape[1]
    own = owner[...].astype(F32)
    own_wide = jnp.broadcast_to(own, (tiles, tiles))
    earlier = lax.broadcasted_iota(jnp.int32, (tiles, tiles), 0) < lax.broadcasted_iota(
        jnp.int32, (tiles, tiles), 1
    )
    same = (own_wide.T == own_wide) & earlier
    slot = jnp.sum(jnp.where(same, 1.0, 0.0), axis=0, keepdims=True)
    dest = owner[...] * capacity + slot.astype(jnp.int32)
    dest = jnp.where(mask[...] != 0, dest, -1)
    hit = lax.broadcasted_iota(jnp.int32, place.shape, 0) == dest
    place[...] = jnp.where(hit, 1.0, 0.0).astype(BF16)


def yee(bufs, keys, eps_of, change_of, src_of, grad, coef_x, coef_first, next_col, prev_col, other):
    n_tiles = (bufs[0].shape[-2] - 2 * SUB) // SUB
    for step in range(STEPS):
        old, new = ((0, 1), (1, 0), (0, 1), (1, 2))[step]
        old, new = bufs[old], bufs[new]
        low = 0 if step < 2 else 1
        high = n_tiles if step == 0 else n_tiles - 1
        for t in range(low, high):
            at = pl.ds(SUB + t * SUB, SUB)
            under = pl.ds(SUB + t * SUB + 1, SUB)
            over = pl.ds(SUB + t * SUB - 1, SUB)
            coef_y = coef_first if t < PAD // SUB else COURANT
            e = {key: old[(0,) + key + (at, slice(None))] for key in keys}
            e_right = next_col(e)
            hx, hy = {}, {}
            for key in keys:
                hx[key] = old[(1,) + key + (at, slice(None))] + coef_x * (e_right[key] - e[key])
                below = old[(0,) + key + (under, slice(None))]
                hy[key] = old[(2,) + key + (at, slice(None))] - coef_y * (below - e[key])
                new[(1,) + key + (at, slice(None))] = hx[key]
                new[(2,) + key + (at, slice(None))] = hy[key]
            hx_left = prev_col(hx)
            for key in keys:
                hy_above = new[(2,) + key + (over, slice(None))]
                curl = (hy[key] - hy_above) - (hx[key] - hx_left[key])
                curl = curl + COUPLING * (other(e, key) - e[key])
                value = e[key] - eps_of(key, t) * curl + src_of(step, key, t)
                new[(0,) + key + (at, slice(None))] = value
                if 1 <= t < n_tiles - 1:
                    change = value * change_of(step, key, t)
                    where = key + (pl.ds(t * SUB, SUB), slice(None))
                    grad[where] = -change if step == 0 else grad[where] - change


def coef_above():
    return jnp.where((subs() * 0 + lax.axis_index("gx")) > 0, COURANT, 0.0).astype(F32)


def clear_rims(buf):
    size = buf.shape[-2]
    zero = jnp.zeros(buf.shape[:-2] + (SUB, LANES), F32)
    lead = (slice(None),) * (len(buf.shape) - 2)
    buf[lead + (pl.ds(0, SUB), slice(None))] = zero
    buf[lead + (pl.ds(size - SUB, SUB), slice(None))] = zero


def row_pairs(ref, lead, count):
    even = ref[lead + (pl.ds(0, count, stride=PIX), slice(None))]
    return even + ref[lead + (pl.ds(1, count, stride=PIX), slice(None))]


def inner_kernel(fields, eps, fwd, cross, near, src, base_in, last, g, base, a, b, e):
    rows, cols = fields.shape[2], fields.shape[3]
    n_tiles = (rows + 2 * PAD) // SUB
    n_lanes = cols // LANES
    lane, odd = lanes(), is_odd("gx")
    halo_of = {0: 0, 1: 1, n_tiles - 2: 2, n_tiles - 1: 3}

    def load(kind, layer, t, k):
        if t in halo_of:
            return halo_tile(cross, near, odd, halo_of[t], kind, layer, lane_tile(k))
        return core_tile(fields, eps, fwd, pl.ds(t * SUB - PAD, SUB), kind, layer, lane_tile(k))

    for buf in (a, b, last):
        clear_rims(buf)
    for t in range(n_tiles):
        for layer in range(2):
            for k in range(n_lanes):
                for kind in range(3):
                    a[kind, layer, k, pl.ds(SUB + t * SUB, SUB), :] = load(kind, layer, t, k)
                e[layer, k, pl.ds(t * SUB, SUB), :] = COURANT * load(3, layer, t, k)

    at_end, at_start = lane == LANES - 1, lane == 0
    keys = [(layer, k) for layer in range(2) for k in range(n_lanes)]

    def next_col(values):
        moved = {key: turn(value, -1, 1) for key, value in values.items()}
        return {
            (l, k): jnp.where(at_end, moved[l, (k + 1) % n_lanes], moved[l, k]) for l, k in keys
        }

    def prev_col(values):
        moved = {key: turn(value, 1, 1) for key, value in values.items()}
        return {
            (l, k): jnp.where(at_start, moved[l, (k - 1) % n_lanes], moved[l, k]) for l, k in keys
        }

    yee(
        (a, b, last), keys,
        lambda key, t: e[key + (pl.ds(t * SUB, SUB), slice(None))],
        lambda step, key, t: load(4 + step, key[0], t, key[1]),
        lambda step, key, t: src[step, key[0], pl.ds(t * SUB, SUB), lane_tile(key[1])],
        g, COURANT, coef_above(), next_col, prev_col,
        lambda values, key: values[1 - key[0], key[1]],
    )
    for t in range(n_tiles):
        for kind in range(4 + STEPS):
            at = pl.ds(t * SUB, SUB)
            if t not in halo_of:
                base[kind, at, :] = base_in[kind, at, :]
            elif kind < 4 or t not in (0, n_tiles - 1):
                base[kind, at, :] = edge_tile(
                    lambda kind, layer, k: load(kind, layer, t, k), kind, lane, n_lanes
                )


def inner_tiles_kernel(g, mats, vals, pooled):
    n_lanes, ext_rows = g.shape[1], g.shape[2]
    for layer in range(2):
        total = None
        for k in range(n_lanes):
            for part in split2(row_pairs(g, (layer, k), ext_rows // PIX)):
                term = dot(part, mats[k])
                total = term if total is None else total + term
        pooled[layer] = total

    out_pix = ext_rows // PIX - 2 * PAD // PIX
    vals[...] = by_tile([cone_filter(pooled.at[layer], out_pix, PAD // PIX) for layer in range(2)])


def cone_filter(pooled, out_pix, first):
    weights = cone_weights(RADIUS)
    reach = RADIUS - 1
    lane = lax.broadcasted_iota(jnp.int32, (out_pix, LANES), 1)
    at = [pooled[pl.ds(first + s, out_pix), :] for s in range(-reach, reach + 1)]
    sums = [at[reach]] + [at[reach + s] + at[reach - s] for s in range(1, reach + 1)]
    total = None
    for shift in range(reach + 1):
        mixed = None
        for s in range(reach + 1):
            weight = float(weights[reach + s, reach + shift])
            if weight > 0.0:
                term = weight * sums[s]
                mixed = term if mixed is None else mixed + term
        if shift == 0:
            total = mixed
        else:
            total = total + turn(jnp.where(lane < shift, 0.0, mixed), -shift, 1)
            total = total + turn(jnp.where(lane >= LANES - shift, 0.0, mixed), shift, 1)
    return total


def by_tile(blocks):
    span = TS // PIX
    tile_rows = blocks[0].shape[0] // span
    x = jnp.stack([block.reshape(tile_rows, span, LANES) for block in blocks], axis=1)
    x = x.reshape(tile_rows * 2, span, LANES)
    group = lax.broadcasted_iota(jnp.int32, x.shape, 2) // span
    row = lax.broadcasted_iota(jnp.int32, x.shape, 1)
    for bit in (1, 2, 4):
        row_on, lane_on = (row & bit) != 0, (group & bit) != 0
        ahead = turn(turn(x, -bit, 1), bit * span, 2)
        behind = turn(turn(x, bit, 1), -bit * span, 2)
        x = jnp.where(row_on == lane_on, x, jnp.where(lane_on, ahead, behind))
    x = x.reshape(tile_rows, 2, span, LANES)
    even, odd = x[:, 0], x[:, 1]
    upper = lax.broadcasted_iota(jnp.int32, even.shape, 2) >= HALF
    new_even = jnp.where(upper, turn(odd, HALF, 2), even)
    new_odd = jnp.where(upper, odd, turn(even, HALF, 2))
    return jnp.stack([new_even, new_odd], axis=1).reshape(tile_rows * 2 * span, LANES)


def merge_spans(rows_of, lane):
    even = (lane & 1) == 0
    window = ((lane - OUT) & (HALF - 1)) < SIDE
    merged = []
    for e in (0, 4):
        low = jnp.where(even, rows_of(e), turn(rows_of(e + 1), 1, 1))
        high = jnp.where(even, turn(rows_of(e + 2), SIDE, 1), turn(rows_of(e + 3), SIDE + 1, 1))
        merged.append(jnp.where(window, low, high))
    return jnp.concatenate(merged, axis=1)


def edge_kernel(base, cross, near, src, c, g, a, b, e, d):
    ext_rows = base.shape[1]
    rows = ext_rows - 2 * PAD
    n_tiles = ext_rows // SUB
    lane, odd = lanes(), is_odd("gy")
    spot = lane & (HALF - 1)
    is_left, is_right = spot < OUT, spot >= HALF - OUT

    for buf in (a, b, c):
        clear_rims(buf)
    for t in range(n_tiles):
        at = pl.ds(t * SUB, SUB)
        far, close = cross[at, :], near[at, :]
        high, low = jnp.where(odd, close, far), jnp.where(odd, far, close)
        for kind, width in enumerate(WIDTHS):
            if kind >= 4 and t in (0, n_tiles - 1):
                continue
            value = jnp.where(is_left, turn(high, OUT - width - FIRST[kind], 1), base[kind, at, :])
            value = jnp.where(is_right, turn(low, HALF - OUT - FIRST[kind], 1), value)
            if kind < 3:
                a[kind, pl.ds(SUB + t * SUB, SUB), :] = value
            elif kind == 3:
                e[at, :] = COURANT * value
            else:
                d[kind - 4, at, :] = value

    before = (lax.axis_index("gy") + lane * 0) > 0
    coef_x = jnp.where(before | (spot >= OUT), COURANT, 0.0).astype(F32)
    yee(
        (a, b, c), [()],
        lambda key, t: e[pl.ds(t * SUB, SUB), :],
        lambda step, key, t: d[step, pl.ds(t * SUB, SUB), :],
        lambda step, key, t: src[step, pl.ds(t * SUB, SUB), :],
        g, coef_x, coef_above(),
        lambda values: {(): turn(values[()], -1, 1)},
        lambda values: {(): turn(values[()], 1, 1)},
        lambda values, key: turn(values[()], HALF, 1),
    )

    inside = (spot >= OUT - NEAR) & (spot < OUT + KEEP)
    inside = inside | ((spot >= HALF - OUT - KEEP) & (spot < HALF - OUT + NEAR))
    for t in range(1, n_tiles - 1):
        at = pl.ds(t * SUB, SUB)
        g[at, :] = jnp.where(inside, g[at, :], 0.0)


def tiles_kernel(vals_in, g, place, spread, out_slots, pooled, pixels, vals):
    ext_rows = g.shape[0]
    rows = ext_rows - 2 * PAD
    lane = lanes()
    summed = row_pairs(g, (), ext_rows // PIX)
    pooled[...] = summed + turn(summed, -1, 1)
    weights = cone_weights(RADIUS)
    reach = RADIUS - 1
    out_pix, top = rows // PIX, PAD // PIX
    at = [pooled[pl.ds(top + s, out_pix), :] for s in range(-reach, reach + 1)]
    sums = [at[reach]] + [at[reach + s] + at[reach - s] for s in range(1, reach + 1)]
    total = None
    for shift in range(reach + 1):
        mixed = None
        for s in range(reach + 1):
            weight = float(weights[reach + s, reach + shift])
            if weight > 0.0:
                term = weight * sums[s]
                mixed = term if mixed is None else mixed + term
        if shift:
            mixed = turn(mixed, -PIX * shift, 1) + turn(mixed, PIX * shift, 1)
        total = mixed if total is None else total + mixed
    pixels[...] = total

    span = TS // PIX
    tile_rows, tile_cols = rows // TS, vals.shape[0] // (rows // TS)
    merged = merge_spans(lambda row: pixels[pl.ds(row, tile_rows, stride=span), :], lane)
    high, low = split2(merged)
    edge = dot(high, spread[...]) + dot(low, spread[...])
    vals[...] = vals_in[...]
    for side, row in enumerate((0, tile_cols - 1)):
        spots = pl.ds(row, tile_rows, stride=tile_cols)
        vals[spots, :] = vals[spots, :] + edge[:, side * LANES : (side + 1) * LANES]
    high, low = split2(vals[...])
    out_slots[...] = dot(place[...], high) + dot(place[...], low)


def merge_kernel(last, edge_last, out_fields, merged, sem):
    rows, cols = merged.shape[2], merged.shape[3]
    n_lanes = cols // LANES
    lane = lanes()
    for t in range(rows // SUB):
        at, out_at = pl.ds(SUB + PAD + t * SUB, SUB), pl.ds(t * SUB, SUB)
        for kind in range(3):
            edge = edge_last[kind, at, :]
            for layer in range(2):
                for k in range(n_lanes):
                    value = last[kind, layer, k, at, :]
                    if k == 0:
                        value = jnp.where(lane < KEEP, turn(edge, -HALF * layer - OUT, 1), value)
                    if k == n_lanes - 1:
                        value = jnp.where(
                            lane >= LANES - KEEP, turn(edge, -HALF * layer - SIDE - OUT, 1), value
                        )
                    merged[kind, layer, out_at, lane_tile(k)] = value
    copy = pltpu.make_async_copy(merged, out_fields, sem)
    copy.start()
    copy.wait()


def vmem():
    return pl.BlockSpec(memory_space=pltpu.VMEM)


def shape(*dims, dtype=F32):
    return jax.ShapeDtypeStruct(dims, dtype)


def call(kernel, outs, n_in, *, in_space=pltpu.VMEM, out_specs=None, scratch=(), flops=0, size=0):
    return pl.pallas_call(
        kernel,
        out_shape=outs,
        in_specs=[pl.BlockSpec(memory_space=in_space)] * n_in,
        out_specs=out_specs or tuple(vmem() for _ in outs),
        scratch_shapes=list(scratch),
        compiler_params=pltpu.CompilerParams(vmem_limit_bytes=40 * 1024 * 1024),
        cost_estimate=pl.CostEstimate(flops=flops, bytes_accessed=size, transcendentals=0),
    )


def on_device(adj_fields, inv_eps, fwd_diff, mon_x, mon_y, mon_amp, design_mask, tile_owner):
    rows, cols = adj_fields.shape[2], adj_fields.shape[3]
    assert cols == 2 * LANES and rows % TS == 0
    gx_count, gy_count = lax.axis_size("gx"), lax.axis_size("gy")
    owners = gx_count * gy_count
    tiles = (rows // TS) * (cols // TS)
    width = 2 * (TS // PIX) ** 2
    assert width == LANES
    capacity = max(8, 2 * tiles // owners)
    assert rows == TS * SUB and cols == 2 * TS * SUB
    ext_rows = rows + 2 * PAD
    n_lanes = cols // LANES
    cells = rows * cols
    blocks = (adj_fields, inv_eps, fwd_diff)


    strip = shape(16, SUB, cols)
    cross, near = call(
        rows_kernel, (strip, strip), 3, in_space=pltpu.HBM,
        scratch=(
            pltpu.VMEM((2, 4, 2, PAD, cols), F32),
            pltpu.VMEM((2, STEPS, 2, SUB, cols), F32),
            pltpu.SemaphoreType.DMA((6,)),
        ),
        size=2**20,
    )(*(pltpu.with_memory_space_constraint(block, pltpu.HBM) for block in blocks))

    def pairs(count, start):
        some = [(i, i + 1) for i in range(start, count - 1, 2)]
        return some + [(j, i) for i, j in some]

    cross = lax.ppermute(cross, "gx", pairs(gx_count, 1))
    near = lax.ppermute(near, "gx", pairs(gx_count, 0))

    packed = shape(ext_rows, LANES)
    channels = mon_x.shape[0]
    cross_cols, near_cols, base, src, src_edge, place = call(
        lambda *refs: prep_kernel(capacity, *refs),
        (
            packed,
            packed,
            shape(4 + STEPS, ext_rows, LANES),
            shape(STEPS, 2, ext_rows, cols),
            shape(STEPS, ext_rows, LANES),
            shape(owners * capacity, tiles, dtype=BF16),
        ),
        8,
        flops=16 * ext_rows * (cols + LANES) * 3 * channels,
        size=64 * cells,
    )(
        *blocks,
        mon_x.reshape(1, channels),
        mon_y.reshape(1, channels),
        mon_amp,
        design_mask.reshape(1, tiles),
        tile_owner.reshape(1, tiles),
    )
    cross_cols, near_cols = call(
        corners_kernel, (packed, packed), 4, flops=cells, size=8 * ext_rows * LANES
    )(cross_cols, near_cols, cross, near)
    cross_cols = lax.ppermute(cross_cols, "gy", pairs(gy_count, 1))
    near_cols = lax.ppermute(near_cols, "gy", pairs(gy_count, 0))

    state = (3, 2, n_lanes, ext_rows + 2 * SUB, LANES)
    last, g, base = call(
        inner_kernel,
        (shape(*state), shape(2, n_lanes, ext_rows, LANES), shape(4 + STEPS, ext_rows, LANES)),
        7,
        scratch=(
            pltpu.VMEM(state, F32),
            pltpu.VMEM(state, F32),
            pltpu.VMEM((2, n_lanes, ext_rows, LANES), F32),
        ),
        flops=200 * cells,
        size=96 * cells,
    )(*blocks, cross, near, src, base)
    (vals,) = call(
        inner_tiles_kernel,
        (shape(tiles, LANES),),
        2,
        scratch=(pltpu.VMEM((2, ext_rows // PIX, LANES), F32),),
        flops=100 * cells,
        size=32 * cells,
    )(g, pool_matrices())

    edge_state = (3, ext_rows + 2 * SUB, LANES)
    edge_last, edge_g = call(
        edge_kernel,
        (shape(*edge_state), shape(ext_rows, LANES)),
        4,
        scratch=(
            pltpu.VMEM(edge_state, F32),
            pltpu.VMEM(edge_state, F32),
            pltpu.VMEM((ext_rows, LANES), F32),
            pltpu.VMEM((STEPS, ext_rows, LANES), F32),
        ),
        flops=50 * cells,
        size=16 * cells,
    )(base, cross_cols, near_cols, src_edge)
    (outgoing,) = call(
        tiles_kernel,
        (shape(owners * capacity, width),),
        4,
        scratch=(
            pltpu.VMEM((ext_rows // PIX, LANES), F32),
            pltpu.VMEM((rows // PIX, LANES), F32),
            pltpu.VMEM((tiles, LANES), F32),
        ),
        flops=50 * cells,
        size=16 * cells,
    )(vals, edge_g, place, spread_matrix())
    (fields,) = call(
        merge_kernel,
        (shape(3, 2, rows, cols),),
        2,
        out_specs=(pl.BlockSpec(memory_space=pl.ANY),),
        scratch=(pltpu.VMEM((3, 2, rows, cols), F32), pltpu.SemaphoreType.DMA),
        flops=20 * cells,
        size=48 * cells,
    )(last, edge_last)

    outgoing = outgoing.reshape(owners, capacity, width)
    incoming = lax.all_to_all(outgoing, ("gx", "gy"), split_axis=0, concat_axis=0, tiled=True)
    return fields, incoming[None]


def solution(mesh):
    placed = (
        P(None, None, ("parts", "gx"), "gy"),
        P(None, ("parts", "gx"), "gy"),
        P(None, None, ("parts", "gx"), "gy"),
        P("parts"),
        P("parts"),
        P(None, "parts"),
        P(("parts", "gx"), "gy", None),
        P(("parts", "gx"), "gy", None, None),
    )
    return jax.shard_map(
        on_device,
        mesh=mesh,
        in_specs=placed,
        out_specs=(
            P(None, None, ("parts", "gx"), "gy"),
            P(("parts", "gx", "gy"), None, None, None),
        ),
        check_vma=False,
    )
```

```python
import jax
import jax.numpy as jnp
import ml_dtypes
import numpy as np
from jax import lax
from jax.experimental import pallas as pl
from jax.experimental.pallas import tpu as pltpu
from jax.sharding import PartitionSpec as P

STEPS = 4
PIX = 2
TS = 16
RADIUS = 4
COURANT = 0.6
COUPLING = 0.25

LANES = 128
SUB = 8
FAR = STEPS + PIX * (RADIUS - 1)
NEAR = PIX * (RADIUS - 1)
LEFT_OVER = FAR - SUB
PAD = 2 * SUB
HALF = LANES // 2
SIDE = HALF // 2
OUT = SIDE // 2
KEEP = 8
F32 = jnp.float32
BF16 = jnp.bfloat16
WIDTHS = (FAR,) * 4 + (NEAR,) * STEPS
FIRST = tuple(sum(WIDTHS[:k]) for k in range(len(WIDTHS)))
assert sum(WIDTHS) <= HALF and FAR <= OUT and STEPS + KEEP <= OUT


def cone_weights(radius):
    reach_cells = radius - 1
    offsets = np.arange(-reach_cells, reach_cells + 1)
    distance = np.sqrt(offsets[:, None] * offsets[:, None] + offsets[None, :] * offsets[None, :])
    weights = np.maximum(radius - distance, 0.0)
    return weights / weights.sum()


def pool_matrices():
    inner = np.zeros((2, LANES, LANES), np.float32)
    for j in range(KEEP, 2 * LANES - KEEP):
        inner[j // LANES, j % LANES, j // PIX] = 1.0
    return inner.astype(ml_dtypes.bfloat16)


def spread_matrix():
    span = TS // PIX
    result = np.zeros((2, LANES, 2, 2, span, span), np.float32)
    for e in range(span):
        move = (e % 2) + SIDE * (e % 4 // 2)
        for layer in range(2):
            for side in range(2):
                for f in range(span):
                    lane = (HALF * layer + OUT + OUT * side + PIX * f + move) % LANES
                    result[e // 4, lane, side, layer, e, f] = 1.0
    return result.reshape(2 * LANES, 2 * LANES).astype(ml_dtypes.bfloat16)


def split2(value):
    high = value.astype(BF16)
    return high, (value - high.astype(F32)).astype(BF16)


def split3(value):
    high = value.astype(BF16)
    rest = value - high.astype(F32)
    mid = rest.astype(BF16)
    return high, mid, (rest - mid.astype(F32)).astype(BF16)


def dot(a, b):
    return jnp.dot(a, b, preferred_element_type=F32)


def turn(value, shift, axis):
    size = value.shape[axis]
    return pltpu.roll(value, shift % size, axis) if shift % size else value


def lanes():
    return lax.broadcasted_iota(jnp.int32, (SUB, LANES), 1)


def subs():
    return lax.broadcasted_iota(jnp.int32, (SUB, LANES), 0)


def lane_tile(k):
    return pl.ds(k * LANES, LANES)


def is_odd(axis):
    return ((subs() * 0 + lax.axis_index(axis)) & 1) == 1


def rows_kernel(fields, eps, fwd, cross, near, hold, hold_fwd, sems):
    rows, cols = fields.shape[2], fields.shape[3]
    copies = []
    for n, at in enumerate((0, rows - PAD)):
        at_fwd = 0 if n == 0 else rows - SUB
        pairs = (
            (fields.at[:, :, pl.ds(at, PAD), :], hold.at[n, pl.ds(0, 3)]),
            (eps.at[:, pl.ds(at, PAD), :], hold.at[n, 3]),
            (fwd.at[:, :, pl.ds(at_fwd, SUB), :], hold_fwd.at[n]),
        )
        for m, (src, dst) in enumerate(pairs):
            copies.append(pltpu.make_async_copy(src, dst, sems.at[3 * n + m]))
    for copy in copies:
        copy.start()
    for copy in copies:
        copy.wait()
    odd, sub = is_odd("gx"), subs()
    for kind in range(4):
        for layer in range(2):
            plane = 2 * kind + layer
            for k in range(cols // LANES):
                at = lane_tile(k)
                low = hold[0, kind, layer, pl.ds(0, SUB), at]
                high = hold[1, kind, layer, pl.ds(SUB, SUB), at]
                cross[plane, :, at] = jnp.where(odd, high, low)
                near[plane, :, at] = jnp.where(odd, low, high)
                rest_low = turn(hold[0, kind, layer, pl.ds(SUB, SUB), at], -LEFT_OVER, 0)
                rest_high = turn(hold[1, kind, layer, pl.ds(0, SUB), at], LEFT_OVER, 0)
                low = jnp.where(sub >= NEAR, rest_low, hold_fwd[0, kind, layer, :, at])
                high = jnp.where(sub < SUB - NEAR, rest_high, hold_fwd[1, kind, layer, :, at])
                cross[8 + plane, :, at] = jnp.where(odd, high, low)
                near[8 + plane, :, at] = jnp.where(odd, low, high)


def halo_tile(cross, near, odd, tile, kind, layer, at):
    is_above = tile < 2
    outer = tile in (0, 3)
    if outer and kind >= 4:
        return None
    plane = 2 * kind + layer + (8 if outer else 0)
    a, b = near[plane, :, at], cross[plane, :, at]
    value = jnp.where(odd, a, b) if is_above else jnp.where(odd, b, a)
    if outer:
        value = turn(value, -LEFT_OVER if is_above else LEFT_OVER, 0)
    return value


def core_tile(fields, eps, fwd, at, kind, layer, cols):
    if kind < 3:
        return fields[kind, layer, at, cols]
    if kind == 3:
        return eps[layer, at, cols]
    return fwd[kind - 4, layer, at, cols]


def pack_tile(load, lane, right):
    total = jnp.zeros((SUB, LANES), F32)
    for kind, width in enumerate(WIDTHS):
        for layer in range(2):
            value = load(kind, layer)
            if value is None:
                continue
            first = FIRST[kind] + HALF * layer
            value = turn(value, first + width if right else first, 1)
            total = jnp.where((lane >= first) & (lane < first + width), value, total)
    return total


def edge_tile(load, kind, lane, n_lanes):
    spot = lane & (HALF - 1)
    total = None
    for layer in range(2):
        low = turn(load(kind, layer, 0), HALF * layer + OUT, 1)
        high = turn(load(kind, layer, n_lanes - 1), HALF * layer + SIDE + OUT, 1)
        value = jnp.where(spot < SIDE, low, high)
        total = value if total is None else jnp.where(lane < HALF, total, value)
    return total


def cols_kernel(fields, eps, fwd, cross, near, base):
    rows, cols = fields.shape[2], fields.shape[3]
    n_lanes = cols // LANES
    lane, odd = lanes(), is_odd("gy")

    def tile(t, carry):
        at = pl.ds(pl.multiple_of(t * SUB, SUB), SUB)
        out_at = pl.ds(pl.multiple_of(t * SUB + PAD, SUB), SUB)

        def load(kind, layer, k):
            return core_tile(fields, eps, fwd, at, kind, layer, lane_tile(k))

        left = pack_tile(lambda kind, layer: load(kind, layer, 0), lane, False)
        right = pack_tile(lambda kind, layer: load(kind, layer, n_lanes - 1), lane, True)
        cross[out_at, :] = jnp.where(odd, right, left)
        near[out_at, :] = jnp.where(odd, left, right)
        for kind in range(4 + STEPS):
            base[kind, at, :] = edge_tile(load, kind, lane, n_lanes)
        return carry

    lax.fori_loop(0, rows // SUB, tile, 0, unroll=4)
    zero = jnp.zeros((PAD, LANES), F32)
    for out in (cross, near):
        out[pl.ds(0, PAD), :] = zero
        out[pl.ds(PAD + rows, PAD), :] = zero


def corners_kernel(cross_in, near_in, cross_rows, near_rows, cross, near):
    rows, cols = cross.shape[0] - 2 * PAD, cross_rows.shape[2]
    lane, odd, odd_col = lanes(), is_odd("gx"), is_odd("gy")
    core = pl.ds(PAD, rows)
    cross[core, :] = cross_in[core, :]
    near[core, :] = near_in[core, :]
    for tile in range(4):
        at = pl.ds(tile * SUB if tile < 2 else PAD + rows + (tile - 2) * SUB, SUB)
        left, right = (
            pack_tile(
                lambda kind, layer: halo_tile(
                    cross_rows, near_rows, odd, tile, kind, layer, pl.ds(lo, LANES)
                ),
                lane, is_right,
            )
            for lo, is_right in ((0, False), (cols - LANES, True))
        )
        cross[at, :] = jnp.where(odd_col, right, left)
        near[at, :] = jnp.where(odd_col, left, right)


def prep_kernel(
    capacity, fields, eps, fwd, mon_x, mon_y, amp, mask, owner, cross, near, base, src, src_edge, place, place_edge
):
    cols_kernel(fields, eps, fwd, cross, near, base)
    side_kernel(capacity, fields.shape[2], mon_x, mon_y, amp, mask, owner, src, src_edge, place, place_edge)


def side_kernel(capacity, rows, mon_x, mon_y, amp, mask, owner, src, src_edge, place, place_edge):
    _, _, ext_rows, cols = src.shape
    channels = mon_x.shape[1]
    row = mon_x[...] - lax.axis_index("gx") * rows + PAD
    col = mon_y[...] - lax.axis_index("gy") * cols
    in_left = (col >= -OUT) & (col < OUT)
    in_right = (col >= cols - OUT) & (col < cols + OUT)
    edge = jnp.where(in_left, col + OUT, jnp.where(in_right, col - cols + OUT + SIDE, -LANES))
    layer = lax.broadcasted_iota(jnp.int32, (1, channels), 1) & 1
    edge = edge + HALF * layer
    inside = jnp.where((col >= 0) & (col < cols), col, -1)
    one_y = lax.broadcasted_iota(jnp.int32, (cols, channels), 0) == inside
    one_e = lax.broadcasted_iota(jnp.int32, (LANES, channels), 0) == edge
    one_y = jnp.where(one_y, 1.0, 0.0).astype(BF16)
    one_e = jnp.where(one_e, 1.0, 0.0).astype(BF16)
    one_y = jnp.concatenate([one_y] * 3, axis=1)
    one_e = jnp.concatenate([one_e] * 3, axis=1)
    one_x = lax.broadcasted_iota(jnp.int32, (ext_rows, channels), 0) == row
    one_x = jnp.where(one_x, 1.0, 0.0).astype(F32)
    nt = (((1,), (1,)), ((), ()))
    for step in range(STEPS):
        parts = [part.astype(F32) for part in split3(amp[pl.ds(step, 1), :])]
        lhs = jnp.concatenate([one_x * part for part in parts], axis=1)
        src_edge[step] = lax.dot_general(lhs.astype(BF16), one_e, nt, preferred_element_type=F32)
        layer_wide = jnp.concatenate([layer] * 3, axis=1)
        for which in range(2):
            some = jnp.where(layer_wide == which, lhs, 0.0).astype(BF16)
            src[step, which] = lax.dot_general(some, one_y, nt, preferred_element_type=F32)
    tiles = owner.shape[1]
    own = owner[...].astype(F32)
    own_wide = jnp.broadcast_to(own, (tiles, tiles))
    earlier = lax.broadcasted_iota(jnp.int32, (tiles, tiles), 0) < lax.broadcasted_iota(
        jnp.int32, (tiles, tiles), 1
    )
    same = (own_wide.T == own_wide) & earlier
    slot = jnp.sum(jnp.where(same, 1.0, 0.0), axis=0, keepdims=True)
    dest = owner[...] * capacity + slot.astype(jnp.int32)
    dest = jnp.where(mask[...] != 0, dest, -1)
    hit = lax.broadcasted_iota(jnp.int32, place.shape, 0) == dest
    hit = jnp.where(hit, 1.0, 0.0).astype(BF16)
    place[...] = hit
    tile_cols = cols // TS
    column = lax.broadcasted_iota(jnp.int32, (tiles, 4 * SUB), 1)
    wanted = (column % SUB) * tile_cols + ((column // SUB) & 1) * (tile_cols - 1)
    picked = lax.broadcasted_iota(jnp.int32, (tiles, 4 * SUB), 0) == wanted
    place_edge[...] = dot(hit, jnp.where(picked, 1.0, 0.0).astype(BF16)).astype(BF16)


def yee(bufs, keys, eps_of, change_of, src_of, grad, coef_x, coef_first, next_col, prev_col, other):
    n_tiles = (bufs[0].shape[-2] - 2 * SUB) // SUB
    for step in range(STEPS):
        old, new = ((0, 1), (1, 0), (0, 1), (1, 2))[step]
        old, new = bufs[old], bufs[new]
        low = 0 if step < 2 else 1
        high = n_tiles if step == 0 else n_tiles - 1
        for t in range(low, high):
            at = pl.ds(SUB + t * SUB, SUB)
            under = pl.ds(SUB + t * SUB + 1, SUB)
            over = pl.ds(SUB + t * SUB - 1, SUB)
            coef_y = coef_first if t < PAD // SUB else COURANT
            e = {key: old[(0,) + key + (at, slice(None))] for key in keys}
            e_right = next_col(e)
            hx, hy = {}, {}
            for key in keys:
                hx[key] = old[(1,) + key + (at, slice(None))] + coef_x * (e_right[key] - e[key])
                below = old[(0,) + key + (under, slice(None))]
                hy[key] = old[(2,) + key + (at, slice(None))] - coef_y * (below - e[key])
                new[(1,) + key + (at, slice(None))] = hx[key]
                new[(2,) + key + (at, slice(None))] = hy[key]
            hx_left = prev_col(hx)
            for key in keys:
                hy_above = new[(2,) + key + (over, slice(None))]
                curl = (hy[key] - hy_above) - (hx[key] - hx_left[key])
                curl = curl + COUPLING * (other(e, key) - e[key])
                value = e[key] - eps_of(key, t) * curl + src_of(step, key, t)
                new[(0,) + key + (at, slice(None))] = value
                if 1 <= t < n_tiles - 1:
                    change = value * change_of(step, key, t)
                    where = key + (pl.ds(t * SUB, SUB), slice(None))
                    grad[where] = -change if step == 0 else grad[where] - change


def coef_above():
    return jnp.where((subs() * 0 + lax.axis_index("gx")) > 0, COURANT, 0.0).astype(F32)


def clear_rims(buf):
    size = buf.shape[-2]
    zero = jnp.zeros(buf.shape[:-2] + (SUB, LANES), F32)
    lead = (slice(None),) * (len(buf.shape) - 2)
    buf[lead + (pl.ds(0, SUB), slice(None))] = zero
    buf[lead + (pl.ds(size - SUB, SUB), slice(None))] = zero


def row_pairs(ref, lead, count):
    even = ref[lead + (pl.ds(0, count, stride=PIX), slice(None))]
    return even + ref[lead + (pl.ds(1, count, stride=PIX), slice(None))]


def inner_kernel(fields, eps, fwd, cross, near, src, last, g_out, base, a, b, c, e, g):
    rows, cols = fields.shape[2], fields.shape[3]
    n_tiles = (rows + 2 * PAD) // SUB
    n_lanes = cols // LANES
    lane, odd = lanes(), is_odd("gx")
    halo_of = {0: 0, 1: 1, n_tiles - 2: 2, n_tiles - 1: 3}

    def load(kind, layer, t, k):
        if t in halo_of:
            return halo_tile(cross, near, odd, halo_of[t], kind, layer, lane_tile(k))
        return core_tile(fields, eps, fwd, pl.ds(t * SUB - PAD, SUB), kind, layer, lane_tile(k))

    for buf in (a, b, c):
        clear_rims(buf)
    for t in range(n_tiles):
        for layer in range(2):
            for k in range(n_lanes):
                for kind in range(3):
                    a[kind, layer, k, pl.ds(SUB + t * SUB, SUB), :] = load(kind, layer, t, k)
                e[layer, k, pl.ds(t * SUB, SUB), :] = COURANT * load(3, layer, t, k)

    at_end, at_start = lane == LANES - 1, lane == 0
    keys = [(layer, k) for layer in range(2) for k in range(n_lanes)]

    def next_col(values):
        moved = {key: turn(value, -1, 1) for key, value in values.items()}
        return {
            (l, k): jnp.where(at_end, moved[l, (k + 1) % n_lanes], moved[l, k]) for l, k in keys
        }

    def prev_col(values):
        moved = {key: turn(value, 1, 1) for key, value in values.items()}
        return {
            (l, k): jnp.where(at_start, moved[l, (k - 1) % n_lanes], moved[l, k]) for l, k in keys
        }

    yee(
        (a, b, c), keys,
        lambda key, t: e[key + (pl.ds(t * SUB, SUB), slice(None))],
        lambda step, key, t: load(4 + step, key[0], t, key[1]),
        lambda step, key, t: src[step, key[0], pl.ds(t * SUB, SUB), lane_tile(key[1])],
        g, COURANT, coef_above(), next_col, prev_col,
        lambda values, key: values[1 - key[0], key[1]],
    )
    last[...] = c[:, :, :, pl.ds(SUB + PAD, rows), :]
    g_out[...] = g[...]
    for t, row in halo_of.items():
        for kind in range(4 + STEPS):
            if kind < 4 or row in (1, 2):
                base[kind, pl.ds(row * SUB, SUB), :] = edge_tile(
                    lambda kind, layer, k: load(kind, layer, t, k), kind, lane, n_lanes
                )


def inner_tiles_kernel(g, mats, place, slots, pooled):
    n_lanes, ext_rows = g.shape[1], g.shape[2]
    for layer in range(2):
        total = None
        for k in range(n_lanes):
            for part in split2(row_pairs(g, (layer, k), ext_rows // PIX)):
                term = dot(part, mats[k])
                total = term if total is None else total + term
        pooled[layer] = total

    out_pix = ext_rows // PIX - 2 * PAD // PIX
    vals = by_tile([cone_filter(pooled.at[layer], out_pix, PAD // PIX) for layer in range(2)])
    high, low = split2(vals)
    slots[...] = dot(place[...], high) + dot(place[...], low)


def cone_filter(pooled, out_pix, first):
    weights = cone_weights(RADIUS)
    reach = RADIUS - 1
    lane = lax.broadcasted_iota(jnp.int32, (out_pix, LANES), 1)
    at = [pooled[pl.ds(first + s, out_pix), :] for s in range(-reach, reach + 1)]
    sums = [at[reach]] + [at[reach + s] + at[reach - s] for s in range(1, reach + 1)]
    total = None
    for shift in range(reach + 1):
        mixed = None
        for s in range(reach + 1):
            weight = float(weights[reach + s, reach + shift])
            if weight > 0.0:
                term = weight * sums[s]
                mixed = term if mixed is None else mixed + term
        if shift == 0:
            total = mixed
        else:
            total = total + turn(jnp.where(lane < shift, 0.0, mixed), -shift, 1)
            total = total + turn(jnp.where(lane >= LANES - shift, 0.0, mixed), shift, 1)
    return total


def by_tile(blocks):
    span = TS // PIX
    tile_rows = blocks[0].shape[0] // span
    x = jnp.stack([block.reshape(tile_rows, span, LANES) for block in blocks], axis=1)
    x = x.reshape(tile_rows * 2, span, LANES)
    group = lax.broadcasted_iota(jnp.int32, x.shape, 2) // span
    row = lax.broadcasted_iota(jnp.int32, x.shape, 1)
    for bit in (1, 2, 4):
        row_on, lane_on = (row & bit) != 0, (group & bit) != 0
        ahead = turn(turn(x, -bit, 1), bit * span, 2)
        behind = turn(turn(x, bit, 1), -bit * span, 2)
        x = jnp.where(row_on == lane_on, x, jnp.where(lane_on, ahead, behind))
    x = x.reshape(tile_rows, 2, span, LANES)
    even, odd = x[:, 0], x[:, 1]
    upper = lax.broadcasted_iota(jnp.int32, even.shape, 2) >= HALF
    new_even = jnp.where(upper, turn(odd, HALF, 2), even)
    new_odd = jnp.where(upper, odd, turn(even, HALF, 2))
    return jnp.stack([new_even, new_odd], axis=1).reshape(tile_rows * 2 * span, LANES)


def merge_spans(spans, lane):
    even = (lane & 1) == 0
    window = ((lane - OUT) & (HALF - 1)) < SIDE
    merged = []
    for e in (0, 4):
        low = jnp.where(even, spans[e], turn(spans[e + 1], 1, 1))
        high = jnp.where(even, turn(spans[e + 2], SIDE, 1), turn(spans[e + 3], SIDE + 1, 1))
        merged.append(jnp.where(window, low, high))
    return jnp.concatenate(merged, axis=1)


def edge_kernel(
    slots_in, base, base_halo, cross, near, src, place, spread, last, slots, a, b, c, e, d, g
):
    rows = base.shape[1]
    ext_rows = rows + 2 * PAD
    n_tiles = ext_rows // SUB
    lane, odd = lanes(), is_odd("gy")
    spot = lane & (HALF - 1)
    is_left, is_right = spot < OUT, spot >= HALF - OUT
    halo_of = {0: 0, 1: 1, n_tiles - 2: 2, n_tiles - 1: 3}

    for buf in (a, b, c):
        clear_rims(buf)
    for t in range(n_tiles):
        at = pl.ds(t * SUB, SUB)
        far, close = cross[at, :], near[at, :]
        high, low = jnp.where(odd, close, far), jnp.where(odd, far, close)
        for kind, width in enumerate(WIDTHS):
            if kind >= 4 and t in (0, n_tiles - 1):
                continue
            if t in halo_of:
                value = base_halo[kind, pl.ds(halo_of[t] * SUB, SUB), :]
            else:
                value = base[kind, pl.ds(t * SUB - PAD, SUB), :]
            value = jnp.where(is_left, turn(high, OUT - width - FIRST[kind], 1), value)
            value = jnp.where(is_right, turn(low, HALF - OUT - FIRST[kind], 1), value)
            if kind < 3:
                a[kind, pl.ds(SUB + t * SUB, SUB), :] = value
            elif kind == 3:
                e[at, :] = COURANT * value
            else:
                d[kind - 4, at, :] = value

    before = (lax.axis_index("gy") + lane * 0) > 0
    coef_x = jnp.where(before | (spot >= OUT), COURANT, 0.0).astype(F32)
    yee(
        (a, b, c), [()],
        lambda key, t: e[pl.ds(t * SUB, SUB), :],
        lambda step, key, t: d[step, pl.ds(t * SUB, SUB), :],
        lambda step, key, t: src[step, pl.ds(t * SUB, SUB), :],
        g, coef_x, coef_above(),
        lambda values: {(): turn(values[()], -1, 1)},
        lambda values: {(): turn(values[()], 1, 1)},
        lambda values, key: turn(values[()], HALF, 1),
    )

    inside = (spot >= OUT - NEAR) & (spot < OUT + KEEP)
    inside = inside | ((spot >= HALF - OUT - KEEP) & (spot < HALF - OUT + NEAR))
    span, reach = TS // PIX, RADIUS - 1
    pixel = {}
    for j in range(-reach, span + reach):
        value = g[pl.ds(PAD + PIX * j, SUB, stride=TS), :]
        value = jnp.where(inside, value + g[pl.ds(PAD + PIX * j + 1, SUB, stride=TS), :], 0.0)
        pixel[j] = value + turn(value, -1, 1)

    weights = cone_weights(RADIUS)
    spans = []
    for row in range(span):
        sums = [pixel[row]] + [pixel[row + s] + pixel[row - s] for s in range(1, reach + 1)]
        total = None
        for shift in range(reach + 1):
            mixed = None
            for s in range(reach + 1):
                weight = float(weights[reach + s, reach + shift])
                if weight > 0.0:
                    term = weight * sums[s]
                    mixed = term if mixed is None else mixed + term
            if shift:
                mixed = turn(mixed, -PIX * shift, 1) + turn(mixed, PIX * shift, 1)
            total = mixed if total is None else total + mixed
        spans.append(total)

    edge = dot(jnp.concatenate(split2(merge_spans(spans, lane)), axis=0), spread[...])
    edge = edge[:SUB] + edge[SUB:]
    edge = jnp.concatenate([edge[:, :LANES], edge[:, LANES:]], axis=0)
    slots[...] = slots_in[...] + dot(place[...], jnp.concatenate(split2(edge), axis=0))
    last[...] = c[:, pl.ds(SUB + PAD, rows), :]


def merge_kernel(last, edge_last, out_fields, merged, sem):
    rows, cols = merged.shape[2], merged.shape[3]
    n_lanes = cols // LANES
    lane = lanes()
    for t in range(rows // SUB):
        at = pl.ds(t * SUB, SUB)
        for kind in range(3):
            edge = edge_last[kind, at, :]
            for layer in range(2):
                for k in range(n_lanes):
                    value = last[kind, layer, k, at, :]
                    if k == 0:
                        value = jnp.where(lane < KEEP, turn(edge, -HALF * layer - OUT, 1), value)
                    if k == n_lanes - 1:
                        value = jnp.where(
                            lane >= LANES - KEEP, turn(edge, -HALF * layer - SIDE - OUT, 1), value
                        )
                    merged[kind, layer, at, lane_tile(k)] = value
    copy = pltpu.make_async_copy(merged, out_fields, sem)
    copy.start()
    copy.wait()


def vmem():
    return pl.BlockSpec(memory_space=pltpu.VMEM)


def shape(*dims, dtype=F32):
    return jax.ShapeDtypeStruct(dims, dtype)


def call(kernel, outs, n_in, *, in_space=pltpu.VMEM, out_specs=None, scratch=(), flops=0, size=0):
    return pl.pallas_call(
        kernel,
        out_shape=outs,
        in_specs=[pl.BlockSpec(memory_space=in_space)] * n_in,
        out_specs=out_specs or tuple(vmem() for _ in outs),
        scratch_shapes=list(scratch),
        compiler_params=pltpu.CompilerParams(vmem_limit_bytes=40 * 1024 * 1024),
        cost_estimate=pl.CostEstimate(flops=flops, bytes_accessed=size, transcendentals=0),
    )


def on_device(adj_fields, inv_eps, fwd_diff, mon_x, mon_y, mon_amp, design_mask, tile_owner):
    rows, cols = adj_fields.shape[2], adj_fields.shape[3]
    assert cols == 2 * LANES and rows % TS == 0
    gx_count, gy_count = lax.axis_size("gx"), lax.axis_size("gy")
    owners = gx_count * gy_count
    tiles = (rows // TS) * (cols // TS)
    width = 2 * (TS // PIX) ** 2
    assert width == LANES
    capacity = max(8, 2 * tiles // owners)
    assert rows == TS * SUB and cols == 2 * TS * SUB
    ext_rows = rows + 2 * PAD
    n_lanes = cols // LANES
    cells = rows * cols
    blocks = (adj_fields, inv_eps, fwd_diff)


    strip = shape(16, SUB, cols)
    cross, near = call(
        rows_kernel, (strip, strip), 3, in_space=pltpu.HBM,
        scratch=(
            pltpu.VMEM((2, 4, 2, PAD, cols), F32),
            pltpu.VMEM((2, STEPS, 2, SUB, cols), F32),
            pltpu.SemaphoreType.DMA((6,)),
        ),
        size=2**20,
    )(*(pltpu.with_memory_space_constraint(block, pltpu.HBM) for block in blocks))

    def pairs(count, start):
        some = [(i, i + 1) for i in range(start, count - 1, 2)]
        return some + [(j, i) for i, j in some]

    cross = lax.ppermute(cross, "gx", pairs(gx_count, 1))
    near = lax.ppermute(near, "gx", pairs(gx_count, 0))

    packed = shape(ext_rows, LANES)
    channels = mon_x.shape[0]
    cross_cols, near_cols, base, src, src_edge, place, place_edge = call(
        lambda *refs: prep_kernel(capacity, *refs),
        (
            packed,
            packed,
            shape(4 + STEPS, rows, LANES),
            shape(STEPS, 2, ext_rows, cols),
            shape(STEPS, ext_rows, LANES),
            shape(owners * capacity, tiles, dtype=BF16),
            shape(owners * capacity, 4 * SUB, dtype=BF16),
        ),
        8,
        flops=16 * ext_rows * (cols + LANES) * 3 * channels,
        size=64 * cells,
    )(
        *blocks,
        mon_x.reshape(1, channels),
        mon_y.reshape(1, channels),
        mon_amp,
        design_mask.reshape(1, tiles),
        tile_owner.reshape(1, tiles),
    )
    cross_cols, near_cols = call(
        corners_kernel, (packed, packed), 4, flops=cells, size=8 * ext_rows * LANES
    )(cross_cols, near_cols, cross, near)
    cross_cols = lax.ppermute(cross_cols, "gy", pairs(gy_count, 1))
    near_cols = lax.ppermute(near_cols, "gy", pairs(gy_count, 0))

    state = (3, 2, n_lanes, ext_rows + 2 * SUB, LANES)
    last, g, base_halo = call(
        inner_kernel,
        (
            shape(3, 2, n_lanes, rows, LANES),
            shape(2, n_lanes, ext_rows, LANES),
            shape(4 + STEPS, 2 * PAD, LANES),
        ),
        6,
        scratch=(
            pltpu.VMEM(state, F32),
            pltpu.VMEM(state, F32),
            pltpu.VMEM(state, F32),
            pltpu.VMEM((2, n_lanes, ext_rows, LANES), F32),
            pltpu.VMEM((2, n_lanes, ext_rows, LANES), F32),
        ),
        flops=200 * cells,
        size=96 * cells,
    )(*blocks, cross, near, src)
    (slots,) = call(
        inner_tiles_kernel,
        (shape(owners * capacity, width),),
        3,
        scratch=(pltpu.VMEM((2, ext_rows // PIX, LANES), F32),),
        flops=100 * cells,
        size=32 * cells,
    )(g, pool_matrices(), place)

    edge_state = (3, ext_rows + 2 * SUB, LANES)
    edge_last, outgoing = call(
        edge_kernel,
        (shape(3, rows, LANES), shape(owners * capacity, width)),
        8,
        scratch=(
            pltpu.VMEM(edge_state, F32),
            pltpu.VMEM(edge_state, F32),
            pltpu.VMEM(edge_state, F32),
            pltpu.VMEM((ext_rows, LANES), F32),
            pltpu.VMEM((STEPS, ext_rows, LANES), F32),
            pltpu.VMEM((ext_rows, LANES), F32),
        ),
        flops=50 * cells,
        size=16 * cells,
    )(slots, base, base_halo, cross_cols, near_cols, src_edge, place_edge, spread_matrix())
    (fields,) = call(
        merge_kernel,
        (shape(3, 2, rows, cols),),
        2,
        out_specs=(pl.BlockSpec(memory_space=pl.ANY),),
        scratch=(pltpu.VMEM((3, 2, rows, cols), F32), pltpu.SemaphoreType.DMA),
        flops=20 * cells,
        size=48 * cells,
    )(last, edge_last)

    outgoing = outgoing.reshape(owners, capacity, width)
    incoming = lax.all_to_all(outgoing, ("gx", "gy"), split_axis=0, concat_axis=0, tiled=True)
    return fields, incoming[None]


def solution(mesh):
    placed = (
        P(None, None, ("parts", "gx"), "gy"),
        P(None, ("parts", "gx"), "gy"),
        P(None, None, ("parts", "gx"), "gy"),
        P("parts"),
        P("parts"),
        P(None, "parts"),
        P(("parts", "gx"), "gy", None),
        P(("parts", "gx"), "gy", None, None),
    )
    return jax.shard_map(
        on_device,
        mesh=mesh,
        in_specs=placed,
        out_specs=(
            P(None, None, ("parts", "gx"), "gy"),
            P(("parts", "gx", "gy"), None, None, None),
        ),
        check_vma=False,
    )
```

```python
import jax
import jax.numpy as jnp
import ml_dtypes
import numpy as np
from jax import lax
from jax.experimental import pallas as pl
from jax.experimental.pallas import tpu as pltpu
from jax.sharding import PartitionSpec as P

STEPS = 4
PIX = 2
TS = 16
RADIUS = 4
COURANT = 0.6
COUPLING = 0.25

LANES = 128
SUB = 8
FAR = STEPS + PIX * (RADIUS - 1)
NEAR = PIX * (RADIUS - 1)
LEFT_OVER = FAR - SUB
PAD = 2 * SUB
HALF = LANES // 2
SIDE = HALF // 2
OUT = SIDE // 2
KEEP = 8
F32 = jnp.float32
BF16 = jnp.bfloat16
WIDTHS = (FAR,) * 4 + (NEAR,) * STEPS
FIRST = tuple(sum(WIDTHS[:k]) for k in range(len(WIDTHS)))
assert sum(WIDTHS) <= HALF and FAR <= OUT and STEPS + KEEP <= OUT


def cone_weights(radius):
    reach_cells = radius - 1
    offsets = np.arange(-reach_cells, reach_cells + 1)
    distance = np.sqrt(offsets[:, None] * offsets[:, None] + offsets[None, :] * offsets[None, :])
    weights = np.maximum(radius - distance, 0.0)
    return weights / weights.sum()


def pool_matrices():
    inner = np.zeros((2, LANES, LANES), np.float32)
    for j in range(KEEP, 2 * LANES - KEEP):
        inner[j // LANES, j % LANES, j // PIX] = 1.0
    return inner.astype(ml_dtypes.bfloat16)


def spread_matrix():
    span = TS // PIX
    result = np.zeros((2, LANES, 2, 2, span, span), np.float32)
    for e in range(span):
        move = (e % 2) + SIDE * (e % 4 // 2)
        for layer in range(2):
            for side in range(2):
                for f in range(span):
                    lane = (HALF * layer + OUT + OUT * side + PIX * f + move) % LANES
                    result[e // 4, lane, side, layer, e, f] = 1.0
    return result.reshape(2 * LANES, 2 * LANES).astype(ml_dtypes.bfloat16)


def split2(value):
    high = value.astype(BF16)
    return high, (value - high.astype(F32)).astype(BF16)


def split3(value):
    high = value.astype(BF16)
    rest = value - high.astype(F32)
    mid = rest.astype(BF16)
    return high, mid, (rest - mid.astype(F32)).astype(BF16)


def dot(a, b):
    return jnp.dot(a, b, preferred_element_type=F32)


def turn(value, shift, axis):
    size = value.shape[axis]
    return pltpu.roll(value, shift % size, axis) if shift % size else value


def lanes():
    return lax.broadcasted_iota(jnp.int32, (SUB, LANES), 1)


def subs():
    return lax.broadcasted_iota(jnp.int32, (SUB, LANES), 0)


def lane_tile(k):
    return pl.ds(k * LANES, LANES)


def is_odd(axis):
    return ((subs() * 0 + lax.axis_index(axis)) & 1) == 1


def rows_kernel(fields, eps, fwd, cross, near, hold, hold_fwd, sems):
    rows, cols = fields.shape[2], fields.shape[3]
    copies = []
    for n, at in enumerate((0, rows - PAD)):
        at_fwd = 0 if n == 0 else rows - SUB
        pairs = (
            (fields.at[:, :, pl.ds(at, PAD), :], hold.at[n, pl.ds(0, 3)]),
            (eps.at[:, pl.ds(at, PAD), :], hold.at[n, 3]),
            (fwd.at[:, :, pl.ds(at_fwd, SUB), :], hold_fwd.at[n]),
        )
        for m, (src, dst) in enumerate(pairs):
            copies.append(pltpu.make_async_copy(src, dst, sems.at[3 * n + m]))
    for copy in copies:
        copy.start()
    for copy in copies:
        copy.wait()
    odd, sub = is_odd("gx"), subs()
    for kind in range(4):
        for layer in range(2):
            plane = 2 * kind + layer
            for k in range(cols // LANES):
                at = lane_tile(k)
                low = hold[0, kind, layer, pl.ds(0, SUB), at]
                high = hold[1, kind, layer, pl.ds(SUB, SUB), at]
                cross[plane, :, at] = jnp.where(odd, high, low)
                near[plane, :, at] = jnp.where(odd, low, high)
                rest_low = turn(hold[0, kind, layer, pl.ds(SUB, SUB), at], -LEFT_OVER, 0)
                rest_high = turn(hold[1, kind, layer, pl.ds(0, SUB), at], LEFT_OVER, 0)
                low = jnp.where(sub >= NEAR, rest_low, hold_fwd[0, kind, layer, :, at])
                high = jnp.where(sub < SUB - NEAR, rest_high, hold_fwd[1, kind, layer, :, at])
                cross[8 + plane, :, at] = jnp.where(odd, high, low)
                near[8 + plane, :, at] = jnp.where(odd, low, high)


def halo_tile(cross, near, odd, tile, kind, layer, at):
    is_above = tile < 2
    outer = tile in (0, 3)
    if outer and kind >= 4:
        return None
    plane = 2 * kind + layer + (8 if outer else 0)
    a, b = near[plane, :, at], cross[plane, :, at]
    value = jnp.where(odd, a, b) if is_above else jnp.where(odd, b, a)
    if outer:
        value = turn(value, -LEFT_OVER if is_above else LEFT_OVER, 0)
    return value


def core_tile(fields, eps, fwd, at, kind, layer, cols):
    if kind < 3:
        return fields[kind, layer, at, cols]
    if kind == 3:
        return eps[layer, at, cols]
    return fwd[kind - 4, layer, at, cols]


def pack_tile(load, lane, right):
    total = jnp.zeros((SUB, LANES), F32)
    for kind, width in enumerate(WIDTHS):
        for layer in range(2):
            value = load(kind, layer)
            if value is None:
                continue
            first = FIRST[kind] + HALF * layer
            value = turn(value, first + width if right else first, 1)
            total = jnp.where((lane >= first) & (lane < first + width), value, total)
    return total


def edge_tile(load, kind, lane, n_lanes):
    spot = lane & (HALF - 1)
    total = None
    for layer in range(2):
        low = turn(load(kind, layer, 0), HALF * layer + OUT, 1)
        high = turn(load(kind, layer, n_lanes - 1), HALF * layer + SIDE + OUT, 1)
        value = jnp.where(spot < SIDE, low, high)
        total = value if total is None else jnp.where(lane < HALF, total, value)
    return total


def cols_kernel(fields, eps, fwd, cross, near, base):
    rows, cols = fields.shape[2], fields.shape[3]
    n_lanes = cols // LANES
    lane, odd = lanes(), is_odd("gy")

    def tile(t, carry):
        at = pl.ds(pl.multiple_of(t * SUB, SUB), SUB)
        out_at = pl.ds(pl.multiple_of(t * SUB + PAD, SUB), SUB)

        def load(kind, layer, k):
            return core_tile(fields, eps, fwd, at, kind, layer, lane_tile(k))

        left = pack_tile(lambda kind, layer: load(kind, layer, 0), lane, False)
        right = pack_tile(lambda kind, layer: load(kind, layer, n_lanes - 1), lane, True)
        cross[out_at, :] = jnp.where(odd, right, left)
        near[out_at, :] = jnp.where(odd, left, right)
        for kind in range(4 + STEPS):
            base[kind, out_at, :] = edge_tile(load, kind, lane, n_lanes)
        return carry

    lax.fori_loop(0, rows // SUB, tile, 0, unroll=4)
    zero = jnp.zeros((PAD, LANES), F32)
    for out in (cross, near):
        out[pl.ds(0, PAD), :] = zero
        out[pl.ds(PAD + rows, PAD), :] = zero


def corners_kernel(cross_in, near_in, cross_rows, near_rows, cross, near):
    rows, cols = cross.shape[0] - 2 * PAD, cross_rows.shape[2]
    lane, odd, odd_col = lanes(), is_odd("gx"), is_odd("gy")
    core = pl.ds(PAD, rows)
    cross[core, :] = cross_in[core, :]
    near[core, :] = near_in[core, :]
    for tile in range(4):
        at = pl.ds(tile * SUB if tile < 2 else PAD + rows + (tile - 2) * SUB, SUB)
        left, right = (
            pack_tile(
                lambda kind, layer: halo_tile(
                    cross_rows, near_rows, odd, tile, kind, layer, pl.ds(lo, LANES)
                ),
                lane, is_right,
            )
            for lo, is_right in ((0, False), (cols - LANES, True))
        )
        cross[at, :] = jnp.where(odd_col, right, left)
        near[at, :] = jnp.where(odd_col, left, right)


def prep_kernel(
    capacity, fields, eps, fwd, mon_x, mon_y, amp, mask, owner, cross, near, base, src, src_edge, place, place_edge
):
    cols_kernel(fields, eps, fwd, cross, near, base)
    side_kernel(capacity, fields.shape[2], mon_x, mon_y, amp, mask, owner, src, src_edge, place, place_edge)


def side_kernel(capacity, rows, mon_x, mon_y, amp, mask, owner, src, src_edge, place, place_edge):
    _, _, ext_rows, cols = src.shape
    channels = mon_x.shape[1]
    row = mon_x[...] - lax.axis_index("gx") * rows + PAD
    col = mon_y[...] - lax.axis_index("gy") * cols
    in_left = (col >= -OUT) & (col < OUT)
    in_right = (col >= cols - OUT) & (col < cols + OUT)
    edge = jnp.where(in_left, col + OUT, jnp.where(in_right, col - cols + OUT + SIDE, -LANES))
    layer = lax.broadcasted_iota(jnp.int32, (1, channels), 1) & 1
    edge = edge + HALF * layer
    inside = jnp.where((col >= 0) & (col < cols), col, -1)
    one_y = lax.broadcasted_iota(jnp.int32, (cols, channels), 0) == inside
    one_e = lax.broadcasted_iota(jnp.int32, (LANES, channels), 0) == edge
    one_y = jnp.where(one_y, 1.0, 0.0).astype(BF16)
    one_e = jnp.where(one_e, 1.0, 0.0).astype(BF16)
    one_y = jnp.concatenate([one_y] * 3, axis=1)
    one_e = jnp.concatenate([one_e] * 3, axis=1)
    one_x = lax.broadcasted_iota(jnp.int32, (ext_rows, channels), 0) == row
    one_x = jnp.where(one_x, 1.0, 0.0).astype(F32)
    nt = (((1,), (1,)), ((), ()))
    for step in range(STEPS):
        parts = [part.astype(F32) for part in split3(amp[pl.ds(step, 1), :])]
        lhs = jnp.concatenate([one_x * part for part in parts], axis=1)
        src_edge[step] = lax.dot_general(lhs.astype(BF16), one_e, nt, preferred_element_type=F32)
        layer_wide = jnp.concatenate([layer] * 3, axis=1)
        for which in range(2):
            some = jnp.where(layer_wide == which, lhs, 0.0).astype(BF16)
            src[step, which] = lax.dot_general(some, one_y, nt, preferred_element_type=F32)
    tiles = owner.shape[1]
    own = owner[...].astype(F32)
    own_wide = jnp.broadcast_to(own, (tiles, tiles))
    earlier = lax.broadcasted_iota(jnp.int32, (tiles, tiles), 0) < lax.broadcasted_iota(
        jnp.int32, (tiles, tiles), 1
    )
    same = (own_wide.T == own_wide) & earlier
    slot = jnp.sum(jnp.where(same, 1.0, 0.0), axis=0, keepdims=True)
    dest = owner[...] * capacity + slot.astype(jnp.int32)
    dest = jnp.where(mask[...] != 0, dest, -1)
    hit = lax.broadcasted_iota(jnp.int32, place.shape, 0) == dest
    hit = jnp.where(hit, 1.0, 0.0).astype(BF16)
    place[...] = hit
    tile_cols = cols // TS
    column = lax.broadcasted_iota(jnp.int32, (tiles, 4 * SUB), 1)
    wanted = (column % SUB) * tile_cols + ((column // SUB) & 1) * (tile_cols - 1)
    picked = lax.broadcasted_iota(jnp.int32, (tiles, 4 * SUB), 0) == wanted
    place_edge[...] = dot(hit, jnp.where(picked, 1.0, 0.0).astype(BF16)).astype(BF16)


def yee(bufs, keys, eps_of, change_of, src_of, grad, coef_x, coef_first, next_col, prev_col, other):
    n_tiles = (bufs[0].shape[-2] - 2 * SUB) // SUB
    for step in range(STEPS):
        old, new = ((0, 1), (1, 0), (0, 1), (1, 2))[step]
        old, new = bufs[old], bufs[new]
        low = 0 if step < 2 else 1
        high = n_tiles if step == 0 else n_tiles - 1
        for t in range(low, high):
            at = pl.ds(SUB + t * SUB, SUB)
            under = pl.ds(SUB + t * SUB + 1, SUB)
            over = pl.ds(SUB + t * SUB - 1, SUB)
            coef_y = coef_first if t < PAD // SUB else COURANT
            e = {key: old[(0,) + key + (at, slice(None))] for key in keys}
            e_right = next_col(e)
            hx, hy = {}, {}
            for key in keys:
                hx[key] = old[(1,) + key + (at, slice(None))] + coef_x * (e_right[key] - e[key])
                below = old[(0,) + key + (under, slice(None))]
                hy[key] = old[(2,) + key + (at, slice(None))] - coef_y * (below - e[key])
                new[(1,) + key + (at, slice(None))] = hx[key]
                new[(2,) + key + (at, slice(None))] = hy[key]
            hx_left = prev_col(hx)
            for key in keys:
                hy_above = new[(2,) + key + (over, slice(None))]
                curl = (hy[key] - hy_above) - (hx[key] - hx_left[key])
                curl = curl + COUPLING * (other(e, key) - e[key])
                value = e[key] - eps_of(key, t) * curl + src_of(step, key, t)
                new[(0,) + key + (at, slice(None))] = value
                if 1 <= t < n_tiles - 1:
                    change = value * change_of(step, key, t)
                    where = key + (pl.ds(t * SUB, SUB), slice(None))
                    grad[where] = -change if step == 0 else grad[where] - change


def coef_above():
    return jnp.where((subs() * 0 + lax.axis_index("gx")) > 0, COURANT, 0.0).astype(F32)


def clear_rims(buf):
    size = buf.shape[-2]
    zero = jnp.zeros(buf.shape[:-2] + (SUB, LANES), F32)
    lead = (slice(None),) * (len(buf.shape) - 2)
    buf[lead + (pl.ds(0, SUB), slice(None))] = zero
    buf[lead + (pl.ds(size - SUB, SUB), slice(None))] = zero


def row_pairs(ref, lead, count):
    even = ref[lead + (pl.ds(0, count, stride=PIX), slice(None))]
    return even + ref[lead + (pl.ds(1, count, stride=PIX), slice(None))]


def inner_kernel(fields, eps, fwd, cross, near, src, mats, base_in, place, last, slots, base, a, b, e, g, pooled):
    rows, cols = fields.shape[2], fields.shape[3]
    n_tiles = (rows + 2 * PAD) // SUB
    n_lanes = cols // LANES
    lane, odd = lanes(), is_odd("gx")
    halo_of = {0: 0, 1: 1, n_tiles - 2: 2, n_tiles - 1: 3}

    def load(kind, layer, t, k):
        if t in halo_of:
            return halo_tile(cross, near, odd, halo_of[t], kind, layer, lane_tile(k))
        return core_tile(fields, eps, fwd, pl.ds(t * SUB - PAD, SUB), kind, layer, lane_tile(k))

    for buf in (a, b, last):
        clear_rims(buf)
    for t in range(n_tiles):
        for layer in range(2):
            for k in range(n_lanes):
                for kind in range(3):
                    a[kind, layer, k, pl.ds(SUB + t * SUB, SUB), :] = load(kind, layer, t, k)
                e[layer, k, pl.ds(t * SUB, SUB), :] = COURANT * load(3, layer, t, k)

    at_end, at_start = lane == LANES - 1, lane == 0
    keys = [(layer, k) for layer in range(2) for k in range(n_lanes)]

    def next_col(values):
        moved = {key: turn(value, -1, 1) for key, value in values.items()}
        return {
            (l, k): jnp.where(at_end, moved[l, (k + 1) % n_lanes], moved[l, k]) for l, k in keys
        }

    def prev_col(values):
        moved = {key: turn(value, 1, 1) for key, value in values.items()}
        return {
            (l, k): jnp.where(at_start, moved[l, (k - 1) % n_lanes], moved[l, k]) for l, k in keys
        }

    yee(
        (a, b, last), keys,
        lambda key, t: e[key + (pl.ds(t * SUB, SUB), slice(None))],
        lambda step, key, t: load(4 + step, key[0], t, key[1]),
        lambda step, key, t: src[step, key[0], pl.ds(t * SUB, SUB), lane_tile(key[1])],
        g, COURANT, coef_above(), next_col, prev_col,
        lambda values, key: values[1 - key[0], key[1]],
    )
    for layer in range(2):
        total = None
        for k in range(n_lanes):
            for part in split2(row_pairs(g, (layer, k), n_tiles * SUB // PIX)):
                term = dot(part, mats[k])
                total = term if total is None else total + term
        pooled[layer] = total

    vals = by_tile([cone_filter(pooled.at[layer], rows // PIX, PAD // PIX) for layer in range(2)])
    high, low = split2(vals)
    slots[...] = dot(place[...], high) + dot(place[...], low)

    for t in range(n_tiles):
        for kind in range(4 + STEPS):
            at = pl.ds(t * SUB, SUB)
            if t not in halo_of:
                base[kind, at, :] = base_in[kind, at, :]
            elif kind < 4 or t not in (0, n_tiles - 1):
                base[kind, at, :] = edge_tile(
                    lambda kind, layer, k: load(kind, layer, t, k), kind, lane, n_lanes
                )


def cone_filter(pooled, out_pix, first):
    weights = cone_weights(RADIUS)
    reach = RADIUS - 1
    lane = lax.broadcasted_iota(jnp.int32, (out_pix, LANES), 1)
    at = [pooled[pl.ds(first + s, out_pix), :] for s in range(-reach, reach + 1)]
    sums = [at[reach]] + [at[reach + s] + at[reach - s] for s in range(1, reach + 1)]
    total = None
    for shift in range(reach + 1):
        mixed = None
        for s in range(reach + 1):
            weight = float(weights[reach + s, reach + shift])
            if weight > 0.0:
                term = weight * sums[s]
                mixed = term if mixed is None else mixed + term
        if shift == 0:
            total = mixed
        else:
            total = total + turn(jnp.where(lane < shift, 0.0, mixed), -shift, 1)
            total = total + turn(jnp.where(lane >= LANES - shift, 0.0, mixed), shift, 1)
    return total


def by_tile(blocks):
    span = TS // PIX
    tile_rows = blocks[0].shape[0] // span
    x = jnp.stack([block.reshape(tile_rows, span, LANES) for block in blocks], axis=1)
    x = x.reshape(tile_rows * 2, span, LANES)
    group = lax.broadcasted_iota(jnp.int32, x.shape, 2) // span
    row = lax.broadcasted_iota(jnp.int32, x.shape, 1)
    for bit in (1, 2, 4):
        row_on, lane_on = (row & bit) != 0, (group & bit) != 0
        ahead = turn(turn(x, -bit, 1), bit * span, 2)
        behind = turn(turn(x, bit, 1), -bit * span, 2)
        x = jnp.where(row_on == lane_on, x, jnp.where(lane_on, ahead, behind))
    x = x.reshape(tile_rows, 2, span, LANES)
    even, odd = x[:, 0], x[:, 1]
    upper = lax.broadcasted_iota(jnp.int32, even.shape, 2) >= HALF
    new_even = jnp.where(upper, turn(odd, HALF, 2), even)
    new_odd = jnp.where(upper, odd, turn(even, HALF, 2))
    return jnp.stack([new_even, new_odd], axis=1).reshape(tile_rows * 2 * span, LANES)


def merge_spans(spans, lane):
    even = (lane & 1) == 0
    window = ((lane - OUT) & (HALF - 1)) < SIDE
    merged = []
    for e in (0, 4):
        low = jnp.where(even, spans[e], turn(spans[e + 1], 1, 1))
        high = jnp.where(even, turn(spans[e + 2], SIDE, 1), turn(spans[e + 3], SIDE + 1, 1))
        merged.append(jnp.where(window, low, high))
    return jnp.concatenate(merged, axis=1)


def edge_kernel(
    last, slots_in, base, cross, near, src, place, spread, out_fields, slots, a, b, c, e, d, g, merged, sem
):
    ext_rows = base.shape[1]
    rows = ext_rows - 2 * PAD
    n_tiles = ext_rows // SUB
    lane, odd = lanes(), is_odd("gy")
    spot = lane & (HALF - 1)
    is_left, is_right = spot < OUT, spot >= HALF - OUT

    for buf in (a, b, c):
        clear_rims(buf)
    for t in range(n_tiles):
        at = pl.ds(t * SUB, SUB)
        far, close = cross[at, :], near[at, :]
        high, low = jnp.where(odd, close, far), jnp.where(odd, far, close)
        for kind, width in enumerate(WIDTHS):
            if kind >= 4 and t in (0, n_tiles - 1):
                continue
            value = jnp.where(is_left, turn(high, OUT - width - FIRST[kind], 1), base[kind, at, :])
            value = jnp.where(is_right, turn(low, HALF - OUT - FIRST[kind], 1), value)
            if kind < 3:
                a[kind, pl.ds(SUB + t * SUB, SUB), :] = value
            elif kind == 3:
                e[at, :] = COURANT * value
            else:
                d[kind - 4, at, :] = value

    before = (lax.axis_index("gy") + lane * 0) > 0
    coef_x = jnp.where(before | (spot >= OUT), COURANT, 0.0).astype(F32)
    yee(
        (a, b, c), [()],
        lambda key, t: e[pl.ds(t * SUB, SUB), :],
        lambda step, key, t: d[step, pl.ds(t * SUB, SUB), :],
        lambda step, key, t: src[step, pl.ds(t * SUB, SUB), :],
        g, coef_x, coef_above(),
        lambda values: {(): turn(values[()], -1, 1)},
        lambda values: {(): turn(values[()], 1, 1)},
        lambda values, key: turn(values[()], HALF, 1),
    )

    n_lanes = merged.shape[3] // LANES
    for t in range(rows // SUB):
        at, out_at = pl.ds(SUB + PAD + t * SUB, SUB), pl.ds(t * SUB, SUB)
        for kind in range(3):
            edge = c[kind, at, :]
            for layer in range(2):
                for k in range(n_lanes):
                    value = last[kind, layer, k, at, :]
                    if k == 0:
                        value = jnp.where(lane < KEEP, turn(edge, -HALF * layer - OUT, 1), value)
                    if k == n_lanes - 1:
                        value = jnp.where(
                            lane >= LANES - KEEP, turn(edge, -HALF * layer - SIDE - OUT, 1), value
                        )
                    merged[kind, layer, out_at, lane_tile(k)] = value
    copy = pltpu.make_async_copy(merged, out_fields, sem)
    copy.start()

    inside = (spot >= OUT - NEAR) & (spot < OUT + KEEP)
    inside = inside | ((spot >= HALF - OUT - KEEP) & (spot < HALF - OUT + NEAR))
    span, reach = TS // PIX, RADIUS - 1
    pixel = {}
    for j in range(-reach, span + reach):
        value = g[pl.ds(PAD + PIX * j, SUB, stride=TS), :]
        value = jnp.where(inside, value + g[pl.ds(PAD + PIX * j + 1, SUB, stride=TS), :], 0.0)
        pixel[j] = value + turn(value, -1, 1)

    weights = cone_weights(RADIUS)
    spans = []
    for row in range(span):
        sums = [pixel[row]] + [pixel[row + s] + pixel[row - s] for s in range(1, reach + 1)]
        total = None
        for shift in range(reach + 1):
            mixed = None
            for s in range(reach + 1):
                weight = float(weights[reach + s, reach + shift])
                if weight > 0.0:
                    term = weight * sums[s]
                    mixed = term if mixed is None else mixed + term
            if shift:
                mixed = turn(mixed, -PIX * shift, 1) + turn(mixed, PIX * shift, 1)
            total = mixed if total is None else total + mixed
        spans.append(total)

    edge = dot(jnp.concatenate(split2(merge_spans(spans, lane)), axis=0), spread[...])
    edge = edge[:SUB] + edge[SUB:]
    edge = jnp.concatenate([edge[:, :LANES], edge[:, LANES:]], axis=0)
    slots[...] = slots_in[...] + dot(place[...], jnp.concatenate(split2(edge), axis=0))
    copy.wait()


def vmem():
    return pl.BlockSpec(memory_space=pltpu.VMEM)


def shape(*dims, dtype=F32):
    return jax.ShapeDtypeStruct(dims, dtype)


def call(kernel, outs, n_in, *, in_space=pltpu.VMEM, out_specs=None, scratch=(), flops=0, size=0):
    return pl.pallas_call(
        kernel,
        out_shape=outs,
        in_specs=[pl.BlockSpec(memory_space=in_space)] * n_in,
        out_specs=out_specs or tuple(vmem() for _ in outs),
        scratch_shapes=list(scratch),
        compiler_params=pltpu.CompilerParams(vmem_limit_bytes=40 * 1024 * 1024),
        cost_estimate=pl.CostEstimate(flops=flops, bytes_accessed=size, transcendentals=0),
    )


def on_device(adj_fields, inv_eps, fwd_diff, mon_x, mon_y, mon_amp, design_mask, tile_owner):
    rows, cols = adj_fields.shape[2], adj_fields.shape[3]
    assert cols == 2 * LANES and rows % TS == 0
    gx_count, gy_count = lax.axis_size("gx"), lax.axis_size("gy")
    owners = gx_count * gy_count
    tiles = (rows // TS) * (cols // TS)
    width = 2 * (TS // PIX) ** 2
    assert width == LANES
    capacity = max(8, 2 * tiles // owners)
    assert rows == TS * SUB and cols == 2 * TS * SUB
    ext_rows = rows + 2 * PAD
    n_lanes = cols // LANES
    cells = rows * cols
    blocks = (adj_fields, inv_eps, fwd_diff)


    strip = shape(16, SUB, cols)
    cross, near = call(
        rows_kernel, (strip, strip), 3, in_space=pltpu.HBM,
        scratch=(
            pltpu.VMEM((2, 4, 2, PAD, cols), F32),
            pltpu.VMEM((2, STEPS, 2, SUB, cols), F32),
            pltpu.SemaphoreType.DMA((6,)),
        ),
        size=2**20,
    )(*(pltpu.with_memory_space_constraint(block, pltpu.HBM) for block in blocks))

    def pairs(count, start):
        some = [(i, i + 1) for i in range(start, count - 1, 2)]
        return some + [(j, i) for i, j in some]

    cross = lax.ppermute(cross, "gx", pairs(gx_count, 1))
    near = lax.ppermute(near, "gx", pairs(gx_count, 0))

    packed = shape(ext_rows, LANES)
    channels = mon_x.shape[0]
    cross_cols, near_cols, base, src, src_edge, place, place_edge = call(
        lambda *refs: prep_kernel(capacity, *refs),
        (
            packed,
            packed,
            shape(4 + STEPS, ext_rows, LANES),
            shape(STEPS, 2, ext_rows, cols),
            shape(STEPS, ext_rows, LANES),
            shape(owners * capacity, tiles, dtype=BF16),
            shape(owners * capacity, 4 * SUB, dtype=BF16),
        ),
        8,
        flops=16 * ext_rows * (cols + LANES) * 3 * channels,
        size=64 * cells,
    )(
        *blocks,
        mon_x.reshape(1, channels),
        mon_y.reshape(1, channels),
        mon_amp,
        design_mask.reshape(1, tiles),
        tile_owner.reshape(1, tiles),
    )
    cross_cols, near_cols = call(
        corners_kernel, (packed, packed), 4, flops=cells, size=8 * ext_rows * LANES
    )(cross_cols, near_cols, cross, near)
    cross_cols = lax.ppermute(cross_cols, "gy", pairs(gy_count, 1))
    near_cols = lax.ppermute(near_cols, "gy", pairs(gy_count, 0))

    state = (3, 2, n_lanes, ext_rows + 2 * SUB, LANES)
    last, slots, base = call(
        inner_kernel,
        (shape(*state), shape(owners * capacity, width), shape(4 + STEPS, ext_rows, LANES)),
        9,
        scratch=(
            pltpu.VMEM(state, F32),
            pltpu.VMEM(state, F32),
            pltpu.VMEM((2, n_lanes, ext_rows, LANES), F32),
            pltpu.VMEM((2, n_lanes, ext_rows, LANES), F32),
            pltpu.VMEM((2, ext_rows // PIX, LANES), F32),
        ),
        flops=200 * cells,
        size=96 * cells,
    )(*blocks, cross, near, src, pool_matrices(), base, place)

    edge_state = (3, ext_rows + 2 * SUB, LANES)
    fields, outgoing = call(
        edge_kernel,
        (shape(3, 2, rows, cols), shape(owners * capacity, width)),
        8,
        out_specs=(pl.BlockSpec(memory_space=pl.ANY), vmem()),
        scratch=(
            pltpu.VMEM(edge_state, F32),
            pltpu.VMEM(edge_state, F32),
            pltpu.VMEM(edge_state, F32),
            pltpu.VMEM((ext_rows, LANES), F32),
            pltpu.VMEM((STEPS, ext_rows, LANES), F32),
            pltpu.VMEM((ext_rows, LANES), F32),
            pltpu.VMEM((3, 2, rows, cols), F32),
            pltpu.SemaphoreType.DMA,
        ),
        flops=50 * cells,
        size=16 * cells,
    )(last, slots, base, cross_cols, near_cols, src_edge, place_edge, spread_matrix())

    outgoing = outgoing.reshape(owners, capacity, width)
    incoming = lax.all_to_all(outgoing, ("gx", "gy"), split_axis=0, concat_axis=0, tiled=True)
    return fields, incoming[None]


def solution(mesh):
    placed = (
        P(None, None, ("parts", "gx"), "gy"),
        P(None, ("parts", "gx"), "gy"),
        P(None, None, ("parts", "gx"), "gy"),
        P("parts"),
        P("parts"),
        P(None, "parts"),
        P(("parts", "gx"), "gy", None),
        P(("parts", "gx"), "gy", None, None),
    )
    return jax.shard_map(
        on_device,
        mesh=mesh,
        in_specs=placed,
        out_specs=(
            P(None, None, ("parts", "gx"), "gy"),
            P(("parts", "gx", "gy"), None, None, None),
        ),
        check_vma=False,
    )
```

```python
import jax
import jax.numpy as jnp
import ml_dtypes
import numpy as np
from jax import lax
from jax.experimental import pallas as pl
from jax.experimental.pallas import tpu as pltpu
from jax.sharding import PartitionSpec as P

STEPS = 4
PIX = 2
TS = 16
RADIUS = 4
COURANT = 0.6
COUPLING = 0.25

LANES = 128
SUB = 8
FAR = STEPS + PIX * (RADIUS - 1)
NEAR = PIX * (RADIUS - 1)
LEFT_OVER = FAR - SUB
PAD = 2 * SUB
HALF = LANES // 2
SIDE = HALF // 2
OUT = SIDE // 2
KEEP = 8
F32 = jnp.float32
BF16 = jnp.bfloat16
WIDTHS = (FAR,) * 4 + (NEAR,) * STEPS
FIRST = tuple(sum(WIDTHS[:k]) for k in range(len(WIDTHS)))
assert sum(WIDTHS) <= HALF and FAR <= OUT and STEPS + KEEP <= OUT


def cone_weights(radius):
    reach_cells = radius - 1
    offsets = np.arange(-reach_cells, reach_cells + 1)
    distance = np.sqrt(offsets[:, None] * offsets[:, None] + offsets[None, :] * offsets[None, :])
    weights = np.maximum(radius - distance, 0.0)
    return weights / weights.sum()


def pool_matrices():
    inner = np.zeros((2, LANES, LANES), np.float32)
    for j in range(KEEP, 2 * LANES - KEEP):
        inner[j // LANES, j % LANES, j // PIX] = 1.0
    return inner.astype(ml_dtypes.bfloat16)


def split2(value):
    high = value.astype(BF16)
    return high, (value - high.astype(F32)).astype(BF16)


def split3(value):
    high = value.astype(BF16)
    rest = value - high.astype(F32)
    mid = rest.astype(BF16)
    return high, mid, (rest - mid.astype(F32)).astype(BF16)


def dot(a, b):
    return jnp.dot(a, b, preferred_element_type=F32)


def turn(value, shift, axis):
    size = value.shape[axis]
    return pltpu.roll(value, shift % size, axis) if shift % size else value


def lanes():
    return lax.broadcasted_iota(jnp.int32, (SUB, LANES), 1)


def subs():
    return lax.broadcasted_iota(jnp.int32, (SUB, LANES), 0)


def lane_tile(k):
    return pl.ds(k * LANES, LANES)


def is_odd(axis):
    return ((subs() * 0 + lax.axis_index(axis)) & 1) == 1


def rows_kernel(fields, eps, fwd, cross, near, hold, hold_fwd, sems):
    rows, cols = fields.shape[2], fields.shape[3]
    copies = []
    for n, at in enumerate((0, rows - PAD)):
        at_fwd = 0 if n == 0 else rows - SUB
        pairs = (
            (fields.at[:, :, pl.ds(at, PAD), :], hold.at[n, pl.ds(0, 3)]),
            (eps.at[:, pl.ds(at, PAD), :], hold.at[n, 3]),
            (fwd.at[:, :, pl.ds(at_fwd, SUB), :], hold_fwd.at[n]),
        )
        for m, (src, dst) in enumerate(pairs):
            copies.append(pltpu.make_async_copy(src, dst, sems.at[3 * n + m]))
    for copy in copies:
        copy.start()
    for copy in copies:
        copy.wait()
    odd, sub = is_odd("gx"), subs()
    for kind in range(4):
        for layer in range(2):
            plane = 2 * kind + layer
            for k in range(cols // LANES):
                at = lane_tile(k)
                low = hold[0, kind, layer, pl.ds(0, SUB), at]
                high = hold[1, kind, layer, pl.ds(SUB, SUB), at]
                cross[plane, :, at] = jnp.where(odd, high, low)
                near[plane, :, at] = jnp.where(odd, low, high)
                rest_low = turn(hold[0, kind, layer, pl.ds(SUB, SUB), at], -LEFT_OVER, 0)
                rest_high = turn(hold[1, kind, layer, pl.ds(0, SUB), at], LEFT_OVER, 0)
                low = jnp.where(sub >= NEAR, rest_low, hold_fwd[0, kind, layer, :, at])
                high = jnp.where(sub < SUB - NEAR, rest_high, hold_fwd[1, kind, layer, :, at])
                cross[8 + plane, :, at] = jnp.where(odd, high, low)
                near[8 + plane, :, at] = jnp.where(odd, low, high)


def halo_tile(cross, near, odd, tile, kind, layer, at):
    is_above = tile < 2
    outer = tile in (0, 3)
    if outer and kind >= 4:
        return None
    plane = 2 * kind + layer + (8 if outer else 0)
    a, b = near[plane, :, at], cross[plane, :, at]
    value = jnp.where(odd, a, b) if is_above else jnp.where(odd, b, a)
    if outer:
        value = turn(value, -LEFT_OVER if is_above else LEFT_OVER, 0)
    return value


def core_tile(fields, eps, fwd, at, kind, layer, cols):
    if kind < 3:
        return fields[kind, layer, at, cols]
    if kind == 3:
        return eps[layer, at, cols]
    return fwd[kind - 4, layer, at, cols]


def pack_tile(load, lane, right):
    total = jnp.zeros((SUB, LANES), F32)
    for kind, width in enumerate(WIDTHS):
        for layer in range(2):
            value = load(kind, layer)
            if value is None:
                continue
            first = FIRST[kind] + HALF * layer
            value = turn(value, first + width if right else first, 1)
            total = jnp.where((lane >= first) & (lane < first + width), value, total)
    return total


def edge_tile(load, kind, lane, n_lanes):
    spot = lane & (HALF - 1)
    total = None
    for layer in range(2):
        low = turn(load(kind, layer, 0), HALF * layer + OUT, 1)
        high = turn(load(kind, layer, n_lanes - 1), HALF * layer + SIDE + OUT, 1)
        value = jnp.where(spot < SIDE, low, high)
        total = value if total is None else jnp.where(lane < HALF, total, value)
    return total


def cols_kernel(fields, eps, fwd, cross, near, base):
    rows, cols = fields.shape[2], fields.shape[3]
    n_lanes = cols // LANES
    lane, odd = lanes(), is_odd("gy")

    def tile(t, carry):
        at = pl.ds(pl.multiple_of(t * SUB, SUB), SUB)
        out_at = pl.ds(pl.multiple_of(t * SUB + PAD, SUB), SUB)

        def load(kind, layer, k):
            return core_tile(fields, eps, fwd, at, kind, layer, lane_tile(k))

        left = pack_tile(lambda kind, layer: load(kind, layer, 0), lane, False)
        right = pack_tile(lambda kind, layer: load(kind, layer, n_lanes - 1), lane, True)
        cross[out_at, :] = jnp.where(odd, right, left)
        near[out_at, :] = jnp.where(odd, left, right)
        for kind in range(4 + STEPS):
            base[kind, out_at, :] = edge_tile(load, kind, lane, n_lanes)
        return carry

    lax.fori_loop(0, rows // SUB, tile, 0, unroll=4)
    zero = jnp.zeros((PAD, LANES), F32)
    for out in (cross, near):
        out[pl.ds(0, PAD), :] = zero
        out[pl.ds(PAD + rows, PAD), :] = zero


def corners_kernel(cross_in, near_in, cross_rows, near_rows, cross, near):
    rows, cols = cross.shape[0] - 2 * PAD, cross_rows.shape[2]
    lane, odd, odd_col = lanes(), is_odd("gx"), is_odd("gy")
    core = pl.ds(PAD, rows)
    cross[core, :] = cross_in[core, :]
    near[core, :] = near_in[core, :]
    for tile in range(4):
        at = pl.ds(tile * SUB if tile < 2 else PAD + rows + (tile - 2) * SUB, SUB)
        left, right = (
            pack_tile(
                lambda kind, layer: halo_tile(
                    cross_rows, near_rows, odd, tile, kind, layer, pl.ds(lo, LANES)
                ),
                lane, is_right,
            )
            for lo, is_right in ((0, False), (cols - LANES, True))
        )
        cross[at, :] = jnp.where(odd_col, right, left)
        near[at, :] = jnp.where(odd_col, left, right)


def prep_kernel(
    capacity, fields, eps, fwd, mon_x, mon_y, amp, mask, owner, cross, near, base, src, src_edge, place, place_edge
):
    cols_kernel(fields, eps, fwd, cross, near, base)
    side_kernel(capacity, fields.shape[2], mon_x, mon_y, amp, mask, owner, src, src_edge, place, place_edge)


def side_kernel(capacity, rows, mon_x, mon_y, amp, mask, owner, src, src_edge, place, place_edge):
    _, _, ext_rows, cols = src.shape
    channels = mon_x.shape[1]
    row = mon_x[...] - lax.axis_index("gx") * rows + PAD
    col = mon_y[...] - lax.axis_index("gy") * cols
    in_left = (col >= -OUT) & (col < OUT)
    in_right = (col >= cols - OUT) & (col < cols + OUT)
    edge = jnp.where(in_left, col + OUT, jnp.where(in_right, col - cols + OUT + SIDE, -LANES))
    layer = lax.broadcasted_iota(jnp.int32, (1, channels), 1) & 1
    edge = edge + HALF * layer
    inside = jnp.where((col >= 0) & (col < cols), col, -1)
    one_y = lax.broadcasted_iota(jnp.int32, (cols, channels), 0) == inside
    one_e = lax.broadcasted_iota(jnp.int32, (LANES, channels), 0) == edge
    one_y = jnp.where(one_y, 1.0, 0.0).astype(BF16)
    one_e = jnp.where(one_e, 1.0, 0.0).astype(BF16)
    one_y = jnp.concatenate([one_y] * 3, axis=1)
    one_e = jnp.concatenate([one_e] * 3, axis=1)
    one_x = lax.broadcasted_iota(jnp.int32, (ext_rows, channels), 0) == row
    one_x = jnp.where(one_x, 1.0, 0.0).astype(F32)
    nt = (((1,), (1,)), ((), ()))
    for step in range(STEPS):
        parts = [part.astype(F32) for part in split3(amp[pl.ds(step, 1), :])]
        lhs = jnp.concatenate([one_x * part for part in parts], axis=1)
        src_edge[step] = lax.dot_general(lhs.astype(BF16), one_e, nt, preferred_element_type=F32)
        layer_wide = jnp.concatenate([layer] * 3, axis=1)
        for which in range(2):
            some = jnp.where(layer_wide == which, lhs, 0.0).astype(BF16)
            src[step, which] = lax.dot_general(some, one_y, nt, preferred_element_type=F32)
    tiles = owner.shape[1]
    own = owner[...].astype(F32)
    own_wide = jnp.broadcast_to(own, (tiles, tiles))
    earlier = lax.broadcasted_iota(jnp.int32, (tiles, tiles), 0) < lax.broadcasted_iota(
        jnp.int32, (tiles, tiles), 1
    )
    same = (own_wide.T == own_wide) & earlier
    slot = jnp.sum(jnp.where(same, 1.0, 0.0), axis=0, keepdims=True)
    dest = owner[...] * capacity + slot.astype(jnp.int32)
    dest = jnp.where(mask[...] != 0, dest, -1)
    hit = lax.broadcasted_iota(jnp.int32, place.shape, 0) == dest
    hit = jnp.where(hit, 1.0, 0.0).astype(BF16)
    place[...] = hit
    tile_cols = cols // TS
    column = lax.broadcasted_iota(jnp.int32, (tiles, 4 * SUB), 1)
    wanted = (column % SUB) * tile_cols + ((column // SUB) & 1) * (tile_cols - 1)
    picked = lax.broadcasted_iota(jnp.int32, (tiles, 4 * SUB), 0) == wanted
    place_edge[...] = dot(hit, jnp.where(picked, 1.0, 0.0).astype(BF16)).astype(BF16)


class Shifts:
    def __init__(self, next_col, prev_col):
        self.next_col, self.prev_col = next_col, prev_col
        self.bottom, self.top = subs() == SUB - 1, subs() == 0

    def up(self, tile):
        return {key: turn(value, -1, 0) for key, value in tile.items()}

    def down(self, tile):
        return {key: turn(value, 1, 0) for key, value in tile.items()}

    def below(self, up_here, up_next):
        return {key: jnp.where(self.bottom, up_next[key], up_here[key]) for key in up_here}

    def above(self, down_here, down_before):
        return {key: jnp.where(self.top, down_before[key], down_here[key]) for key in down_here}


def tile_at(t):
    return (pl.ds(t * SUB, SUB), slice(None))


def first_curl(n_tiles, shifts, load_hx, load_hy, curl):
    before = None
    for t in range(n_tiles):
        hx, hy = load_hx(t), load_hy(t)
        down = shifts.down(hy)
        over = shifts.above(down, before if t else down)
        left = shifts.prev_col(hx)
        for key in hx:
            curl[key + tile_at(t)] = (hy[key] - over[key]) - (hx[key] - left[key])
        before = down


def steps(n_tiles, keys, shifts, e, curl, eps_of, src_of, other):
    no_above = shifts.top & ((lax.axis_index("gx") + subs() * 0) == 0)
    for step in range(STEPS):
        low, high = (0, n_tiles) if step == 0 else (1, n_tiles - 1)

        def load(t):
            return {key: e[(step,) + key + tile_at(t)] for key in keys}

        here = load(low)
        up = shifts.up(here)
        down_before = shifts.down(load(max(low - 1, 0)))
        for t in range(low, high):
            after = load(min(t + 1, n_tiles - 1))
            up_next, down = shifts.up(after), shifts.down(here)
            below, above = shifts.below(up, up_next), shifts.above(down, down_before)
            right, left = shifts.next_col(here), shifts.prev_col(here)
            for key in keys:
                center, over = here[key], above[key]
                if t == PAD // SUB:
                    over = jnp.where(no_above, center, over)
                ring = (below[key] + over) + (right[key] + left[key]) - 4.0 * center
                change = curl[key + tile_at(t)] - COURANT * ring
                if step < STEPS - 1:
                    curl[key + tile_at(t)] = change
                change = change + COUPLING * (other(here, key) - center)
                e[(step + 1,) + key + tile_at(t)] = (
                    center - eps_of(key, t) * change + src_of(step, key, t)
                )
            here, up, down_before = after, up_next, down


def gradient(keys, t, e, change_of):
    result = {}
    for key in keys:
        total = None
        for step in range(STEPS):
            term = e[(step + 1,) + key + tile_at(t)] * change_of(step, key, t)
            total = term if total is None else total + term
        result[key] = -total
    return result


def last_fields(tiles, keys, shifts, e, load_hx, load_hy, store):
    def total(t):
        result = {}
        for key in keys:
            parts = [e[(step,) + key + tile_at(t)] for step in range(STEPS)]
            result[key] = (parts[0] + parts[1]) + (parts[2] + parts[3])
        return result

    here = total(tiles[0])
    up = shifts.up(here)
    for t in tiles:
        after = total(t + 1)
        up_next = shifts.up(after)
        below, right = shifts.below(up, up_next), shifts.next_col(here)
        hx, hy = load_hx(t), load_hy(t)
        for key in keys:
            store(0, key, t, e[(STEPS,) + key + tile_at(t)])
            store(1, key, t, hx[key] + COURANT * (right[key] - here[key]))
            store(2, key, t, hy[key] - COURANT * (below[key] - here[key]))
        here, up = after, up_next


def row_pairs(ref, lead, count):
    even = ref[lead + (pl.ds(0, count, stride=PIX), slice(None))]
    return even + ref[lead + (pl.ds(1, count, stride=PIX), slice(None))]


def inner_kernel(
    fields, eps, fwd, cross, near, src, mats, base_in, place, last, slots, base, e, curl, eps_c, g, pooled
):
    rows, cols = fields.shape[2], fields.shape[3]
    n_tiles = (rows + 2 * PAD) // SUB
    n_lanes = cols // LANES
    lane, odd = lanes(), is_odd("gx")
    halo_of = {0: 0, 1: 1, n_tiles - 2: 2, n_tiles - 1: 3}
    keys = [(layer, k) for layer in range(2) for k in range(n_lanes)]

    def load(kind, layer, t, k):
        if t in halo_of:
            return halo_tile(cross, near, odd, halo_of[t], kind, layer, lane_tile(k))
        return core_tile(fields, eps, fwd, pl.ds(t * SUB - PAD, SUB), kind, layer, lane_tile(k))

    def load_all(kind, t):
        return {key: load(kind, key[0], t, key[1]) for key in keys}

    at_end, at_start = lane == LANES - 1, lane == 0

    def next_col(values):
        moved = {key: turn(value, -1, 1) for key, value in values.items()}
        return {
            (l, k): jnp.where(at_end, moved[l, (k + 1) % n_lanes], moved[l, k]) for l, k in keys
        }

    def prev_col(values):
        moved = {key: turn(value, 1, 1) for key, value in values.items()}
        return {
            (l, k): jnp.where(at_start, moved[l, (k - 1) % n_lanes], moved[l, k]) for l, k in keys
        }

    shifts = Shifts(next_col, prev_col)
    for t in range(n_tiles):
        for key in keys:
            e[(0,) + key + tile_at(t)] = load(0, key[0], t, key[1])
            eps_c[key + tile_at(t)] = COURANT * load(3, key[0], t, key[1])
    first_curl(n_tiles, shifts, lambda t: load_all(1, t), lambda t: load_all(2, t), curl)
    steps(
        n_tiles, keys, shifts, e, curl,
        lambda key, t: eps_c[key + tile_at(t)],
        lambda step, key, t: src[step, key[0], pl.ds(t * SUB, SUB), lane_tile(key[1])],
        lambda values, key: values[1 - key[0], key[1]],
    )
    for t in range(1, n_tiles - 1):
        values = gradient(keys, t, e, lambda step, key, t: load(4 + step, key[0], t, key[1]))
        for key in keys:
            g[key + tile_at(t)] = values[key]

    def store(kind, key, t, value):
        last[(kind,) + key + (pl.ds(t * SUB - PAD, SUB), slice(None))] = value

    last_fields(
        range(PAD // SUB, n_tiles - PAD // SUB), keys, shifts, e,
        lambda t: load_all(1, t), lambda t: load_all(2, t), store,
    )
    for layer in range(2):
        total = None
        for k in range(n_lanes):
            for part in split2(row_pairs(g, (layer, k), n_tiles * SUB // PIX)):
                term = dot(part, mats[k])
                total = term if total is None else total + term
        pooled[layer] = total

    vals = by_tile([cone_filter(pooled.at[layer], rows // PIX, PAD // PIX) for layer in range(2)])
    high, low = split2(vals)
    slots[...] = dot(place[...], high) + dot(place[...], low)

    for t in range(n_tiles):
        for kind in range(4 + STEPS):
            at = pl.ds(t * SUB, SUB)
            if t not in halo_of:
                base[kind, at, :] = base_in[kind, at, :]
            elif kind < 4 or t not in (0, n_tiles - 1):
                base[kind, at, :] = edge_tile(
                    lambda kind, layer, k: load(kind, layer, t, k), kind, lane, n_lanes
                )


def cone_filter(pooled, out_pix, first):
    weights = cone_weights(RADIUS)
    reach = RADIUS - 1
    lane = lax.broadcasted_iota(jnp.int32, (out_pix, LANES), 1)
    at = [pooled[pl.ds(first + s, out_pix), :] for s in range(-reach, reach + 1)]
    sums = [at[reach]] + [at[reach + s] + at[reach - s] for s in range(1, reach + 1)]
    total = None
    for shift in range(reach + 1):
        mixed = None
        for s in range(reach + 1):
            weight = float(weights[reach + s, reach + shift])
            if weight > 0.0:
                term = weight * sums[s]
                mixed = term if mixed is None else mixed + term
        if shift == 0:
            total = mixed
        else:
            total = total + turn(jnp.where(lane < shift, 0.0, mixed), -shift, 1)
            total = total + turn(jnp.where(lane >= LANES - shift, 0.0, mixed), shift, 1)
    return total


def by_tile(blocks):
    span = TS // PIX
    tile_rows = blocks[0].shape[0] // span
    x = jnp.stack([block.reshape(tile_rows, span, LANES) for block in blocks], axis=1)
    x = x.reshape(tile_rows * 2, span, LANES)
    group = lax.broadcasted_iota(jnp.int32, x.shape, 2) // span
    row = lax.broadcasted_iota(jnp.int32, x.shape, 1)
    for bit in (1, 2, 4):
        row_on, lane_on = (row & bit) != 0, (group & bit) != 0
        ahead = turn(turn(x, -bit, 1), bit * span, 2)
        behind = turn(turn(x, bit, 1), -bit * span, 2)
        x = jnp.where(row_on == lane_on, x, jnp.where(lane_on, ahead, behind))
    x = x.reshape(tile_rows, 2, span, LANES)
    even, odd = x[:, 0], x[:, 1]
    upper = lax.broadcasted_iota(jnp.int32, even.shape, 2) >= HALF
    new_even = jnp.where(upper, turn(odd, HALF, 2), even)
    new_odd = jnp.where(upper, odd, turn(even, HALF, 2))
    return jnp.stack([new_even, new_odd], axis=1).reshape(tile_rows * 2 * span, LANES)


def merge_spans(spans, lane):
    even = (lane & 1) == 0
    window = ((lane - OUT) & (HALF - 1)) < SIDE
    merged = []
    for e in (0, 4):
        low = jnp.where(even, spans[e], turn(spans[e + 1], 1, 1))
        high = jnp.where(even, turn(spans[e + 2], SIDE, 1), turn(spans[e + 3], SIDE + 1, 1))
        merged.append(jnp.where(window, low, high))
    span = TS // PIX
    row, pixel = lane // span % span, lane % span
    start = (lane & HALF) + OUT + PIX * pixel + (row & 1) + SIDE * ((row >> 1) & 1)
    result = []
    for side in range(2):
        index = (start + OUT * side) & (LANES - 1)
        low, high = (jnp.take_along_axis(value, index, axis=1) for value in merged)
        result.append(jnp.where(row < span // 2, low, high))
    return result


def edge_kernel(
    last, slots_in, base, cross, near, src, place, out_fields, slots, e, first, curl, eps_c, d, g, merged, sem
):
    ext_rows = base.shape[1]
    rows = ext_rows - 2 * PAD
    n_tiles = ext_rows // SUB
    lane, odd = lanes(), is_odd("gy")
    spot = lane & (HALF - 1)
    is_left, is_right = spot < OUT, spot >= HALF - OUT

    for t in range(n_tiles):
        at = pl.ds(t * SUB, SUB)
        far, close = cross[at, :], near[at, :]
        high, low = jnp.where(odd, close, far), jnp.where(odd, far, close)
        for kind, width in enumerate(WIDTHS):
            if kind >= 4 and t in (0, n_tiles - 1):
                continue
            value = jnp.where(is_left, turn(high, OUT - width - FIRST[kind], 1), base[kind, at, :])
            value = jnp.where(is_right, turn(low, HALF - OUT - FIRST[kind], 1), value)
            if kind == 0:
                e[0, at, :] = value
            elif kind < 3:
                first[kind - 1, at, :] = value
            elif kind == 3:
                eps_c[at, :] = COURANT * value
            else:
                d[kind - 4, at, :] = value

    no_left = (spot == OUT) & ((lax.axis_index("gy") + lane * 0) == 0)
    shifts = Shifts(
        lambda values: {(): turn(values[()], -1, 1)},
        lambda values: {(): turn(values[()], 1, 1)},
    )

    def load_hx(t):
        return {(): first[0, pl.ds(t * SUB, SUB), :]}

    def load_hy(t):
        return {(): first[1, pl.ds(t * SUB, SUB), :]}

    first_curl(n_tiles, shifts, load_hx, load_hy, curl)
    shifts.prev_col = lambda values: {(): jnp.where(no_left, values[()], turn(values[()], 1, 1))}
    steps(
        n_tiles, [()], shifts, e, curl,
        lambda key, t: eps_c[pl.ds(t * SUB, SUB), :],
        lambda step, key, t: src[step, pl.ds(t * SUB, SUB), :],
        lambda values, key: turn(values[()], HALF, 1),
    )
    inside = (spot >= OUT - NEAR) & (spot < OUT + KEEP)
    inside = inside | ((spot >= HALF - OUT - KEEP) & (spot < HALF - OUT + NEAR))
    for t in range(1, n_tiles - 1):
        value = gradient([()], t, e, lambda step, key, t: d[step, pl.ds(t * SUB, SUB), :])[()]
        g[pl.ds(t * SUB, SUB), :] = jnp.where(inside, value, 0.0)

    n_lanes = merged.shape[3] // LANES

    def store(kind, key, t, edge):
        at = pl.ds(t * SUB - PAD, SUB)
        for layer in range(2):
            for k in range(n_lanes):
                value = last[kind, layer, k, at, :]
                if k == 0:
                    value = jnp.where(lane < KEEP, turn(edge, -HALF * layer - OUT, 1), value)
                if k == n_lanes - 1:
                    value = jnp.where(
                        lane >= LANES - KEEP, turn(edge, -HALF * layer - SIDE - OUT, 1), value
                    )
                merged[kind, layer, at, lane_tile(k)] = value

    last_fields(
        range(PAD // SUB, n_tiles - PAD // SUB), [()], shifts, e, load_hx, load_hy, store
    )
    copy = pltpu.make_async_copy(merged, out_fields, sem)
    copy.start()

    span, reach = TS // PIX, RADIUS - 1
    pixel = {}
    for j in range(-reach, span + reach):
        value = g[pl.ds(PAD + PIX * j, SUB, stride=TS), :]
        value = value + g[pl.ds(PAD + PIX * j + 1, SUB, stride=TS), :]
        pixel[j] = value + turn(value, -1, 1)

    weights = cone_weights(RADIUS)
    spans = []
    for row in range(span):
        sums = [pixel[row]] + [pixel[row + s] + pixel[row - s] for s in range(1, reach + 1)]
        total = None
        for shift in range(reach + 1):
            mixed = None
            for s in range(reach + 1):
                weight = float(weights[reach + s, reach + shift])
                if weight > 0.0:
                    term = weight * sums[s]
                    mixed = term if mixed is None else mixed + term
            if shift:
                mixed = turn(mixed, -PIX * shift, 1) + turn(mixed, PIX * shift, 1)
            total = mixed if total is None else total + mixed
        spans.append(total)

    edge = jnp.concatenate(merge_spans(spans, lane), axis=0)
    slots[...] = slots_in[...] + dot(place[...], jnp.concatenate(split2(edge), axis=0))
    copy.wait()


def vmem():
    return pl.BlockSpec(memory_space=pltpu.VMEM)


def shape(*dims, dtype=F32):
    return jax.ShapeDtypeStruct(dims, dtype)


def call(kernel, outs, n_in, *, in_space=pltpu.VMEM, out_specs=None, scratch=(), flops=0, size=0):
    return pl.pallas_call(
        kernel,
        out_shape=outs,
        in_specs=[pl.BlockSpec(memory_space=in_space)] * n_in,
        out_specs=out_specs or tuple(vmem() for _ in outs),
        scratch_shapes=list(scratch),
        compiler_params=pltpu.CompilerParams(vmem_limit_bytes=40 * 1024 * 1024),
        cost_estimate=pl.CostEstimate(flops=flops, bytes_accessed=size, transcendentals=0),
    )


def on_device(adj_fields, inv_eps, fwd_diff, mon_x, mon_y, mon_amp, design_mask, tile_owner):
    rows, cols = adj_fields.shape[2], adj_fields.shape[3]
    assert cols == 2 * LANES and rows % TS == 0
    gx_count, gy_count = lax.axis_size("gx"), lax.axis_size("gy")
    owners = gx_count * gy_count
    tiles = (rows // TS) * (cols // TS)
    width = 2 * (TS // PIX) ** 2
    assert width == LANES
    capacity = max(8, 2 * tiles // owners)
    assert rows == TS * SUB and cols == 2 * TS * SUB
    ext_rows = rows + 2 * PAD
    n_lanes = cols // LANES
    cells = rows * cols
    blocks = (adj_fields, inv_eps, fwd_diff)


    strip = shape(16, SUB, cols)
    cross, near = call(
        rows_kernel, (strip, strip), 3, in_space=pltpu.HBM,
        scratch=(
            pltpu.VMEM((2, 4, 2, PAD, cols), F32),
            pltpu.VMEM((2, STEPS, 2, SUB, cols), F32),
            pltpu.SemaphoreType.DMA((6,)),
        ),
        size=2**20,
    )(*(pltpu.with_memory_space_constraint(block, pltpu.HBM) for block in blocks))

    def pairs(count, start):
        some = [(i, i + 1) for i in range(start, count - 1, 2)]
        return some + [(j, i) for i, j in some]

    cross = lax.ppermute(cross, "gx", pairs(gx_count, 1))
    near = lax.ppermute(near, "gx", pairs(gx_count, 0))

    packed = shape(ext_rows, LANES)
    channels = mon_x.shape[0]
    cross_cols, near_cols, base, src, src_edge, place, place_edge = call(
        lambda *refs: prep_kernel(capacity, *refs),
        (
            packed,
            packed,
            shape(4 + STEPS, ext_rows, LANES),
            shape(STEPS, 2, ext_rows, cols),
            shape(STEPS, ext_rows, LANES),
            shape(owners * capacity, tiles, dtype=BF16),
            shape(owners * capacity, 4 * SUB, dtype=BF16),
        ),
        8,
        flops=16 * ext_rows * (cols + LANES) * 3 * channels,
        size=64 * cells,
    )(
        *blocks,
        mon_x.reshape(1, channels),
        mon_y.reshape(1, channels),
        mon_amp,
        design_mask.reshape(1, tiles),
        tile_owner.reshape(1, tiles),
    )
    cross_cols, near_cols = call(
        corners_kernel, (packed, packed), 4, flops=cells, size=8 * ext_rows * LANES
    )(cross_cols, near_cols, cross, near)
    cross_cols = lax.ppermute(cross_cols, "gy", pairs(gy_count, 1))
    near_cols = lax.ppermute(near_cols, "gy", pairs(gy_count, 0))

    plane = (2, n_lanes, ext_rows, LANES)
    last, slots, base = call(
        inner_kernel,
        (
            shape(3, 2, n_lanes, rows, LANES),
            shape(owners * capacity, width),
            shape(4 + STEPS, ext_rows, LANES),
        ),
        9,
        scratch=(
            pltpu.VMEM((1 + STEPS,) + plane, F32),
            pltpu.VMEM(plane, F32),
            pltpu.VMEM(plane, F32),
            pltpu.VMEM(plane, F32),
            pltpu.VMEM((2, ext_rows // PIX, LANES), F32),
        ),
        flops=200 * cells,
        size=96 * cells,
    )(*blocks, cross, near, src, pool_matrices(), base, place)

    plane = (ext_rows, LANES)
    fields, outgoing = call(
        edge_kernel,
        (shape(3, 2, rows, cols), shape(owners * capacity, width)),
        7,
        out_specs=(pl.BlockSpec(memory_space=pl.ANY), vmem()),
        scratch=(
            pltpu.VMEM((1 + STEPS,) + plane, F32),
            pltpu.VMEM((2,) + plane, F32),
            pltpu.VMEM(plane, F32),
            pltpu.VMEM(plane, F32),
            pltpu.VMEM((STEPS,) + plane, F32),
            pltpu.VMEM(plane, F32),
            pltpu.VMEM((3, 2, rows, cols), F32),
            pltpu.SemaphoreType.DMA,
        ),
        flops=50 * cells,
        size=16 * cells,
    )(last, slots, base, cross_cols, near_cols, src_edge, place_edge)

    outgoing = outgoing.reshape(owners, capacity, width)
    incoming = lax.all_to_all(outgoing, ("gx", "gy"), split_axis=0, concat_axis=0, tiled=True)
    return fields, incoming[None]


def solution(mesh):
    placed = (
        P(None, None, ("parts", "gx"), "gy"),
        P(None, ("parts", "gx"), "gy"),
        P(None, None, ("parts", "gx"), "gy"),
        P("parts"),
        P("parts"),
        P(None, "parts"),
        P(("parts", "gx"), "gy", None),
        P(("parts", "gx"), "gy", None, None),
    )
    return jax.shard_map(
        on_device,
        mesh=mesh,
        in_specs=placed,
        out_specs=(
            P(None, None, ("parts", "gx"), "gy"),
            P(("parts", "gx", "gy"), None, None, None),
        ),
        check_vma=False,
    )
```

```python
import jax
import jax.numpy as jnp
import ml_dtypes
import numpy as np
from jax import lax
from jax.experimental import pallas as pl
from jax.experimental.pallas import tpu as pltpu
from jax.sharding import PartitionSpec as P

STEPS = 4
PIX = 2
TS = 16
RADIUS = 4
COURANT = 0.6
COUPLING = 0.25

LANES = 128
SUB = 8
FAR = STEPS + PIX * (RADIUS - 1)
NEAR = PIX * (RADIUS - 1)
LEFT_OVER = FAR - SUB
PAD = 2 * SUB
HALF = LANES // 2
SIDE = HALF // 2
OUT = SIDE // 2
KEEP = 8
F32 = jnp.float32
BF16 = jnp.bfloat16
WIDTHS = (FAR,) * 4 + (NEAR,) * STEPS
FIRST = tuple(sum(WIDTHS[:k]) for k in range(len(WIDTHS)))
assert sum(WIDTHS) <= HALF and FAR <= OUT and STEPS + KEEP <= OUT


def cone_weights(radius):
    reach_cells = radius - 1
    offsets = np.arange(-reach_cells, reach_cells + 1)
    distance = np.sqrt(offsets[:, None] * offsets[:, None] + offsets[None, :] * offsets[None, :])
    weights = np.maximum(radius - distance, 0.0)
    return weights / weights.sum()


def pool_matrices():
    inner = np.zeros((2, LANES, LANES), np.float32)
    for j in range(KEEP, 2 * LANES - KEEP):
        inner[j // LANES, j % LANES, j // PIX] = 1.0
    return inner.astype(ml_dtypes.bfloat16)


def split2(value):
    high = value.astype(BF16)
    return high, (value - high.astype(F32)).astype(BF16)


def split3(value):
    high = value.astype(BF16)
    rest = value - high.astype(F32)
    mid = rest.astype(BF16)
    return high, mid, (rest - mid.astype(F32)).astype(BF16)


def dot(a, b):
    return jnp.dot(a, b, preferred_element_type=F32)


def turn(value, shift, axis):
    size = value.shape[axis]
    return pltpu.roll(value, shift % size, axis) if shift % size else value


def lanes():
    return lax.broadcasted_iota(jnp.int32, (SUB, LANES), 1)


def subs():
    return lax.broadcasted_iota(jnp.int32, (SUB, LANES), 0)


def lane_tile(k):
    return pl.ds(k * LANES, LANES)


def is_odd(axis):
    return ((subs() * 0 + lax.axis_index(axis)) & 1) == 1


def rows_kernel(fields, eps, fwd, cross, near, hold, hold_fwd, sems):
    rows, cols = fields.shape[2], fields.shape[3]
    copies = []
    for n, at in enumerate((0, rows - PAD)):
        at_fwd = 0 if n == 0 else rows - SUB
        pairs = (
            (fields.at[:, :, pl.ds(at, PAD), :], hold.at[n, pl.ds(0, 3)]),
            (eps.at[:, pl.ds(at, PAD), :], hold.at[n, 3]),
            (fwd.at[:, :, pl.ds(at_fwd, SUB), :], hold_fwd.at[n]),
        )
        for m, (src, dst) in enumerate(pairs):
            copies.append(pltpu.make_async_copy(src, dst, sems.at[3 * n + m]))
    for copy in copies:
        copy.start()
    for copy in copies:
        copy.wait()
    odd, sub = is_odd("gx"), subs()
    for kind in range(4):
        for layer in range(2):
            plane = 2 * kind + layer
            for k in range(cols // LANES):
                at = lane_tile(k)
                low = hold[0, kind, layer, pl.ds(0, SUB), at]
                high = hold[1, kind, layer, pl.ds(SUB, SUB), at]
                cross[plane, :, at] = jnp.where(odd, high, low)
                near[plane, :, at] = jnp.where(odd, low, high)
                rest_low = turn(hold[0, kind, layer, pl.ds(SUB, SUB), at], -LEFT_OVER, 0)
                rest_high = turn(hold[1, kind, layer, pl.ds(0, SUB), at], LEFT_OVER, 0)
                low = jnp.where(sub >= NEAR, rest_low, hold_fwd[0, kind, layer, :, at])
                high = jnp.where(sub < SUB - NEAR, rest_high, hold_fwd[1, kind, layer, :, at])
                cross[8 + plane, :, at] = jnp.where(odd, high, low)
                near[8 + plane, :, at] = jnp.where(odd, low, high)


def halo_tile(cross, near, odd, tile, kind, layer, at):
    is_above = tile < 2
    outer = tile in (0, 3)
    if outer and kind >= 4:
        return None
    plane = 2 * kind + layer + (8 if outer else 0)
    a, b = near[plane, :, at], cross[plane, :, at]
    value = jnp.where(odd, a, b) if is_above else jnp.where(odd, b, a)
    if outer:
        value = turn(value, -LEFT_OVER if is_above else LEFT_OVER, 0)
    return value


def core_tile(fields, eps, fwd, at, kind, layer, cols):
    if kind < 3:
        return fields[kind, layer, at, cols]
    if kind == 3:
        return eps[layer, at, cols]
    return fwd[kind - 4, layer, at, cols]


def pack_tile(load, lane, right):
    total = jnp.zeros((SUB, LANES), F32)
    for kind, width in enumerate(WIDTHS):
        for layer in range(2):
            value = load(kind, layer)
            if value is None:
                continue
            first = FIRST[kind] + HALF * layer
            value = turn(value, first + width if right else first, 1)
            total = jnp.where((lane >= first) & (lane < first + width), value, total)
    return total


def edge_tile(load, kind, lane, n_lanes):
    spot = lane & (HALF - 1)
    total = None
    for layer in range(2):
        low = turn(load(kind, layer, 0), HALF * layer + OUT, 1)
        high = turn(load(kind, layer, n_lanes - 1), HALF * layer + SIDE + OUT, 1)
        value = jnp.where(spot < SIDE, low, high)
        total = value if total is None else jnp.where(lane < HALF, total, value)
    return total


def cols_kernel(fields, eps, fwd, cross, near, base):
    rows, cols = fields.shape[2], fields.shape[3]
    n_lanes = cols // LANES
    lane, odd = lanes(), is_odd("gy")

    def tile(t, carry):
        at = pl.ds(pl.multiple_of(t * SUB, SUB), SUB)
        out_at = pl.ds(pl.multiple_of(t * SUB + PAD, SUB), SUB)

        def load(kind, layer, k):
            return core_tile(fields, eps, fwd, at, kind, layer, lane_tile(k))

        left = pack_tile(lambda kind, layer: load(kind, layer, 0), lane, False)
        right = pack_tile(lambda kind, layer: load(kind, layer, n_lanes - 1), lane, True)
        cross[out_at, :] = jnp.where(odd, right, left)
        near[out_at, :] = jnp.where(odd, left, right)
        for kind in range(4 + STEPS):
            base[kind, out_at, :] = edge_tile(load, kind, lane, n_lanes)
        return carry

    lax.fori_loop(0, rows // SUB, tile, 0, unroll=4)
    zero = jnp.zeros((PAD, LANES), F32)
    for out in (cross, near):
        out[pl.ds(0, PAD), :] = zero
        out[pl.ds(PAD + rows, PAD), :] = zero


def corners_kernel(cross_in, near_in, cross_rows, near_rows, cross, near):
    rows, cols = cross.shape[0] - 2 * PAD, cross_rows.shape[2]
    lane, odd, odd_col = lanes(), is_odd("gx"), is_odd("gy")
    core = pl.ds(PAD, rows)
    cross[core, :] = cross_in[core, :]
    near[core, :] = near_in[core, :]
    for tile in range(4):
        at = pl.ds(tile * SUB if tile < 2 else PAD + rows + (tile - 2) * SUB, SUB)
        left, right = (
            pack_tile(
                lambda kind, layer: halo_tile(
                    cross_rows, near_rows, odd, tile, kind, layer, pl.ds(lo, LANES)
                ),
                lane, is_right,
            )
            for lo, is_right in ((0, False), (cols - LANES, True))
        )
        cross[at, :] = jnp.where(odd_col, right, left)
        near[at, :] = jnp.where(odd_col, left, right)


def prep_kernel(
    capacity, fields, eps, fwd, mon_x, mon_y, amp, mask, owner, cross, near, base, src, src_edge, place, place_edge
):
    cols_kernel(fields, eps, fwd, cross, near, base)
    side_kernel(capacity, fields.shape[2], mon_x, mon_y, amp, mask, owner, src, src_edge, place, place_edge)


def side_kernel(capacity, rows, mon_x, mon_y, amp, mask, owner, src, src_edge, place, place_edge):
    _, _, ext_rows, cols = src.shape
    channels = mon_x.shape[1]
    row = mon_x[...] - lax.axis_index("gx") * rows + PAD
    col = mon_y[...] - lax.axis_index("gy") * cols
    in_left = (col >= -OUT) & (col < OUT)
    in_right = (col >= cols - OUT) & (col < cols + OUT)
    edge = jnp.where(in_left, col + OUT, jnp.where(in_right, col - cols + OUT + SIDE, -LANES))
    layer = lax.broadcasted_iota(jnp.int32, (1, channels), 1) & 1
    edge = edge + HALF * layer
    inside = jnp.where((col >= 0) & (col < cols), col, -1)
    one_y = lax.broadcasted_iota(jnp.int32, (cols, channels), 0) == inside
    one_e = lax.broadcasted_iota(jnp.int32, (LANES, channels), 0) == edge
    one_y = jnp.where(one_y, 1.0, 0.0).astype(BF16)
    one_e = jnp.where(one_e, 1.0, 0.0).astype(BF16)
    one_y = jnp.concatenate([one_y] * 3, axis=1)
    one_e = jnp.concatenate([one_e] * 3, axis=1)
    one_x = lax.broadcasted_iota(jnp.int32, (ext_rows, channels), 0) == row
    one_x = jnp.where(one_x, 1.0, 0.0).astype(F32)
    nt = (((1,), (1,)), ((), ()))
    for step in range(STEPS):
        parts = [part.astype(F32) for part in split3(amp[pl.ds(step, 1), :])]
        lhs = jnp.concatenate([one_x * part for part in parts], axis=1)
        src_edge[step] = lax.dot_general(lhs.astype(BF16), one_e, nt, preferred_element_type=F32)
        layer_wide = jnp.concatenate([layer] * 3, axis=1)
        for which in range(2):
            some = jnp.where(layer_wide == which, lhs, 0.0).astype(BF16)
            src[step, which] = lax.dot_general(some, one_y, nt, preferred_element_type=F32)
    tiles = owner.shape[1]
    own = owner[...].astype(F32)
    own_wide = jnp.broadcast_to(own, (tiles, tiles))
    earlier = lax.broadcasted_iota(jnp.int32, (tiles, tiles), 0) < lax.broadcasted_iota(
        jnp.int32, (tiles, tiles), 1
    )
    same = (own_wide.T == own_wide) & earlier
    slot = jnp.sum(jnp.where(same, 1.0, 0.0), axis=0, keepdims=True)
    dest = owner[...] * capacity + slot.astype(jnp.int32)
    dest = jnp.where(mask[...] != 0, dest, -1)
    hit = lax.broadcasted_iota(jnp.int32, place.shape, 0) == dest
    hit = jnp.where(hit, 1.0, 0.0).astype(BF16)
    place[...] = hit
    tile_cols = cols // TS
    column = lax.broadcasted_iota(jnp.int32, (tiles, 4 * SUB), 1)
    wanted = (column % SUB) * tile_cols + ((column // SUB) & 1) * (tile_cols - 1)
    picked = lax.broadcasted_iota(jnp.int32, (tiles, 4 * SUB), 0) == wanted
    place_edge[...] = dot(hit, jnp.where(picked, 1.0, 0.0).astype(BF16)).astype(BF16)


class Shifts:
    def __init__(self, next_col, prev_col):
        self.next_col, self.prev_col = next_col, prev_col
        self.bottom, self.top = subs() == SUB - 1, subs() == 0

    def up(self, tile):
        return {key: turn(value, -1, 0) for key, value in tile.items()}

    def down(self, tile):
        return {key: turn(value, 1, 0) for key, value in tile.items()}

    def below(self, up_here, up_next):
        return {key: jnp.where(self.bottom, up_next[key], up_here[key]) for key in up_here}

    def above(self, down_here, down_before):
        return {key: jnp.where(self.top, down_before[key], down_here[key]) for key in down_here}


def tile_at(t):
    return (pl.ds(t * SUB, SUB), slice(None))


def first_curl(n_tiles, shifts, load_hx, load_hy, curl):
    before = None
    for t in range(n_tiles):
        hx, hy = load_hx(t), load_hy(t)
        down = shifts.down(hy)
        over = shifts.above(down, before if t else down)
        left = shifts.prev_col(hx)
        for key in hx:
            curl[key + tile_at(t)] = (hy[key] - over[key]) - (hx[key] - left[key])
        before = down


def steps(n_tiles, keys, shifts, e, curl, eps_of, src_of, other):
    no_above = shifts.top & ((lax.axis_index("gx") + subs() * 0) == 0)
    for step in range(STEPS):
        low, high = (0, n_tiles) if step == 0 else (1, n_tiles - 1)

        def load(t):
            return {key: e[(step,) + key + tile_at(t)] for key in keys}

        here = load(low)
        up = shifts.up(here)
        down_before = shifts.down(load(max(low - 1, 0)))
        for t in range(low, high):
            after = load(min(t + 1, n_tiles - 1))
            up_next, down = shifts.up(after), shifts.down(here)
            below, above = shifts.below(up, up_next), shifts.above(down, down_before)
            right, left = shifts.next_col(here), shifts.prev_col(here)
            for key in keys:
                center, over = here[key], above[key]
                if t == PAD // SUB:
                    over = jnp.where(no_above, center, over)
                ring = (below[key] + over) + (right[key] + left[key]) - 4.0 * center
                change = curl[key + tile_at(t)] - COURANT * ring
                if step < STEPS - 1:
                    curl[key + tile_at(t)] = change
                change = change + COUPLING * (other(here, key) - center)
                e[(step + 1,) + key + tile_at(t)] = (
                    center - eps_of(key, t) * change + src_of(step, key, t)
                )
            here, up, down_before = after, up_next, down


def gradient(keys, t, e, change_of):
    result = {}
    for key in keys:
        total = None
        for step in range(STEPS):
            term = e[(step + 1,) + key + tile_at(t)] * change_of(step, key, t)
            total = term if total is None else total + term
        result[key] = -total
    return result


def last_fields(tiles, keys, shifts, e, load_hx, load_hy, store):
    def total(t):
        result = {}
        for key in keys:
            parts = [e[(step,) + key + tile_at(t)] for step in range(STEPS)]
            result[key] = (parts[0] + parts[1]) + (parts[2] + parts[3])
        return result

    here = total(tiles[0])
    up = shifts.up(here)
    for t in tiles:
        after = total(t + 1)
        up_next = shifts.up(after)
        below, right = shifts.below(up, up_next), shifts.next_col(here)
        hx, hy = load_hx(t), load_hy(t)
        for key in keys:
            store(0, key, t, e[(STEPS,) + key + tile_at(t)])
            store(1, key, t, hx[key] + COURANT * (right[key] - here[key]))
            store(2, key, t, hy[key] - COURANT * (below[key] - here[key]))
        here, up = after, up_next


def row_pairs(ref, lead, count):
    even = ref[lead + (pl.ds(0, count, stride=PIX), slice(None))]
    return even + ref[lead + (pl.ds(1, count, stride=PIX), slice(None))]


def inner_kernel(
    fields, eps, fwd, cross, near, src, mats, base_in, place, last, slots, base, e, curl, eps_c, g, pooled
):
    rows, cols = fields.shape[2], fields.shape[3]
    n_tiles = (rows + 2 * PAD) // SUB
    n_lanes = cols // LANES
    lane, odd = lanes(), is_odd("gx")
    halo_of = {0: 0, 1: 1, n_tiles - 2: 2, n_tiles - 1: 3}
    keys = [(layer, k) for layer in range(2) for k in range(n_lanes)]

    def load(kind, layer, t, k):
        if t in halo_of:
            return halo_tile(cross, near, odd, halo_of[t], kind, layer, lane_tile(k))
        return core_tile(fields, eps, fwd, pl.ds(t * SUB - PAD, SUB), kind, layer, lane_tile(k))

    def load_all(kind, t):
        return {key: load(kind, key[0], t, key[1]) for key in keys}

    at_end, at_start = lane == LANES - 1, lane == 0

    def next_col(values):
        moved = {key: turn(value, -1, 1) for key, value in values.items()}
        return {
            (l, k): jnp.where(at_end, moved[l, (k + 1) % n_lanes], moved[l, k]) for l, k in keys
        }

    def prev_col(values):
        moved = {key: turn(value, 1, 1) for key, value in values.items()}
        return {
            (l, k): jnp.where(at_start, moved[l, (k - 1) % n_lanes], moved[l, k]) for l, k in keys
        }

    shifts = Shifts(next_col, prev_col)
    for t in range(n_tiles):
        for key in keys:
            e[(0,) + key + tile_at(t)] = load(0, key[0], t, key[1])
            eps_c[key + tile_at(t)] = COURANT * load(3, key[0], t, key[1])
    first_curl(n_tiles, shifts, lambda t: load_all(1, t), lambda t: load_all(2, t), curl)
    steps(
        n_tiles, keys, shifts, e, curl,
        lambda key, t: eps_c[key + tile_at(t)],
        lambda step, key, t: src[step, key[0], pl.ds(t * SUB, SUB), lane_tile(key[1])],
        lambda values, key: values[1 - key[0], key[1]],
    )
    for t in range(1, n_tiles - 1):
        values = gradient(keys, t, e, lambda step, key, t: load(4 + step, key[0], t, key[1]))
        for key in keys:
            g[key + tile_at(t)] = values[key]

    def store(kind, key, t, value):
        last[(kind,) + key + (pl.ds(t * SUB - PAD, SUB), slice(None))] = value

    last_fields(
        range(PAD // SUB, n_tiles - PAD // SUB), keys, shifts, e,
        lambda t: load_all(1, t), lambda t: load_all(2, t), store,
    )
    for layer in range(2):
        total = None
        for k in range(n_lanes):
            for part in split2(row_pairs(g, (layer, k), n_tiles * SUB // PIX)):
                term = dot(part, mats[k])
                total = term if total is None else total + term
        pooled[layer] = total

    vals = by_tile([cone_filter(pooled.at[layer], rows // PIX, PAD // PIX) for layer in range(2)])
    high, low = split2(vals)
    slots[...] = dot(place[...], high) + dot(place[...], low)

    for t in range(n_tiles):
        for kind in range(4 + STEPS):
            at = pl.ds(t * SUB, SUB)
            if t not in halo_of:
                base[kind, at, :] = base_in[kind, at, :]
            elif kind < 4 or t not in (0, n_tiles - 1):
                base[kind, at, :] = edge_tile(
                    lambda kind, layer, k: load(kind, layer, t, k), kind, lane, n_lanes
                )


def cone_filter(pooled, out_pix, first):
    weights = cone_weights(RADIUS)
    reach = RADIUS - 1
    lane = lax.broadcasted_iota(jnp.int32, (out_pix, LANES), 1)
    at = [pooled[pl.ds(first + s, out_pix), :] for s in range(-reach, reach + 1)]
    sums = [at[reach]] + [at[reach + s] + at[reach - s] for s in range(1, reach + 1)]
    total = None
    for shift in range(reach + 1):
        mixed = None
        for s in range(reach + 1):
            weight = float(weights[reach + s, reach + shift])
            if weight > 0.0:
                term = weight * sums[s]
                mixed = term if mixed is None else mixed + term
        if shift == 0:
            total = mixed
        else:
            total = total + turn(jnp.where(lane < shift, 0.0, mixed), -shift, 1)
            total = total + turn(jnp.where(lane >= LANES - shift, 0.0, mixed), shift, 1)
    return total


def by_tile(blocks):
    span = TS // PIX
    tile_rows = blocks[0].shape[0] // span
    x = jnp.stack([block.reshape(tile_rows, span, LANES) for block in blocks], axis=1)
    x = x.reshape(tile_rows * 2, span, LANES)
    group = lax.broadcasted_iota(jnp.int32, x.shape, 2) // span
    row = lax.broadcasted_iota(jnp.int32, x.shape, 1)
    for bit in (1, 2, 4):
        row_on, lane_on = (row & bit) != 0, (group & bit) != 0
        ahead = turn(turn(x, -bit, 1), bit * span, 2)
        behind = turn(turn(x, bit, 1), -bit * span, 2)
        x = jnp.where(row_on == lane_on, x, jnp.where(lane_on, ahead, behind))
    x = x.reshape(tile_rows, 2, span, LANES)
    even, odd = x[:, 0], x[:, 1]
    upper = lax.broadcasted_iota(jnp.int32, even.shape, 2) >= HALF
    new_even = jnp.where(upper, turn(odd, HALF, 2), even)
    new_odd = jnp.where(upper, odd, turn(even, HALF, 2))
    return jnp.stack([new_even, new_odd], axis=1).reshape(tile_rows * 2 * span, LANES)


def merge_spans(spans, lane):
    even = (lane & 1) == 0
    window = ((lane - OUT) & (HALF - 1)) < SIDE
    merged = []
    for e in (0, 4):
        low = jnp.where(even, spans[e], turn(spans[e + 1], 1, 1))
        high = jnp.where(even, turn(spans[e + 2], SIDE, 1), turn(spans[e + 3], SIDE + 1, 1))
        merged.append(jnp.where(window, low, high))
    span = TS // PIX
    row, pixel = lane // span % span, lane % span
    start = (lane & HALF) + OUT + PIX * pixel + (row & 1) + SIDE * ((row >> 1) & 1)
    result = []
    for side in range(2):
        index = (start + OUT * side) & (LANES - 1)
        low, high = (jnp.take_along_axis(value, index, axis=1) for value in merged)
        result.append(jnp.where(row < span // 2, low, high))
    return result


def edge_kernel(
    base, cross, near, src, out, g_out, e, first, curl, eps_c, d, g, result
):
    ext_rows = base.shape[1]
    rows = ext_rows - 2 * PAD
    n_tiles = ext_rows // SUB
    lane, odd = lanes(), is_odd("gy")
    spot = lane & (HALF - 1)
    is_left, is_right = spot < OUT, spot >= HALF - OUT

    for t in range(n_tiles):
        at = pl.ds(t * SUB, SUB)
        far, close = cross[at, :], near[at, :]
        high, low = jnp.where(odd, close, far), jnp.where(odd, far, close)
        for kind, width in enumerate(WIDTHS):
            if kind >= 4 and t in (0, n_tiles - 1):
                continue
            value = jnp.where(is_left, turn(high, OUT - width - FIRST[kind], 1), base[kind, at, :])
            value = jnp.where(is_right, turn(low, HALF - OUT - FIRST[kind], 1), value)
            if kind == 0:
                e[0, at, :] = value
            elif kind < 3:
                first[kind - 1, at, :] = value
            elif kind == 3:
                eps_c[at, :] = COURANT * value
            else:
                d[kind - 4, at, :] = value

    no_left = (spot == OUT) & ((lax.axis_index("gy") + lane * 0) == 0)
    shifts = Shifts(
        lambda values: {(): turn(values[()], -1, 1)},
        lambda values: {(): turn(values[()], 1, 1)},
    )

    def load_hx(t):
        return {(): first[0, pl.ds(t * SUB, SUB), :]}

    def load_hy(t):
        return {(): first[1, pl.ds(t * SUB, SUB), :]}

    first_curl(n_tiles, shifts, load_hx, load_hy, curl)
    shifts.prev_col = lambda values: {(): jnp.where(no_left, values[()], turn(values[()], 1, 1))}
    steps(
        n_tiles, [()], shifts, e, curl,
        lambda key, t: eps_c[pl.ds(t * SUB, SUB), :],
        lambda step, key, t: src[step, pl.ds(t * SUB, SUB), :],
        lambda values, key: turn(values[()], HALF, 1),
    )
    inside = (spot >= OUT - NEAR) & (spot < OUT + KEEP)
    inside = inside | ((spot >= HALF - OUT - KEEP) & (spot < HALF - OUT + NEAR))
    for t in range(1, n_tiles - 1):
        value = gradient([()], t, e, lambda step, key, t: d[step, pl.ds(t * SUB, SUB), :])[()]
        g[pl.ds(t * SUB, SUB), :] = jnp.where(inside, value, 0.0)

    def store(kind, key, t, value):
        result[kind, pl.ds(t * SUB - PAD, SUB), :] = value

    last_fields(
        range(PAD // SUB, n_tiles - PAD // SUB), [()], shifts, e, load_hx, load_hy, store
    )
    g_out[...] = g[...]
    out[...] = result[...]


def tiles_kernel(g, slots_in, place, slots):
    lane = lanes()
    span, reach = TS // PIX, RADIUS - 1
    pixel = {}
    for j in range(-reach, span + reach):
        value = g[pl.ds(PAD + PIX * j, SUB, stride=TS), :]
        value = value + g[pl.ds(PAD + PIX * j + 1, SUB, stride=TS), :]
        pixel[j] = value + turn(value, -1, 1)

    weights = cone_weights(RADIUS)
    spans = []
    for row in range(span):
        sums = [pixel[row]] + [pixel[row + s] + pixel[row - s] for s in range(1, reach + 1)]
        total = None
        for shift in range(reach + 1):
            mixed = None
            for s in range(reach + 1):
                weight = float(weights[reach + s, reach + shift])
                if weight > 0.0:
                    term = weight * sums[s]
                    mixed = term if mixed is None else mixed + term
            if shift:
                mixed = turn(mixed, -PIX * shift, 1) + turn(mixed, PIX * shift, 1)
            total = mixed if total is None else total + mixed
        spans.append(total)

    edge = jnp.concatenate(merge_spans(spans, lane), axis=0)
    slots[...] = slots_in[...] + dot(place[...], jnp.concatenate(split2(edge), axis=0))


def merge_kernel(last, edge_last, out_fields, merged, sem):
    rows, cols = merged.shape[2], merged.shape[3]
    n_lanes = cols // LANES
    lane = lanes()
    for t in range(rows // SUB):
        at = pl.ds(t * SUB, SUB)
        for kind in range(3):
            edge = edge_last[kind, at, :]
            for layer in range(2):
                for k in range(n_lanes):
                    value = last[kind, layer, k, at, :]
                    if k == 0:
                        value = jnp.where(lane < KEEP, turn(edge, -HALF * layer - OUT, 1), value)
                    if k == n_lanes - 1:
                        value = jnp.where(
                            lane >= LANES - KEEP, turn(edge, -HALF * layer - SIDE - OUT, 1), value
                        )
                    merged[kind, layer, at, lane_tile(k)] = value
    copy = pltpu.make_async_copy(merged, out_fields, sem)
    copy.start()
    copy.wait()


def vmem():
    return pl.BlockSpec(memory_space=pltpu.VMEM)


def shape(*dims, dtype=F32):
    return jax.ShapeDtypeStruct(dims, dtype)


def call(kernel, outs, n_in, *, in_space=pltpu.VMEM, out_specs=None, scratch=(), flops=0, size=0):
    return pl.pallas_call(
        kernel,
        out_shape=outs,
        in_specs=[pl.BlockSpec(memory_space=in_space)] * n_in,
        out_specs=out_specs or tuple(vmem() for _ in outs),
        scratch_shapes=list(scratch),
        compiler_params=pltpu.CompilerParams(vmem_limit_bytes=40 * 1024 * 1024),
        cost_estimate=pl.CostEstimate(flops=flops, bytes_accessed=size, transcendentals=0),
    )


def on_device(adj_fields, inv_eps, fwd_diff, mon_x, mon_y, mon_amp, design_mask, tile_owner):
    rows, cols = adj_fields.shape[2], adj_fields.shape[3]
    assert cols == 2 * LANES and rows % TS == 0
    gx_count, gy_count = lax.axis_size("gx"), lax.axis_size("gy")
    owners = gx_count * gy_count
    tiles = (rows // TS) * (cols // TS)
    width = 2 * (TS // PIX) ** 2
    assert width == LANES
    capacity = max(8, 2 * tiles // owners)
    assert rows == TS * SUB and cols == 2 * TS * SUB
    ext_rows = rows + 2 * PAD
    n_lanes = cols // LANES
    cells = rows * cols
    blocks = (adj_fields, inv_eps, fwd_diff)


    strip = shape(16, SUB, cols)
    cross, near = call(
        rows_kernel, (strip, strip), 3, in_space=pltpu.HBM,
        scratch=(
            pltpu.VMEM((2, 4, 2, PAD, cols), F32),
            pltpu.VMEM((2, STEPS, 2, SUB, cols), F32),
            pltpu.SemaphoreType.DMA((6,)),
        ),
        size=2**20,
    )(*(pltpu.with_memory_space_constraint(block, pltpu.HBM) for block in blocks))

    def pairs(count, start):
        some = [(i, i + 1) for i in range(start, count - 1, 2)]
        return some + [(j, i) for i, j in some]

    cross = lax.ppermute(cross, "gx", pairs(gx_count, 1))
    near = lax.ppermute(near, "gx", pairs(gx_count, 0))

    packed = shape(ext_rows, LANES)
    channels = mon_x.shape[0]
    cross_cols, near_cols, base, src, src_edge, place, place_edge = call(
        lambda *refs: prep_kernel(capacity, *refs),
        (
            packed,
            packed,
            shape(4 + STEPS, ext_rows, LANES),
            shape(STEPS, 2, ext_rows, cols),
            shape(STEPS, ext_rows, LANES),
            shape(owners * capacity, tiles, dtype=BF16),
            shape(owners * capacity, 4 * SUB, dtype=BF16),
        ),
        8,
        flops=16 * ext_rows * (cols + LANES) * 3 * channels,
        size=64 * cells,
    )(
        *blocks,
        mon_x.reshape(1, channels),
        mon_y.reshape(1, channels),
        mon_amp,
        design_mask.reshape(1, tiles),
        tile_owner.reshape(1, tiles),
    )
    cross_cols, near_cols = call(
        corners_kernel, (packed, packed), 4, flops=cells, size=8 * ext_rows * LANES
    )(cross_cols, near_cols, cross, near)
    cross_cols = lax.ppermute(cross_cols, "gy", pairs(gy_count, 1))
    near_cols = lax.ppermute(near_cols, "gy", pairs(gy_count, 0))

    plane = (2, n_lanes, ext_rows, LANES)
    last, slots, base = call(
        inner_kernel,
        (
            shape(3, 2, n_lanes, rows, LANES),
            shape(owners * capacity, width),
            shape(4 + STEPS, ext_rows, LANES),
        ),
        9,
        scratch=(
            pltpu.VMEM((1 + STEPS,) + plane, F32),
            pltpu.VMEM(plane, F32),
            pltpu.VMEM(plane, F32),
            pltpu.VMEM(plane, F32),
            pltpu.VMEM((2, ext_rows // PIX, LANES), F32),
        ),
        flops=200 * cells,
        size=96 * cells,
    )(*blocks, cross, near, src, pool_matrices(), base, place)

    plane = (ext_rows, LANES)
    edge_last, edge_g = call(
        edge_kernel,
        (shape(3, rows, LANES), shape(*plane)),
        4,
        scratch=(
            pltpu.VMEM((1 + STEPS,) + plane, F32),
            pltpu.VMEM((2,) + plane, F32),
            pltpu.VMEM(plane, F32),
            pltpu.VMEM(plane, F32),
            pltpu.VMEM((STEPS,) + plane, F32),
            pltpu.VMEM(plane, F32),
            pltpu.VMEM((3, rows, LANES), F32),
        ),
        flops=50 * cells,
        size=16 * cells,
    )(base, cross_cols, near_cols, src_edge)
    (outgoing,) = call(
        tiles_kernel, (shape(owners * capacity, width),), 3, flops=20 * cells, size=4 * cells
    )(edge_g, slots, place_edge)
    (fields,) = call(
        merge_kernel,
        (shape(3, 2, rows, cols),),
        2,
        out_specs=(pl.BlockSpec(memory_space=pl.ANY),),
        scratch=(pltpu.VMEM((3, 2, rows, cols), F32), pltpu.SemaphoreType.DMA),
        flops=20 * cells,
        size=48 * cells,
    )(last, edge_last)

    outgoing = outgoing.reshape(owners, capacity, width)
    incoming = lax.all_to_all(outgoing, ("gx", "gy"), split_axis=0, concat_axis=0, tiled=True)
    return fields, incoming[None]


def solution(mesh):
    placed = (
        P(None, None, ("parts", "gx"), "gy"),
        P(None, ("parts", "gx"), "gy"),
        P(None, None, ("parts", "gx"), "gy"),
        P("parts"),
        P("parts"),
        P(None, "parts"),
        P(("parts", "gx"), "gy", None),
        P(("parts", "gx"), "gy", None, None),
    )
    return jax.shard_map(
        on_device,
        mesh=mesh,
        in_specs=placed,
        out_specs=(
            P(None, None, ("parts", "gx"), "gy"),
            P(("parts", "gx", "gy"), None, None, None),
        ),
        check_vma=False,
    )
```

```python
import jax
import jax.numpy as jnp
import ml_dtypes
import numpy as np
from jax import lax
from jax.experimental import pallas as pl
from jax.experimental.pallas import tpu as pltpu
from jax.sharding import PartitionSpec as P

STEPS = 4
PIX = 2
TS = 16
RADIUS = 4
COURANT = 0.6
COUPLING = 0.25

LANES = 128
SUB = 8
FAR = STEPS + PIX * (RADIUS - 1)
NEAR = PIX * (RADIUS - 1)
LEFT_OVER = FAR - SUB
PAD = 2 * SUB
HALF = LANES // 2
SIDE = HALF // 2
OUT = SIDE // 2
KEEP = 8
F32 = jnp.float32
BF16 = jnp.bfloat16
WIDTHS = (FAR,) * 4 + (NEAR,) * STEPS
FIRST = tuple(sum(WIDTHS[:k]) for k in range(len(WIDTHS)))
assert sum(WIDTHS) <= HALF and FAR <= OUT and STEPS + KEEP <= OUT


def cone_weights(radius):
    reach_cells = radius - 1
    offsets = np.arange(-reach_cells, reach_cells + 1)
    distance = np.sqrt(offsets[:, None] * offsets[:, None] + offsets[None, :] * offsets[None, :])
    weights = np.maximum(radius - distance, 0.0)
    return weights / weights.sum()


def pool_matrices():
    inner = np.zeros((2, LANES, LANES), np.float32)
    for j in range(KEEP, 2 * LANES - KEEP):
        inner[j // LANES, j % LANES, j // PIX] = 1.0
    return inner.astype(ml_dtypes.bfloat16)


def split2(value):
    high = value.astype(BF16)
    return high, (value - high.astype(F32)).astype(BF16)


def split3(value):
    high = value.astype(BF16)
    rest = value - high.astype(F32)
    mid = rest.astype(BF16)
    return high, mid, (rest - mid.astype(F32)).astype(BF16)


def dot(a, b):
    return jnp.dot(a, b, preferred_element_type=F32)


def turn(value, shift, axis):
    size = value.shape[axis]
    return pltpu.roll(value, shift % size, axis) if shift % size else value


def lanes():
    return lax.broadcasted_iota(jnp.int32, (SUB, LANES), 1)


def subs():
    return lax.broadcasted_iota(jnp.int32, (SUB, LANES), 0)


def lane_tile(k):
    return pl.ds(k * LANES, LANES)


def is_odd(axis):
    return ((subs() * 0 + lax.axis_index(axis)) & 1) == 1


def rows_kernel(fields, eps, fwd, cross, near, hold, hold_fwd, sems):
    rows, cols = fields.shape[2], fields.shape[3]
    copies = []
    for n, at in enumerate((0, rows - PAD)):
        at_fwd = 0 if n == 0 else rows - SUB
        pairs = (
            (fields.at[:, :, pl.ds(at, PAD), :], hold.at[n, pl.ds(0, 3)]),
            (eps.at[:, pl.ds(at, PAD), :], hold.at[n, 3]),
            (fwd.at[:, :, pl.ds(at_fwd, SUB), :], hold_fwd.at[n]),
        )
        for m, (src, dst) in enumerate(pairs):
            copies.append(pltpu.make_async_copy(src, dst, sems.at[3 * n + m]))
    for copy in copies:
        copy.start()
    for copy in copies:
        copy.wait()
    odd, sub = is_odd("gx"), subs()
    for kind in range(4):
        for layer in range(2):
            plane = 2 * kind + layer
            for k in range(cols // LANES):
                at = lane_tile(k)
                low = hold[0, kind, layer, pl.ds(0, SUB), at]
                high = hold[1, kind, layer, pl.ds(SUB, SUB), at]
                cross[plane, :, at] = jnp.where(odd, high, low)
                near[plane, :, at] = jnp.where(odd, low, high)
                rest_low = turn(hold[0, kind, layer, pl.ds(SUB, SUB), at], -LEFT_OVER, 0)
                rest_high = turn(hold[1, kind, layer, pl.ds(0, SUB), at], LEFT_OVER, 0)
                low = jnp.where(sub >= NEAR, rest_low, hold_fwd[0, kind, layer, :, at])
                high = jnp.where(sub < SUB - NEAR, rest_high, hold_fwd[1, kind, layer, :, at])
                cross[8 + plane, :, at] = jnp.where(odd, high, low)
                near[8 + plane, :, at] = jnp.where(odd, low, high)


def halo_tile(cross, near, odd, tile, kind, layer, at):
    is_above = tile < 2
    outer = tile in (0, 3)
    if outer and kind >= 4:
        return None
    plane = 2 * kind + layer + (8 if outer else 0)
    a, b = near[plane, :, at], cross[plane, :, at]
    value = jnp.where(odd, a, b) if is_above else jnp.where(odd, b, a)
    if outer:
        value = turn(value, -LEFT_OVER if is_above else LEFT_OVER, 0)
    return value


def core_tile(fields, eps, fwd, at, kind, layer, cols):
    if kind < 3:
        return fields[kind, layer, at, cols]
    if kind == 3:
        return eps[layer, at, cols]
    return fwd[kind - 4, layer, at, cols]


def pack_tile(load, lane, right):
    total = jnp.zeros((SUB, LANES), F32)
    for kind, width in enumerate(WIDTHS):
        for layer in range(2):
            value = load(kind, layer)
            if value is None:
                continue
            first = FIRST[kind] + HALF * layer
            value = turn(value, first + width if right else first, 1)
            total = jnp.where((lane >= first) & (lane < first + width), value, total)
    return total


def edge_tile(load, kind, lane, n_lanes):
    spot = lane & (HALF - 1)
    total = None
    for layer in range(2):
        low = turn(load(kind, layer, 0), HALF * layer + OUT, 1)
        high = turn(load(kind, layer, n_lanes - 1), HALF * layer + SIDE + OUT, 1)
        value = jnp.where(spot < SIDE, low, high)
        total = value if total is None else jnp.where(lane < HALF, total, value)
    return total


def cols_kernel(fields, eps, fwd, cross, near, base):
    rows, cols = fields.shape[2], fields.shape[3]
    n_lanes = cols // LANES
    lane, odd = lanes(), is_odd("gy")

    def tile(t, carry):
        at = pl.ds(pl.multiple_of(t * SUB, SUB), SUB)
        out_at = pl.ds(pl.multiple_of(t * SUB + PAD, SUB), SUB)

        def load(kind, layer, k):
            return core_tile(fields, eps, fwd, at, kind, layer, lane_tile(k))

        left = pack_tile(lambda kind, layer: load(kind, layer, 0), lane, False)
        right = pack_tile(lambda kind, layer: load(kind, layer, n_lanes - 1), lane, True)
        cross[out_at, :] = jnp.where(odd, right, left)
        near[out_at, :] = jnp.where(odd, left, right)
        for kind in range(4 + STEPS):
            base[kind, out_at, :] = edge_tile(load, kind, lane, n_lanes)
        return carry

    lax.fori_loop(0, rows // SUB, tile, 0, unroll=4)
    zero = jnp.zeros((PAD, LANES), F32)
    for out in (cross, near):
        out[pl.ds(0, PAD), :] = zero
        out[pl.ds(PAD + rows, PAD), :] = zero


def corners_kernel(cross_in, near_in, cross_rows, near_rows, cross, near):
    rows, cols = cross.shape[0] - 2 * PAD, cross_rows.shape[2]
    lane, odd, odd_col = lanes(), is_odd("gx"), is_odd("gy")
    core = pl.ds(PAD, rows)
    cross[core, :] = cross_in[core, :]
    near[core, :] = near_in[core, :]
    for tile in range(4):
        at = pl.ds(tile * SUB if tile < 2 else PAD + rows + (tile - 2) * SUB, SUB)
        left, right = (
            pack_tile(
                lambda kind, layer: halo_tile(
                    cross_rows, near_rows, odd, tile, kind, layer, pl.ds(lo, LANES)
                ),
                lane, is_right,
            )
            for lo, is_right in ((0, False), (cols - LANES, True))
        )
        cross[at, :] = jnp.where(odd_col, right, left)
        near[at, :] = jnp.where(odd_col, left, right)


def prep_kernel(
    capacity, fields, eps, fwd, mon_x, mon_y, amp, mask, owner, cross, near, base, src, src_edge, place, place_edge
):
    cols_kernel(fields, eps, fwd, cross, near, base)
    side_kernel(capacity, fields.shape[2], mon_x, mon_y, amp, mask, owner, src, src_edge, place, place_edge)


def side_kernel(capacity, rows, mon_x, mon_y, amp, mask, owner, src, src_edge, place, place_edge):
    _, _, ext_rows, cols = src.shape
    channels = mon_x.shape[1]
    row = mon_x[...] - lax.axis_index("gx") * rows + PAD
    col = mon_y[...] - lax.axis_index("gy") * cols
    in_left = (col >= -OUT) & (col < OUT)
    in_right = (col >= cols - OUT) & (col < cols + OUT)
    edge = jnp.where(in_left, col + OUT, jnp.where(in_right, col - cols + OUT + SIDE, -LANES))
    layer = lax.broadcasted_iota(jnp.int32, (1, channels), 1) & 1
    edge = edge + HALF * layer
    inside = jnp.where((col >= 0) & (col < cols), col, -1)
    one_y = lax.broadcasted_iota(jnp.int32, (cols, channels), 0) == inside
    one_e = lax.broadcasted_iota(jnp.int32, (LANES, channels), 0) == edge
    one_y = jnp.where(one_y, 1.0, 0.0).astype(BF16)
    one_e = jnp.where(one_e, 1.0, 0.0).astype(BF16)
    one_y = jnp.concatenate([one_y] * 3, axis=1)
    one_e = jnp.concatenate([one_e] * 3, axis=1)
    one_x = lax.broadcasted_iota(jnp.int32, (ext_rows, channels), 0) == row
    one_x = jnp.where(one_x, 1.0, 0.0).astype(F32)
    nt = (((1,), (1,)), ((), ()))
    for step in range(STEPS):
        parts = [part.astype(F32) for part in split3(amp[pl.ds(step, 1), :])]
        lhs = jnp.concatenate([one_x * part for part in parts], axis=1)
        src_edge[step] = lax.dot_general(lhs.astype(BF16), one_e, nt, preferred_element_type=F32)
        layer_wide = jnp.concatenate([layer] * 3, axis=1)
        for which in range(2):
            some = jnp.where(layer_wide == which, lhs, 0.0).astype(BF16)
            src[step, which] = lax.dot_general(some, one_y, nt, preferred_element_type=F32)
    tiles = owner.shape[1]
    own = owner[...].astype(F32)
    own_wide = jnp.broadcast_to(own, (tiles, tiles))
    earlier = lax.broadcasted_iota(jnp.int32, (tiles, tiles), 0) < lax.broadcasted_iota(
        jnp.int32, (tiles, tiles), 1
    )
    same = (own_wide.T == own_wide) & earlier
    slot = jnp.sum(jnp.where(same, 1.0, 0.0), axis=0, keepdims=True)
    dest = owner[...] * capacity + slot.astype(jnp.int32)
    dest = jnp.where(mask[...] != 0, dest, -1)
    hit = lax.broadcasted_iota(jnp.int32, place.shape, 0) == dest
    hit = jnp.where(hit, 1.0, 0.0).astype(BF16)
    place[...] = hit
    tile_cols = cols // TS
    column = lax.broadcasted_iota(jnp.int32, (tiles, 4 * SUB), 1)
    wanted = (column % SUB) * tile_cols + ((column // SUB) & 1) * (tile_cols - 1)
    picked = lax.broadcasted_iota(jnp.int32, (tiles, 4 * SUB), 0) == wanted
    place_edge[...] = dot(hit, jnp.where(picked, 1.0, 0.0).astype(BF16)).astype(BF16)


class Shifts:
    def __init__(self, next_col, prev_col):
        self.next_col, self.prev_col = next_col, prev_col
        self.bottom, self.top = subs() == SUB - 1, subs() == 0

    def up(self, tile):
        return {key: turn(value, -1, 0) for key, value in tile.items()}

    def down(self, tile):
        return {key: turn(value, 1, 0) for key, value in tile.items()}

    def below(self, up_here, up_next):
        return {key: jnp.where(self.bottom, up_next[key], up_here[key]) for key in up_here}

    def above(self, down_here, down_before):
        return {key: jnp.where(self.top, down_before[key], down_here[key]) for key in down_here}


def tile_at(t):
    return (pl.ds(t * SUB, SUB), slice(None))


def first_curl(n_tiles, shifts, load_hx, load_hy, curl):
    before = None
    for t in range(n_tiles):
        hx, hy = load_hx(t), load_hy(t)
        down = shifts.down(hy)
        over = shifts.above(down, before if t else down)
        left = shifts.prev_col(hx)
        for key in hx:
            curl[key + tile_at(t)] = (hy[key] - over[key]) - (hx[key] - left[key])
        before = down


def steps(n_tiles, keys, shifts, e, curl, eps_of, src_of, other):
    no_above = shifts.top & ((lax.axis_index("gx") + subs() * 0) == 0)
    for step in range(STEPS):
        low, high = (0, n_tiles) if step == 0 else (1, n_tiles - 1)

        def load(t):
            return {key: e[(step,) + key + tile_at(t)] for key in keys}

        here = load(low)
        up = shifts.up(here)
        down_before = shifts.down(load(max(low - 1, 0)))
        for t in range(low, high):
            after = load(min(t + 1, n_tiles - 1))
            up_next, down = shifts.up(after), shifts.down(here)
            below, above = shifts.below(up, up_next), shifts.above(down, down_before)
            right, left = shifts.next_col(here), shifts.prev_col(here)
            for key in keys:
                center, over = here[key], above[key]
                if t == PAD // SUB:
                    over = jnp.where(no_above, center, over)
                ring = (below[key] + over) + (right[key] + left[key]) - 4.0 * center
                change = curl[key + tile_at(t)] - COURANT * ring
                if step < STEPS - 1:
                    curl[key + tile_at(t)] = change
                change = change + COUPLING * (other(here, key) - center)
                e[(step + 1,) + key + tile_at(t)] = (
                    center - eps_of(key, t) * change + src_of(step, key, t)
                )
            here, up, down_before = after, up_next, down


def gradient(keys, t, e, change_of):
    result = {}
    for key in keys:
        total = None
        for step in range(STEPS):
            term = e[(step + 1,) + key + tile_at(t)] * change_of(step, key, t)
            total = term if total is None else total + term
        result[key] = -total
    return result


def last_fields(tiles, keys, shifts, e, load_hx, load_hy, store):
    def total(t):
        result = {}
        for key in keys:
            parts = [e[(step,) + key + tile_at(t)] for step in range(STEPS)]
            result[key] = (parts[0] + parts[1]) + (parts[2] + parts[3])
        return result

    here = total(tiles[0])
    up = shifts.up(here)
    for t in tiles:
        after = total(t + 1)
        up_next = shifts.up(after)
        below, right = shifts.below(up, up_next), shifts.next_col(here)
        hx, hy = load_hx(t), load_hy(t)
        for key in keys:
            store(0, key, t, e[(STEPS,) + key + tile_at(t)])
            store(1, key, t, hx[key] + COURANT * (right[key] - here[key]))
            store(2, key, t, hy[key] - COURANT * (below[key] - here[key]))
        here, up = after, up_next


def row_pairs(ref, lead, count):
    even = ref[lead + (pl.ds(0, count, stride=PIX), slice(None))]
    return even + ref[lead + (pl.ds(1, count, stride=PIX), slice(None))]


def inner_kernel(
    fields, eps, fwd, cross, near, src, mats, base_in, place, last, slots, base, e, curl, eps_c, g, pooled
):
    rows, cols = fields.shape[2], fields.shape[3]
    n_tiles = (rows + 2 * PAD) // SUB
    n_lanes = cols // LANES
    lane, odd = lanes(), is_odd("gx")
    halo_of = {0: 0, 1: 1, n_tiles - 2: 2, n_tiles - 1: 3}
    keys = [(layer, k) for layer in range(2) for k in range(n_lanes)]

    def load(kind, layer, t, k):
        if t in halo_of:
            return halo_tile(cross, near, odd, halo_of[t], kind, layer, lane_tile(k))
        return core_tile(fields, eps, fwd, pl.ds(t * SUB - PAD, SUB), kind, layer, lane_tile(k))

    def load_all(kind, t):
        return {key: load(kind, key[0], t, key[1]) for key in keys}

    at_end, at_start = lane == LANES - 1, lane == 0

    def next_col(values):
        moved = {key: turn(value, -1, 1) for key, value in values.items()}
        return {
            (l, k): jnp.where(at_end, moved[l, (k + 1) % n_lanes], moved[l, k]) for l, k in keys
        }

    def prev_col(values):
        moved = {key: turn(value, 1, 1) for key, value in values.items()}
        return {
            (l, k): jnp.where(at_start, moved[l, (k - 1) % n_lanes], moved[l, k]) for l, k in keys
        }

    shifts = Shifts(next_col, prev_col)
    for t in range(n_tiles):
        for key in keys:
            e[(0,) + key + tile_at(t)] = load(0, key[0], t, key[1])
            eps_c[key + tile_at(t)] = COURANT * load(3, key[0], t, key[1])
    first_curl(n_tiles, shifts, lambda t: load_all(1, t), lambda t: load_all(2, t), curl)
    steps(
        n_tiles, keys, shifts, e, curl,
        lambda key, t: eps_c[key + tile_at(t)],
        lambda step, key, t: src[step, key[0], pl.ds(t * SUB, SUB), lane_tile(key[1])],
        lambda values, key: values[1 - key[0], key[1]],
    )
    for t in range(1, n_tiles - 1):
        values = gradient(keys, t, e, lambda step, key, t: load(4 + step, key[0], t, key[1]))
        for key in keys:
            g[key + tile_at(t)] = values[key]

    def store(kind, key, t, value):
        last[(kind,) + key + (pl.ds(t * SUB - PAD, SUB), slice(None))] = value

    last_fields(
        range(PAD // SUB, n_tiles - PAD // SUB), keys, shifts, e,
        lambda t: load_all(1, t), lambda t: load_all(2, t), store,
    )
    for layer in range(2):
        total = None
        for k in range(n_lanes):
            for part in split2(row_pairs(g, (layer, k), n_tiles * SUB // PIX)):
                term = dot(part, mats[k])
                total = term if total is None else total + term
        pooled[layer] = total

    vals = by_tile([cone_filter(pooled.at[layer], rows // PIX, PAD // PIX) for layer in range(2)])
    high, low = split2(vals)
    slots[...] = dot(place[...], high) + dot(place[...], low)

    for t in range(n_tiles):
        for kind in range(4 + STEPS):
            at = pl.ds(t * SUB, SUB)
            if t not in halo_of:
                base[kind, at, :] = base_in[kind, at, :]
            elif kind < 4 or t not in (0, n_tiles - 1):
                base[kind, at, :] = edge_tile(
                    lambda kind, layer, k: load(kind, layer, t, k), kind, lane, n_lanes
                )


def cone_filter(pooled, out_pix, first):
    weights = cone_weights(RADIUS)
    reach = RADIUS - 1
    lane = lax.broadcasted_iota(jnp.int32, (out_pix, LANES), 1)
    at = [pooled[pl.ds(first + s, out_pix), :] for s in range(-reach, reach + 1)]
    sums = [at[reach]] + [at[reach + s] + at[reach - s] for s in range(1, reach + 1)]
    total = None
    for shift in range(reach + 1):
        mixed = None
        for s in range(reach + 1):
            weight = float(weights[reach + s, reach + shift])
            if weight > 0.0:
                term = weight * sums[s]
                mixed = term if mixed is None else mixed + term
        if shift == 0:
            total = mixed
        else:
            total = total + turn(jnp.where(lane < shift, 0.0, mixed), -shift, 1)
            total = total + turn(jnp.where(lane >= LANES - shift, 0.0, mixed), shift, 1)
    return total


def by_tile(blocks):
    span = TS // PIX
    tile_rows = blocks[0].shape[0] // span
    x = jnp.stack([block.reshape(tile_rows, span, LANES) for block in blocks], axis=1)
    x = x.reshape(tile_rows * 2, span, LANES)
    group = lax.broadcasted_iota(jnp.int32, x.shape, 2) // span
    row = lax.broadcasted_iota(jnp.int32, x.shape, 1)
    for bit in (1, 2, 4):
        row_on, lane_on = (row & bit) != 0, (group & bit) != 0
        ahead = turn(turn(x, -bit, 1), bit * span, 2)
        behind = turn(turn(x, bit, 1), -bit * span, 2)
        x = jnp.where(row_on == lane_on, x, jnp.where(lane_on, ahead, behind))
    x = x.reshape(tile_rows, 2, span, LANES)
    even, odd = x[:, 0], x[:, 1]
    upper = lax.broadcasted_iota(jnp.int32, even.shape, 2) >= HALF
    new_even = jnp.where(upper, turn(odd, HALF, 2), even)
    new_odd = jnp.where(upper, odd, turn(even, HALF, 2))
    return jnp.stack([new_even, new_odd], axis=1).reshape(tile_rows * 2 * span, LANES)


def edge_kernel(
    base, cross, near, src, out, g_out, e, first, curl, eps_c, d, g, result
):
    ext_rows = base.shape[1]
    rows = ext_rows - 2 * PAD
    n_tiles = ext_rows // SUB
    lane, odd = lanes(), is_odd("gy")
    spot = lane & (HALF - 1)
    is_left, is_right = spot < OUT, spot >= HALF - OUT

    for t in range(n_tiles):
        at = pl.ds(t * SUB, SUB)
        far, close = cross[at, :], near[at, :]
        high, low = jnp.where(odd, close, far), jnp.where(odd, far, close)
        for kind, width in enumerate(WIDTHS):
            if kind >= 4 and t in (0, n_tiles - 1):
                continue
            value = jnp.where(is_left, turn(high, OUT - width - FIRST[kind], 1), base[kind, at, :])
            value = jnp.where(is_right, turn(low, HALF - OUT - FIRST[kind], 1), value)
            if kind == 0:
                e[0, at, :] = value
            elif kind < 3:
                first[kind - 1, at, :] = value
            elif kind == 3:
                eps_c[at, :] = COURANT * value
            else:
                d[kind - 4, at, :] = value

    no_left = (spot == OUT) & ((lax.axis_index("gy") + lane * 0) == 0)
    shifts = Shifts(
        lambda values: {(): turn(values[()], -1, 1)},
        lambda values: {(): turn(values[()], 1, 1)},
    )

    def load_hx(t):
        return {(): first[0, pl.ds(t * SUB, SUB), :]}

    def load_hy(t):
        return {(): first[1, pl.ds(t * SUB, SUB), :]}

    first_curl(n_tiles, shifts, load_hx, load_hy, curl)
    shifts.prev_col = lambda values: {(): jnp.where(no_left, values[()], turn(values[()], 1, 1))}
    steps(
        n_tiles, [()], shifts, e, curl,
        lambda key, t: eps_c[pl.ds(t * SUB, SUB), :],
        lambda step, key, t: src[step, pl.ds(t * SUB, SUB), :],
        lambda values, key: turn(values[()], HALF, 1),
    )
    inside = (spot >= OUT - NEAR) & (spot < OUT + KEEP)
    inside = inside | ((spot >= HALF - OUT - KEEP) & (spot < HALF - OUT + NEAR))
    for t in range(1, n_tiles - 1):
        value = gradient([()], t, e, lambda step, key, t: d[step, pl.ds(t * SUB, SUB), :])[()]
        g[pl.ds(t * SUB, SUB), :] = jnp.where(inside, value, 0.0)

    def store(kind, key, t, value):
        result[kind, pl.ds(t * SUB - PAD, SUB), :] = value

    last_fields(
        range(PAD // SUB, n_tiles - PAD // SUB), [()], shifts, e, load_hx, load_hy, store
    )
    g_out[...] = g[...]
    out[...] = result[...]


def edge_filter_kernel(g, merged):
    lane = lanes()
    span, reach = TS // PIX, RADIUS - 1
    pixel = {}
    for j in range(-reach, span + reach):
        value = g[pl.ds(PAD + PIX * j, SUB, stride=TS), :]
        pixel[j] = value + g[pl.ds(PAD + PIX * j + 1, SUB, stride=TS), :]

    weights = cone_weights(RADIUS)
    spans = []
    for row in range(span):
        sums = [pixel[row]] + [pixel[row + s] + pixel[row - s] for s in range(1, reach + 1)]
        move = (row & 1) + SIDE * ((row >> 1) & 1)
        total = None
        for shift in range(reach + 1):
            mixed = None
            for s in range(reach + 1):
                weight = float(weights[reach + s, reach + shift])
                if weight > 0.0:
                    term = weight * sums[s]
                    mixed = term if mixed is None else mixed + term
            for place in {PIX * shift, -PIX * shift}:
                term = turn(mixed, move + place, 1) + turn(mixed, move + place - 1, 1)
                total = term if total is None else total + term
        spans.append(total)
    even = (lane & 1) == 0
    window = ((lane - OUT) & (HALF - 1)) < SIDE
    for n in range(2):
        a, b, c, d = spans[4 * n : 4 * n + 4]
        merged[n] = jnp.where(window, jnp.where(even, a, b), jnp.where(even, c, d))


def edge_slots_kernel(merged, slots_in, place, slots):
    lane = lanes()
    span = TS // PIX
    row, pixel = lane // span % span, lane % span
    start = (lane & HALF) + OUT + PIX * pixel + (row & 1) + SIDE * ((row >> 1) & 1)
    edge = []
    for side in range(2):
        index = (start + OUT * side) & (LANES - 1)
        low, high = (jnp.take_along_axis(merged[n], index, axis=1) for n in range(2))
        edge.append(jnp.where(row < span // 2, low, high))
    parts = split2(jnp.concatenate(edge, axis=0))
    slots[...] = slots_in[...] + dot(place[...], jnp.concatenate(parts, axis=0))


def merge_kernel(last, edge_last, out_fields, merged, sem):
    rows, cols = merged.shape[2], merged.shape[3]
    n_lanes = cols // LANES
    lane = lanes()
    for t in range(rows // SUB):
        at = pl.ds(t * SUB, SUB)
        for kind in range(3):
            edge = edge_last[kind, at, :]
            for layer in range(2):
                for k in range(n_lanes):
                    value = last[kind, layer, k, at, :]
                    if k == 0:
                        value = jnp.where(lane < KEEP, turn(edge, -HALF * layer - OUT, 1), value)
                    if k == n_lanes - 1:
                        value = jnp.where(
                            lane >= LANES - KEEP, turn(edge, -HALF * layer - SIDE - OUT, 1), value
                        )
                    merged[kind, layer, at, lane_tile(k)] = value
    copy = pltpu.make_async_copy(merged, out_fields, sem)
    copy.start()
    copy.wait()


def vmem():
    return pl.BlockSpec(memory_space=pltpu.VMEM)


def shape(*dims, dtype=F32):
    return jax.ShapeDtypeStruct(dims, dtype)


def call(kernel, outs, n_in, *, in_space=pltpu.VMEM, out_specs=None, scratch=(), flops=0, size=0):
    return pl.pallas_call(
        kernel,
        out_shape=outs,
        in_specs=[pl.BlockSpec(memory_space=in_space)] * n_in,
        out_specs=out_specs or tuple(vmem() for _ in outs),
        scratch_shapes=list(scratch),
        compiler_params=pltpu.CompilerParams(vmem_limit_bytes=40 * 1024 * 1024),
        cost_estimate=pl.CostEstimate(flops=flops, bytes_accessed=size, transcendentals=0),
    )


def on_device(adj_fields, inv_eps, fwd_diff, mon_x, mon_y, mon_amp, design_mask, tile_owner):
    rows, cols = adj_fields.shape[2], adj_fields.shape[3]
    assert cols == 2 * LANES and rows % TS == 0
    gx_count, gy_count = lax.axis_size("gx"), lax.axis_size("gy")
    owners = gx_count * gy_count
    tiles = (rows // TS) * (cols // TS)
    width = 2 * (TS // PIX) ** 2
    assert width == LANES
    capacity = max(8, 2 * tiles // owners)
    assert rows == TS * SUB and cols == 2 * TS * SUB
    ext_rows = rows + 2 * PAD
    n_lanes = cols // LANES
    cells = rows * cols
    blocks = (adj_fields, inv_eps, fwd_diff)


    strip = shape(16, SUB, cols)
    cross, near = call(
        rows_kernel, (strip, strip), 3, in_space=pltpu.HBM,
        scratch=(
            pltpu.VMEM((2, 4, 2, PAD, cols), F32),
            pltpu.VMEM((2, STEPS, 2, SUB, cols), F32),
            pltpu.SemaphoreType.DMA((6,)),
        ),
        size=2**20,
    )(*(pltpu.with_memory_space_constraint(block, pltpu.HBM) for block in blocks))

    def pairs(count, start):
        some = [(i, i + 1) for i in range(start, count - 1, 2)]
        return some + [(j, i) for i, j in some]

    cross = lax.ppermute(cross, "gx", pairs(gx_count, 1))
    near = lax.ppermute(near, "gx", pairs(gx_count, 0))

    packed = shape(ext_rows, LANES)
    channels = mon_x.shape[0]
    cross_cols, near_cols, base, src, src_edge, place, place_edge = call(
        lambda *refs: prep_kernel(capacity, *refs),
        (
            packed,
            packed,
            shape(4 + STEPS, ext_rows, LANES),
            shape(STEPS, 2, ext_rows, cols),
            shape(STEPS, ext_rows, LANES),
            shape(owners * capacity, tiles, dtype=BF16),
            shape(owners * capacity, 4 * SUB, dtype=BF16),
        ),
        8,
        flops=16 * ext_rows * (cols + LANES) * 3 * channels,
        size=64 * cells,
    )(
        *blocks,
        mon_x.reshape(1, channels),
        mon_y.reshape(1, channels),
        mon_amp,
        design_mask.reshape(1, tiles),
        tile_owner.reshape(1, tiles),
    )
    cross_cols, near_cols = call(
        corners_kernel, (packed, packed), 4, flops=cells, size=8 * ext_rows * LANES
    )(cross_cols, near_cols, cross, near)
    cross_cols = lax.ppermute(cross_cols, "gy", pairs(gy_count, 1))
    near_cols = lax.ppermute(near_cols, "gy", pairs(gy_count, 0))

    plane = (2, n_lanes, ext_rows, LANES)
    last, slots, base = call(
        inner_kernel,
        (
            shape(3, 2, n_lanes, rows, LANES),
            shape(owners * capacity, width),
            shape(4 + STEPS, ext_rows, LANES),
        ),
        9,
        scratch=(
            pltpu.VMEM((1 + STEPS,) + plane, F32),
            pltpu.VMEM(plane, F32),
            pltpu.VMEM(plane, F32),
            pltpu.VMEM(plane, F32),
            pltpu.VMEM((2, ext_rows // PIX, LANES), F32),
        ),
        flops=200 * cells,
        size=96 * cells,
    )(*blocks, cross, near, src, pool_matrices(), base, place)

    plane = (ext_rows, LANES)
    edge_last, edge_g = call(
        edge_kernel,
        (shape(3, rows, LANES), shape(*plane)),
        4,
        scratch=(
            pltpu.VMEM((1 + STEPS,) + plane, F32),
            pltpu.VMEM((2,) + plane, F32),
            pltpu.VMEM(plane, F32),
            pltpu.VMEM(plane, F32),
            pltpu.VMEM((STEPS,) + plane, F32),
            pltpu.VMEM(plane, F32),
            pltpu.VMEM((3, rows, LANES), F32),
        ),
        flops=50 * cells,
        size=16 * cells,
    )(base, cross_cols, near_cols, src_edge)
    (merged,) = call(
        edge_filter_kernel, (shape(2, SUB, LANES),), 1, flops=20 * cells, size=4 * cells
    )(edge_g)
    (outgoing,) = call(
        edge_slots_kernel, (shape(owners * capacity, width),), 3, flops=20 * cells, size=4 * cells
    )(merged, slots, place_edge)
    (fields,) = call(
        merge_kernel,
        (shape(3, 2, rows, cols),),
        2,
        out_specs=(pl.BlockSpec(memory_space=pl.ANY),),
        scratch=(pltpu.VMEM((3, 2, rows, cols), F32), pltpu.SemaphoreType.DMA),
        flops=20 * cells,
        size=48 * cells,
    )(last, edge_last)

    outgoing = outgoing.reshape(owners, capacity, width)
    incoming = lax.all_to_all(outgoing, ("gx", "gy"), split_axis=0, concat_axis=0, tiled=True)
    return fields, incoming[None]


def solution(mesh):
    placed = (
        P(None, None, ("parts", "gx"), "gy"),
        P(None, ("parts", "gx"), "gy"),
        P(None, None, ("parts", "gx"), "gy"),
        P("parts"),
        P("parts"),
        P(None, "parts"),
        P(("parts", "gx"), "gy", None),
        P(("parts", "gx"), "gy", None, None),
    )
    return jax.shard_map(
        on_device,
        mesh=mesh,
        in_specs=placed,
        out_specs=(
            P(None, None, ("parts", "gx"), "gy"),
            P(("parts", "gx", "gy"), None, None, None),
        ),
        check_vma=False,
    )
```

```python
import jax
import jax.numpy as jnp
import ml_dtypes
import numpy as np
from jax import lax
from jax.experimental import pallas as pl
from jax.experimental.pallas import tpu as pltpu
from jax.sharding import PartitionSpec as P

STEPS = 4
PIX = 2
TS = 16
RADIUS = 4
COURANT = 0.6
COUPLING = 0.25

LANES = 128
SUB = 8
FAR = STEPS + PIX * (RADIUS - 1)
NEAR = PIX * (RADIUS - 1)
LEFT_OVER = FAR - SUB
PAD = 2 * SUB
HALF = LANES // 2
SIDE = HALF // 2
OUT = SIDE // 2
KEEP = 8
F32 = jnp.float32
BF16 = jnp.bfloat16
WIDTHS = (FAR,) * 4 + (NEAR,) * STEPS
FIRST = tuple(sum(WIDTHS[:k]) for k in range(len(WIDTHS)))
assert sum(WIDTHS) <= HALF and FAR <= OUT and STEPS + KEEP <= OUT


def cone_weights(radius):
    reach_cells = radius - 1
    offsets = np.arange(-reach_cells, reach_cells + 1)
    distance = np.sqrt(offsets[:, None] * offsets[:, None] + offsets[None, :] * offsets[None, :])
    weights = np.maximum(radius - distance, 0.0)
    return weights / weights.sum()


def pool_matrices():
    inner = np.zeros((2, LANES, LANES), np.float32)
    for j in range(KEEP, 2 * LANES - KEEP):
        inner[j // LANES, j % LANES, j // PIX] = 1.0
    return inner.astype(ml_dtypes.bfloat16)


def split2(value):
    high = value.astype(BF16)
    return high, (value - high.astype(F32)).astype(BF16)


def split3(value):
    high = value.astype(BF16)
    rest = value - high.astype(F32)
    mid = rest.astype(BF16)
    return high, mid, (rest - mid.astype(F32)).astype(BF16)


def dot(a, b):
    return jnp.dot(a, b, preferred_element_type=F32)


def turn(value, shift, axis):
    size = value.shape[axis]
    return pltpu.roll(value, shift % size, axis) if shift % size else value


def lanes():
    return lax.broadcasted_iota(jnp.int32, (SUB, LANES), 1)


def subs():
    return lax.broadcasted_iota(jnp.int32, (SUB, LANES), 0)


def lane_tile(k):
    return pl.ds(k * LANES, LANES)


def is_odd(axis):
    return ((subs() * 0 + lax.axis_index(axis)) & 1) == 1


def rows_kernel(fields, eps, fwd, cross, near, hold, hold_fwd, sems):
    rows, cols = fields.shape[2], fields.shape[3]
    copies = []
    for n, at in enumerate((0, rows - PAD)):
        at_fwd = 0 if n == 0 else rows - SUB
        pairs = (
            (fields.at[:, :, pl.ds(at, PAD), :], hold.at[n, pl.ds(0, 3)]),
            (eps.at[:, pl.ds(at, PAD), :], hold.at[n, 3]),
            (fwd.at[:, :, pl.ds(at_fwd, SUB), :], hold_fwd.at[n]),
        )
        for m, (src, dst) in enumerate(pairs):
            copies.append(pltpu.make_async_copy(src, dst, sems.at[3 * n + m]))
    for copy in copies:
        copy.start()
    for copy in copies:
        copy.wait()
    odd, sub = is_odd("gx"), subs()
    for kind in range(4):
        for layer in range(2):
            plane = 2 * kind + layer
            for k in range(cols // LANES):
                at = lane_tile(k)
                low = hold[0, kind, layer, pl.ds(0, SUB), at]
                high = hold[1, kind, layer, pl.ds(SUB, SUB), at]
                cross[plane, :, at] = jnp.where(odd, high, low)
                near[plane, :, at] = jnp.where(odd, low, high)
                rest_low = turn(hold[0, kind, layer, pl.ds(SUB, SUB), at], -LEFT_OVER, 0)
                rest_high = turn(hold[1, kind, layer, pl.ds(0, SUB), at], LEFT_OVER, 0)
                low = jnp.where(sub >= NEAR, rest_low, hold_fwd[0, kind, layer, :, at])
                high = jnp.where(sub < SUB - NEAR, rest_high, hold_fwd[1, kind, layer, :, at])
                cross[8 + plane, :, at] = jnp.where(odd, high, low)
                near[8 + plane, :, at] = jnp.where(odd, low, high)


def halo_tile(cross, near, odd, tile, kind, layer, at):
    is_above = tile < 2
    outer = tile in (0, 3)
    if outer and kind >= 4:
        return None
    plane = 2 * kind + layer + (8 if outer else 0)
    a, b = near[plane, :, at], cross[plane, :, at]
    value = jnp.where(odd, a, b) if is_above else jnp.where(odd, b, a)
    if outer:
        value = turn(value, -LEFT_OVER if is_above else LEFT_OVER, 0)
    return value


def core_tile(fields, eps, fwd, at, kind, layer, cols):
    if kind < 3:
        return fields[kind, layer, at, cols]
    if kind == 3:
        return eps[layer, at, cols]
    return fwd[kind - 4, layer, at, cols]


def pack_tile(load, lane, right):
    total = jnp.zeros((SUB, LANES), F32)
    for kind, width in enumerate(WIDTHS):
        for layer in range(2):
            value = load(kind, layer)
            if value is None:
                continue
            first = FIRST[kind] + HALF * layer
            value = turn(value, first + width if right else first, 1)
            total = jnp.where((lane >= first) & (lane < first + width), value, total)
    return total


def edge_tile(load, kind, lane, n_lanes):
    spot = lane & (HALF - 1)
    total = None
    for layer in range(2):
        low = turn(load(kind, layer, 0), HALF * layer + OUT, 1)
        high = turn(load(kind, layer, n_lanes - 1), HALF * layer + SIDE + OUT, 1)
        value = jnp.where(spot < SIDE, low, high)
        total = value if total is None else jnp.where(lane < HALF, total, value)
    return total


def cols_kernel(fields, eps, fwd, cross, near, base):
    rows, cols = fields.shape[2], fields.shape[3]
    n_lanes = cols // LANES
    lane, odd = lanes(), is_odd("gy")

    def tile(t, carry):
        at = pl.ds(pl.multiple_of(t * SUB, SUB), SUB)
        out_at = pl.ds(pl.multiple_of(t * SUB + PAD, SUB), SUB)

        def load(kind, layer, k):
            return core_tile(fields, eps, fwd, at, kind, layer, lane_tile(k))

        left = pack_tile(lambda kind, layer: load(kind, layer, 0), lane, False)
        right = pack_tile(lambda kind, layer: load(kind, layer, n_lanes - 1), lane, True)
        cross[out_at, :] = jnp.where(odd, right, left)
        near[out_at, :] = jnp.where(odd, left, right)
        for kind in range(4 + STEPS):
            base[kind, out_at, :] = edge_tile(load, kind, lane, n_lanes)
        return carry

    lax.fori_loop(0, rows // SUB, tile, 0, unroll=4)
    zero = jnp.zeros((PAD, LANES), F32)
    for out in (cross, near):
        out[pl.ds(0, PAD), :] = zero
        out[pl.ds(PAD + rows, PAD), :] = zero


def corners_kernel(cross_in, near_in, cross_rows, near_rows, cross, near):
    rows, cols = cross.shape[0] - 2 * PAD, cross_rows.shape[2]
    lane, odd, odd_col = lanes(), is_odd("gx"), is_odd("gy")
    core = pl.ds(PAD, rows)
    cross[core, :] = cross_in[core, :]
    near[core, :] = near_in[core, :]
    for tile in range(4):
        at = pl.ds(tile * SUB if tile < 2 else PAD + rows + (tile - 2) * SUB, SUB)
        left, right = (
            pack_tile(
                lambda kind, layer: halo_tile(
                    cross_rows, near_rows, odd, tile, kind, layer, pl.ds(lo, LANES)
                ),
                lane, is_right,
            )
            for lo, is_right in ((0, False), (cols - LANES, True))
        )
        cross[at, :] = jnp.where(odd_col, right, left)
        near[at, :] = jnp.where(odd_col, left, right)


def prep_kernel(
    capacity, fields, eps, fwd, mon_x, mon_y, amp, mask, owner, cross, near, base, src, src_edge, place, place_edge
):
    cols_kernel(fields, eps, fwd, cross, near, base)
    side_kernel(capacity, fields.shape[2], mon_x, mon_y, amp, mask, owner, src, src_edge, place, place_edge)


def side_kernel(capacity, rows, mon_x, mon_y, amp, mask, owner, src, src_edge, place, place_edge):
    _, _, ext_rows, cols = src.shape
    channels = mon_x.shape[1]
    row = mon_x[...] - lax.axis_index("gx") * rows + PAD
    col = mon_y[...] - lax.axis_index("gy") * cols
    in_left = (col >= -OUT) & (col < OUT)
    in_right = (col >= cols - OUT) & (col < cols + OUT)
    edge = jnp.where(in_left, col + OUT, jnp.where(in_right, col - cols + OUT + SIDE, -LANES))
    layer = lax.broadcasted_iota(jnp.int32, (1, channels), 1) & 1
    edge = edge + HALF * layer
    inside = jnp.where((col >= 0) & (col < cols), col, -1)
    one_y = lax.broadcasted_iota(jnp.int32, (cols, channels), 0) == inside
    one_e = lax.broadcasted_iota(jnp.int32, (LANES, channels), 0) == edge
    one_y = jnp.where(one_y, 1.0, 0.0).astype(BF16)
    one_e = jnp.where(one_e, 1.0, 0.0).astype(BF16)
    one_y = jnp.concatenate([one_y] * 3, axis=1)
    one_e = jnp.concatenate([one_e] * 3, axis=1)
    one_x = lax.broadcasted_iota(jnp.int32, (ext_rows, channels), 0) == row
    one_x = jnp.where(one_x, 1.0, 0.0).astype(F32)
    nt = (((1,), (1,)), ((), ()))
    for step in range(STEPS):
        parts = [part.astype(F32) for part in split3(amp[pl.ds(step, 1), :])]
        lhs = jnp.concatenate([one_x * part for part in parts], axis=1)
        src_edge[step] = lax.dot_general(lhs.astype(BF16), one_e, nt, preferred_element_type=F32)
        layer_wide = jnp.concatenate([layer] * 3, axis=1)
        for which in range(2):
            some = jnp.where(layer_wide == which, lhs, 0.0).astype(BF16)
            src[step, which] = lax.dot_general(some, one_y, nt, preferred_element_type=F32)
    tiles = owner.shape[1]
    own = owner[...].astype(F32)
    own_wide = jnp.broadcast_to(own, (tiles, tiles))
    earlier = lax.broadcasted_iota(jnp.int32, (tiles, tiles), 0) < lax.broadcasted_iota(
        jnp.int32, (tiles, tiles), 1
    )
    same = (own_wide.T == own_wide) & earlier
    slot = jnp.sum(jnp.where(same, 1.0, 0.0), axis=0, keepdims=True)
    dest = owner[...] * capacity + slot.astype(jnp.int32)
    dest = jnp.where(mask[...] != 0, dest, -1)
    hit = lax.broadcasted_iota(jnp.int32, place.shape, 0) == dest
    hit = jnp.where(hit, 1.0, 0.0).astype(BF16)
    place[...] = hit
    tile_cols = cols // TS
    column = lax.broadcasted_iota(jnp.int32, (tiles, 4 * SUB), 1)
    wanted = (column % SUB) * tile_cols + ((column // SUB) & 1) * (tile_cols - 1)
    picked = lax.broadcasted_iota(jnp.int32, (tiles, 4 * SUB), 0) == wanted
    place_edge[...] = dot(hit, jnp.where(picked, 1.0, 0.0).astype(BF16)).astype(BF16)


class Shifts:
    def __init__(self, next_col, prev_col):
        self.next_col, self.prev_col = next_col, prev_col
        self.bottom, self.top = subs() == SUB - 1, subs() == 0

    def up(self, tile):
        return {key: turn(value, -1, 0) for key, value in tile.items()}

    def down(self, tile):
        return {key: turn(value, 1, 0) for key, value in tile.items()}

    def below(self, up_here, up_next):
        return {key: jnp.where(self.bottom, up_next[key], up_here[key]) for key in up_here}

    def above(self, down_here, down_before):
        return {key: jnp.where(self.top, down_before[key], down_here[key]) for key in down_here}


def tile_at(t):
    return (pl.ds(t * SUB, SUB), slice(None))


def first_curl(n_tiles, shifts, load_hx, load_hy, curl):
    before = None
    for t in range(n_tiles):
        hx, hy = load_hx(t), load_hy(t)
        down = shifts.down(hy)
        over = shifts.above(down, before if t else down)
        left = shifts.prev_col(hx)
        for key in hx:
            curl[key + tile_at(t)] = (hy[key] - over[key]) - (hx[key] - left[key])
        before = down


def steps(n_tiles, keys, shifts, e, curl, eps_of, src_of, other):
    no_above = shifts.top & ((lax.axis_index("gx") + subs() * 0) == 0)
    for step in range(STEPS):
        low, high = (0, n_tiles) if step == 0 else (1, n_tiles - 1)

        def load(t):
            return {key: e[(step,) + key + tile_at(t)] for key in keys}

        here = load(low)
        up = shifts.up(here)
        down_before = shifts.down(load(max(low - 1, 0)))
        for t in range(low, high):
            after = load(min(t + 1, n_tiles - 1))
            up_next, down = shifts.up(after), shifts.down(here)
            below, above = shifts.below(up, up_next), shifts.above(down, down_before)
            right, left = shifts.next_col(here), shifts.prev_col(here)
            for key in keys:
                center, over = here[key], above[key]
                if t == PAD // SUB:
                    over = jnp.where(no_above, center, over)
                ring = (below[key] + over) + (right[key] + left[key]) - 4.0 * center
                change = curl[key + tile_at(t)] - COURANT * ring
                if step < STEPS - 1:
                    curl[key + tile_at(t)] = change
                change = change + COUPLING * (other(here, key) - center)
                e[(step + 1,) + key + tile_at(t)] = (
                    center - eps_of(key, t) * change + src_of(step, key, t)
                )
            here, up, down_before = after, up_next, down


def gradient(keys, t, e, change_of):
    result = {}
    for key in keys:
        total = None
        for step in range(STEPS):
            term = e[(step + 1,) + key + tile_at(t)] * change_of(step, key, t)
            total = term if total is None else total + term
        result[key] = -total
    return result


def last_fields(tiles, keys, shifts, e, load_hx, load_hy, store):
    def total(t):
        result = {}
        for key in keys:
            parts = [e[(step,) + key + tile_at(t)] for step in range(STEPS)]
            result[key] = (parts[0] + parts[1]) + (parts[2] + parts[3])
        return result

    here = total(tiles[0])
    up = shifts.up(here)
    for t in tiles:
        after = total(t + 1)
        up_next = shifts.up(after)
        below, right = shifts.below(up, up_next), shifts.next_col(here)
        hx, hy = load_hx(t), load_hy(t)
        for key in keys:
            store(0, key, t, e[(STEPS,) + key + tile_at(t)])
            store(1, key, t, hx[key] + COURANT * (right[key] - here[key]))
            store(2, key, t, hy[key] - COURANT * (below[key] - here[key]))
        here, up = after, up_next


def row_pairs(ref, lead, count):
    even = ref[lead + (pl.ds(0, count, stride=PIX), slice(None))]
    return even + ref[lead + (pl.ds(1, count, stride=PIX), slice(None))]


def inner_kernel(
    fields, eps, fwd, cross, near, src, mats, base_in, place, last, slots, base, e, curl, eps_c, g, pooled
):
    rows, cols = fields.shape[2], fields.shape[3]
    n_tiles = (rows + 2 * PAD) // SUB
    n_lanes = cols // LANES
    lane, odd = lanes(), is_odd("gx")
    halo_of = {0: 0, 1: 1, n_tiles - 2: 2, n_tiles - 1: 3}
    keys = [(layer, k) for layer in range(2) for k in range(n_lanes)]

    def load(kind, layer, t, k):
        if t in halo_of:
            return halo_tile(cross, near, odd, halo_of[t], kind, layer, lane_tile(k))
        return core_tile(fields, eps, fwd, pl.ds(t * SUB - PAD, SUB), kind, layer, lane_tile(k))

    def load_all(kind, t):
        return {key: load(kind, key[0], t, key[1]) for key in keys}

    at_end, at_start = lane == LANES - 1, lane == 0

    def next_col(values):
        moved = {key: turn(value, -1, 1) for key, value in values.items()}
        return {
            (l, k): jnp.where(at_end, moved[l, (k + 1) % n_lanes], moved[l, k]) for l, k in keys
        }

    def prev_col(values):
        moved = {key: turn(value, 1, 1) for key, value in values.items()}
        return {
            (l, k): jnp.where(at_start, moved[l, (k - 1) % n_lanes], moved[l, k]) for l, k in keys
        }

    shifts = Shifts(next_col, prev_col)
    for t in range(n_tiles):
        for key in keys:
            e[(0,) + key + tile_at(t)] = load(0, key[0], t, key[1])
            eps_c[key + tile_at(t)] = COURANT * load(3, key[0], t, key[1])
    first_curl(n_tiles, shifts, lambda t: load_all(1, t), lambda t: load_all(2, t), curl)
    steps(
        n_tiles, keys, shifts, e, curl,
        lambda key, t: eps_c[key + tile_at(t)],
        lambda step, key, t: src[step, key[0], pl.ds(t * SUB, SUB), lane_tile(key[1])],
        lambda values, key: values[1 - key[0], key[1]],
    )
    for t in range(1, n_tiles - 1):
        values = gradient(keys, t, e, lambda step, key, t: load(4 + step, key[0], t, key[1]))
        for key in keys:
            g[key + tile_at(t)] = values[key]

    def store(kind, key, t, value):
        last[(kind,) + key + (pl.ds(t * SUB - PAD, SUB), slice(None))] = value

    last_fields(
        range(PAD // SUB, n_tiles - PAD // SUB), keys, shifts, e,
        lambda t: load_all(1, t), lambda t: load_all(2, t), store,
    )
    for layer in range(2):
        total = None
        for k in range(n_lanes):
            for part in split2(row_pairs(g, (layer, k), n_tiles * SUB // PIX)):
                term = dot(part, mats[k])
                total = term if total is None else total + term
        pooled[layer] = total

    vals = by_tile([cone_filter(pooled.at[layer], rows // PIX, PAD // PIX) for layer in range(2)])
    high, low = split2(vals)
    slots[...] = dot(place[...], high) + dot(place[...], low)

    for t in range(n_tiles):
        for kind in range(4 + STEPS):
            at = pl.ds(t * SUB, SUB)
            if t not in halo_of:
                base[kind, at, :] = base_in[kind, at, :]
            elif kind < 4 or t not in (0, n_tiles - 1):
                base[kind, at, :] = edge_tile(
                    lambda kind, layer, k: load(kind, layer, t, k), kind, lane, n_lanes
                )


def cone_filter(pooled, out_pix, first):
    weights = cone_weights(RADIUS)
    reach = RADIUS - 1
    lane = lax.broadcasted_iota(jnp.int32, (out_pix, LANES), 1)
    at = [pooled[pl.ds(first + s, out_pix), :] for s in range(-reach, reach + 1)]
    sums = [at[reach]] + [at[reach + s] + at[reach - s] for s in range(1, reach + 1)]
    total = None
    for shift in range(reach + 1):
        mixed = None
        for s in range(reach + 1):
            weight = float(weights[reach + s, reach + shift])
            if weight > 0.0:
                term = weight * sums[s]
                mixed = term if mixed is None else mixed + term
        if shift == 0:
            total = mixed
        else:
            total = total + turn(jnp.where(lane < shift, 0.0, mixed), -shift, 1)
            total = total + turn(jnp.where(lane >= LANES - shift, 0.0, mixed), shift, 1)
    return total


def by_tile(blocks):
    span = TS // PIX
    tile_rows = blocks[0].shape[0] // span
    x = jnp.stack([block.reshape(tile_rows, span, LANES) for block in blocks], axis=1)
    x = x.reshape(tile_rows * 2, span, LANES)
    group = lax.broadcasted_iota(jnp.int32, x.shape, 2) // span
    row = lax.broadcasted_iota(jnp.int32, x.shape, 1)
    for bit in (1, 2, 4):
        row_on, lane_on = (row & bit) != 0, (group & bit) != 0
        ahead = turn(turn(x, -bit, 1), bit * span, 2)
        behind = turn(turn(x, bit, 1), -bit * span, 2)
        x = jnp.where(row_on == lane_on, x, jnp.where(lane_on, ahead, behind))
    x = x.reshape(tile_rows, 2, span, LANES)
    even, odd = x[:, 0], x[:, 1]
    upper = lax.broadcasted_iota(jnp.int32, even.shape, 2) >= HALF
    new_even = jnp.where(upper, turn(odd, HALF, 2), even)
    new_odd = jnp.where(upper, odd, turn(even, HALF, 2))
    return jnp.stack([new_even, new_odd], axis=1).reshape(tile_rows * 2 * span, LANES)


def edge_kernel(
    base, cross, near, src, out, g_out, e, first, curl, eps_c, d, g, result
):
    ext_rows = base.shape[1]
    rows = ext_rows - 2 * PAD
    n_tiles = ext_rows // SUB
    lane, odd = lanes(), is_odd("gy")
    spot = lane & (HALF - 1)
    is_left, is_right = spot < OUT, spot >= HALF - OUT

    for t in range(n_tiles):
        at = pl.ds(t * SUB, SUB)
        far, close = cross[at, :], near[at, :]
        high, low = jnp.where(odd, close, far), jnp.where(odd, far, close)
        for kind, width in enumerate(WIDTHS):
            if kind >= 4 and t in (0, n_tiles - 1):
                continue
            value = jnp.where(is_left, turn(high, OUT - width - FIRST[kind], 1), base[kind, at, :])
            value = jnp.where(is_right, turn(low, HALF - OUT - FIRST[kind], 1), value)
            if kind == 0:
                e[0, at, :] = value
            elif kind < 3:
                first[kind - 1, at, :] = value
            elif kind == 3:
                eps_c[at, :] = COURANT * value
            else:
                d[kind - 4, at, :] = value

    no_left = (spot == OUT) & ((lax.axis_index("gy") + lane * 0) == 0)
    shifts = Shifts(
        lambda values: {(): turn(values[()], -1, 1)},
        lambda values: {(): turn(values[()], 1, 1)},
    )

    def load_hx(t):
        return {(): first[0, pl.ds(t * SUB, SUB), :]}

    def load_hy(t):
        return {(): first[1, pl.ds(t * SUB, SUB), :]}

    first_curl(n_tiles, shifts, load_hx, load_hy, curl)
    shifts.prev_col = lambda values: {(): jnp.where(no_left, values[()], turn(values[()], 1, 1))}
    steps(
        n_tiles, [()], shifts, e, curl,
        lambda key, t: eps_c[pl.ds(t * SUB, SUB), :],
        lambda step, key, t: src[step, pl.ds(t * SUB, SUB), :],
        lambda values, key: turn(values[()], HALF, 1),
    )
    inside = (spot >= OUT - NEAR) & (spot < OUT + KEEP)
    inside = inside | ((spot >= HALF - OUT - KEEP) & (spot < HALF - OUT + NEAR))
    for t in range(1, n_tiles - 1):
        value = gradient([()], t, e, lambda step, key, t: d[step, pl.ds(t * SUB, SUB), :])[()]
        g[pl.ds(t * SUB, SUB), :] = jnp.where(inside, value, 0.0)

    def store(kind, key, t, value):
        result[kind, pl.ds(t * SUB - PAD, SUB), :] = value

    last_fields(
        range(PAD // SUB, n_tiles - PAD // SUB), [()], shifts, e, load_hx, load_hy, store
    )
    g_out[...] = g[...]
    out[...] = result[...]


def edge_filter_kernel(g, merged):
    lane = lanes()
    span, reach = TS // PIX, RADIUS - 1
    pixel = {}
    for j in range(-reach, span + reach):
        value = g[pl.ds(PAD + PIX * j, SUB, stride=TS), :]
        pixel[j] = value + g[pl.ds(PAD + PIX * j + 1, SUB, stride=TS), :]

    weights = cone_weights(RADIUS)
    spans = []
    for row in range(span):
        sums = [pixel[row]] + [pixel[row + s] + pixel[row - s] for s in range(1, reach + 1)]
        move = (row & 1) + SIDE * ((row >> 1) & 1)
        total = None
        for shift in range(reach + 1):
            mixed = None
            for s in range(reach + 1):
                weight = float(weights[reach + s, reach + shift])
                if weight > 0.0:
                    term = weight * sums[s]
                    mixed = term if mixed is None else mixed + term
            for place in {PIX * shift, -PIX * shift}:
                term = turn(mixed, move + place, 1) + turn(mixed, move + place - 1, 1)
                total = term if total is None else total + term
        spans.append(total)
    even = (lane & 1) == 0
    window = ((lane - OUT) & (HALF - 1)) < SIDE
    for n in range(2):
        a, b, c, d = spans[4 * n : 4 * n + 4]
        merged[n] = jnp.where(window, jnp.where(even, a, b), jnp.where(even, c, d))


def edge_slots_kernel(merged, slots_in, place, slots):
    lane = lanes()
    span = TS // PIX
    row, pixel = lane // span % span, lane % span
    start = (lane & HALF) + OUT + PIX * pixel + (row & 1) + SIDE * ((row >> 1) & 1)
    edge = []
    for side in range(2):
        index = (start + OUT * side) & (LANES - 1)
        low, high = (jnp.take_along_axis(merged[n], index, axis=1) for n in range(2))
        edge.append(jnp.where(row < span // 2, low, high))
    parts = split2(jnp.concatenate(edge, axis=0))
    slots[...] = slots_in[...] + dot(place[...], jnp.concatenate(parts, axis=0))


def merge_kernel(last, edge_last, out_fields, merged, sem):
    rows, cols = merged.shape[2], merged.shape[3]
    n_lanes = cols // LANES
    lane = lanes()
    for t in range(rows // SUB):
        at = pl.ds(t * SUB, SUB)
        for kind in range(3):
            edge = edge_last[kind, at, :]
            for layer in range(2):
                for k in range(n_lanes):
                    value = last[kind, layer, k, at, :]
                    if k == 0:
                        value = jnp.where(lane < KEEP, turn(edge, -HALF * layer - OUT, 1), value)
                    if k == n_lanes - 1:
                        value = jnp.where(
                            lane >= LANES - KEEP, turn(edge, -HALF * layer - SIDE - OUT, 1), value
                        )
                    merged[kind, layer, at, lane_tile(k)] = value
    copy = pltpu.make_async_copy(merged, out_fields, sem)
    copy.start()
    copy.wait()


def vmem():
    return pl.BlockSpec(memory_space=pltpu.VMEM)


def shape(*dims, dtype=F32):
    return jax.ShapeDtypeStruct(dims, dtype)


def call(kernel, outs, n_in, *, in_space=pltpu.VMEM, out_specs=None, scratch=(), flops=0, size=0):
    return pl.pallas_call(
        kernel,
        out_shape=outs,
        in_specs=[pl.BlockSpec(memory_space=in_space)] * n_in,
        out_specs=out_specs or tuple(vmem() for _ in outs),
        scratch_shapes=list(scratch),
        compiler_params=pltpu.CompilerParams(vmem_limit_bytes=40 * 1024 * 1024),
        cost_estimate=pl.CostEstimate(flops=flops, bytes_accessed=size, transcendentals=0),
    )


def on_device(adj_fields, inv_eps, fwd_diff, mon_x, mon_y, mon_amp, design_mask, tile_owner):
    rows, cols = adj_fields.shape[2], adj_fields.shape[3]
    assert cols == 2 * LANES and rows % TS == 0
    gx_count, gy_count = lax.axis_size("gx"), lax.axis_size("gy")
    owners = gx_count * gy_count
    tiles = (rows // TS) * (cols // TS)
    width = 2 * (TS // PIX) ** 2
    assert width == LANES
    capacity = max(8, 2 * tiles // owners)
    assert rows == TS * SUB and cols == 2 * TS * SUB
    ext_rows = rows + 2 * PAD
    n_lanes = cols // LANES
    cells = rows * cols
    blocks = (adj_fields, inv_eps, fwd_diff)


    strip = shape(16, SUB, cols)
    cross, near = call(
        rows_kernel, (strip, strip), 3, in_space=pltpu.HBM,
        scratch=(
            pltpu.VMEM((2, 4, 2, PAD, cols), F32),
            pltpu.VMEM((2, STEPS, 2, SUB, cols), F32),
            pltpu.SemaphoreType.DMA((6,)),
        ),
        size=2**20,
    )(*(pltpu.with_memory_space_constraint(block, pltpu.HBM) for block in blocks))

    def pairs(count, start):
        some = [(i, i + 1) for i in range(start, count - 1, 2)]
        return some + [(j, i) for i, j in some]

    cross = lax.ppermute(cross, "gx", pairs(gx_count, 1))
    near = lax.ppermute(near, "gx", pairs(gx_count, 0))

    packed = shape(ext_rows, LANES)
    channels = mon_x.shape[0]
    cross_cols, near_cols, base, src, src_edge, place, place_edge = call(
        lambda *refs: prep_kernel(capacity, *refs),
        (
            packed,
            packed,
            shape(4 + STEPS, ext_rows, LANES),
            shape(STEPS, 2, ext_rows, cols),
            shape(STEPS, ext_rows, LANES),
            shape(owners * capacity, tiles, dtype=BF16),
            shape(owners * capacity, 4 * SUB, dtype=BF16),
        ),
        8,
        flops=16 * ext_rows * (cols + LANES) * 3 * channels,
        size=64 * cells,
    )(
        *blocks,
        mon_x.reshape(1, channels),
        mon_y.reshape(1, channels),
        mon_amp,
        design_mask.reshape(1, tiles),
        tile_owner.reshape(1, tiles),
    )
    cross_cols, near_cols = call(
        corners_kernel, (packed, packed), 4, flops=cells, size=8 * ext_rows * LANES
    )(cross_cols, near_cols, cross, near)
    cross_cols = lax.ppermute(cross_cols, "gy", pairs(gy_count, 1))
    near_cols = lax.ppermute(near_cols, "gy", pairs(gy_count, 0))

    plane = (2, n_lanes, ext_rows, LANES)
    last, slots, base = call(
        inner_kernel,
        (
            shape(3, 2, n_lanes, rows, LANES),
            shape(owners * capacity, width),
            shape(4 + STEPS, ext_rows, LANES),
        ),
        9,
        scratch=(
            pltpu.VMEM((1 + STEPS,) + plane, F32),
            pltpu.VMEM(plane, F32),
            pltpu.VMEM(plane, F32),
            pltpu.VMEM(plane, F32),
            pltpu.VMEM((2, ext_rows // PIX, LANES), F32),
        ),
        flops=200 * cells,
        size=96 * cells,
    )(*blocks, cross, near, src, pool_matrices(), base, place)

    plane = (ext_rows, LANES)
    edge_last, edge_g = call(
        edge_kernel,
        (shape(3, rows, LANES), shape(*plane)),
        4,
        scratch=(
            pltpu.VMEM((1 + STEPS,) + plane, F32),
            pltpu.VMEM((2,) + plane, F32),
            pltpu.VMEM(plane, F32),
            pltpu.VMEM(plane, F32),
            pltpu.VMEM((STEPS,) + plane, F32),
            pltpu.VMEM(plane, F32),
            pltpu.VMEM((3, rows, LANES), F32),
        ),
        flops=50 * cells,
        size=16 * cells,
    )(base, cross_cols, near_cols, src_edge)
    (merged,) = call(
        edge_filter_kernel, (shape(2, SUB, LANES),), 1, flops=20 * cells, size=4 * cells
    )(edge_g)
    (outgoing,) = call(
        edge_slots_kernel, (pltpu.VMEM((owners * capacity, width), F32),), 3, flops=20 * cells, size=4 * cells
    )(merged, slots, place_edge)
    (fields,) = call(
        merge_kernel,
        (shape(3, 2, rows, cols),),
        2,
        out_specs=(pl.BlockSpec(memory_space=pl.ANY),),
        scratch=(pltpu.VMEM((3, 2, rows, cols), F32), pltpu.SemaphoreType.DMA),
        flops=20 * cells,
        size=48 * cells,
    )(last, edge_last)

    outgoing = outgoing.reshape(owners, capacity, width)
    incoming = lax.all_to_all(outgoing, ("gx", "gy"), split_axis=0, concat_axis=0, tiled=True)
    return fields, incoming[None]


def solution(mesh):
    placed = (
        P(None, None, ("parts", "gx"), "gy"),
        P(None, ("parts", "gx"), "gy"),
        P(None, None, ("parts", "gx"), "gy"),
        P("parts"),
        P("parts"),
        P(None, "parts"),
        P(("parts", "gx"), "gy", None),
        P(("parts", "gx"), "gy", None, None),
    )
    return jax.shard_map(
        on_device,
        mesh=mesh,
        in_specs=placed,
        out_specs=(
            P(None, None, ("parts", "gx"), "gy"),
            P(("parts", "gx", "gy"), None, None, None),
        ),
        check_vma=False,
    )
```

```python
import jax
import jax.numpy as jnp
import ml_dtypes
import numpy as np
from jax import lax
from jax.experimental import pallas as pl
from jax.experimental.pallas import tpu as pltpu
from jax.sharding import PartitionSpec as P

STEPS = 4
PIX = 2
TS = 16
RADIUS = 4
COURANT = 0.6
COUPLING = 0.25

LANES = 128
SUB = 8
FAR = STEPS + PIX * (RADIUS - 1)
NEAR = PIX * (RADIUS - 1)
LEFT_OVER = FAR - SUB
PAD = 2 * SUB
HALF = LANES // 2
SIDE = HALF // 2
OUT = SIDE // 2
KEEP = 8
F32 = jnp.float32
BF16 = jnp.bfloat16
WIDTHS = (FAR,) * 4 + (NEAR,) * STEPS
FIRST = tuple(sum(WIDTHS[:k]) for k in range(len(WIDTHS)))
assert sum(WIDTHS) <= HALF and FAR <= OUT and STEPS + KEEP <= OUT


def cone_weights(radius):
    reach_cells = radius - 1
    offsets = np.arange(-reach_cells, reach_cells + 1)
    distance = np.sqrt(offsets[:, None] * offsets[:, None] + offsets[None, :] * offsets[None, :])
    weights = np.maximum(radius - distance, 0.0)
    return weights / weights.sum()


def pool_matrices():
    inner = np.zeros((2, LANES, LANES), np.float32)
    for j in range(KEEP, 2 * LANES - KEEP):
        inner[j // LANES, j % LANES, j // PIX] = 1.0
    return inner.astype(ml_dtypes.bfloat16)


def split2(value):
    high = value.astype(BF16)
    return high, (value - high.astype(F32)).astype(BF16)


def split3(value):
    high = value.astype(BF16)
    rest = value - high.astype(F32)
    mid = rest.astype(BF16)
    return high, mid, (rest - mid.astype(F32)).astype(BF16)


def dot(a, b):
    return jnp.dot(a, b, preferred_element_type=F32)


def turn(value, shift, axis):
    size = value.shape[axis]
    return pltpu.roll(value, shift % size, axis) if shift % size else value


def lanes():
    return lax.broadcasted_iota(jnp.int32, (SUB, LANES), 1)


def subs():
    return lax.broadcasted_iota(jnp.int32, (SUB, LANES), 0)


def lane_tile(k):
    return pl.ds(k * LANES, LANES)


def is_odd(axis):
    return ((subs() * 0 + lax.axis_index(axis)) & 1) == 1


def rows_kernel(fields, eps, fwd, cross, near, hold, hold_fwd, sems):
    rows, cols = fields.shape[2], fields.shape[3]
    copies = []
    for n, at in enumerate((0, rows - PAD)):
        at_fwd = 0 if n == 0 else rows - SUB
        pairs = (
            (fields.at[:, :, pl.ds(at, PAD), :], hold.at[n, pl.ds(0, 3)]),
            (eps.at[:, pl.ds(at, PAD), :], hold.at[n, 3]),
            (fwd.at[:, :, pl.ds(at_fwd, SUB), :], hold_fwd.at[n]),
        )
        for m, (src, dst) in enumerate(pairs):
            copies.append(pltpu.make_async_copy(src, dst, sems.at[3 * n + m]))
    for copy in copies:
        copy.start()
    for copy in copies:
        copy.wait()
    odd, sub = is_odd("gx"), subs()
    for kind in range(4):
        for layer in range(2):
            plane = 2 * kind + layer
            for k in range(cols // LANES):
                at = lane_tile(k)
                low = hold[0, kind, layer, pl.ds(0, SUB), at]
                high = hold[1, kind, layer, pl.ds(SUB, SUB), at]
                cross[plane, :, at] = jnp.where(odd, high, low)
                near[plane, :, at] = jnp.where(odd, low, high)
                rest_low = turn(hold[0, kind, layer, pl.ds(SUB, SUB), at], -LEFT_OVER, 0)
                rest_high = turn(hold[1, kind, layer, pl.ds(0, SUB), at], LEFT_OVER, 0)
                low = jnp.where(sub >= NEAR, rest_low, hold_fwd[0, kind, layer, :, at])
                high = jnp.where(sub < SUB - NEAR, rest_high, hold_fwd[1, kind, layer, :, at])
                cross[8 + plane, :, at] = jnp.where(odd, high, low)
                near[8 + plane, :, at] = jnp.where(odd, low, high)


def halo_tile(cross, near, odd, tile, kind, layer, at):
    is_above = tile < 2
    outer = tile in (0, 3)
    if outer and kind >= 4:
        return None
    plane = 2 * kind + layer + (8 if outer else 0)
    a, b = near[plane, :, at], cross[plane, :, at]
    value = jnp.where(odd, a, b) if is_above else jnp.where(odd, b, a)
    if outer:
        value = turn(value, -LEFT_OVER if is_above else LEFT_OVER, 0)
    return value


def core_tile(fields, eps, fwd, at, kind, layer, cols):
    if kind < 3:
        return fields[kind, layer, at, cols]
    if kind == 3:
        return eps[layer, at, cols]
    return fwd[kind - 4, layer, at, cols]


def pack_tile(load, lane, right):
    total = jnp.zeros((SUB, LANES), F32)
    for kind, width in enumerate(WIDTHS):
        for layer in range(2):
            value = load(kind, layer)
            if value is None:
                continue
            first = FIRST[kind] + HALF * layer
            value = turn(value, first + width if right else first, 1)
            total = jnp.where((lane >= first) & (lane < first + width), value, total)
    return total


def edge_tile(load, kind, lane, n_lanes):
    spot = lane & (HALF - 1)
    total = None
    for layer in range(2):
        low = turn(load(kind, layer, 0), HALF * layer + OUT, 1)
        high = turn(load(kind, layer, n_lanes - 1), HALF * layer + SIDE + OUT, 1)
        value = jnp.where(spot < SIDE, low, high)
        total = value if total is None else jnp.where(lane < HALF, total, value)
    return total


def cols_kernel(fields, eps, fwd, cross, near, base):
    rows, cols = fields.shape[2], fields.shape[3]
    n_lanes = cols // LANES
    lane, odd = lanes(), is_odd("gy")

    def tile(t, carry):
        at = pl.ds(pl.multiple_of(t * SUB, SUB), SUB)
        out_at = pl.ds(pl.multiple_of(t * SUB + PAD, SUB), SUB)

        def load(kind, layer, k):
            return core_tile(fields, eps, fwd, at, kind, layer, lane_tile(k))

        left = pack_tile(lambda kind, layer: load(kind, layer, 0), lane, False)
        right = pack_tile(lambda kind, layer: load(kind, layer, n_lanes - 1), lane, True)
        cross[out_at, :] = jnp.where(odd, right, left)
        near[out_at, :] = jnp.where(odd, left, right)
        for kind in range(4 + STEPS):
            base[kind, out_at, :] = edge_tile(load, kind, lane, n_lanes)
        return carry

    lax.fori_loop(0, rows // SUB, tile, 0, unroll=4)
    zero = jnp.zeros((PAD, LANES), F32)
    for out in (cross, near):
        out[pl.ds(0, PAD), :] = zero
        out[pl.ds(PAD + rows, PAD), :] = zero


def corners_kernel(cross_in, near_in, cross_rows, near_rows, cross, near):
    rows, cols = cross.shape[0] - 2 * PAD, cross_rows.shape[2]
    lane, odd, odd_col = lanes(), is_odd("gx"), is_odd("gy")
    core = pl.ds(PAD, rows)
    cross[core, :] = cross_in[core, :]
    near[core, :] = near_in[core, :]
    for tile in range(4):
        at = pl.ds(tile * SUB if tile < 2 else PAD + rows + (tile - 2) * SUB, SUB)
        left, right = (
            pack_tile(
                lambda kind, layer: halo_tile(
                    cross_rows, near_rows, odd, tile, kind, layer, pl.ds(lo, LANES)
                ),
                lane, is_right,
            )
            for lo, is_right in ((0, False), (cols - LANES, True))
        )
        cross[at, :] = jnp.where(odd_col, right, left)
        near[at, :] = jnp.where(odd_col, left, right)


def prep_kernel(
    capacity, fields, eps, fwd, mon_x, mon_y, amp, mask, owner, cross, near, base, src, src_edge, place, place_edge
):
    cols_kernel(fields, eps, fwd, cross, near, base)
    side_kernel(capacity, fields.shape[2], mon_x, mon_y, amp, mask, owner, src, src_edge, place, place_edge)


def side_kernel(capacity, rows, mon_x, mon_y, amp, mask, owner, src, src_edge, place, place_edge):
    _, _, ext_rows, cols = src.shape
    channels = mon_x.shape[1]
    row = mon_x[...] - lax.axis_index("gx") * rows + PAD
    col = mon_y[...] - lax.axis_index("gy") * cols
    in_left = (col >= -OUT) & (col < OUT)
    in_right = (col >= cols - OUT) & (col < cols + OUT)
    edge = jnp.where(in_left, col + OUT, jnp.where(in_right, col - cols + OUT + SIDE, -LANES))
    layer = lax.broadcasted_iota(jnp.int32, (1, channels), 1) & 1
    edge = edge + HALF * layer
    inside = jnp.where((col >= 0) & (col < cols), col, -1)
    one_y = lax.broadcasted_iota(jnp.int32, (cols, channels), 0) == inside
    one_e = lax.broadcasted_iota(jnp.int32, (LANES, channels), 0) == edge
    one_y = jnp.where(one_y, 1.0, 0.0).astype(BF16)
    one_e = jnp.where(one_e, 1.0, 0.0).astype(BF16)
    one_y = jnp.concatenate([one_y] * 3, axis=1)
    one_e = jnp.concatenate([one_e] * 3, axis=1)
    one_x = lax.broadcasted_iota(jnp.int32, (ext_rows, channels), 0) == row
    one_x = jnp.where(one_x, 1.0, 0.0).astype(F32)
    nt = (((1,), (1,)), ((), ()))
    for step in range(STEPS):
        parts = [part.astype(F32) for part in split3(amp[pl.ds(step, 1), :])]
        lhs = jnp.concatenate([one_x * part for part in parts], axis=1)
        src_edge[step] = lax.dot_general(lhs.astype(BF16), one_e, nt, preferred_element_type=F32)
        layer_wide = jnp.concatenate([layer] * 3, axis=1)
        for which in range(2):
            some = jnp.where(layer_wide == which, lhs, 0.0).astype(BF16)
            src[step, which] = lax.dot_general(some, one_y, nt, preferred_element_type=F32)
    tiles = owner.shape[1]
    own = owner[...].astype(F32)
    own_wide = jnp.broadcast_to(own, (tiles, tiles))
    earlier = lax.broadcasted_iota(jnp.int32, (tiles, tiles), 0) < lax.broadcasted_iota(
        jnp.int32, (tiles, tiles), 1
    )
    same = (own_wide.T == own_wide) & earlier
    slot = jnp.sum(jnp.where(same, 1.0, 0.0), axis=0, keepdims=True)
    dest = owner[...] * capacity + slot.astype(jnp.int32)
    dest = jnp.where(mask[...] != 0, dest, -1)
    hit = lax.broadcasted_iota(jnp.int32, place.shape, 0) == dest
    hit = jnp.where(hit, 1.0, 0.0).astype(BF16)
    place[...] = hit
    tile_cols = cols // TS
    column = lax.broadcasted_iota(jnp.int32, (tiles, 4 * SUB), 1)
    wanted = (column % SUB) * tile_cols + ((column // SUB) & 1) * (tile_cols - 1)
    picked = lax.broadcasted_iota(jnp.int32, (tiles, 4 * SUB), 0) == wanted
    place_edge[...] = dot(hit, jnp.where(picked, 1.0, 0.0).astype(BF16)).astype(BF16)


class Shifts:
    def __init__(self, next_col, prev_col):
        self.next_col, self.prev_col = next_col, prev_col
        self.bottom, self.top = subs() == SUB - 1, subs() == 0

    def up(self, tile):
        return {key: turn(value, -1, 0) for key, value in tile.items()}

    def down(self, tile):
        return {key: turn(value, 1, 0) for key, value in tile.items()}

    def below(self, up_here, up_next):
        return {key: jnp.where(self.bottom, up_next[key], up_here[key]) for key in up_here}

    def above(self, down_here, down_before):
        return {key: jnp.where(self.top, down_before[key], down_here[key]) for key in down_here}


def tile_at(t):
    return (pl.ds(t * SUB, SUB), slice(None))


def first_curl(n_tiles, shifts, load_hx, load_hy, curl):
    before = None
    for t in range(n_tiles):
        hx, hy = load_hx(t), load_hy(t)
        down = shifts.down(hy)
        over = shifts.above(down, before if t else down)
        left = shifts.prev_col(hx)
        for key in hx:
            curl[key + tile_at(t)] = (hy[key] - over[key]) - (hx[key] - left[key])
        before = down


def steps(n_tiles, keys, shifts, e, curl, eps_of, src_of, other):
    no_above = shifts.top & ((lax.axis_index("gx") + subs() * 0) == 0)
    for step in range(STEPS):
        low, high = (0, n_tiles) if step == 0 else (1, n_tiles - 1)

        def load(t):
            return {key: e[(step,) + key + tile_at(t)] for key in keys}

        here = load(low)
        up = shifts.up(here)
        down_before = shifts.down(load(max(low - 1, 0)))
        for t in range(low, high):
            after = load(min(t + 1, n_tiles - 1))
            up_next, down = shifts.up(after), shifts.down(here)
            below, above = shifts.below(up, up_next), shifts.above(down, down_before)
            right, left = shifts.next_col(here), shifts.prev_col(here)
            for key in keys:
                center, over = here[key], above[key]
                if t == PAD // SUB:
                    over = jnp.where(no_above, center, over)
                ring = (below[key] + over) + (right[key] + left[key]) - 4.0 * center
                change = curl[key + tile_at(t)] - COURANT * ring
                if step < STEPS - 1:
                    curl[key + tile_at(t)] = change
                change = change + COUPLING * (other(here, key) - center)
                e[(step + 1,) + key + tile_at(t)] = (
                    center - eps_of(key, t) * change + src_of(step, key, t)
                )
            here, up, down_before = after, up_next, down


def gradient(keys, t, e, change_of):
    result = {}
    for key in keys:
        total = None
        for step in range(STEPS):
            term = e[(step + 1,) + key + tile_at(t)] * change_of(step, key, t)
            total = term if total is None else total + term
        result[key] = -total
    return result


def last_fields(tiles, keys, shifts, e, load_hx, load_hy, store):
    def total(t):
        result = {}
        for key in keys:
            parts = [e[(step,) + key + tile_at(t)] for step in range(STEPS)]
            result[key] = (parts[0] + parts[1]) + (parts[2] + parts[3])
        return result

    here = total(tiles[0])
    up = shifts.up(here)
    for t in tiles:
        after = total(t + 1)
        up_next = shifts.up(after)
        below, right = shifts.below(up, up_next), shifts.next_col(here)
        hx, hy = load_hx(t), load_hy(t)
        for key in keys:
            store(
                key, t, e[(STEPS,) + key + tile_at(t)],
                hx[key] + COURANT * (right[key] - here[key]),
                hy[key] - COURANT * (below[key] - here[key]),
            )
        here, up = after, up_next


def row_pairs(ref, lead, count):
    even = ref[lead + (pl.ds(0, count, stride=PIX), slice(None))]
    return even + ref[lead + (pl.ds(1, count, stride=PIX), slice(None))]


def inner_kernel(
    fields, eps, fwd, cross, near, src, mats, base_in, place, last, slots, base, e, curl, eps_c, g, pooled
):
    rows, cols = fields.shape[2], fields.shape[3]
    n_tiles = (rows + 2 * PAD) // SUB
    n_lanes = cols // LANES
    lane, odd = lanes(), is_odd("gx")
    halo_of = {0: 0, 1: 1, n_tiles - 2: 2, n_tiles - 1: 3}
    keys = [(layer, k) for layer in range(2) for k in range(n_lanes)]

    def load(kind, layer, t, k):
        if t in halo_of:
            return halo_tile(cross, near, odd, halo_of[t], kind, layer, lane_tile(k))
        return core_tile(fields, eps, fwd, pl.ds(t * SUB - PAD, SUB), kind, layer, lane_tile(k))

    def load_all(kind, t):
        return {key: load(kind, key[0], t, key[1]) for key in keys}

    at_end, at_start = lane == LANES - 1, lane == 0

    def next_col(values):
        moved = {key: turn(value, -1, 1) for key, value in values.items()}
        return {
            (l, k): jnp.where(at_end, moved[l, (k + 1) % n_lanes], moved[l, k]) for l, k in keys
        }

    def prev_col(values):
        moved = {key: turn(value, 1, 1) for key, value in values.items()}
        return {
            (l, k): jnp.where(at_start, moved[l, (k - 1) % n_lanes], moved[l, k]) for l, k in keys
        }

    shifts = Shifts(next_col, prev_col)
    for t in range(n_tiles):
        for key in keys:
            e[(0,) + key + tile_at(t)] = load(0, key[0], t, key[1])
            eps_c[key + tile_at(t)] = COURANT * load(3, key[0], t, key[1])
    first_curl(n_tiles, shifts, lambda t: load_all(1, t), lambda t: load_all(2, t), curl)
    steps(
        n_tiles, keys, shifts, e, curl,
        lambda key, t: eps_c[key + tile_at(t)],
        lambda step, key, t: src[step, key[0], pl.ds(t * SUB, SUB), lane_tile(key[1])],
        lambda values, key: values[1 - key[0], key[1]],
    )
    for t in range(1, n_tiles - 1):
        values = gradient(keys, t, e, lambda step, key, t: load(4 + step, key[0], t, key[1]))
        for key in keys:
            g[key + tile_at(t)] = values[key]

    def store(key, t, *values):
        for kind, value in enumerate(values):
            last[(kind,) + key + (pl.ds(t * SUB - PAD, SUB), slice(None))] = value

    last_fields(
        range(PAD // SUB, n_tiles - PAD // SUB), keys, shifts, e,
        lambda t: load_all(1, t), lambda t: load_all(2, t), store,
    )
    for layer in range(2):
        total = None
        for k in range(n_lanes):
            for part in split2(row_pairs(g, (layer, k), n_tiles * SUB // PIX)):
                term = dot(part, mats[k])
                total = term if total is None else total + term
        pooled[layer] = total

    vals = by_tile([cone_filter(pooled.at[layer], rows // PIX, PAD // PIX) for layer in range(2)])
    high, low = split2(vals)
    slots[...] = dot(place[...], high) + dot(place[...], low)

    for t in range(n_tiles):
        for kind in range(4 + STEPS):
            at = pl.ds(t * SUB, SUB)
            if t not in halo_of:
                base[kind, at, :] = base_in[kind, at, :]
            elif kind < 4 or t not in (0, n_tiles - 1):
                base[kind, at, :] = edge_tile(
                    lambda kind, layer, k: load(kind, layer, t, k), kind, lane, n_lanes
                )


def cone_filter(pooled, out_pix, first):
    weights = cone_weights(RADIUS)
    reach = RADIUS - 1
    lane = lax.broadcasted_iota(jnp.int32, (out_pix, LANES), 1)
    at = [pooled[pl.ds(first + s, out_pix), :] for s in range(-reach, reach + 1)]
    sums = [at[reach]] + [at[reach + s] + at[reach - s] for s in range(1, reach + 1)]
    total = None
    for shift in range(reach + 1):
        mixed = None
        for s in range(reach + 1):
            weight = float(weights[reach + s, reach + shift])
            if weight > 0.0:
                term = weight * sums[s]
                mixed = term if mixed is None else mixed + term
        if shift == 0:
            total = mixed
        else:
            total = total + turn(jnp.where(lane < shift, 0.0, mixed), -shift, 1)
            total = total + turn(jnp.where(lane >= LANES - shift, 0.0, mixed), shift, 1)
    return total


def by_tile(blocks):
    span = TS // PIX
    tile_rows = blocks[0].shape[0] // span
    x = jnp.stack([block.reshape(tile_rows, span, LANES) for block in blocks], axis=1)
    x = x.reshape(tile_rows * 2, span, LANES)
    group = lax.broadcasted_iota(jnp.int32, x.shape, 2) // span
    row = lax.broadcasted_iota(jnp.int32, x.shape, 1)
    for bit in (1, 2, 4):
        row_on, lane_on = (row & bit) != 0, (group & bit) != 0
        ahead = turn(turn(x, -bit, 1), bit * span, 2)
        behind = turn(turn(x, bit, 1), -bit * span, 2)
        x = jnp.where(row_on == lane_on, x, jnp.where(lane_on, ahead, behind))
    x = x.reshape(tile_rows, 2, span, LANES)
    even, odd = x[:, 0], x[:, 1]
    upper = lax.broadcasted_iota(jnp.int32, even.shape, 2) >= HALF
    new_even = jnp.where(upper, turn(odd, HALF, 2), even)
    new_odd = jnp.where(upper, odd, turn(even, HALF, 2))
    return jnp.stack([new_even, new_odd], axis=1).reshape(tile_rows * 2 * span, LANES)


def edge_kernel(
    last, slots_in, base, cross, near, src, place, fields, slots, e, first, curl, eps_c, d, g, merged
):
    ext_rows = base.shape[1]
    rows = ext_rows - 2 * PAD
    n_tiles = ext_rows // SUB
    lane, odd = lanes(), is_odd("gy")
    spot = lane & (HALF - 1)
    is_left, is_right = spot < OUT, spot >= HALF - OUT

    for t in range(n_tiles):
        at = pl.ds(t * SUB, SUB)
        far, close = cross[at, :], near[at, :]
        high, low = jnp.where(odd, close, far), jnp.where(odd, far, close)
        for kind, width in enumerate(WIDTHS):
            if kind >= 4 and t in (0, n_tiles - 1):
                continue
            value = jnp.where(is_left, turn(high, OUT - width - FIRST[kind], 1), base[kind, at, :])
            value = jnp.where(is_right, turn(low, HALF - OUT - FIRST[kind], 1), value)
            if kind == 0:
                e[0, at, :] = value
            elif kind < 3:
                first[kind - 1, at, :] = value
            elif kind == 3:
                eps_c[at, :] = COURANT * value
            else:
                d[kind - 4, at, :] = value

    no_left = (spot == OUT) & ((lax.axis_index("gy") + lane * 0) == 0)
    shifts = Shifts(
        lambda values: {(): turn(values[()], -1, 1)},
        lambda values: {(): turn(values[()], 1, 1)},
    )

    def load_hx(t):
        return {(): first[0, pl.ds(t * SUB, SUB), :]}

    def load_hy(t):
        return {(): first[1, pl.ds(t * SUB, SUB), :]}

    first_curl(n_tiles, shifts, load_hx, load_hy, curl)
    shifts.prev_col = lambda values: {(): jnp.where(no_left, values[()], turn(values[()], 1, 1))}
    steps(
        n_tiles, [()], shifts, e, curl,
        lambda key, t: eps_c[pl.ds(t * SUB, SUB), :],
        lambda step, key, t: src[step, pl.ds(t * SUB, SUB), :],
        lambda values, key: turn(values[()], HALF, 1),
    )
    inside = (spot >= OUT - NEAR) & (spot < OUT + KEEP)
    inside = inside | ((spot >= HALF - OUT - KEEP) & (spot < HALF - OUT + NEAR))
    for t in range(1, n_tiles - 1):
        value = gradient([()], t, e, lambda step, key, t: d[step, pl.ds(t * SUB, SUB), :])[()]
        g[pl.ds(t * SUB, SUB), :] = jnp.where(inside, value, 0.0)

    n_lanes = fields.shape[3] // LANES

    def store(key, t, *edges):
        at = pl.ds(t * SUB - PAD, SUB)
        result = {}
        for kind, edge in enumerate(edges):
            for layer in range(2):
                for k in range(n_lanes):
                    value = last[kind, layer, k, at, :]
                    if k == 0:
                        value = jnp.where(lane < KEEP, turn(edge, -HALF * layer - OUT, 1), value)
                    if k == n_lanes - 1:
                        value = jnp.where(
                            lane >= LANES - KEEP, turn(edge, -HALF * layer - SIDE - OUT, 1), value
                        )
                    result[kind, layer, k] = value
        for (kind, layer, k), value in result.items():
            fields[kind, layer, at, lane_tile(k)] = value

    edge_filter(g, merged)
    edge_slots(merged, slots_in, place, slots)
    last_fields(
        range(PAD // SUB, n_tiles - PAD // SUB), [()], shifts, e, load_hx, load_hy, store
    )


def edge_filter(g, merged):
    lane = lanes()
    span, reach = TS // PIX, RADIUS - 1
    pixel = {}
    for j in range(-reach, span + reach):
        value = g[pl.ds(PAD + PIX * j, SUB, stride=TS), :]
        pixel[j] = value + g[pl.ds(PAD + PIX * j + 1, SUB, stride=TS), :]

    weights = cone_weights(RADIUS)
    spans = []
    for row in range(span):
        sums = [pixel[row]] + [pixel[row + s] + pixel[row - s] for s in range(1, reach + 1)]
        move = (row & 1) + SIDE * ((row >> 1) & 1)
        total = None
        for shift in range(reach + 1):
            mixed = None
            for s in range(reach + 1):
                weight = float(weights[reach + s, reach + shift])
                if weight > 0.0:
                    term = weight * sums[s]
                    mixed = term if mixed is None else mixed + term
            for place in {PIX * shift, -PIX * shift}:
                term = turn(mixed, move + place, 1) + turn(mixed, move + place - 1, 1)
                total = term if total is None else total + term
        spans.append(total)
    even = (lane & 1) == 0
    window = ((lane - OUT) & (HALF - 1)) < SIDE
    for n in range(2):
        a, b, c, d = spans[4 * n : 4 * n + 4]
        merged[n] = jnp.where(window, jnp.where(even, a, b), jnp.where(even, c, d))


def edge_slots(merged, slots_in, place, slots):
    lane = lanes()
    span = TS // PIX
    row, pixel = lane // span % span, lane % span
    start = (lane & HALF) + OUT + PIX * pixel + (row & 1) + SIDE * ((row >> 1) & 1)
    edge = []
    for side in range(2):
        index = (start + OUT * side) & (LANES - 1)
        low, high = (jnp.take_along_axis(merged[n], index, axis=1) for n in range(2))
        edge.append(jnp.where(row < span // 2, low, high))
    parts = split2(jnp.concatenate(edge, axis=0))
    slots[...] = slots_in[...] + dot(place[...], jnp.concatenate(parts, axis=0))


def deliver_kernel(fields, slots, out_fields, out_slots, sems):
    copies = [
        pltpu.make_async_copy(fields.at[kind], out_fields.at[kind], sems.at[kind]) for kind in range(3)
    ]
    copies.append(pltpu.make_async_copy(slots, out_slots.at[0], sems.at[3]))
    for copy in copies:
        copy.start()
    for copy in copies:
        copy.wait()


def vmem():
    return pl.BlockSpec(memory_space=pltpu.VMEM)


def shape(*dims, dtype=F32):
    return jax.ShapeDtypeStruct(dims, dtype)


def call(kernel, outs, n_in, *, in_space=pltpu.VMEM, out_specs=None, scratch=(), flops=0, size=0):
    return pl.pallas_call(
        kernel,
        out_shape=outs,
        in_specs=[pl.BlockSpec(memory_space=in_space)] * n_in,
        out_specs=out_specs or tuple(vmem() for _ in outs),
        scratch_shapes=list(scratch),
        compiler_params=pltpu.CompilerParams(vmem_limit_bytes=40 * 1024 * 1024),
        cost_estimate=pl.CostEstimate(flops=flops, bytes_accessed=size, transcendentals=0),
    )


def on_device(adj_fields, inv_eps, fwd_diff, mon_x, mon_y, mon_amp, design_mask, tile_owner):
    rows, cols = adj_fields.shape[2], adj_fields.shape[3]
    assert cols == 2 * LANES and rows % TS == 0
    gx_count, gy_count = lax.axis_size("gx"), lax.axis_size("gy")
    owners = gx_count * gy_count
    tiles = (rows // TS) * (cols // TS)
    width = 2 * (TS // PIX) ** 2
    assert width == LANES
    capacity = max(8, 2 * tiles // owners)
    assert rows == TS * SUB and cols == 2 * TS * SUB
    ext_rows = rows + 2 * PAD
    n_lanes = cols // LANES
    cells = rows * cols
    blocks = (adj_fields, inv_eps, fwd_diff)


    strip = shape(16, SUB, cols)
    cross, near = call(
        rows_kernel, (strip, strip), 3, in_space=pltpu.HBM,
        scratch=(
            pltpu.VMEM((2, 4, 2, PAD, cols), F32),
            pltpu.VMEM((2, STEPS, 2, SUB, cols), F32),
            pltpu.SemaphoreType.DMA((6,)),
        ),
        size=2**20,
    )(*(pltpu.with_memory_space_constraint(block, pltpu.HBM) for block in blocks))

    def pairs(count, start):
        some = [(i, i + 1) for i in range(start, count - 1, 2)]
        return some + [(j, i) for i, j in some]

    cross = lax.ppermute(cross, "gx", pairs(gx_count, 1))
    near = lax.ppermute(near, "gx", pairs(gx_count, 0))

    packed = shape(ext_rows, LANES)
    channels = mon_x.shape[0]
    cross_cols, near_cols, base, src, src_edge, place, place_edge = call(
        lambda *refs: prep_kernel(capacity, *refs),
        (
            packed,
            packed,
            shape(4 + STEPS, ext_rows, LANES),
            shape(STEPS, 2, ext_rows, cols),
            shape(STEPS, ext_rows, LANES),
            shape(owners * capacity, tiles, dtype=BF16),
            shape(owners * capacity, 4 * SUB, dtype=BF16),
        ),
        8,
        flops=16 * ext_rows * (cols + LANES) * 3 * channels,
        size=64 * cells,
    )(
        *blocks,
        mon_x.reshape(1, channels),
        mon_y.reshape(1, channels),
        mon_amp,
        design_mask.reshape(1, tiles),
        tile_owner.reshape(1, tiles),
    )
    cross_cols, near_cols = call(
        corners_kernel, (packed, packed), 4, flops=cells, size=8 * ext_rows * LANES
    )(cross_cols, near_cols, cross, near)
    cross_cols = lax.ppermute(cross_cols, "gy", pairs(gy_count, 1))
    near_cols = lax.ppermute(near_cols, "gy", pairs(gy_count, 0))

    plane = (2, n_lanes, ext_rows, LANES)
    last, slots, base = call(
        inner_kernel,
        (
            shape(3, 2, n_lanes, rows, LANES),
            shape(owners * capacity, width),
            shape(4 + STEPS, ext_rows, LANES),
        ),
        9,
        scratch=(
            pltpu.VMEM((1 + STEPS,) + plane, F32),
            pltpu.VMEM(plane, F32),
            pltpu.VMEM(plane, F32),
            pltpu.VMEM(plane, F32),
            pltpu.VMEM((2, ext_rows // PIX, LANES), F32),
        ),
        flops=200 * cells,
        size=96 * cells,
    )(*blocks, cross, near, src, pool_matrices(), base, place)

    plane = (ext_rows, LANES)
    fields, outgoing = call(
        edge_kernel,
        (pltpu.VMEM((3, 2, rows, cols), F32), pltpu.VMEM((owners * capacity, width), F32)),
        7,
        scratch=(
            pltpu.VMEM((1 + STEPS,) + plane, F32),
            pltpu.VMEM((2,) + plane, F32),
            pltpu.VMEM(plane, F32),
            pltpu.VMEM(plane, F32),
            pltpu.VMEM((STEPS,) + plane, F32),
            pltpu.VMEM(plane, F32),
            pltpu.VMEM((2, SUB, LANES), F32),
        ),
        flops=50 * cells,
        size=16 * cells,
    )(last, slots, base, cross_cols, near_cols, src_edge, place_edge)

    outgoing = outgoing.reshape(owners, capacity, width)
    incoming = lax.all_to_all(outgoing, ("gx", "gy"), split_axis=0, concat_axis=0, tiled=True)
    anywhere = pl.BlockSpec(memory_space=pl.ANY)
    return call(
        deliver_kernel,
        (shape(*fields.shape), shape(1, *incoming.shape)),
        2,
        out_specs=(anywhere, anywhere),
        scratch=(pltpu.SemaphoreType.DMA((4,)),),
        size=16 * cells,
    )(fields, pltpu.with_memory_space_constraint(incoming, pltpu.VMEM))


def solution(mesh):
    placed = (
        P(None, None, ("parts", "gx"), "gy"),
        P(None, ("parts", "gx"), "gy"),
        P(None, None, ("parts", "gx"), "gy"),
        P("parts"),
        P("parts"),
        P(None, "parts"),
        P(("parts", "gx"), "gy", None),
        P(("parts", "gx"), "gy", None, None),
    )
    return jax.shard_map(
        on_device,
        mesh=mesh,
        in_specs=placed,
        out_specs=(
            P(None, None, ("parts", "gx"), "gy"),
            P(("parts", "gx", "gy"), None, None, None),
        ),
        check_vma=False,
    )
```

```python
import jax
import jax.numpy as jnp
import ml_dtypes
import numpy as np
from jax import lax
from jax.experimental import pallas as pl
from jax.experimental.pallas import tpu as pltpu
from jax.sharding import PartitionSpec as P

STEPS = 4
PIX = 2
TS = 16
RADIUS = 4
COURANT = 0.6
COUPLING = 0.25

LANES = 128
SUB = 8
FAR = STEPS + PIX * (RADIUS - 1)
NEAR = PIX * (RADIUS - 1)
LEFT_OVER = FAR - SUB
PAD = 2 * SUB
HALF = LANES // 2
SIDE = HALF // 2
OUT = SIDE // 2
KEEP = 8
F32 = jnp.float32
BF16 = jnp.bfloat16
WIDTHS = (FAR,) * 4 + (NEAR,) * STEPS
FIRST = tuple(sum(WIDTHS[:k]) for k in range(len(WIDTHS)))
assert sum(WIDTHS) <= HALF and FAR <= OUT and STEPS + KEEP <= OUT


def cone_weights(radius):
    reach_cells = radius - 1
    offsets = np.arange(-reach_cells, reach_cells + 1)
    distance = np.sqrt(offsets[:, None] * offsets[:, None] + offsets[None, :] * offsets[None, :])
    weights = np.maximum(radius - distance, 0.0)
    return weights / weights.sum()


def pool_matrices():
    inner = np.zeros((2, LANES, LANES), np.float32)
    for j in range(KEEP, 2 * LANES - KEEP):
        inner[j // LANES, j % LANES, j // PIX] = 1.0
    return inner.astype(ml_dtypes.bfloat16)


def split2(value):
    high = value.astype(BF16)
    return high, (value - high.astype(F32)).astype(BF16)


def split3(value):
    high = value.astype(BF16)
    rest = value - high.astype(F32)
    mid = rest.astype(BF16)
    return high, mid, (rest - mid.astype(F32)).astype(BF16)


def dot(a, b):
    return jnp.dot(a, b, preferred_element_type=F32)


def turn(value, shift, axis):
    size = value.shape[axis]
    return pltpu.roll(value, shift % size, axis) if shift % size else value


def lanes():
    return lax.broadcasted_iota(jnp.int32, (SUB, LANES), 1)


def subs():
    return lax.broadcasted_iota(jnp.int32, (SUB, LANES), 0)


def lane_tile(k):
    return pl.ds(k * LANES, LANES)


def is_odd(axis):
    return ((subs() * 0 + lax.axis_index(axis)) & 1) == 1


def rows_kernel(fields, eps, fwd, cross, near, hold, hold_fwd, sems):
    rows, cols = fields.shape[2], fields.shape[3]
    copies = []
    for n, at in enumerate((0, rows - PAD)):
        at_fwd = 0 if n == 0 else rows - SUB
        pairs = (
            (fields.at[:, :, pl.ds(at, PAD), :], hold.at[n, pl.ds(0, 3)]),
            (eps.at[:, pl.ds(at, PAD), :], hold.at[n, 3]),
            (fwd.at[:, :, pl.ds(at_fwd, SUB), :], hold_fwd.at[n]),
        )
        for m, (src, dst) in enumerate(pairs):
            copies.append(pltpu.make_async_copy(src, dst, sems.at[3 * n + m]))
    for copy in copies:
        copy.start()
    for copy in copies:
        copy.wait()
    odd, sub = is_odd("gx"), subs()
    for kind in range(4):
        for layer in range(2):
            plane = 2 * kind + layer
            for k in range(cols // LANES):
                at = lane_tile(k)
                low = hold[0, kind, layer, pl.ds(0, SUB), at]
                high = hold[1, kind, layer, pl.ds(SUB, SUB), at]
                cross[plane, :, at] = jnp.where(odd, high, low)
                near[plane, :, at] = jnp.where(odd, low, high)
                rest_low = turn(hold[0, kind, layer, pl.ds(SUB, SUB), at], -LEFT_OVER, 0)
                rest_high = turn(hold[1, kind, layer, pl.ds(0, SUB), at], LEFT_OVER, 0)
                low = jnp.where(sub >= NEAR, rest_low, hold_fwd[0, kind, layer, :, at])
                high = jnp.where(sub < SUB - NEAR, rest_high, hold_fwd[1, kind, layer, :, at])
                cross[8 + plane, :, at] = jnp.where(odd, high, low)
                near[8 + plane, :, at] = jnp.where(odd, low, high)


def halo_tile(cross, near, odd, tile, kind, layer, at):
    is_above = tile < 2
    outer = tile in (0, 3)
    if outer and kind >= 4:
        return None
    plane = 2 * kind + layer + (8 if outer else 0)
    a, b = near[plane, :, at], cross[plane, :, at]
    value = jnp.where(odd, a, b) if is_above else jnp.where(odd, b, a)
    if outer:
        value = turn(value, -LEFT_OVER if is_above else LEFT_OVER, 0)
    return value


def core_tile(fields, eps, fwd, at, kind, layer, cols):
    if kind < 3:
        return fields[kind, layer, at, cols]
    if kind == 3:
        return eps[layer, at, cols]
    return fwd[kind - 4, layer, at, cols]


def pack_tile(load, lane, right):
    total = jnp.zeros((SUB, LANES), F32)
    for kind, width in enumerate(WIDTHS):
        for layer in range(2):
            value = load(kind, layer)
            if value is None:
                continue
            first = FIRST[kind] + HALF * layer
            value = turn(value, first + width if right else first, 1)
            total = jnp.where((lane >= first) & (lane < first + width), value, total)
    return total


def edge_tile(load, kind, lane, n_lanes):
    spot = lane & (HALF - 1)
    total = None
    for layer in range(2):
        low = turn(load(kind, layer, 0), HALF * layer + OUT, 1)
        high = turn(load(kind, layer, n_lanes - 1), HALF * layer + SIDE + OUT, 1)
        value = jnp.where(spot < SIDE, low, high)
        total = value if total is None else jnp.where(lane < HALF, total, value)
    return total


def cols_kernel(fields, eps, fwd, cross, near, base):
    rows, cols = fields.shape[2], fields.shape[3]
    n_lanes = cols // LANES
    lane, odd = lanes(), is_odd("gy")

    def tile(t, carry):
        at = pl.ds(pl.multiple_of(t * SUB, SUB), SUB)
        out_at = pl.ds(pl.multiple_of(t * SUB + PAD, SUB), SUB)

        def load(kind, layer, k):
            return core_tile(fields, eps, fwd, at, kind, layer, lane_tile(k))

        left = pack_tile(lambda kind, layer: load(kind, layer, 0), lane, False)
        right = pack_tile(lambda kind, layer: load(kind, layer, n_lanes - 1), lane, True)
        cross[out_at, :] = jnp.where(odd, right, left)
        near[out_at, :] = jnp.where(odd, left, right)
        for kind in range(4 + STEPS):
            base[kind, out_at, :] = edge_tile(load, kind, lane, n_lanes)
        return carry

    lax.fori_loop(0, rows // SUB, tile, 0, unroll=4)
    zero = jnp.zeros((PAD, LANES), F32)
    for out in (cross, near):
        out[pl.ds(0, PAD), :] = zero
        out[pl.ds(PAD + rows, PAD), :] = zero


def corners_kernel(cross_in, near_in, cross_rows, near_rows, cross, near):
    rows, cols = cross.shape[0] - 2 * PAD, cross_rows.shape[2]
    lane, odd, odd_col = lanes(), is_odd("gx"), is_odd("gy")
    core = pl.ds(PAD, rows)
    cross[core, :] = cross_in[core, :]
    near[core, :] = near_in[core, :]
    for tile in range(4):
        at = pl.ds(tile * SUB if tile < 2 else PAD + rows + (tile - 2) * SUB, SUB)
        left, right = (
            pack_tile(
                lambda kind, layer: halo_tile(
                    cross_rows, near_rows, odd, tile, kind, layer, pl.ds(lo, LANES)
                ),
                lane, is_right,
            )
            for lo, is_right in ((0, False), (cols - LANES, True))
        )
        cross[at, :] = jnp.where(odd_col, right, left)
        near[at, :] = jnp.where(odd_col, left, right)


def prep_kernel(
    capacity, fields, eps, fwd, mon_x, mon_y, amp, mask, owner, cross, near, base, src, src_edge, place, place_edge
):
    cols_kernel(fields, eps, fwd, cross, near, base)
    side_kernel(capacity, fields.shape[2], mon_x, mon_y, amp, mask, owner, src, src_edge, place, place_edge)


def side_kernel(capacity, rows, mon_x, mon_y, amp, mask, owner, src, src_edge, place, place_edge):
    _, _, ext_rows, cols = src.shape
    channels = mon_x.shape[1]
    row = mon_x[...] - lax.axis_index("gx") * rows + PAD
    col = mon_y[...] - lax.axis_index("gy") * cols
    in_left = (col >= -OUT) & (col < OUT)
    in_right = (col >= cols - OUT) & (col < cols + OUT)
    edge = jnp.where(in_left, col + OUT, jnp.where(in_right, col - cols + OUT + SIDE, -LANES))
    layer = lax.broadcasted_iota(jnp.int32, (1, channels), 1) & 1
    edge = edge + HALF * layer
    inside = jnp.where((col >= 0) & (col < cols), col, -1)
    one_y = lax.broadcasted_iota(jnp.int32, (cols, channels), 0) == inside
    one_e = lax.broadcasted_iota(jnp.int32, (LANES, channels), 0) == edge
    one_y = jnp.where(one_y, 1.0, 0.0).astype(BF16)
    one_e = jnp.where(one_e, 1.0, 0.0).astype(BF16)
    one_y = jnp.concatenate([one_y] * 3, axis=1)
    one_e = jnp.concatenate([one_e] * 3, axis=1)
    one_x = lax.broadcasted_iota(jnp.int32, (ext_rows, channels), 0) == row
    one_x = jnp.where(one_x, 1.0, 0.0).astype(F32)
    nt = (((1,), (1,)), ((), ()))
    for step in range(STEPS):
        parts = [part.astype(F32) for part in split3(amp[pl.ds(step, 1), :])]
        lhs = jnp.concatenate([one_x * part for part in parts], axis=1)
        src_edge[step] = lax.dot_general(lhs.astype(BF16), one_e, nt, preferred_element_type=F32)
        layer_wide = jnp.concatenate([layer] * 3, axis=1)
        for which in range(2):
            some = jnp.where(layer_wide == which, lhs, 0.0).astype(BF16)
            src[step, which] = lax.dot_general(some, one_y, nt, preferred_element_type=F32)
    tiles = owner.shape[1]
    own = owner[...].astype(F32)
    own_wide = jnp.broadcast_to(own, (tiles, tiles))
    earlier = lax.broadcasted_iota(jnp.int32, (tiles, tiles), 0) < lax.broadcasted_iota(
        jnp.int32, (tiles, tiles), 1
    )
    same = (own_wide.T == own_wide) & earlier
    slot = jnp.sum(jnp.where(same, 1.0, 0.0), axis=0, keepdims=True)
    dest = owner[...] * capacity + slot.astype(jnp.int32)
    dest = jnp.where(mask[...] != 0, dest, -1)
    hit = lax.broadcasted_iota(jnp.int32, place.shape, 0) == dest
    hit = jnp.where(hit, 1.0, 0.0).astype(BF16)
    place[...] = hit
    tile_cols = cols // TS
    column = lax.broadcasted_iota(jnp.int32, (tiles, 4 * SUB), 1)
    wanted = (column % SUB) * tile_cols + ((column // SUB) & 1) * (tile_cols - 1)
    picked = lax.broadcasted_iota(jnp.int32, (tiles, 4 * SUB), 0) == wanted
    place_edge[...] = dot(hit, jnp.where(picked, 1.0, 0.0).astype(BF16)).astype(BF16)


class Shifts:
    def __init__(self, next_col, prev_col):
        self.next_col, self.prev_col = next_col, prev_col
        self.bottom, self.top = subs() == SUB - 1, subs() == 0

    def up(self, tile):
        return {key: turn(value, -1, 0) for key, value in tile.items()}

    def down(self, tile):
        return {key: turn(value, 1, 0) for key, value in tile.items()}

    def below(self, up_here, up_next):
        return {key: jnp.where(self.bottom, up_next[key], up_here[key]) for key in up_here}

    def above(self, down_here, down_before):
        return {key: jnp.where(self.top, down_before[key], down_here[key]) for key in down_here}


def tile_at(t):
    return (pl.ds(t * SUB, SUB), slice(None))


def first_curl(n_tiles, shifts, load_hx, load_hy, curl):
    before = None
    for t in range(n_tiles):
        hx, hy = load_hx(t), load_hy(t)
        down = shifts.down(hy)
        over = shifts.above(down, before if t else down)
        left = shifts.prev_col(hx)
        for key in hx:
            curl[key + tile_at(t)] = (hy[key] - over[key]) - (hx[key] - left[key])
        before = down


def steps(n_tiles, keys, shifts, e, curl, eps_of, src_of, other):
    no_above = shifts.top & ((lax.axis_index("gx") + subs() * 0) == 0)
    for step in range(STEPS):
        low, high = (0, n_tiles) if step == 0 else (1, n_tiles - 1)

        def load(t):
            return {key: e[(step,) + key + tile_at(t)] for key in keys}

        here = load(low)
        up = shifts.up(here)
        down_before = shifts.down(load(max(low - 1, 0)))
        for t in range(low, high):
            after = load(min(t + 1, n_tiles - 1))
            up_next, down = shifts.up(after), shifts.down(here)
            below, above = shifts.below(up, up_next), shifts.above(down, down_before)
            right, left = shifts.next_col(here), shifts.prev_col(here)
            for key in keys:
                center, over = here[key], above[key]
                if t == PAD // SUB:
                    over = jnp.where(no_above, center, over)
                ring = (below[key] + over) + (right[key] + left[key]) - 4.0 * center
                change = curl[key + tile_at(t)] - COURANT * ring
                if step < STEPS - 1:
                    curl[key + tile_at(t)] = change
                change = change + COUPLING * (other(here, key) - center)
                e[(step + 1,) + key + tile_at(t)] = (
                    center - eps_of(key, t) * change + src_of(step, key, t)
                )
            here, up, down_before = after, up_next, down


def gradient(keys, t, e, change_of):
    result = {}
    for key in keys:
        total = None
        for step in range(STEPS):
            term = e[(step + 1,) + key + tile_at(t)] * change_of(step, key, t)
            total = term if total is None else total + term
        result[key] = -total
    return result


def last_fields(tiles, keys, shifts, e, load_hx, load_hy, store):
    def total(t):
        result = {}
        for key in keys:
            parts = [e[(step,) + key + tile_at(t)] for step in range(STEPS)]
            result[key] = (parts[0] + parts[1]) + (parts[2] + parts[3])
        return result

    here = total(tiles[0])
    up = shifts.up(here)
    for t in tiles:
        after = total(t + 1)
        up_next = shifts.up(after)
        below, right = shifts.below(up, up_next), shifts.next_col(here)
        hx, hy = load_hx(t), load_hy(t)
        for key in keys:
            store(
                key, t, e[(STEPS,) + key + tile_at(t)],
                hx[key] + COURANT * (right[key] - here[key]),
                hy[key] - COURANT * (below[key] - here[key]),
            )
        here, up = after, up_next


def row_pairs(ref, lead, count):
    even = ref[lead + (pl.ds(0, count, stride=PIX), slice(None))]
    return even + ref[lead + (pl.ds(1, count, stride=PIX), slice(None))]


def inner_kernel(
    fields, eps, fwd, cross, near, src, mats, base_in, place, last, slots, base, e, curl, eps_c, g, pooled
):
    rows, cols = fields.shape[2], fields.shape[3]
    n_tiles = (rows + 2 * PAD) // SUB
    n_lanes = cols // LANES
    lane, odd = lanes(), is_odd("gx")
    halo_of = {0: 0, 1: 1, n_tiles - 2: 2, n_tiles - 1: 3}
    keys = [(layer, k) for layer in range(2) for k in range(n_lanes)]

    def load(kind, layer, t, k):
        if t in halo_of:
            return halo_tile(cross, near, odd, halo_of[t], kind, layer, lane_tile(k))
        return core_tile(fields, eps, fwd, pl.ds(t * SUB - PAD, SUB), kind, layer, lane_tile(k))

    def load_all(kind, t):
        return {key: load(kind, key[0], t, key[1]) for key in keys}

    at_end, at_start = lane == LANES - 1, lane == 0

    def next_col(values):
        moved = {key: turn(value, -1, 1) for key, value in values.items()}
        return {
            (l, k): jnp.where(at_end, moved[l, (k + 1) % n_lanes], moved[l, k]) for l, k in keys
        }

    def prev_col(values):
        moved = {key: turn(value, 1, 1) for key, value in values.items()}
        return {
            (l, k): jnp.where(at_start, moved[l, (k - 1) % n_lanes], moved[l, k]) for l, k in keys
        }

    shifts = Shifts(next_col, prev_col)
    for t in range(n_tiles):
        for key in keys:
            e[(0,) + key + tile_at(t)] = load(0, key[0], t, key[1])
            eps_c[key + tile_at(t)] = COURANT * load(3, key[0], t, key[1])
    first_curl(n_tiles, shifts, lambda t: load_all(1, t), lambda t: load_all(2, t), curl)
    steps(
        n_tiles, keys, shifts, e, curl,
        lambda key, t: eps_c[key + tile_at(t)],
        lambda step, key, t: src[step, key[0], pl.ds(t * SUB, SUB), lane_tile(key[1])],
        lambda values, key: values[1 - key[0], key[1]],
    )
    for t in range(1, n_tiles - 1):
        values = gradient(keys, t, e, lambda step, key, t: load(4 + step, key[0], t, key[1]))
        for key in keys:
            g[key + tile_at(t)] = values[key]

    def store(key, t, *values):
        for kind, value in enumerate(values):
            last[(kind,) + key + (pl.ds(t * SUB - PAD, SUB), slice(None))] = value

    last_fields(
        range(PAD // SUB, n_tiles - PAD // SUB), keys, shifts, e,
        lambda t: load_all(1, t), lambda t: load_all(2, t), store,
    )
    for layer in range(2):
        total = None
        for k in range(n_lanes):
            for part in split2(row_pairs(g, (layer, k), n_tiles * SUB // PIX)):
                term = dot(part, mats[k])
                total = term if total is None else total + term
        pooled[layer] = total

    vals = by_tile([cone_filter(pooled.at[layer], rows // PIX, PAD // PIX) for layer in range(2)])
    high, low = split2(vals)
    slots[...] = dot(place[...], high) + dot(place[...], low)

    for t in range(n_tiles):
        for kind in range(4 + STEPS):
            at = pl.ds(t * SUB, SUB)
            if t not in halo_of:
                base[kind, at, :] = base_in[kind, at, :]
            elif kind < 4 or t not in (0, n_tiles - 1):
                base[kind, at, :] = edge_tile(
                    lambda kind, layer, k: load(kind, layer, t, k), kind, lane, n_lanes
                )


def cone_filter(pooled, out_pix, first):
    weights = cone_weights(RADIUS)
    reach = RADIUS - 1
    lane = lax.broadcasted_iota(jnp.int32, (out_pix, LANES), 1)
    at = [pooled[pl.ds(first + s, out_pix), :] for s in range(-reach, reach + 1)]
    sums = [at[reach]] + [at[reach + s] + at[reach - s] for s in range(1, reach + 1)]
    total = None
    for shift in range(reach + 1):
        mixed = None
        for s in range(reach + 1):
            weight = float(weights[reach + s, reach + shift])
            if weight > 0.0:
                term = weight * sums[s]
                mixed = term if mixed is None else mixed + term
        if shift == 0:
            total = mixed
        else:
            total = total + turn(jnp.where(lane < shift, 0.0, mixed), -shift, 1)
            total = total + turn(jnp.where(lane >= LANES - shift, 0.0, mixed), shift, 1)
    return total


def by_tile(blocks):
    span = TS // PIX
    tile_rows = blocks[0].shape[0] // span
    x = jnp.stack([block.reshape(tile_rows, span, LANES) for block in blocks], axis=1)
    x = x.reshape(tile_rows * 2, span, LANES)
    group = lax.broadcasted_iota(jnp.int32, x.shape, 2) // span
    row = lax.broadcasted_iota(jnp.int32, x.shape, 1)
    for bit in (1, 2, 4):
        row_on, lane_on = (row & bit) != 0, (group & bit) != 0
        ahead = turn(turn(x, -bit, 1), bit * span, 2)
        behind = turn(turn(x, bit, 1), -bit * span, 2)
        x = jnp.where(row_on == lane_on, x, jnp.where(lane_on, ahead, behind))
    x = x.reshape(tile_rows, 2, span, LANES)
    even, odd = x[:, 0], x[:, 1]
    upper = lax.broadcasted_iota(jnp.int32, even.shape, 2) >= HALF
    new_even = jnp.where(upper, turn(odd, HALF, 2), even)
    new_odd = jnp.where(upper, odd, turn(even, HALF, 2))
    return jnp.stack([new_even, new_odd], axis=1).reshape(tile_rows * 2 * span, LANES)


def from_partner(is_cross, lane):
    next_one = (lax.axis_index("gy") + (0 if is_cross else 1)) & 1
    spot = lane & (HALF - 1)
    start = next_one * (HALF - OUT)
    mine = (spot >= start) & (spot < start + OUT)
    shifts = []
    for kind, width in enumerate(WIDTHS):
        left, right = (OUT - width - FIRST[kind]) % LANES, (HALF - OUT - FIRST[kind]) % LANES
        shifts.append(left + next_one * (right - left))
    return mine, shifts


def edge_cross_kernel(base, cross, result):
    n_tiles = base.shape[1] // SUB
    mine, shifts = from_partner(True, lanes())
    for t in range(n_tiles):
        at = pl.ds(t * SUB, SUB)
        kinds = range(4 if t in (0, n_tiles - 1) else 4 + STEPS)
        values = [
            jnp.where(mine, pltpu.roll(cross[at, :], shifts[kind], 1), base[kind, at, :])
            for kind in kinds
        ]
        for kind in kinds:
            result[kind, at, :] = values[kind]


def edge_kernel(
    slots_in, base, near, src, place, edge_last, slots, e, first, curl, eps_c, d, g, merged
):
    ext_rows = base.shape[1]
    rows = ext_rows - 2 * PAD
    n_tiles = ext_rows // SUB
    lane = lanes()
    spot = lane & (HALF - 1)
    mine, moves = from_partner(False, lane)

    for t in range(n_tiles):
        at = pl.ds(t * SUB, SUB)
        for kind in range(4 if t in (0, n_tiles - 1) else 4 + STEPS):
            value = jnp.where(mine, pltpu.roll(near[at, :], moves[kind], 1), base[kind, at, :])
            if kind == 0:
                e[0, at, :] = value
            elif kind < 3:
                first[kind - 1, at, :] = value
            elif kind == 3:
                eps_c[at, :] = COURANT * value
            else:
                d[kind - 4, at, :] = value

    no_left = (spot == OUT) & ((lax.axis_index("gy") + lane * 0) == 0)
    shifts = Shifts(
        lambda values: {(): turn(values[()], -1, 1)},
        lambda values: {(): turn(values[()], 1, 1)},
    )

    def load_hx(t):
        return {(): first[0, pl.ds(t * SUB, SUB), :]}

    def load_hy(t):
        return {(): first[1, pl.ds(t * SUB, SUB), :]}

    first_curl(n_tiles, shifts, load_hx, load_hy, curl)
    shifts.prev_col = lambda values: {(): jnp.where(no_left, values[()], turn(values[()], 1, 1))}
    steps(
        n_tiles, [()], shifts, e, curl,
        lambda key, t: eps_c[pl.ds(t * SUB, SUB), :],
        lambda step, key, t: src[step, pl.ds(t * SUB, SUB), :],
        lambda values, key: turn(values[()], HALF, 1),
    )
    inside = (spot >= OUT - NEAR) & (spot < OUT + KEEP)
    inside = inside | ((spot >= HALF - OUT - KEEP) & (spot < HALF - OUT + NEAR))
    for t in range(1, n_tiles - 1):
        value = gradient([()], t, e, lambda step, key, t: d[step, pl.ds(t * SUB, SUB), :])[()]
        g[pl.ds(t * SUB, SUB), :] = jnp.where(inside, value, 0.0)

    def store(key, t, *values):
        for kind, value in enumerate(values):
            edge_last[kind, pl.ds(t * SUB - PAD, SUB), :] = value

    edge_filter(g, merged)
    edge_slots(merged, slots_in, place, slots)
    last_fields(
        range(PAD // SUB, n_tiles - PAD // SUB), [()], shifts, e, load_hx, load_hy, store
    )


def edge_filter(g, merged):
    lane = lanes()
    span, reach = TS // PIX, RADIUS - 1
    pixel = {}
    for j in range(-reach, span + reach):
        value = g[pl.ds(PAD + PIX * j, SUB, stride=TS), :]
        pixel[j] = value + g[pl.ds(PAD + PIX * j + 1, SUB, stride=TS), :]

    weights = cone_weights(RADIUS)
    spans = []
    for row in range(span):
        sums = [pixel[row]] + [pixel[row + s] + pixel[row - s] for s in range(1, reach + 1)]
        move = (row & 1) + SIDE * ((row >> 1) & 1)
        total = None
        for shift in range(reach + 1):
            mixed = None
            for s in range(reach + 1):
                weight = float(weights[reach + s, reach + shift])
                if weight > 0.0:
                    term = weight * sums[s]
                    mixed = term if mixed is None else mixed + term
            for place in {PIX * shift, -PIX * shift}:
                term = turn(mixed, move + place, 1) + turn(mixed, move + place - 1, 1)
                total = term if total is None else total + term
        spans.append(total)
    even = (lane & 1) == 0
    window = ((lane - OUT) & (HALF - 1)) < SIDE
    for n in range(2):
        a, b, c, d = spans[4 * n : 4 * n + 4]
        merged[n] = jnp.where(window, jnp.where(even, a, b), jnp.where(even, c, d))


def edge_slots(merged, slots_in, place, slots):
    lane = lanes()
    span = TS // PIX
    row, pixel = lane // span % span, lane % span
    start = (lane & HALF) + OUT + PIX * pixel + (row & 1) + SIDE * ((row >> 1) & 1)
    edge = []
    for side in range(2):
        index = (start + OUT * side) & (LANES - 1)
        low, high = (jnp.take_along_axis(merged[n], index, axis=1) for n in range(2))
        edge.append(jnp.where(row < span // 2, low, high))
    parts = split2(jnp.concatenate(edge, axis=0))
    slots[...] = slots_in[...] + dot(place[...], jnp.concatenate(parts, axis=0))


def deliver_kernel(last, edge_last, slots, out_fields, out_slots, merged, sems):
    rows, cols = merged.shape[2], merged.shape[3]
    n_lanes = cols // LANES
    lane = lanes()
    copies = [pltpu.make_async_copy(slots, out_slots.at[0], sems.at[3])]
    copies[0].start()
    for kind in range(3):
        for t in range(rows // SUB):
            at = pl.ds(t * SUB, SUB)
            edge = edge_last[kind, at, :]
            for layer in range(2):
                for k in range(n_lanes):
                    value = last[kind, layer, k, at, :]
                    if k == 0:
                        value = jnp.where(lane < KEEP, turn(edge, -HALF * layer - OUT, 1), value)
                    if k == n_lanes - 1:
                        value = jnp.where(
                            lane >= LANES - KEEP, turn(edge, -HALF * layer - SIDE - OUT, 1), value
                        )
                    merged[kind, layer, at, lane_tile(k)] = value
        copies.append(pltpu.make_async_copy(merged.at[kind], out_fields.at[kind], sems.at[kind]))
        copies[-1].start()
    for copy in copies:
        copy.wait()


def vmem():
    return pl.BlockSpec(memory_space=pltpu.VMEM)


def shape(*dims, dtype=F32):
    return jax.ShapeDtypeStruct(dims, dtype)


def call(kernel, outs, n_in, *, in_space=pltpu.VMEM, out_specs=None, scratch=(), flops=0, size=0):
    return pl.pallas_call(
        kernel,
        out_shape=outs,
        in_specs=[pl.BlockSpec(memory_space=in_space)] * n_in,
        out_specs=out_specs or tuple(vmem() for _ in outs),
        scratch_shapes=list(scratch),
        compiler_params=pltpu.CompilerParams(vmem_limit_bytes=40 * 1024 * 1024),
        cost_estimate=pl.CostEstimate(flops=flops, bytes_accessed=size, transcendentals=0),
    )


def on_device(adj_fields, inv_eps, fwd_diff, mon_x, mon_y, mon_amp, design_mask, tile_owner):
    rows, cols = adj_fields.shape[2], adj_fields.shape[3]
    assert cols == 2 * LANES and rows % TS == 0
    gx_count, gy_count = lax.axis_size("gx"), lax.axis_size("gy")
    owners = gx_count * gy_count
    tiles = (rows // TS) * (cols // TS)
    width = 2 * (TS // PIX) ** 2
    assert width == LANES
    capacity = max(8, 2 * tiles // owners)
    assert rows == TS * SUB and cols == 2 * TS * SUB
    ext_rows = rows + 2 * PAD
    n_lanes = cols // LANES
    cells = rows * cols
    blocks = (adj_fields, inv_eps, fwd_diff)


    strip = shape(16, SUB, cols)
    cross, near = call(
        rows_kernel, (strip, strip), 3, in_space=pltpu.HBM,
        scratch=(
            pltpu.VMEM((2, 4, 2, PAD, cols), F32),
            pltpu.VMEM((2, STEPS, 2, SUB, cols), F32),
            pltpu.SemaphoreType.DMA((6,)),
        ),
        size=2**20,
    )(*(pltpu.with_memory_space_constraint(block, pltpu.HBM) for block in blocks))

    def pairs(count, start):
        some = [(i, i + 1) for i in range(start, count - 1, 2)]
        return some + [(j, i) for i, j in some]

    cross = lax.ppermute(cross, "gx", pairs(gx_count, 1))
    near = lax.ppermute(near, "gx", pairs(gx_count, 0))

    packed = shape(ext_rows, LANES)
    channels = mon_x.shape[0]
    cross_cols, near_cols, base, src, src_edge, place, place_edge = call(
        lambda *refs: prep_kernel(capacity, *refs),
        (
            packed,
            packed,
            shape(4 + STEPS, ext_rows, LANES),
            shape(STEPS, 2, ext_rows, cols),
            shape(STEPS, ext_rows, LANES),
            shape(owners * capacity, tiles, dtype=BF16),
            shape(owners * capacity, 4 * SUB, dtype=BF16),
        ),
        8,
        flops=16 * ext_rows * (cols + LANES) * 3 * channels,
        size=64 * cells,
    )(
        *blocks,
        mon_x.reshape(1, channels),
        mon_y.reshape(1, channels),
        mon_amp,
        design_mask.reshape(1, tiles),
        tile_owner.reshape(1, tiles),
    )
    cross_cols, near_cols = call(
        corners_kernel, (packed, packed), 4, flops=cells, size=8 * ext_rows * LANES
    )(cross_cols, near_cols, cross, near)
    cross_cols = lax.ppermute(cross_cols, "gy", pairs(gy_count, 1))
    near_cols = lax.ppermute(near_cols, "gy", pairs(gy_count, 0))

    plane = (2, n_lanes, ext_rows, LANES)
    last, slots, base = call(
        inner_kernel,
        (
            shape(3, 2, n_lanes, rows, LANES),
            shape(owners * capacity, width),
            shape(4 + STEPS, ext_rows, LANES),
        ),
        9,
        scratch=(
            pltpu.VMEM((1 + STEPS,) + plane, F32),
            pltpu.VMEM(plane, F32),
            pltpu.VMEM(plane, F32),
            pltpu.VMEM(plane, F32),
            pltpu.VMEM((2, ext_rows // PIX, LANES), F32),
        ),
        flops=200 * cells,
        size=96 * cells,
    )(*blocks, cross, near, src, pool_matrices(), base, place)

    plane = (ext_rows, LANES)
    (base,) = call(
        edge_cross_kernel, (shape(4 + STEPS, *plane),), 2, flops=10 * cells, size=8 * cells
    )(base, cross_cols)
    edge_last, outgoing = call(
        edge_kernel,
        (shape(3, rows, LANES), pltpu.VMEM((owners * capacity, width), F32)),
        5,
        scratch=(
            pltpu.VMEM((1 + STEPS,) + plane, F32),
            pltpu.VMEM((2,) + plane, F32),
            pltpu.VMEM(plane, F32),
            pltpu.VMEM(plane, F32),
            pltpu.VMEM((STEPS,) + plane, F32),
            pltpu.VMEM(plane, F32),
            pltpu.VMEM((2, SUB, LANES), F32),
        ),
        flops=50 * cells,
        size=16 * cells,
    )(slots, base, near_cols, src_edge, place_edge)

    outgoing = outgoing.reshape(owners, capacity, width)
    incoming = lax.all_to_all(outgoing, ("gx", "gy"), split_axis=0, concat_axis=0, tiled=True)
    anywhere = pl.BlockSpec(memory_space=pl.ANY)
    return call(
        deliver_kernel,
        (shape(3, 2, rows, cols), shape(1, *incoming.shape)),
        3,
        out_specs=(anywhere, anywhere),
        scratch=(pltpu.VMEM((3, 2, rows, cols), F32), pltpu.SemaphoreType.DMA((4,))),
        flops=20 * cells,
        size=48 * cells,
    )(last, edge_last, pltpu.with_memory_space_constraint(incoming, pltpu.VMEM))


def solution(mesh):
    placed = (
        P(None, None, ("parts", "gx"), "gy"),
        P(None, ("parts", "gx"), "gy"),
        P(None, None, ("parts", "gx"), "gy"),
        P("parts"),
        P("parts"),
        P(None, "parts"),
        P(("parts", "gx"), "gy", None),
        P(("parts", "gx"), "gy", None, None),
    )
    return jax.shard_map(
        on_device,
        mesh=mesh,
        in_specs=placed,
        out_specs=(
            P(None, None, ("parts", "gx"), "gy"),
            P(("parts", "gx", "gy"), None, None, None),
        ),
        check_vma=False,
    )
```

```python
import jax
import jax.numpy as jnp
import ml_dtypes
import numpy as np
from jax import lax
from jax.experimental import pallas as pl
from jax.experimental.pallas import tpu as pltpu
from jax.sharding import PartitionSpec as P

STEPS = 4
PIX = 2
TS = 16
RADIUS = 4
COURANT = 0.6
COUPLING = 0.25

LANES = 128
SUB = 8
FAR = STEPS + PIX * (RADIUS - 1)
NEAR = PIX * (RADIUS - 1)
LEFT_OVER = FAR - SUB
PAD = 2 * SUB
HALF = LANES // 2
SIDE = HALF // 2
OUT = SIDE // 2
KEEP = 8
F32 = jnp.float32
BF16 = jnp.bfloat16
WIDTHS = (FAR,) * 4 + (NEAR,) * STEPS
FIRST = tuple(sum(WIDTHS[:k]) for k in range(len(WIDTHS)))
assert sum(WIDTHS) <= HALF and FAR <= OUT and STEPS + KEEP <= OUT


def cone_weights(radius):
    reach_cells = radius - 1
    offsets = np.arange(-reach_cells, reach_cells + 1)
    distance = np.sqrt(offsets[:, None] * offsets[:, None] + offsets[None, :] * offsets[None, :])
    weights = np.maximum(radius - distance, 0.0)
    return weights / weights.sum()


def pool_matrices():
    inner = np.zeros((2, LANES, LANES), np.float32)
    for j in range(KEEP, 2 * LANES - KEEP):
        inner[j // LANES, j % LANES, j // PIX] = 1.0
    return inner.astype(ml_dtypes.bfloat16)


def split2(value):
    high = value.astype(BF16)
    return high, (value - high.astype(F32)).astype(BF16)


def split3(value):
    high = value.astype(BF16)
    rest = value - high.astype(F32)
    mid = rest.astype(BF16)
    return high, mid, (rest - mid.astype(F32)).astype(BF16)


def dot(a, b):
    return jnp.dot(a, b, preferred_element_type=F32)


def turn(value, shift, axis):
    size = value.shape[axis]
    return pltpu.roll(value, shift % size, axis) if shift % size else value


def lanes():
    return lax.broadcasted_iota(jnp.int32, (SUB, LANES), 1)


def subs():
    return lax.broadcasted_iota(jnp.int32, (SUB, LANES), 0)


def lane_tile(k):
    return pl.ds(k * LANES, LANES)


def is_odd(axis):
    return ((subs() * 0 + lax.axis_index(axis)) & 1) == 1


def rows_kernel(fields, eps, fwd, cross, near, hold, sems):
    rows, cols = fields.shape[2], fields.shape[3]
    sub = subs()
    odd = lax.axis_index("gx") & 1
    parts = []
    for n, (out, at_end) in enumerate(((cross, odd), (near, 1 - odd))):
        at = pl.ds(pl.multiple_of(at_end * (rows - SUB), SUB), SUB)
        rest = pl.ds(pl.multiple_of(SUB + at_end * (rows - 3 * SUB), SUB), SUB)
        pairs = (
            (fields.at[:, :, rest, :], hold.at[n, pl.ds(0, 3)]),
            (eps.at[:, rest, :], hold.at[n, 3]),
            (fwd.at[:, :, at, :], out.at[pl.ds(4, STEPS)]),
            (fields.at[:, :, at, :], out.at[pl.ds(0, 3)]),
            (eps.at[:, at, :], out.at[3]),
        )
        copies = [
            pltpu.make_async_copy(src, dst, sems.at[len(pairs) * n + m])
            for m, (src, dst) in enumerate(pairs)
        ]
        parts.append((n, out, at_end, copies))
    for group in (slice(0, 3), slice(3, 5)):
        for part in parts:
            for copy in part[3][group]:
                copy.start()
    for n, out, at_end, copies in parts:
        for copy in copies[:3]:
            copy.wait()
        low = (1 - at_end) * NEAR
        rest = (sub >= low) & (sub < low + LEFT_OVER)
        shift = NEAR + at_end * (LEFT_OVER - NEAR)
        for kind in range(4):
            for layer in range(2):
                values = []
                for k in range(cols // LANES):
                    moved = pltpu.roll(hold[n, kind, layer, :, lane_tile(k)], shift, 0)
                    values.append(jnp.where(rest, moved, out[4 + kind, layer, :, lane_tile(k)]))
                for k, value in enumerate(values):
                    out[4 + kind, layer, :, lane_tile(k)] = value
    for part in parts:
        for copy in part[3][3:]:
            copy.wait()


def halo_tile(cross, near, odd, tile, kind, layer, at):
    is_above = tile < 2
    outer = tile in (0, 3)
    if outer and kind >= 4:
        return None
    plane = kind + (4 if outer else 0)
    a, b = near[plane, layer, :, at], cross[plane, layer, :, at]
    value = jnp.where(odd, a, b) if is_above else jnp.where(odd, b, a)
    if outer:
        value = turn(value, -LEFT_OVER if is_above else LEFT_OVER, 0)
    return value


def core_tile(fields, eps, fwd, at, kind, layer, cols):
    if kind < 3:
        return fields[kind, layer, at, cols]
    if kind == 3:
        return eps[layer, at, cols]
    return fwd[kind - 4, layer, at, cols]


def pack_tile(load, lane, right):
    total = jnp.zeros((SUB, LANES), F32)
    for kind, width in enumerate(WIDTHS):
        for layer in range(2):
            value = load(kind, layer)
            if value is None:
                continue
            first = FIRST[kind] + HALF * layer
            value = turn(value, first + width if right else first, 1)
            total = jnp.where((lane >= first) & (lane < first + width), value, total)
    return total


def edge_tile(load, kind, lane, n_lanes):
    spot = lane & (HALF - 1)
    total = None
    for layer in range(2):
        low = turn(load(kind, layer, 0), HALF * layer + OUT, 1)
        high = turn(load(kind, layer, n_lanes - 1), HALF * layer + SIDE + OUT, 1)
        value = jnp.where(spot < SIDE, low, high)
        total = value if total is None else jnp.where(lane < HALF, total, value)
    return total


def cols_kernel(fields, eps, fwd, cross, near, base):
    rows, cols = fields.shape[2], fields.shape[3]
    n_lanes = cols // LANES
    lane, odd = lanes(), is_odd("gy")

    def tile(t, carry):
        at = pl.ds(pl.multiple_of(t * SUB, SUB), SUB)
        out_at = pl.ds(pl.multiple_of(t * SUB + PAD, SUB), SUB)

        def load(kind, layer, k):
            return core_tile(fields, eps, fwd, at, kind, layer, lane_tile(k))

        left = pack_tile(lambda kind, layer: load(kind, layer, 0), lane, False)
        right = pack_tile(lambda kind, layer: load(kind, layer, n_lanes - 1), lane, True)
        cross[out_at, :] = jnp.where(odd, right, left)
        near[out_at, :] = jnp.where(odd, left, right)
        for kind in range(4 + STEPS):
            base[kind, out_at, :] = edge_tile(load, kind, lane, n_lanes)
        return carry

    lax.fori_loop(0, rows // SUB, tile, 0, unroll=4)
    zero = jnp.zeros((PAD, LANES), F32)
    for out in (cross, near):
        out[pl.ds(0, PAD), :] = zero
        out[pl.ds(PAD + rows, PAD), :] = zero


def corners_kernel(cross_in, near_in, cross_rows, near_rows, cross, near):
    rows, cols = cross.shape[0] - 2 * PAD, cross_rows.shape[3]
    lane, odd, odd_col = lanes(), is_odd("gx"), is_odd("gy")
    core = pl.ds(PAD, rows)
    cross[core, :] = cross_in[core, :]
    near[core, :] = near_in[core, :]
    for tile in range(4):
        at = pl.ds(tile * SUB if tile < 2 else PAD + rows + (tile - 2) * SUB, SUB)
        left, right = (
            pack_tile(
                lambda kind, layer: halo_tile(
                    cross_rows, near_rows, odd, tile, kind, layer, pl.ds(lo, LANES)
                ),
                lane, is_right,
            )
            for lo, is_right in ((0, False), (cols - LANES, True))
        )
        cross[at, :] = jnp.where(odd_col, right, left)
        near[at, :] = jnp.where(odd_col, left, right)


def prep_kernel(
    capacity, fields, eps, fwd, mon_x, mon_y, amp, mask, owner, cross, near, base, src, src_edge, place, place_edge
):
    cols_kernel(fields, eps, fwd, cross, near, base)
    side_kernel(capacity, fields.shape[2], mon_x, mon_y, amp, mask, owner, src, src_edge, place, place_edge)


def side_kernel(capacity, rows, mon_x, mon_y, amp, mask, owner, src, src_edge, place, place_edge):
    _, _, ext_rows, cols = src.shape
    channels = mon_x.shape[1]
    row = mon_x[...] - lax.axis_index("gx") * rows + PAD
    col = mon_y[...] - lax.axis_index("gy") * cols
    in_left = (col >= -OUT) & (col < OUT)
    in_right = (col >= cols - OUT) & (col < cols + OUT)
    edge = jnp.where(in_left, col + OUT, jnp.where(in_right, col - cols + OUT + SIDE, -LANES))
    layer = lax.broadcasted_iota(jnp.int32, (1, channels), 1) & 1
    edge = edge + HALF * layer
    inside = jnp.where((col >= 0) & (col < cols), col, -1)
    one_y = lax.broadcasted_iota(jnp.int32, (cols, channels), 0) == inside
    one_e = lax.broadcasted_iota(jnp.int32, (LANES, channels), 0) == edge
    one_y = jnp.where(one_y, 1.0, 0.0).astype(BF16)
    one_e = jnp.where(one_e, 1.0, 0.0).astype(BF16)
    one_y = jnp.concatenate([one_y] * 3, axis=1)
    one_e = jnp.concatenate([one_e] * 3, axis=1)
    one_x = lax.broadcasted_iota(jnp.int32, (ext_rows, channels), 0) == row
    one_x = jnp.where(one_x, 1.0, 0.0).astype(F32)
    nt = (((1,), (1,)), ((), ()))
    for step in range(STEPS):
        parts = [part.astype(F32) for part in split3(amp[pl.ds(step, 1), :])]
        lhs = jnp.concatenate([one_x * part for part in parts], axis=1)
        src_edge[step] = lax.dot_general(lhs.astype(BF16), one_e, nt, preferred_element_type=F32)
        layer_wide = jnp.concatenate([layer] * 3, axis=1)
        for which in range(2):
            some = jnp.where(layer_wide == which, lhs, 0.0).astype(BF16)
            src[step, which] = lax.dot_general(some, one_y, nt, preferred_element_type=F32)
    tiles = owner.shape[1]
    own = owner[...].astype(F32)
    own_wide = jnp.broadcast_to(own, (tiles, tiles))
    earlier = lax.broadcasted_iota(jnp.int32, (tiles, tiles), 0) < lax.broadcasted_iota(
        jnp.int32, (tiles, tiles), 1
    )
    same = (own_wide.T == own_wide) & earlier
    slot = jnp.sum(jnp.where(same, 1.0, 0.0), axis=0, keepdims=True)
    dest = owner[...] * capacity + slot.astype(jnp.int32)
    dest = jnp.where(mask[...] != 0, dest, -1)
    hit = lax.broadcasted_iota(jnp.int32, place.shape, 0) == dest
    hit = jnp.where(hit, 1.0, 0.0).astype(BF16)
    place[...] = hit
    tile_cols = cols // TS
    column = lax.broadcasted_iota(jnp.int32, (tiles, 4 * SUB), 1)
    wanted = (column % SUB) * tile_cols + ((column // SUB) & 1) * (tile_cols - 1)
    picked = lax.broadcasted_iota(jnp.int32, (tiles, 4 * SUB), 0) == wanted
    place_edge[...] = dot(hit, jnp.where(picked, 1.0, 0.0).astype(BF16)).astype(BF16)


class Shifts:
    def __init__(self, next_col, prev_col):
        self.next_col, self.prev_col = next_col, prev_col
        self.bottom, self.top = subs() == SUB - 1, subs() == 0

    def up(self, tile):
        return {key: turn(value, -1, 0) for key, value in tile.items()}

    def down(self, tile):
        return {key: turn(value, 1, 0) for key, value in tile.items()}

    def below(self, up_here, up_next):
        return {key: jnp.where(self.bottom, up_next[key], up_here[key]) for key in up_here}

    def above(self, down_here, down_before):
        return {key: jnp.where(self.top, down_before[key], down_here[key]) for key in down_here}


def tile_at(t):
    return (pl.ds(t * SUB, SUB), slice(None))


def first_curl(n_tiles, shifts, load_hx, load_hy, curl):
    before = None
    for t in range(n_tiles):
        hx, hy = load_hx(t), load_hy(t)
        down = shifts.down(hy)
        over = shifts.above(down, before if t else down)
        left = shifts.prev_col(hx)
        for key in hx:
            curl[key + tile_at(t)] = (hy[key] - over[key]) - (hx[key] - left[key])
        before = down


def steps(n_tiles, keys, shifts, e, curl, eps_of, src_of, other):
    no_above = shifts.top & ((lax.axis_index("gx") + subs() * 0) == 0)
    for step in range(STEPS):
        low, high = (0, n_tiles) if step == 0 else (1, n_tiles - 1)

        def load(t):
            return {key: e[(step,) + key + tile_at(t)] for key in keys}

        here = load(low)
        up = shifts.up(here)
        down_before = shifts.down(load(max(low - 1, 0)))
        for t in range(low, high):
            after = load(min(t + 1, n_tiles - 1))
            up_next, down = shifts.up(after), shifts.down(here)
            below, above = shifts.below(up, up_next), shifts.above(down, down_before)
            right, left = shifts.next_col(here), shifts.prev_col(here)
            for key in keys:
                center, over = here[key], above[key]
                if t == PAD // SUB:
                    over = jnp.where(no_above, center, over)
                ring = (below[key] + over) + (right[key] + left[key]) - 4.0 * center
                change = curl[key + tile_at(t)] - COURANT * ring
                if step < STEPS - 1:
                    curl[key + tile_at(t)] = change
                change = change + COUPLING * (other(here, key) - center)
                e[(step + 1,) + key + tile_at(t)] = (
                    center - eps_of(key, t) * change + src_of(step, key, t)
                )
            here, up, down_before = after, up_next, down


def gradient(keys, t, e, change_of):
    result = {}
    for key in keys:
        total = None
        for step in range(STEPS):
            term = e[(step + 1,) + key + tile_at(t)] * change_of(step, key, t)
            total = term if total is None else total + term
        result[key] = -total
    return result


def last_fields(tiles, keys, shifts, e, load_hx, load_hy, store):
    def total(t):
        result = {}
        for key in keys:
            parts = [e[(step,) + key + tile_at(t)] for step in range(STEPS)]
            result[key] = (parts[0] + parts[1]) + (parts[2] + parts[3])
        return result

    here = total(tiles[0])
    up = shifts.up(here)
    for t in tiles:
        after = total(t + 1)
        up_next = shifts.up(after)
        below, right = shifts.below(up, up_next), shifts.next_col(here)
        hx, hy = load_hx(t), load_hy(t)
        for key in keys:
            store(
                key, t, e[(STEPS,) + key + tile_at(t)],
                hx[key] + COURANT * (right[key] - here[key]),
                hy[key] - COURANT * (below[key] - here[key]),
            )
        here, up = after, up_next


def row_pairs(ref, lead, count):
    even = ref[lead + (pl.ds(0, count, stride=PIX), slice(None))]
    return even + ref[lead + (pl.ds(1, count, stride=PIX), slice(None))]


def inner_kernel(
    fields, eps, fwd, cross, near, src, mats, base_in, place, last, slots, base, e, curl, eps_c, g, pooled
):
    rows, cols = fields.shape[2], fields.shape[3]
    n_tiles = (rows + 2 * PAD) // SUB
    n_lanes = cols // LANES
    lane, odd = lanes(), is_odd("gx")
    halo_of = {0: 0, 1: 1, n_tiles - 2: 2, n_tiles - 1: 3}
    keys = [(layer, k) for layer in range(2) for k in range(n_lanes)]

    def load(kind, layer, t, k):
        if t in halo_of:
            return halo_tile(cross, near, odd, halo_of[t], kind, layer, lane_tile(k))
        return core_tile(fields, eps, fwd, pl.ds(t * SUB - PAD, SUB), kind, layer, lane_tile(k))

    def load_all(kind, t):
        return {key: load(kind, key[0], t, key[1]) for key in keys}

    at_end, at_start = lane == LANES - 1, lane == 0

    def next_col(values):
        moved = {key: turn(value, -1, 1) for key, value in values.items()}
        return {
            (l, k): jnp.where(at_end, moved[l, (k + 1) % n_lanes], moved[l, k]) for l, k in keys
        }

    def prev_col(values):
        moved = {key: turn(value, 1, 1) for key, value in values.items()}
        return {
            (l, k): jnp.where(at_start, moved[l, (k - 1) % n_lanes], moved[l, k]) for l, k in keys
        }

    shifts = Shifts(next_col, prev_col)
    for t in range(n_tiles):
        for key in keys:
            e[(0,) + key + tile_at(t)] = load(0, key[0], t, key[1])
            eps_c[key + tile_at(t)] = COURANT * load(3, key[0], t, key[1])
    first_curl(n_tiles, shifts, lambda t: load_all(1, t), lambda t: load_all(2, t), curl)
    steps(
        n_tiles, keys, shifts, e, curl,
        lambda key, t: eps_c[key + tile_at(t)],
        lambda step, key, t: src[step, key[0], pl.ds(t * SUB, SUB), lane_tile(key[1])],
        lambda values, key: values[1 - key[0], key[1]],
    )
    for t in range(1, n_tiles - 1):
        values = gradient(keys, t, e, lambda step, key, t: load(4 + step, key[0], t, key[1]))
        for key in keys:
            g[key + tile_at(t)] = values[key]

    def store(key, t, *values):
        for kind, value in enumerate(values):
            last[(kind,) + key + (pl.ds(t * SUB - PAD, SUB), slice(None))] = value

    last_fields(
        range(PAD // SUB, n_tiles - PAD // SUB), keys, shifts, e,
        lambda t: load_all(1, t), lambda t: load_all(2, t), store,
    )
    for layer in range(2):
        total = None
        for k in range(n_lanes):
            for part in split2(row_pairs(g, (layer, k), n_tiles * SUB // PIX)):
                term = dot(part, mats[k])
                total = term if total is None else total + term
        pooled[layer] = total

    vals = by_tile([cone_filter(pooled.at[layer], rows // PIX, PAD // PIX) for layer in range(2)])
    high, low = split2(vals)
    slots[...] = dot(place[...], high) + dot(place[...], low)

    for t in range(n_tiles):
        for kind in range(4 + STEPS):
            at = pl.ds(t * SUB, SUB)
            if t not in halo_of:
                base[kind, at, :] = base_in[kind, at, :]
            elif kind < 4 or t not in (0, n_tiles - 1):
                base[kind, at, :] = edge_tile(
                    lambda kind, layer, k: load(kind, layer, t, k), kind, lane, n_lanes
                )


def cone_filter(pooled, out_pix, first):
    weights = cone_weights(RADIUS)
    reach = RADIUS - 1
    lane = lax.broadcasted_iota(jnp.int32, (out_pix, LANES), 1)
    at = [pooled[pl.ds(first + s, out_pix), :] for s in range(-reach, reach + 1)]
    sums = [at[reach]] + [at[reach + s] + at[reach - s] for s in range(1, reach + 1)]
    total = None
    for shift in range(reach + 1):
        mixed = None
        for s in range(reach + 1):
            weight = float(weights[reach + s, reach + shift])
            if weight > 0.0:
                term = weight * sums[s]
                mixed = term if mixed is None else mixed + term
        if shift == 0:
            total = mixed
        else:
            total = total + turn(jnp.where(lane < shift, 0.0, mixed), -shift, 1)
            total = total + turn(jnp.where(lane >= LANES - shift, 0.0, mixed), shift, 1)
    return total


def by_tile(blocks):
    span = TS // PIX
    tile_rows = blocks[0].shape[0] // span
    x = jnp.stack([block.reshape(tile_rows, span, LANES) for block in blocks], axis=1)
    x = x.reshape(tile_rows * 2, span, LANES)
    group = lax.broadcasted_iota(jnp.int32, x.shape, 2) // span
    row = lax.broadcasted_iota(jnp.int32, x.shape, 1)
    for bit in (1, 2, 4):
        row_on, lane_on = (row & bit) != 0, (group & bit) != 0
        ahead = turn(turn(x, -bit, 1), bit * span, 2)
        behind = turn(turn(x, bit, 1), -bit * span, 2)
        x = jnp.where(row_on == lane_on, x, jnp.where(lane_on, ahead, behind))
    x = x.reshape(tile_rows, 2, span, LANES)
    even, odd = x[:, 0], x[:, 1]
    upper = lax.broadcasted_iota(jnp.int32, even.shape, 2) >= HALF
    new_even = jnp.where(upper, turn(odd, HALF, 2), even)
    new_odd = jnp.where(upper, odd, turn(even, HALF, 2))
    return jnp.stack([new_even, new_odd], axis=1).reshape(tile_rows * 2 * span, LANES)


def from_partner(is_cross, lane):
    next_one = (lax.axis_index("gy") + (0 if is_cross else 1)) & 1
    spot = lane & (HALF - 1)
    start = next_one * (HALF - OUT)
    mine = (spot >= start) & (spot < start + OUT)
    shifts = []
    for kind, width in enumerate(WIDTHS):
        left, right = (OUT - width - FIRST[kind]) % LANES, (HALF - OUT - FIRST[kind]) % LANES
        shifts.append(left + next_one * (right - left))
    return mine, shifts


def edge_cross_kernel(base, cross, result):
    n_tiles = base.shape[1] // SUB
    mine, shifts = from_partner(True, lanes())
    for t in range(n_tiles):
        at = pl.ds(t * SUB, SUB)
        kinds = range(4 if t in (0, n_tiles - 1) else 4 + STEPS)
        values = [
            jnp.where(mine, pltpu.roll(cross[at, :], shifts[kind], 1), base[kind, at, :])
            for kind in kinds
        ]
        for kind in kinds:
            result[kind, at, :] = values[kind]


def edge_kernel(
    slots_in, base, near, src, place, edge_last, slots, e, first, curl, eps_c, d, g, merged
):
    ext_rows = base.shape[1]
    rows = ext_rows - 2 * PAD
    n_tiles = ext_rows // SUB
    lane = lanes()
    spot = lane & (HALF - 1)
    mine, moves = from_partner(False, lane)

    for t in range(n_tiles):
        at = pl.ds(t * SUB, SUB)
        for kind in range(4 if t in (0, n_tiles - 1) else 4 + STEPS):
            value = jnp.where(mine, pltpu.roll(near[at, :], moves[kind], 1), base[kind, at, :])
            if kind == 0:
                e[0, at, :] = value
            elif kind < 3:
                first[kind - 1, at, :] = value
            elif kind == 3:
                eps_c[at, :] = COURANT * value
            else:
                d[kind - 4, at, :] = value

    no_left = (spot == OUT) & ((lax.axis_index("gy") + lane * 0) == 0)
    shifts = Shifts(
        lambda values: {(): turn(values[()], -1, 1)},
        lambda values: {(): turn(values[()], 1, 1)},
    )

    def load_hx(t):
        return {(): first[0, pl.ds(t * SUB, SUB), :]}

    def load_hy(t):
        return {(): first[1, pl.ds(t * SUB, SUB), :]}

    first_curl(n_tiles, shifts, load_hx, load_hy, curl)
    shifts.prev_col = lambda values: {(): jnp.where(no_left, values[()], turn(values[()], 1, 1))}
    steps(
        n_tiles, [()], shifts, e, curl,
        lambda key, t: eps_c[pl.ds(t * SUB, SUB), :],
        lambda step, key, t: src[step, pl.ds(t * SUB, SUB), :],
        lambda values, key: turn(values[()], HALF, 1),
    )
    inside = (spot >= OUT - NEAR) & (spot < OUT + KEEP)
    inside = inside | ((spot >= HALF - OUT - KEEP) & (spot < HALF - OUT + NEAR))
    for t in range(1, n_tiles - 1):
        value = gradient([()], t, e, lambda step, key, t: d[step, pl.ds(t * SUB, SUB), :])[()]
        g[pl.ds(t * SUB, SUB), :] = jnp.where(inside, value, 0.0)

    def store(key, t, *values):
        for kind, value in enumerate(values):
            edge_last[kind, pl.ds(t * SUB - PAD, SUB), :] = value

    edge_filter(g, merged)
    edge_slots(merged, slots_in, place, slots)
    last_fields(
        range(PAD // SUB, n_tiles - PAD // SUB), [()], shifts, e, load_hx, load_hy, store
    )


def edge_filter(g, merged):
    lane = lanes()
    span, reach = TS // PIX, RADIUS - 1
    pixel = {}
    for j in range(-reach, span + reach):
        value = g[pl.ds(PAD + PIX * j, SUB, stride=TS), :]
        pixel[j] = value + g[pl.ds(PAD + PIX * j + 1, SUB, stride=TS), :]

    weights = cone_weights(RADIUS)
    spans = []
    for row in range(span):
        sums = [pixel[row]] + [pixel[row + s] + pixel[row - s] for s in range(1, reach + 1)]
        move = (row & 1) + SIDE * ((row >> 1) & 1)
        total = None
        for shift in range(reach + 1):
            mixed = None
            for s in range(reach + 1):
                weight = float(weights[reach + s, reach + shift])
                if weight > 0.0:
                    term = weight * sums[s]
                    mixed = term if mixed is None else mixed + term
            for place in {PIX * shift, -PIX * shift}:
                term = turn(mixed, move + place, 1) + turn(mixed, move + place - 1, 1)
                total = term if total is None else total + term
        spans.append(total)
    even = (lane & 1) == 0
    window = ((lane - OUT) & (HALF - 1)) < SIDE
    for n in range(2):
        a, b, c, d = spans[4 * n : 4 * n + 4]
        merged[n] = jnp.where(window, jnp.where(even, a, b), jnp.where(even, c, d))


def edge_slots(merged, slots_in, place, slots):
    lane = lanes()
    span = TS // PIX
    row, pixel = lane // span % span, lane % span
    start = (lane & HALF) + OUT + PIX * pixel + (row & 1) + SIDE * ((row >> 1) & 1)
    edge = []
    for side in range(2):
        index = (start + OUT * side) & (LANES - 1)
        low, high = (jnp.take_along_axis(merged[n], index, axis=1) for n in range(2))
        edge.append(jnp.where(row < span // 2, low, high))
    parts = split2(jnp.concatenate(edge, axis=0))
    slots[...] = slots_in[...] + dot(place[...], jnp.concatenate(parts, axis=0))


def deliver_kernel(last, edge_last, slots, out_fields, out_slots, merged, sems):
    rows, cols = merged.shape[2], merged.shape[3]
    n_lanes = cols // LANES
    lane = lanes()
    copies = [pltpu.make_async_copy(slots, out_slots.at[0], sems.at[6])]
    copies[0].start()
    for kind in range(3):
        for layer in range(2):
            for t in range(rows // SUB):
                at = pl.ds(t * SUB, SUB)
                edge = edge_last[kind, at, :]
                for k in range(n_lanes):
                    value = last[kind, layer, k, at, :]
                    if k == 0:
                        value = jnp.where(lane < KEEP, turn(edge, -HALF * layer - OUT, 1), value)
                    if k == n_lanes - 1:
                        value = jnp.where(
                            lane >= LANES - KEEP, turn(edge, -HALF * layer - SIDE - OUT, 1), value
                        )
                    merged[kind, layer, at, lane_tile(k)] = value
            copies.append(
                pltpu.make_async_copy(
                    merged.at[kind, layer], out_fields.at[kind, layer], sems.at[2 * kind + layer]
                )
            )
            copies[-1].start()
    for copy in copies:
        copy.wait()


def vmem():
    return pl.BlockSpec(memory_space=pltpu.VMEM)


def shape(*dims, dtype=F32):
    return jax.ShapeDtypeStruct(dims, dtype)


def call(kernel, outs, n_in, *, in_space=pltpu.VMEM, out_specs=None, scratch=(), flops=0, size=0):
    return pl.pallas_call(
        kernel,
        out_shape=outs,
        in_specs=[pl.BlockSpec(memory_space=in_space)] * n_in,
        out_specs=out_specs or tuple(vmem() for _ in outs),
        scratch_shapes=list(scratch),
        compiler_params=pltpu.CompilerParams(vmem_limit_bytes=40 * 1024 * 1024),
        cost_estimate=pl.CostEstimate(flops=flops, bytes_accessed=size, transcendentals=0),
    )


def on_device(adj_fields, inv_eps, fwd_diff, mon_x, mon_y, mon_amp, design_mask, tile_owner):
    rows, cols = adj_fields.shape[2], adj_fields.shape[3]
    assert cols == 2 * LANES and rows % TS == 0
    gx_count, gy_count = lax.axis_size("gx"), lax.axis_size("gy")
    owners = gx_count * gy_count
    tiles = (rows // TS) * (cols // TS)
    width = 2 * (TS // PIX) ** 2
    assert width == LANES
    capacity = max(8, 2 * tiles // owners)
    assert rows == TS * SUB and cols == 2 * TS * SUB
    ext_rows = rows + 2 * PAD
    n_lanes = cols // LANES
    cells = rows * cols
    blocks = (adj_fields, inv_eps, fwd_diff)


    strip = shape(4 + STEPS, 2, SUB, cols)
    cross, near = call(
        rows_kernel, (strip, strip), 3, in_space=pltpu.HBM,
        scratch=(
            pltpu.VMEM((2, 4, 2, SUB, cols), F32),
            pltpu.SemaphoreType.DMA((10,)),
        ),
        size=2**20,
    )(*(pltpu.with_memory_space_constraint(block, pltpu.HBM) for block in blocks))

    def pairs(count, start):
        some = [(i, i + 1) for i in range(start, count - 1, 2)]
        return some + [(j, i) for i, j in some]

    cross = lax.ppermute(cross, "gx", pairs(gx_count, 1))
    near = lax.ppermute(near, "gx", pairs(gx_count, 0))

    packed = shape(ext_rows, LANES)
    channels = mon_x.shape[0]
    cross_cols, near_cols, base, src, src_edge, place, place_edge = call(
        lambda *refs: prep_kernel(capacity, *refs),
        (
            packed,
            packed,
            shape(4 + STEPS, ext_rows, LANES),
            shape(STEPS, 2, ext_rows, cols),
            shape(STEPS, ext_rows, LANES),
            shape(owners * capacity, tiles, dtype=BF16),
            shape(owners * capacity, 4 * SUB, dtype=BF16),
        ),
        8,
        flops=16 * ext_rows * (cols + LANES) * 3 * channels,
        size=64 * cells,
    )(
        *blocks,
        mon_x.reshape(1, channels),
        mon_y.reshape(1, channels),
        mon_amp,
        design_mask.reshape(1, tiles),
        tile_owner.reshape(1, tiles),
    )
    cross_cols, near_cols = call(
        corners_kernel, (packed, packed), 4, flops=cells, size=8 * ext_rows * LANES
    )(cross_cols, near_cols, cross, near)
    cross_cols = lax.ppermute(cross_cols, "gy", pairs(gy_count, 1))
    near_cols = lax.ppermute(near_cols, "gy", pairs(gy_count, 0))

    plane = (2, n_lanes, ext_rows, LANES)
    last, slots, base = call(
        inner_kernel,
        (
            shape(3, 2, n_lanes, rows, LANES),
            shape(owners * capacity, width),
            shape(4 + STEPS, ext_rows, LANES),
        ),
        9,
        scratch=(
            pltpu.VMEM((1 + STEPS,) + plane, F32),
            pltpu.VMEM(plane, F32),
            pltpu.VMEM(plane, F32),
            pltpu.VMEM(plane, F32),
            pltpu.VMEM((2, ext_rows // PIX, LANES), F32),
        ),
        flops=200 * cells,
        size=96 * cells,
    )(*blocks, cross, near, src, pool_matrices(), base, place)

    plane = (ext_rows, LANES)
    (base,) = call(
        edge_cross_kernel, (shape(4 + STEPS, *plane),), 2, flops=10 * cells, size=8 * cells
    )(base, cross_cols)
    edge_last, outgoing = call(
        edge_kernel,
        (shape(3, rows, LANES), pltpu.VMEM((owners * capacity, width), F32)),
        5,
        scratch=(
            pltpu.VMEM((1 + STEPS,) + plane, F32),
            pltpu.VMEM((2,) + plane, F32),
            pltpu.VMEM(plane, F32),
            pltpu.VMEM(plane, F32),
            pltpu.VMEM((STEPS,) + plane, F32),
            pltpu.VMEM(plane, F32),
            pltpu.VMEM((2, SUB, LANES), F32),
        ),
        flops=50 * cells,
        size=16 * cells,
    )(slots, base, near_cols, src_edge, place_edge)

    outgoing = outgoing.reshape(owners, capacity, width)
    incoming = lax.all_to_all(outgoing, ("gx", "gy"), split_axis=0, concat_axis=0, tiled=True)
    anywhere = pl.BlockSpec(memory_space=pl.ANY)
    return call(
        deliver_kernel,
        (shape(3, 2, rows, cols), shape(1, *incoming.shape)),
        3,
        out_specs=(anywhere, anywhere),
        scratch=(pltpu.VMEM((3, 2, rows, cols), F32), pltpu.SemaphoreType.DMA((7,))),
        flops=20 * cells,
        size=48 * cells,
    )(last, edge_last, pltpu.with_memory_space_constraint(incoming, pltpu.VMEM))


def solution(mesh):
    placed = (
        P(None, None, ("parts", "gx"), "gy"),
        P(None, ("parts", "gx"), "gy"),
        P(None, None, ("parts", "gx"), "gy"),
        P("parts"),
        P("parts"),
        P(None, "parts"),
        P(("parts", "gx"), "gy", None),
        P(("parts", "gx"), "gy", None, None),
    )
    return jax.shard_map(
        on_device,
        mesh=mesh,
        in_specs=placed,
        out_specs=(
            P(None, None, ("parts", "gx"), "gy"),
            P(("parts", "gx", "gy"), None, None, None),
        ),
        check_vma=False,
    )
```

```python
import jax
import jax.numpy as jnp
import ml_dtypes
import numpy as np
from jax import lax
from jax.experimental import pallas as pl
from jax.experimental.pallas import tpu as pltpu
from jax.sharding import PartitionSpec as P

STEPS = 4
PIX = 2
TS = 16
RADIUS = 4
COURANT = 0.6
COUPLING = 0.25

LANES = 128
SUB = 8
FAR = STEPS + PIX * (RADIUS - 1)
NEAR = PIX * (RADIUS - 1)
LEFT_OVER = FAR - SUB
PAD = 2 * SUB
HALF = LANES // 2
SIDE = HALF // 2
OUT = SIDE // 2
KEEP = 8
F32 = jnp.float32
BF16 = jnp.bfloat16
WIDTHS = (FAR,) * 4 + (NEAR,) * STEPS
FIRST = tuple(sum(WIDTHS[:k]) for k in range(len(WIDTHS)))
assert sum(WIDTHS) <= HALF and FAR <= OUT and STEPS + KEEP <= OUT


def cone_weights(radius):
    reach_cells = radius - 1
    offsets = np.arange(-reach_cells, reach_cells + 1)
    distance = np.sqrt(offsets[:, None] * offsets[:, None] + offsets[None, :] * offsets[None, :])
    weights = np.maximum(radius - distance, 0.0)
    return weights / weights.sum()


def pool_matrices():
    inner = np.zeros((2, LANES, LANES), np.float32)
    for j in range(KEEP, 2 * LANES - KEEP):
        inner[j // LANES, j % LANES, j // PIX] = 1.0
    return inner.astype(ml_dtypes.bfloat16)


def split2(value):
    high = value.astype(BF16)
    return high, (value - high.astype(F32)).astype(BF16)


def split3(value):
    high = value.astype(BF16)
    rest = value - high.astype(F32)
    mid = rest.astype(BF16)
    return high, mid, (rest - mid.astype(F32)).astype(BF16)


def dot(a, b):
    return jnp.dot(a, b, preferred_element_type=F32)


def turn(value, shift, axis):
    size = value.shape[axis]
    return pltpu.roll(value, shift % size, axis) if shift % size else value


def lanes():
    return lax.broadcasted_iota(jnp.int32, (SUB, LANES), 1)


def subs():
    return lax.broadcasted_iota(jnp.int32, (SUB, LANES), 0)


def lane_tile(k):
    return pl.ds(k * LANES, LANES)


def is_odd(axis):
    return ((subs() * 0 + lax.axis_index(axis)) & 1) == 1


def rows_kernel(fields, eps, fwd, cross, near, hold, sems):
    rows, cols = fields.shape[2], fields.shape[3]
    sub = subs()
    odd = lax.axis_index("gx") & 1
    parts = []
    for n, (out, at_end) in enumerate(((cross, odd), (near, 1 - odd))):
        at = pl.ds(pl.multiple_of(at_end * (rows - SUB), SUB), SUB)
        rest = pl.ds(pl.multiple_of(SUB + at_end * (rows - 3 * SUB), SUB), SUB)
        pairs = (
            (fields.at[:, :, rest, :], hold.at[n, pl.ds(0, 3)]),
            (eps.at[:, rest, :], hold.at[n, 3]),
            (fwd.at[:, :, at, :], out.at[pl.ds(4, STEPS)]),
            (fields.at[:, :, at, :], out.at[pl.ds(0, 3)]),
            (eps.at[:, at, :], out.at[3]),
        )
        copies = [
            pltpu.make_async_copy(src, dst, sems.at[len(pairs) * n + m])
            for m, (src, dst) in enumerate(pairs)
        ]
        parts.append((n, out, at_end, copies))
    for group in (slice(0, 3), slice(3, 5)):
        for part in parts:
            for copy in part[3][group]:
                copy.start()
    for n, out, at_end, copies in parts:
        for copy in copies[:3]:
            copy.wait()
        low = (1 - at_end) * NEAR
        rest = (sub >= low) & (sub < low + LEFT_OVER)
        shift = NEAR + at_end * (LEFT_OVER - NEAR)
        for kind in range(4):
            for layer in range(2):
                values = []
                for k in range(cols // LANES):
                    moved = pltpu.roll(hold[n, kind, layer, :, lane_tile(k)], shift, 0)
                    values.append(jnp.where(rest, moved, out[4 + kind, layer, :, lane_tile(k)]))
                for k, value in enumerate(values):
                    out[4 + kind, layer, :, lane_tile(k)] = value
    for part in parts:
        for copy in part[3][3:]:
            copy.wait()


def halo_tile(cross, near, odd, tile, kind, layer, at):
    is_above = tile < 2
    outer = tile in (0, 3)
    if outer and kind >= 4:
        return None
    plane = kind + (4 if outer else 0)
    a, b = near[plane, layer, :, at], cross[plane, layer, :, at]
    value = jnp.where(odd, a, b) if is_above else jnp.where(odd, b, a)
    if outer:
        value = turn(value, -LEFT_OVER if is_above else LEFT_OVER, 0)
    return value


def core_tile(fields, eps, fwd, at, kind, layer, cols):
    if kind < 3:
        return fields[kind, layer, at, cols]
    if kind == 3:
        return eps[layer, at, cols]
    return fwd[kind - 4, layer, at, cols]


def pack_tile(load, lane, right):
    total = jnp.zeros((SUB, LANES), F32)
    for kind, width in enumerate(WIDTHS):
        for layer in range(2):
            value = load(kind, layer)
            if value is None:
                continue
            first = FIRST[kind] + HALF * layer
            value = turn(value, first + width if right else first, 1)
            total = jnp.where((lane >= first) & (lane < first + width), value, total)
    return total


def edge_tile(load, kind, lane, n_lanes):
    spot = lane & (HALF - 1)
    total = None
    for layer in range(2):
        low = turn(load(kind, layer, 0), HALF * layer + OUT, 1)
        high = turn(load(kind, layer, n_lanes - 1), HALF * layer + SIDE + OUT, 1)
        value = jnp.where(spot < SIDE, low, high)
        total = value if total is None else jnp.where(lane < HALF, total, value)
    return total


def cols_kernel(fields, eps, fwd, cross, near, base):
    rows, cols = fields.shape[2], fields.shape[3]
    n_lanes = cols // LANES
    lane, odd = lanes(), is_odd("gy")

    def tile(t, carry):
        at = pl.ds(pl.multiple_of(t * SUB, SUB), SUB)
        out_at = pl.ds(pl.multiple_of(t * SUB + PAD, SUB), SUB)

        def load(kind, layer, k):
            return core_tile(fields, eps, fwd, at, kind, layer, lane_tile(k))

        left = pack_tile(lambda kind, layer: load(kind, layer, 0), lane, False)
        right = pack_tile(lambda kind, layer: load(kind, layer, n_lanes - 1), lane, True)
        cross[out_at, :] = jnp.where(odd, right, left)
        near[out_at, :] = jnp.where(odd, left, right)
        for kind in range(4 + STEPS):
            base[kind, out_at, :] = edge_tile(load, kind, lane, n_lanes)
        return carry

    lax.fori_loop(0, rows // SUB, tile, 0, unroll=4)
    zero = jnp.zeros((PAD, LANES), F32)
    for out in (cross, near):
        out[pl.ds(0, PAD), :] = zero
        out[pl.ds(PAD + rows, PAD), :] = zero


def corners_kernel(cross_in, near_in, cross_rows, near_rows, cross, near):
    rows, cols = cross.shape[0] - 2 * PAD, cross_rows.shape[3]
    lane, odd, odd_col = lanes(), is_odd("gx"), is_odd("gy")
    core = pl.ds(PAD, rows)
    cross[core, :] = cross_in[core, :]
    near[core, :] = near_in[core, :]
    for tile in range(4):
        at = pl.ds(tile * SUB if tile < 2 else PAD + rows + (tile - 2) * SUB, SUB)
        left, right = (
            pack_tile(
                lambda kind, layer: halo_tile(
                    cross_rows, near_rows, odd, tile, kind, layer, pl.ds(lo, LANES)
                ),
                lane, is_right,
            )
            for lo, is_right in ((0, False), (cols - LANES, True))
        )
        cross[at, :] = jnp.where(odd_col, right, left)
        near[at, :] = jnp.where(odd_col, left, right)


def prep_kernel(
    capacity, fields, eps, fwd, mon_x, mon_y, amp, mask, owner, cross, near, base, src, src_edge, place, place_edge
):
    cols_kernel(fields, eps, fwd, cross, near, base)
    side_kernel(capacity, fields.shape[2], mon_x, mon_y, amp, mask, owner, src, src_edge, place, place_edge)


def side_kernel(capacity, rows, mon_x, mon_y, amp, mask, owner, src, src_edge, place, place_edge):
    _, _, ext_rows, cols = src.shape
    channels = mon_x.shape[1]
    row = mon_x[...] - lax.axis_index("gx") * rows + PAD
    col = mon_y[...] - lax.axis_index("gy") * cols
    in_left = (col >= -OUT) & (col < OUT)
    in_right = (col >= cols - OUT) & (col < cols + OUT)
    edge = jnp.where(in_left, col + OUT, jnp.where(in_right, col - cols + OUT + SIDE, -LANES))
    layer = lax.broadcasted_iota(jnp.int32, (1, channels), 1) & 1
    edge = edge + HALF * layer
    inside = jnp.where((col >= 0) & (col < cols), col, -1)
    one_y = lax.broadcasted_iota(jnp.int32, (cols, channels), 0) == inside
    one_e = lax.broadcasted_iota(jnp.int32, (LANES, channels), 0) == edge
    one_y = jnp.where(one_y, 1.0, 0.0).astype(BF16)
    one_e = jnp.where(one_e, 1.0, 0.0).astype(BF16)
    one_y = jnp.concatenate([one_y] * 3, axis=1)
    one_e = jnp.concatenate([one_e] * 3, axis=1)
    one_x = lax.broadcasted_iota(jnp.int32, (ext_rows, channels), 0) == row
    one_x = jnp.where(one_x, 1.0, 0.0).astype(F32)
    nt = (((1,), (1,)), ((), ()))
    for step in range(STEPS):
        parts = [part.astype(F32) for part in split3(amp[pl.ds(step, 1), :])]
        lhs = jnp.concatenate([one_x * part for part in parts], axis=1)
        src_edge[step] = lax.dot_general(lhs.astype(BF16), one_e, nt, preferred_element_type=F32)
        layer_wide = jnp.concatenate([layer] * 3, axis=1)
        for which in range(2):
            some = jnp.where(layer_wide == which, lhs, 0.0).astype(BF16)
            src[step, which] = lax.dot_general(some, one_y, nt, preferred_element_type=F32)
    tiles = owner.shape[1]
    own = owner[...].astype(F32)
    own_wide = jnp.broadcast_to(own, (tiles, tiles))
    earlier = lax.broadcasted_iota(jnp.int32, (tiles, tiles), 0) < lax.broadcasted_iota(
        jnp.int32, (tiles, tiles), 1
    )
    same = (own_wide.T == own_wide) & earlier
    slot = jnp.sum(jnp.where(same, 1.0, 0.0), axis=0, keepdims=True)
    dest = owner[...] * capacity + slot.astype(jnp.int32)
    dest = jnp.where(mask[...] != 0, dest, -1)
    hit = lax.broadcasted_iota(jnp.int32, place.shape, 0) == dest
    hit = jnp.where(hit, 1.0, 0.0).astype(BF16)
    place[...] = hit
    tile_cols = cols // TS
    column = lax.broadcasted_iota(jnp.int32, (tiles, 4 * SUB), 1)
    wanted = (column % SUB) * tile_cols + ((column // SUB) & 1) * (tile_cols - 1)
    picked = lax.broadcasted_iota(jnp.int32, (tiles, 4 * SUB), 0) == wanted
    place_edge[...] = dot(hit, jnp.where(picked, 1.0, 0.0).astype(BF16)).astype(BF16)


class Shifts:
    def __init__(self, next_col, prev_col):
        self.next_col, self.prev_col = next_col, prev_col
        self.bottom, self.top = subs() == SUB - 1, subs() == 0

    def up(self, tile):
        return {key: turn(value, -1, 0) for key, value in tile.items()}

    def down(self, tile):
        return {key: turn(value, 1, 0) for key, value in tile.items()}

    def below(self, up_here, up_next):
        return {key: jnp.where(self.bottom, up_next[key], up_here[key]) for key in up_here}

    def above(self, down_here, down_before):
        return {key: jnp.where(self.top, down_before[key], down_here[key]) for key in down_here}


def tile_at(t):
    return (pl.ds(t * SUB, SUB), slice(None))


def e_at(t, shift=0):
    return (pl.ds(SUB + t * SUB + shift, SUB), slice(None))


def first_curl(n_tiles, shifts, load_hx, load_hy, curl):
    before = None
    for t in range(n_tiles):
        hx, hy = load_hx(t), load_hy(t)
        down = shifts.down(hy)
        over = shifts.above(down, before if t else down)
        left = shifts.prev_col(hx)
        for key in hx:
            curl[key + tile_at(t)] = (hy[key] - over[key]) - (hx[key] - left[key])
        before = down


def steps(n_tiles, keys, shifts, e, curl, eps_of, src_of, other):
    no_above = shifts.top & ((lax.axis_index("gx") + subs() * 0) == 0)
    for step in range(STEPS):
        low, high = (0, n_tiles) if step == 0 else (1, n_tiles - 1)

        for t in range(low, high):
            here = {key: e[(step,) + key + e_at(t)] for key in keys}
            below = {key: e[(step,) + key + e_at(t, 1)] for key in keys}
            above = {key: e[(step,) + key + e_at(t, -1)] for key in keys}
            right, left = shifts.next_col(here), shifts.prev_col(here)
            for key in keys:
                center, over = here[key], above[key]
                if t == PAD // SUB:
                    over = jnp.where(no_above, center, over)
                ring = (below[key] + over) + (right[key] + left[key]) - 4.0 * center
                change = curl[key + tile_at(t)] - COURANT * ring
                if step < STEPS - 1:
                    curl[key + tile_at(t)] = change
                change = change + COUPLING * (other(here, key) - center)
                e[(step + 1,) + key + e_at(t)] = (
                    center - eps_of(key, t) * change + src_of(step, key, t)
                )


def gradient(keys, t, e, change_of):
    result = {}
    for key in keys:
        total = None
        for step in range(STEPS):
            term = e[(step + 1,) + key + e_at(t)] * change_of(step, key, t)
            total = term if total is None else total + term
        result[key] = -total
    return result


def last_fields(tiles, keys, shifts, e, load_hx, load_hy, store):
    def total(t):
        result = {}
        for key in keys:
            parts = [e[(step,) + key + e_at(t)] for step in range(STEPS)]
            result[key] = (parts[0] + parts[1]) + (parts[2] + parts[3])
        return result

    here = total(tiles[0])
    up = shifts.up(here)
    for t in tiles:
        after = total(t + 1)
        up_next = shifts.up(after)
        below, right = shifts.below(up, up_next), shifts.next_col(here)
        hx, hy = load_hx(t), load_hy(t)
        for key in keys:
            store(
                key, t, e[(STEPS,) + key + e_at(t)],
                hx[key] + COURANT * (right[key] - here[key]),
                hy[key] - COURANT * (below[key] - here[key]),
            )
        here, up = after, up_next


def row_pairs(ref, lead, count):
    even = ref[lead + (pl.ds(0, count, stride=PIX), slice(None))]
    return even + ref[lead + (pl.ds(1, count, stride=PIX), slice(None))]


def inner_kernel(
    fields, eps, fwd, cross, near, src, mats, base_in, place, last, slots, base, e, curl, eps_c, g, pooled
):
    rows, cols = fields.shape[2], fields.shape[3]
    n_tiles = (rows + 2 * PAD) // SUB
    n_lanes = cols // LANES
    lane, odd = lanes(), is_odd("gx")
    halo_of = {0: 0, 1: 1, n_tiles - 2: 2, n_tiles - 1: 3}
    keys = [(layer, k) for layer in range(2) for k in range(n_lanes)]

    def load(kind, layer, t, k):
        if t in halo_of:
            return halo_tile(cross, near, odd, halo_of[t], kind, layer, lane_tile(k))
        return core_tile(fields, eps, fwd, pl.ds(t * SUB - PAD, SUB), kind, layer, lane_tile(k))

    def load_all(kind, t):
        return {key: load(kind, key[0], t, key[1]) for key in keys}

    at_end, at_start = lane == LANES - 1, lane == 0

    def next_col(values):
        moved = {key: turn(value, -1, 1) for key, value in values.items()}
        return {
            (l, k): jnp.where(at_end, moved[l, (k + 1) % n_lanes], moved[l, k]) for l, k in keys
        }

    def prev_col(values):
        moved = {key: turn(value, 1, 1) for key, value in values.items()}
        return {
            (l, k): jnp.where(at_start, moved[l, (k - 1) % n_lanes], moved[l, k]) for l, k in keys
        }

    shifts = Shifts(next_col, prev_col)
    for key in keys:
        for t in (-1, n_tiles):
            e[(0,) + key + e_at(t)] = jnp.zeros((SUB, LANES), F32)
    for t in range(n_tiles):
        for key in keys:
            e[(0,) + key + e_at(t)] = load(0, key[0], t, key[1])
            eps_c[key + tile_at(t)] = COURANT * load(3, key[0], t, key[1])
    first_curl(n_tiles, shifts, lambda t: load_all(1, t), lambda t: load_all(2, t), curl)
    steps(
        n_tiles, keys, shifts, e, curl,
        lambda key, t: eps_c[key + tile_at(t)],
        lambda step, key, t: src[step, key[0], pl.ds(t * SUB, SUB), lane_tile(key[1])],
        lambda values, key: values[1 - key[0], key[1]],
    )
    for t in range(1, n_tiles - 1):
        values = gradient(keys, t, e, lambda step, key, t: load(4 + step, key[0], t, key[1]))
        for key in keys:
            g[key + tile_at(t)] = values[key]

    def store(key, t, *values):
        for kind, value in enumerate(values):
            last[(kind,) + key + (pl.ds(t * SUB - PAD, SUB), slice(None))] = value

    last_fields(
        range(PAD // SUB, n_tiles - PAD // SUB), keys, shifts, e,
        lambda t: load_all(1, t), lambda t: load_all(2, t), store,
    )
    for layer in range(2):
        total = None
        for k in range(n_lanes):
            for part in split2(row_pairs(g, (layer, k), n_tiles * SUB // PIX)):
                term = dot(part, mats[k])
                total = term if total is None else total + term
        pooled[layer] = total

    vals = by_tile([cone_filter(pooled.at[layer], rows // PIX, PAD // PIX) for layer in range(2)])
    high, low = split2(vals)
    slots[...] = dot(place[...], high) + dot(place[...], low)

    for t in range(n_tiles):
        for kind in range(4 + STEPS):
            at = pl.ds(t * SUB, SUB)
            if t not in halo_of:
                base[kind, at, :] = base_in[kind, at, :]
            elif kind < 4 or t not in (0, n_tiles - 1):
                base[kind, at, :] = edge_tile(
                    lambda kind, layer, k: load(kind, layer, t, k), kind, lane, n_lanes
                )


def cone_filter(pooled, out_pix, first):
    weights = cone_weights(RADIUS)
    reach = RADIUS - 1
    lane = lax.broadcasted_iota(jnp.int32, (out_pix, LANES), 1)
    at = [pooled[pl.ds(first + s, out_pix), :] for s in range(-reach, reach + 1)]
    sums = [at[reach]] + [at[reach + s] + at[reach - s] for s in range(1, reach + 1)]
    total = None
    for shift in range(reach + 1):
        mixed = None
        for s in range(reach + 1):
            weight = float(weights[reach + s, reach + shift])
            if weight > 0.0:
                term = weight * sums[s]
                mixed = term if mixed is None else mixed + term
        if shift == 0:
            total = mixed
        else:
            total = total + turn(jnp.where(lane < shift, 0.0, mixed), -shift, 1)
            total = total + turn(jnp.where(lane >= LANES - shift, 0.0, mixed), shift, 1)
    return total


def by_tile(blocks):
    span = TS // PIX
    tile_rows = blocks[0].shape[0] // span
    x = jnp.stack([block.reshape(tile_rows, span, LANES) for block in blocks], axis=1)
    x = x.reshape(tile_rows * 2, span, LANES)
    group = lax.broadcasted_iota(jnp.int32, x.shape, 2) // span
    row = lax.broadcasted_iota(jnp.int32, x.shape, 1)
    for bit in (1, 2, 4):
        row_on, lane_on = (row & bit) != 0, (group & bit) != 0
        ahead = turn(turn(x, -bit, 1), bit * span, 2)
        behind = turn(turn(x, bit, 1), -bit * span, 2)
        x = jnp.where(row_on == lane_on, x, jnp.where(lane_on, ahead, behind))
    x = x.reshape(tile_rows, 2, span, LANES)
    even, odd = x[:, 0], x[:, 1]
    upper = lax.broadcasted_iota(jnp.int32, even.shape, 2) >= HALF
    new_even = jnp.where(upper, turn(odd, HALF, 2), even)
    new_odd = jnp.where(upper, odd, turn(even, HALF, 2))
    return jnp.stack([new_even, new_odd], axis=1).reshape(tile_rows * 2 * span, LANES)


def from_partner(is_cross, lane):
    next_one = (lax.axis_index("gy") + (0 if is_cross else 1)) & 1
    spot = lane & (HALF - 1)
    start = next_one * (HALF - OUT)
    mine = (spot >= start) & (spot < start + OUT)
    shifts = []
    for kind, width in enumerate(WIDTHS):
        left, right = (OUT - width - FIRST[kind]) % LANES, (HALF - OUT - FIRST[kind]) % LANES
        shifts.append(left + next_one * (right - left))
    return mine, shifts


def edge_cross_kernel(base, cross, result):
    n_tiles = base.shape[1] // SUB
    mine, shifts = from_partner(True, lanes())
    for t in range(n_tiles):
        at = pl.ds(t * SUB, SUB)
        kinds = range(4 if t in (0, n_tiles - 1) else 4 + STEPS)
        values = [
            jnp.where(mine, pltpu.roll(cross[at, :], shifts[kind], 1), base[kind, at, :])
            for kind in kinds
        ]
        for kind in kinds:
            result[kind, at, :] = values[kind]


def edge_kernel(
    slots_in, base, near, src, place, edge_last, slots, e, first, curl, eps_c, d, g, merged
):
    ext_rows = base.shape[1]
    rows = ext_rows - 2 * PAD
    n_tiles = ext_rows // SUB
    lane = lanes()
    spot = lane & (HALF - 1)
    mine, moves = from_partner(False, lane)
    for t in (-1, n_tiles):
        e[(0,) + e_at(t)] = jnp.zeros((SUB, LANES), F32)

    for t in range(n_tiles):
        at = pl.ds(t * SUB, SUB)
        for kind in range(4 if t in (0, n_tiles - 1) else 4 + STEPS):
            value = jnp.where(mine, pltpu.roll(near[at, :], moves[kind], 1), base[kind, at, :])
            if kind == 0:
                e[(0,) + e_at(t)] = value
            elif kind < 3:
                first[kind - 1, at, :] = value
            elif kind == 3:
                eps_c[at, :] = COURANT * value
            else:
                d[kind - 4, at, :] = value

    no_left = (spot == OUT) & ((lax.axis_index("gy") + lane * 0) == 0)
    shifts = Shifts(
        lambda values: {(): turn(values[()], -1, 1)},
        lambda values: {(): turn(values[()], 1, 1)},
    )

    def load_hx(t):
        return {(): first[0, pl.ds(t * SUB, SUB), :]}

    def load_hy(t):
        return {(): first[1, pl.ds(t * SUB, SUB), :]}

    first_curl(n_tiles, shifts, load_hx, load_hy, curl)
    shifts.prev_col = lambda values: {(): jnp.where(no_left, values[()], turn(values[()], 1, 1))}
    steps(
        n_tiles, [()], shifts, e, curl,
        lambda key, t: eps_c[pl.ds(t * SUB, SUB), :],
        lambda step, key, t: src[step, pl.ds(t * SUB, SUB), :],
        lambda values, key: turn(values[()], HALF, 1),
    )
    inside = (spot >= OUT - NEAR) & (spot < OUT + KEEP)
    inside = inside | ((spot >= HALF - OUT - KEEP) & (spot < HALF - OUT + NEAR))
    for t in range(1, n_tiles - 1):
        value = gradient([()], t, e, lambda step, key, t: d[step, pl.ds(t * SUB, SUB), :])[()]
        g[pl.ds(t * SUB, SUB), :] = jnp.where(inside, value, 0.0)

    def store(key, t, *values):
        for kind, value in enumerate(values):
            edge_last[kind, pl.ds(t * SUB - PAD, SUB), :] = value

    edge_filter(g, merged)
    edge_slots(merged, slots_in, place, slots)
    last_fields(
        range(PAD // SUB, n_tiles - PAD // SUB), [()], shifts, e, load_hx, load_hy, store
    )


def edge_filter(g, merged):
    lane = lanes()
    span, reach = TS // PIX, RADIUS - 1
    pixel = {}
    for j in range(-reach, span + reach):
        value = g[pl.ds(PAD + PIX * j, SUB, stride=TS), :]
        pixel[j] = value + g[pl.ds(PAD + PIX * j + 1, SUB, stride=TS), :]

    weights = cone_weights(RADIUS)
    spans = []
    for row in range(span):
        sums = [pixel[row]] + [pixel[row + s] + pixel[row - s] for s in range(1, reach + 1)]
        move = (row & 1) + SIDE * ((row >> 1) & 1)
        total = None
        for shift in range(reach + 1):
            mixed = None
            for s in range(reach + 1):
                weight = float(weights[reach + s, reach + shift])
                if weight > 0.0:
                    term = weight * sums[s]
                    mixed = term if mixed is None else mixed + term
            for place in {PIX * shift, -PIX * shift}:
                term = turn(mixed, move + place, 1) + turn(mixed, move + place - 1, 1)
                total = term if total is None else total + term
        spans.append(total)
    even = (lane & 1) == 0
    window = ((lane - OUT) & (HALF - 1)) < SIDE
    for n in range(2):
        a, b, c, d = spans[4 * n : 4 * n + 4]
        merged[n] = jnp.where(window, jnp.where(even, a, b), jnp.where(even, c, d))


def edge_slots(merged, slots_in, place, slots):
    lane = lanes()
    span = TS // PIX
    row, pixel = lane // span % span, lane % span
    start = (lane & HALF) + OUT + PIX * pixel + (row & 1) + SIDE * ((row >> 1) & 1)
    edge = []
    for side in range(2):
        index = (start + OUT * side) & (LANES - 1)
        low, high = (jnp.take_along_axis(merged[n], index, axis=1) for n in range(2))
        edge.append(jnp.where(row < span // 2, low, high))
    parts = split2(jnp.concatenate(edge, axis=0))
    slots[...] = slots_in[...] + dot(place[...], jnp.concatenate(parts, axis=0))


def deliver_kernel(last, edge_last, slots, out_fields, out_slots, merged, sems):
    rows, cols = merged.shape[2], merged.shape[3]
    n_lanes = cols // LANES
    lane = lanes()
    copies = [pltpu.make_async_copy(slots, out_slots.at[0], sems.at[6])]
    copies[0].start()
    for kind in range(3):
        for layer in range(2):
            for t in range(rows // SUB):
                at = pl.ds(t * SUB, SUB)
                edge = edge_last[kind, at, :]
                for k in range(n_lanes):
                    value = last[kind, layer, k, at, :]
                    if k == 0:
                        value = jnp.where(lane < KEEP, turn(edge, -HALF * layer - OUT, 1), value)
                    if k == n_lanes - 1:
                        value = jnp.where(
                            lane >= LANES - KEEP, turn(edge, -HALF * layer - SIDE - OUT, 1), value
                        )
                    merged[kind, layer, at, lane_tile(k)] = value
            copies.append(
                pltpu.make_async_copy(
                    merged.at[kind, layer], out_fields.at[kind, layer], sems.at[2 * kind + layer]
                )
            )
            copies[-1].start()
    for copy in copies:
        copy.wait()


def vmem():
    return pl.BlockSpec(memory_space=pltpu.VMEM)


def shape(*dims, dtype=F32):
    return jax.ShapeDtypeStruct(dims, dtype)


def call(kernel, outs, n_in, *, in_space=pltpu.VMEM, out_specs=None, scratch=(), flops=0, size=0):
    return pl.pallas_call(
        kernel,
        out_shape=outs,
        in_specs=[pl.BlockSpec(memory_space=in_space)] * n_in,
        out_specs=out_specs or tuple(vmem() for _ in outs),
        scratch_shapes=list(scratch),
        compiler_params=pltpu.CompilerParams(vmem_limit_bytes=40 * 1024 * 1024),
        cost_estimate=pl.CostEstimate(flops=flops, bytes_accessed=size, transcendentals=0),
    )


def on_device(adj_fields, inv_eps, fwd_diff, mon_x, mon_y, mon_amp, design_mask, tile_owner):
    rows, cols = adj_fields.shape[2], adj_fields.shape[3]
    assert cols == 2 * LANES and rows % TS == 0
    gx_count, gy_count = lax.axis_size("gx"), lax.axis_size("gy")
    owners = gx_count * gy_count
    tiles = (rows // TS) * (cols // TS)
    width = 2 * (TS // PIX) ** 2
    assert width == LANES
    capacity = max(8, 2 * tiles // owners)
    assert rows == TS * SUB and cols == 2 * TS * SUB
    ext_rows = rows + 2 * PAD
    n_lanes = cols // LANES
    cells = rows * cols
    blocks = (adj_fields, inv_eps, fwd_diff)


    strip = shape(4 + STEPS, 2, SUB, cols)
    cross, near = call(
        rows_kernel, (strip, strip), 3, in_space=pltpu.HBM,
        scratch=(
            pltpu.VMEM((2, 4, 2, SUB, cols), F32),
            pltpu.SemaphoreType.DMA((10,)),
        ),
        size=2**20,
    )(*(pltpu.with_memory_space_constraint(block, pltpu.HBM) for block in blocks))

    def pairs(count, start):
        some = [(i, i + 1) for i in range(start, count - 1, 2)]
        return some + [(j, i) for i, j in some]

    cross = lax.ppermute(cross, "gx", pairs(gx_count, 1))
    near = lax.ppermute(near, "gx", pairs(gx_count, 0))

    packed = shape(ext_rows, LANES)
    channels = mon_x.shape[0]
    cross_cols, near_cols, base, src, src_edge, place, place_edge = call(
        lambda *refs: prep_kernel(capacity, *refs),
        (
            packed,
            packed,
            shape(4 + STEPS, ext_rows, LANES),
            shape(STEPS, 2, ext_rows, cols),
            shape(STEPS, ext_rows, LANES),
            shape(owners * capacity, tiles, dtype=BF16),
            shape(owners * capacity, 4 * SUB, dtype=BF16),
        ),
        8,
        flops=16 * ext_rows * (cols + LANES) * 3 * channels,
        size=64 * cells,
    )(
        *blocks,
        mon_x.reshape(1, channels),
        mon_y.reshape(1, channels),
        mon_amp,
        design_mask.reshape(1, tiles),
        tile_owner.reshape(1, tiles),
    )
    cross_cols, near_cols = call(
        corners_kernel, (packed, packed), 4, flops=cells, size=8 * ext_rows * LANES
    )(cross_cols, near_cols, cross, near)
    cross_cols = lax.ppermute(cross_cols, "gy", pairs(gy_count, 1))
    near_cols = lax.ppermute(near_cols, "gy", pairs(gy_count, 0))

    plane = (2, n_lanes, ext_rows, LANES)
    last, slots, base = call(
        inner_kernel,
        (
            shape(3, 2, n_lanes, rows, LANES),
            shape(owners * capacity, width),
            shape(4 + STEPS, ext_rows, LANES),
        ),
        9,
        scratch=(
            pltpu.VMEM((1 + STEPS, 2, n_lanes, ext_rows + 2 * SUB, LANES), F32),
            pltpu.VMEM(plane, F32),
            pltpu.VMEM(plane, F32),
            pltpu.VMEM(plane, F32),
            pltpu.VMEM((2, ext_rows // PIX, LANES), F32),
        ),
        flops=200 * cells,
        size=96 * cells,
    )(*blocks, cross, near, src, pool_matrices(), base, place)

    plane = (ext_rows, LANES)
    (base,) = call(
        edge_cross_kernel, (shape(4 + STEPS, *plane),), 2, flops=10 * cells, size=8 * cells
    )(base, cross_cols)
    edge_last, outgoing = call(
        edge_kernel,
        (shape(3, rows, LANES), pltpu.VMEM((owners * capacity, width), F32)),
        5,
        scratch=(
            pltpu.VMEM((1 + STEPS, ext_rows + 2 * SUB, LANES), F32),
            pltpu.VMEM((2,) + plane, F32),
            pltpu.VMEM(plane, F32),
            pltpu.VMEM(plane, F32),
            pltpu.VMEM((STEPS,) + plane, F32),
            pltpu.VMEM(plane, F32),
            pltpu.VMEM((2, SUB, LANES), F32),
        ),
        flops=50 * cells,
        size=16 * cells,
    )(slots, base, near_cols, src_edge, place_edge)

    outgoing = outgoing.reshape(owners, capacity, width)
    incoming = lax.all_to_all(outgoing, ("gx", "gy"), split_axis=0, concat_axis=0, tiled=True)
    anywhere = pl.BlockSpec(memory_space=pl.ANY)
    return call(
        deliver_kernel,
        (shape(3, 2, rows, cols), shape(1, *incoming.shape)),
        3,
        out_specs=(anywhere, anywhere),
        scratch=(pltpu.VMEM((3, 2, rows, cols), F32), pltpu.SemaphoreType.DMA((7,))),
        flops=20 * cells,
        size=48 * cells,
    )(last, edge_last, pltpu.with_memory_space_constraint(incoming, pltpu.VMEM))


def solution(mesh):
    placed = (
        P(None, None, ("parts", "gx"), "gy"),
        P(None, ("parts", "gx"), "gy"),
        P(None, None, ("parts", "gx"), "gy"),
        P("parts"),
        P("parts"),
        P(None, "parts"),
        P(("parts", "gx"), "gy", None),
        P(("parts", "gx"), "gy", None, None),
    )
    return jax.shard_map(
        on_device,
        mesh=mesh,
        in_specs=placed,
        out_specs=(
            P(None, None, ("parts", "gx"), "gy"),
            P(("parts", "gx", "gy"), None, None, None),
        ),
        check_vma=False,
    )
```

```python
import jax
import jax.numpy as jnp
import ml_dtypes
import numpy as np
from jax import lax
from jax.experimental import pallas as pl
from jax.experimental.pallas import tpu as pltpu
from jax.sharding import PartitionSpec as P

STEPS = 4
PIX = 2
TS = 16
RADIUS = 4
COURANT = 0.6
COUPLING = 0.25

LANES = 128
SUB = 8
FAR = STEPS + PIX * (RADIUS - 1)
NEAR = PIX * (RADIUS - 1)
LEFT_OVER = FAR - SUB
PAD = 2 * SUB
HALF = LANES // 2
SIDE = HALF // 2
OUT = SIDE // 2
KEEP = 8
F32 = jnp.float32
BF16 = jnp.bfloat16
WIDTHS = (FAR,) * 4 + (NEAR,) * STEPS
FIRST = tuple(sum(WIDTHS[:k]) for k in range(len(WIDTHS)))
assert sum(WIDTHS) <= HALF and FAR <= OUT and STEPS + KEEP <= OUT


def cone_weights(radius):
    reach_cells = radius - 1
    offsets = np.arange(-reach_cells, reach_cells + 1)
    distance = np.sqrt(offsets[:, None] * offsets[:, None] + offsets[None, :] * offsets[None, :])
    weights = np.maximum(radius - distance, 0.0)
    return weights / weights.sum()


def pool_matrices():
    inner = np.zeros((2, LANES, LANES), np.float32)
    for j in range(KEEP, 2 * LANES - KEEP):
        inner[j // LANES, j % LANES, j // PIX] = 1.0
    return inner.astype(ml_dtypes.bfloat16)


def split2(value):
    high = value.astype(BF16)
    return high, (value - high.astype(F32)).astype(BF16)


def split3(value):
    high = value.astype(BF16)
    rest = value - high.astype(F32)
    mid = rest.astype(BF16)
    return high, mid, (rest - mid.astype(F32)).astype(BF16)


def dot(a, b):
    return jnp.dot(a, b, preferred_element_type=F32)


def turn(value, shift, axis):
    size = value.shape[axis]
    return pltpu.roll(value, shift % size, axis) if shift % size else value


def lanes():
    return lax.broadcasted_iota(jnp.int32, (SUB, LANES), 1)


def subs():
    return lax.broadcasted_iota(jnp.int32, (SUB, LANES), 0)


def lane_tile(k):
    return pl.ds(k * LANES, LANES)


def is_odd(axis):
    return ((subs() * 0 + lax.axis_index(axis)) & 1) == 1


def rows_kernel(fields, eps, fwd, cross, near, hold, sems):
    rows, cols = fields.shape[2], fields.shape[3]
    sub = subs()
    odd = lax.axis_index("gx") & 1
    parts = []
    for n, (out, at_end) in enumerate(((cross, odd), (near, 1 - odd))):
        at = pl.ds(pl.multiple_of(at_end * (rows - SUB), SUB), SUB)
        rest = pl.ds(pl.multiple_of(SUB + at_end * (rows - 3 * SUB), SUB), SUB)
        pairs = (
            (fields.at[:, :, rest, :], hold.at[n, pl.ds(0, 3)]),
            (eps.at[:, rest, :], hold.at[n, 3]),
            (fwd.at[:, :, at, :], out.at[pl.ds(4, STEPS)]),
            (fields.at[:, :, at, :], out.at[pl.ds(0, 3)]),
            (eps.at[:, at, :], out.at[3]),
        )
        copies = [
            pltpu.make_async_copy(src, dst, sems.at[len(pairs) * n + m])
            for m, (src, dst) in enumerate(pairs)
        ]
        parts.append((n, out, at_end, copies))
    for group in (slice(0, 3), slice(3, 5)):
        for part in parts:
            for copy in part[3][group]:
                copy.start()
    for n, out, at_end, copies in parts:
        for copy in copies[:3]:
            copy.wait()
        low = (1 - at_end) * NEAR
        rest = (sub >= low) & (sub < low + LEFT_OVER)
        shift = NEAR + at_end * (LEFT_OVER - NEAR)
        for kind in range(4):
            for layer in range(2):
                values = []
                for k in range(cols // LANES):
                    moved = pltpu.roll(hold[n, kind, layer, :, lane_tile(k)], shift, 0)
                    values.append(jnp.where(rest, moved, out[4 + kind, layer, :, lane_tile(k)]))
                for k, value in enumerate(values):
                    out[4 + kind, layer, :, lane_tile(k)] = value
    for part in parts:
        for copy in part[3][3:]:
            copy.wait()


def halo_tile(cross, near, odd, tile, kind, layer, at):
    is_above = tile < 2
    outer = tile in (0, 3)
    if outer and kind >= 4:
        return None
    plane = kind + (4 if outer else 0)
    a, b = near[plane, layer, :, at], cross[plane, layer, :, at]
    value = jnp.where(odd, a, b) if is_above else jnp.where(odd, b, a)
    if outer:
        value = turn(value, -LEFT_OVER if is_above else LEFT_OVER, 0)
    return value


def core_tile(fields, eps, fwd, at, kind, layer, cols):
    if kind < 3:
        return fields[kind, layer, at, cols]
    if kind == 3:
        return eps[layer, at, cols]
    return fwd[kind - 4, layer, at, cols]


def pack_tile(load, lane, right):
    total = jnp.zeros((SUB, LANES), F32)
    for kind, width in enumerate(WIDTHS):
        for layer in range(2):
            value = load(kind, layer)
            if value is None:
                continue
            first = FIRST[kind] + HALF * layer
            value = turn(value, first + width if right else first, 1)
            total = jnp.where((lane >= first) & (lane < first + width), value, total)
    return total


def edge_tile(load, kind, lane, n_lanes):
    spot = lane & (HALF - 1)
    total = None
    for layer in range(2):
        low = turn(load(kind, layer, 0), HALF * layer + OUT, 1)
        high = turn(load(kind, layer, n_lanes - 1), HALF * layer + SIDE + OUT, 1)
        value = jnp.where(spot < SIDE, low, high)
        total = value if total is None else jnp.where(lane < HALF, total, value)
    return total


def cols_kernel(fields, eps, fwd, cross, near, base):
    rows, cols = fields.shape[2], fields.shape[3]
    n_lanes = cols // LANES
    lane, odd = lanes(), is_odd("gy")

    def tile(t, carry):
        at = pl.ds(pl.multiple_of(t * SUB, SUB), SUB)
        out_at = pl.ds(pl.multiple_of(t * SUB + PAD, SUB), SUB)

        def load(kind, layer, k):
            return core_tile(fields, eps, fwd, at, kind, layer, lane_tile(k))

        left = pack_tile(lambda kind, layer: load(kind, layer, 0), lane, False)
        right = pack_tile(lambda kind, layer: load(kind, layer, n_lanes - 1), lane, True)
        cross[out_at, :] = jnp.where(odd, right, left)
        near[out_at, :] = jnp.where(odd, left, right)
        for kind in range(4 + STEPS):
            base[kind, out_at, :] = edge_tile(load, kind, lane, n_lanes)
        return carry

    lax.fori_loop(0, rows // SUB, tile, 0, unroll=4)
    zero = jnp.zeros((SUB, LANES), F32)
    for out in (cross, near):
        for at in (0, SUB, PAD + rows):
            out[pl.ds(at, SUB), :] = zero


def packed_at(t, n_tiles):
    return pl.ds((t if t < n_tiles - 1 else 0) * SUB, SUB)


def corners_kernel(cross_in, near_in, cross_rows, near_rows, cross, near):
    rows, cols = cross.shape[0] - 3 * SUB, cross_rows.shape[3]
    lane, odd, odd_col = lanes(), is_odd("gx"), is_odd("gy")
    is_first = subs() >= SUB - LEFT_OVER
    core = pl.ds(PAD, rows)
    cross[core, :] = cross_in[core, :]
    near[core, :] = near_in[core, :]
    for base, tiles in ((0, (0, 3)), (SUB, (1,)), (PAD + rows, (2,))):
        at = pl.ds(base, SUB)
        packs = []
        for lo, is_right in ((0, False), (cols - LANES, True)):

            def load(kind, layer):
                values = [
                    halo_tile(cross_rows, near_rows, odd, tile, kind, layer, pl.ds(lo, LANES))
                    for tile in tiles
                ]
                if len(values) == 1 or values[0] is None:
                    return values[0]
                return jnp.where(is_first, values[0], values[1])

            packs.append(pack_tile(load, lane, is_right))
        left, right = packs
        cross[at, :] = jnp.where(odd_col, right, left)
        near[at, :] = jnp.where(odd_col, left, right)


def prep_kernel(
    capacity, fields, eps, fwd, mon_x, mon_y, amp, mask, owner, cross, near, base, src, src_edge, place, place_edge
):
    cols_kernel(fields, eps, fwd, cross, near, base)
    side_kernel(capacity, fields.shape[2], mon_x, mon_y, amp, mask, owner, src, src_edge, place, place_edge)


def side_kernel(capacity, rows, mon_x, mon_y, amp, mask, owner, src, src_edge, place, place_edge):
    _, _, ext_rows, cols = src.shape
    channels = mon_x.shape[1]
    row = mon_x[...] - lax.axis_index("gx") * rows + PAD
    col = mon_y[...] - lax.axis_index("gy") * cols
    in_left = (col >= -OUT) & (col < OUT)
    in_right = (col >= cols - OUT) & (col < cols + OUT)
    edge = jnp.where(in_left, col + OUT, jnp.where(in_right, col - cols + OUT + SIDE, -LANES))
    layer = lax.broadcasted_iota(jnp.int32, (1, channels), 1) & 1
    edge = edge + HALF * layer
    inside = jnp.where((col >= 0) & (col < cols), col, -1)
    one_y = lax.broadcasted_iota(jnp.int32, (cols, channels), 0) == inside
    one_e = lax.broadcasted_iota(jnp.int32, (LANES, channels), 0) == edge
    one_y = jnp.where(one_y, 1.0, 0.0).astype(BF16)
    one_e = jnp.where(one_e, 1.0, 0.0).astype(BF16)
    one_y = jnp.concatenate([one_y] * 3, axis=1)
    one_e = jnp.concatenate([one_e] * 3, axis=1)
    one_x = lax.broadcasted_iota(jnp.int32, (ext_rows, channels), 0) == row
    one_x = jnp.where(one_x, 1.0, 0.0).astype(F32)
    nt = (((1,), (1,)), ((), ()))
    for step in range(STEPS):
        parts = [part.astype(F32) for part in split3(amp[pl.ds(step, 1), :])]
        lhs = jnp.concatenate([one_x * part for part in parts], axis=1)
        src_edge[step] = lax.dot_general(lhs.astype(BF16), one_e, nt, preferred_element_type=F32)
        layer_wide = jnp.concatenate([layer] * 3, axis=1)
        for which in range(2):
            some = jnp.where(layer_wide == which, lhs, 0.0).astype(BF16)
            src[step, which] = lax.dot_general(some, one_y, nt, preferred_element_type=F32)
    tiles = owner.shape[1]
    own = owner[...].astype(F32)
    own_wide = jnp.broadcast_to(own, (tiles, tiles))
    earlier = lax.broadcasted_iota(jnp.int32, (tiles, tiles), 0) < lax.broadcasted_iota(
        jnp.int32, (tiles, tiles), 1
    )
    same = (own_wide.T == own_wide) & earlier
    slot = jnp.sum(jnp.where(same, 1.0, 0.0), axis=0, keepdims=True)
    dest = owner[...] * capacity + slot.astype(jnp.int32)
    dest = jnp.where(mask[...] != 0, dest, -1)
    hit = lax.broadcasted_iota(jnp.int32, place.shape, 0) == dest
    hit = jnp.where(hit, 1.0, 0.0).astype(BF16)
    place[...] = hit
    tile_cols = cols // TS
    column = lax.broadcasted_iota(jnp.int32, (tiles, 4 * SUB), 1)
    wanted = (column % SUB) * tile_cols + ((column // SUB) & 1) * (tile_cols - 1)
    picked = lax.broadcasted_iota(jnp.int32, (tiles, 4 * SUB), 0) == wanted
    place_edge[...] = dot(hit, jnp.where(picked, 1.0, 0.0).astype(BF16)).astype(BF16)


class Shifts:
    def __init__(self, next_col, prev_col):
        self.next_col, self.prev_col = next_col, prev_col
        self.bottom, self.top = subs() == SUB - 1, subs() == 0

    def up(self, tile):
        return {key: turn(value, -1, 0) for key, value in tile.items()}

    def down(self, tile):
        return {key: turn(value, 1, 0) for key, value in tile.items()}

    def below(self, up_here, up_next):
        return {key: jnp.where(self.bottom, up_next[key], up_here[key]) for key in up_here}

    def above(self, down_here, down_before):
        return {key: jnp.where(self.top, down_before[key], down_here[key]) for key in down_here}


def tile_at(t):
    return (pl.ds(t * SUB, SUB), slice(None))


def first_curl(n_tiles, shifts, load_hx, load_hy, curl):
    before = None
    for t in range(n_tiles):
        hx, hy = load_hx(t), load_hy(t)
        down = shifts.down(hy)
        over = shifts.above(down, before if t else down)
        left = shifts.prev_col(hx)
        for key in hx:
            curl[key + tile_at(t)] = (hy[key] - over[key]) - (hx[key] - left[key])
        before = down


def steps(n_tiles, keys, shifts, e, curl, eps_of, src_of, other):
    no_above = shifts.top & ((lax.axis_index("gx") + subs() * 0) == 0)
    for step in range(STEPS):
        low, high = (0, n_tiles) if step == 0 else (1, n_tiles - 1)

        def load(t):
            return {key: e[(step,) + key + tile_at(t)] for key in keys}

        here = load(low)
        up = shifts.up(here)
        down_before = shifts.down(load(max(low - 1, 0)))
        for t in range(low, high):
            after = load(min(t + 1, n_tiles - 1))
            up_next, down = shifts.up(after), shifts.down(here)
            below, above = shifts.below(up, up_next), shifts.above(down, down_before)
            right, left = shifts.next_col(here), shifts.prev_col(here)
            for key in keys:
                center, over = here[key], above[key]
                if t == PAD // SUB:
                    over = jnp.where(no_above, center, over)
                ring = (below[key] + over) + (right[key] + left[key]) - 4.0 * center
                change = curl[key + tile_at(t)] - COURANT * ring
                if step < STEPS - 1:
                    curl[key + tile_at(t)] = change
                change = change + COUPLING * (other(here, key) - center)
                e[(step + 1,) + key + tile_at(t)] = (
                    center - eps_of(key, t) * change + src_of(step, key, t)
                )
            here, up, down_before = after, up_next, down


def gradient(keys, t, e, change_of):
    result = {}
    for key in keys:
        total = None
        for step in range(STEPS):
            term = e[(step + 1,) + key + tile_at(t)] * change_of(step, key, t)
            total = term if total is None else total + term
        result[key] = -total
    return result


def last_fields(tiles, keys, shifts, e, load_hx, load_hy, store):
    def total(t):
        result = {}
        for key in keys:
            parts = [e[(step,) + key + tile_at(t)] for step in range(STEPS)]
            result[key] = (parts[0] + parts[1]) + (parts[2] + parts[3])
        return result

    here = total(tiles[0])
    up = shifts.up(here)
    for t in tiles:
        after = total(t + 1)
        up_next = shifts.up(after)
        below, right = shifts.below(up, up_next), shifts.next_col(here)
        hx, hy = load_hx(t), load_hy(t)
        for key in keys:
            store(
                key, t, e[(STEPS,) + key + tile_at(t)],
                hx[key] + COURANT * (right[key] - here[key]),
                hy[key] - COURANT * (below[key] - here[key]),
            )
        here, up = after, up_next


def row_pairs(ref, lead, count):
    even = ref[lead + (pl.ds(0, count, stride=PIX), slice(None))]
    return even + ref[lead + (pl.ds(1, count, stride=PIX), slice(None))]


def inner_kernel(
    fields, eps, fwd, cross, near, src, mats, base_in, place, last, slots, base, e, curl, eps_c, g, pooled
):
    rows, cols = fields.shape[2], fields.shape[3]
    n_tiles = (rows + 2 * PAD) // SUB
    n_lanes = cols // LANES
    lane, odd = lanes(), is_odd("gx")
    halo_of = {0: 0, 1: 1, n_tiles - 2: 2, n_tiles - 1: 3}
    keys = [(layer, k) for layer in range(2) for k in range(n_lanes)]

    def load(kind, layer, t, k):
        if t in halo_of:
            return halo_tile(cross, near, odd, halo_of[t], kind, layer, lane_tile(k))
        return core_tile(fields, eps, fwd, pl.ds(t * SUB - PAD, SUB), kind, layer, lane_tile(k))

    def load_all(kind, t):
        return {key: load(kind, key[0], t, key[1]) for key in keys}

    at_end, at_start = lane == LANES - 1, lane == 0

    def next_col(values):
        moved = {key: turn(value, -1, 1) for key, value in values.items()}
        return {
            (l, k): jnp.where(at_end, moved[l, (k + 1) % n_lanes], moved[l, k]) for l, k in keys
        }

    def prev_col(values):
        moved = {key: turn(value, 1, 1) for key, value in values.items()}
        return {
            (l, k): jnp.where(at_start, moved[l, (k - 1) % n_lanes], moved[l, k]) for l, k in keys
        }

    shifts = Shifts(next_col, prev_col)
    for t in range(n_tiles):
        for key in keys:
            e[(0,) + key + tile_at(t)] = load(0, key[0], t, key[1])
            eps_c[key + tile_at(t)] = COURANT * load(3, key[0], t, key[1])
    first_curl(n_tiles, shifts, lambda t: load_all(1, t), lambda t: load_all(2, t), curl)
    steps(
        n_tiles, keys, shifts, e, curl,
        lambda key, t: eps_c[key + tile_at(t)],
        lambda step, key, t: src[step, key[0], pl.ds(t * SUB, SUB), lane_tile(key[1])],
        lambda values, key: values[1 - key[0], key[1]],
    )
    for t in range(1, n_tiles - 1):
        values = gradient(keys, t, e, lambda step, key, t: load(4 + step, key[0], t, key[1]))
        for key in keys:
            g[key + tile_at(t)] = values[key]

    def store(key, t, *values):
        for kind, value in enumerate(values):
            last[(kind,) + key + (pl.ds(t * SUB - PAD, SUB), slice(None))] = value

    last_fields(
        range(PAD // SUB, n_tiles - PAD // SUB), keys, shifts, e,
        lambda t: load_all(1, t), lambda t: load_all(2, t), store,
    )
    for layer in range(2):
        total = None
        for k in range(n_lanes):
            for part in split2(row_pairs(g, (layer, k), n_tiles * SUB // PIX)):
                term = dot(part, mats[k])
                total = term if total is None else total + term
        pooled[layer] = total

    vals = by_tile([cone_filter(pooled.at[layer], rows // PIX, PAD // PIX) for layer in range(2)])
    high, low = split2(vals)
    slots[...] = dot(place[...], high) + dot(place[...], low)

    for t in range(n_tiles):
        for kind in range(4 + STEPS):
            at = pl.ds(t * SUB, SUB)
            if t not in halo_of:
                base[kind, at, :] = base_in[kind, at, :]
            elif kind < 4 or t not in (0, n_tiles - 1):
                base[kind, at, :] = edge_tile(
                    lambda kind, layer, k: load(kind, layer, t, k), kind, lane, n_lanes
                )


def cone_filter(pooled, out_pix, first):
    weights = cone_weights(RADIUS)
    reach = RADIUS - 1
    lane = lax.broadcasted_iota(jnp.int32, (out_pix, LANES), 1)
    at = [pooled[pl.ds(first + s, out_pix), :] for s in range(-reach, reach + 1)]
    sums = [at[reach]] + [at[reach + s] + at[reach - s] for s in range(1, reach + 1)]
    total = None
    for shift in range(reach + 1):
        mixed = None
        for s in range(reach + 1):
            weight = float(weights[reach + s, reach + shift])
            if weight > 0.0:
                term = weight * sums[s]
                mixed = term if mixed is None else mixed + term
        if shift == 0:
            total = mixed
        else:
            total = total + turn(jnp.where(lane < shift, 0.0, mixed), -shift, 1)
            total = total + turn(jnp.where(lane >= LANES - shift, 0.0, mixed), shift, 1)
    return total


def by_tile(blocks):
    span = TS // PIX
    tile_rows = blocks[0].shape[0] // span
    x = jnp.stack([block.reshape(tile_rows, span, LANES) for block in blocks], axis=1)
    x = x.reshape(tile_rows * 2, span, LANES)
    group = lax.broadcasted_iota(jnp.int32, x.shape, 2) // span
    row = lax.broadcasted_iota(jnp.int32, x.shape, 1)
    for bit in (1, 2, 4):
        row_on, lane_on = (row & bit) != 0, (group & bit) != 0
        ahead = turn(turn(x, -bit, 1), bit * span, 2)
        behind = turn(turn(x, bit, 1), -bit * span, 2)
        x = jnp.where(row_on == lane_on, x, jnp.where(lane_on, ahead, behind))
    x = x.reshape(tile_rows, 2, span, LANES)
    even, odd = x[:, 0], x[:, 1]
    upper = lax.broadcasted_iota(jnp.int32, even.shape, 2) >= HALF
    new_even = jnp.where(upper, turn(odd, HALF, 2), even)
    new_odd = jnp.where(upper, odd, turn(even, HALF, 2))
    return jnp.stack([new_even, new_odd], axis=1).reshape(tile_rows * 2 * span, LANES)


def from_partner(is_cross, lane):
    next_one = (lax.axis_index("gy") + (0 if is_cross else 1)) & 1
    spot = lane & (HALF - 1)
    start = next_one * (HALF - OUT)
    mine = (spot >= start) & (spot < start + OUT)
    shifts = []
    for kind, width in enumerate(WIDTHS):
        left, right = (OUT - width - FIRST[kind]) % LANES, (HALF - OUT - FIRST[kind]) % LANES
        shifts.append(left + next_one * (right - left))
    return mine, shifts


def edge_cross_kernel(base, cross, result):
    n_tiles = base.shape[1] // SUB
    mine, shifts = from_partner(True, lanes())
    for t in range(n_tiles):
        at = pl.ds(t * SUB, SUB)
        strip = cross[packed_at(t, n_tiles), :]
        kinds = range(4 if t in (0, n_tiles - 1) else 4 + STEPS)
        values = [
            jnp.where(mine, pltpu.roll(strip, shifts[kind], 1), base[kind, at, :])
            for kind in kinds
        ]
        for kind in kinds:
            result[kind, at, :] = values[kind]


def edge_kernel(
    slots_in, base, near, src, place, edge_last, slots, e, first, curl, eps_c, d, g, merged
):
    ext_rows = base.shape[1]
    rows = ext_rows - 2 * PAD
    n_tiles = ext_rows // SUB
    lane = lanes()
    spot = lane & (HALF - 1)
    mine, moves = from_partner(False, lane)

    for t in range(n_tiles):
        at = pl.ds(t * SUB, SUB)
        strip = near[packed_at(t, n_tiles), :]
        for kind in range(4 if t in (0, n_tiles - 1) else 4 + STEPS):
            value = jnp.where(mine, pltpu.roll(strip, moves[kind], 1), base[kind, at, :])
            if kind == 0:
                e[0, at, :] = value
            elif kind < 3:
                first[kind - 1, at, :] = value
            elif kind == 3:
                eps_c[at, :] = COURANT * value
            else:
                d[kind - 4, at, :] = value

    no_left = (spot == OUT) & ((lax.axis_index("gy") + lane * 0) == 0)
    shifts = Shifts(
        lambda values: {(): turn(values[()], -1, 1)},
        lambda values: {(): turn(values[()], 1, 1)},
    )

    def load_hx(t):
        return {(): first[0, pl.ds(t * SUB, SUB), :]}

    def load_hy(t):
        return {(): first[1, pl.ds(t * SUB, SUB), :]}

    first_curl(n_tiles, shifts, load_hx, load_hy, curl)
    shifts.prev_col = lambda values: {(): jnp.where(no_left, values[()], turn(values[()], 1, 1))}
    steps(
        n_tiles, [()], shifts, e, curl,
        lambda key, t: eps_c[pl.ds(t * SUB, SUB), :],
        lambda step, key, t: src[step, pl.ds(t * SUB, SUB), :],
        lambda values, key: turn(values[()], HALF, 1),
    )
    inside = (spot >= OUT - NEAR) & (spot < OUT + KEEP)
    inside = inside | ((spot >= HALF - OUT - KEEP) & (spot < HALF - OUT + NEAR))
    for t in range(1, n_tiles - 1):
        value = gradient([()], t, e, lambda step, key, t: d[step, pl.ds(t * SUB, SUB), :])[()]
        g[pl.ds(t * SUB, SUB), :] = jnp.where(inside, value, 0.0)

    def store(key, t, *values):
        for kind, value in enumerate(values):
            edge_last[kind, pl.ds(t * SUB - PAD, SUB), :] = value

    edge_filter(g, merged)
    edge_slots(merged, slots_in, place, slots)
    last_fields(
        range(PAD // SUB, n_tiles - PAD // SUB), [()], shifts, e, load_hx, load_hy, store
    )


def edge_filter(g, merged):
    lane = lanes()
    span, reach = TS // PIX, RADIUS - 1
    pixel = {}
    for j in range(-reach, span + reach):
        value = g[pl.ds(PAD + PIX * j, SUB, stride=TS), :]
        pixel[j] = value + g[pl.ds(PAD + PIX * j + 1, SUB, stride=TS), :]

    weights = cone_weights(RADIUS)
    spans = []
    for row in range(span):
        sums = [pixel[row]] + [pixel[row + s] + pixel[row - s] for s in range(1, reach + 1)]
        move = (row & 1) + SIDE * ((row >> 1) & 1)
        total = None
        for shift in range(reach + 1):
            mixed = None
            for s in range(reach + 1):
                weight = float(weights[reach + s, reach + shift])
                if weight > 0.0:
                    term = weight * sums[s]
                    mixed = term if mixed is None else mixed + term
            for place in {PIX * shift, -PIX * shift}:
                term = turn(mixed, move + place, 1) + turn(mixed, move + place - 1, 1)
                total = term if total is None else total + term
        spans.append(total)
    even = (lane & 1) == 0
    window = ((lane - OUT) & (HALF - 1)) < SIDE
    for n in range(2):
        a, b, c, d = spans[4 * n : 4 * n + 4]
        merged[n] = jnp.where(window, jnp.where(even, a, b), jnp.where(even, c, d))


def edge_slots(merged, slots_in, place, slots):
    lane = lanes()
    span = TS // PIX
    row, pixel = lane // span % span, lane % span
    start = (lane & HALF) + OUT + PIX * pixel + (row & 1) + SIDE * ((row >> 1) & 1)
    edge = []
    for side in range(2):
        index = (start + OUT * side) & (LANES - 1)
        low, high = (jnp.take_along_axis(merged[n], index, axis=1) for n in range(2))
        edge.append(jnp.where(row < span // 2, low, high))
    parts = split2(jnp.concatenate(edge, axis=0))
    slots[...] = slots_in[...] + dot(place[...], jnp.concatenate(parts, axis=0))


def deliver_kernel(last, edge_last, slots, out_fields, out_slots, merged, sems):
    rows, cols = merged.shape[2], merged.shape[3]
    n_lanes = cols // LANES
    lane = lanes()
    copies = [pltpu.make_async_copy(slots, out_slots.at[0], sems.at[6])]
    copies[0].start()
    for kind in range(3):
        for layer in range(2):
            for t in range(rows // SUB):
                at = pl.ds(t * SUB, SUB)
                edge = edge_last[kind, at, :]
                for k in range(n_lanes):
                    value = last[kind, layer, k, at, :]
                    if k == 0:
                        value = jnp.where(lane < KEEP, turn(edge, -HALF * layer - OUT, 1), value)
                    if k == n_lanes - 1:
                        value = jnp.where(
                            lane >= LANES - KEEP, turn(edge, -HALF * layer - SIDE - OUT, 1), value
                        )
                    merged[kind, layer, at, lane_tile(k)] = value
            copies.append(
                pltpu.make_async_copy(
                    merged.at[kind, layer], out_fields.at[kind, layer], sems.at[2 * kind + layer]
                )
            )
            copies[-1].start()
    for copy in copies:
        copy.wait()


def vmem():
    return pl.BlockSpec(memory_space=pltpu.VMEM)


def shape(*dims, dtype=F32):
    return jax.ShapeDtypeStruct(dims, dtype)


def call(kernel, outs, n_in, *, in_space=pltpu.VMEM, out_specs=None, scratch=(), flops=0, size=0):
    return pl.pallas_call(
        kernel,
        out_shape=outs,
        in_specs=[pl.BlockSpec(memory_space=in_space)] * n_in,
        out_specs=out_specs or tuple(vmem() for _ in outs),
        scratch_shapes=list(scratch),
        compiler_params=pltpu.CompilerParams(vmem_limit_bytes=40 * 1024 * 1024),
        cost_estimate=pl.CostEstimate(flops=flops, bytes_accessed=size, transcendentals=0),
    )


def on_device(adj_fields, inv_eps, fwd_diff, mon_x, mon_y, mon_amp, design_mask, tile_owner):
    rows, cols = adj_fields.shape[2], adj_fields.shape[3]
    assert cols == 2 * LANES and rows % TS == 0
    gx_count, gy_count = lax.axis_size("gx"), lax.axis_size("gy")
    owners = gx_count * gy_count
    tiles = (rows // TS) * (cols // TS)
    width = 2 * (TS // PIX) ** 2
    assert width == LANES
    capacity = max(8, 2 * tiles // owners)
    assert rows == TS * SUB and cols == 2 * TS * SUB
    ext_rows = rows + 2 * PAD
    n_lanes = cols // LANES
    cells = rows * cols
    blocks = (adj_fields, inv_eps, fwd_diff)


    strip = shape(4 + STEPS, 2, SUB, cols)
    cross, near = call(
        rows_kernel, (strip, strip), 3, in_space=pltpu.HBM,
        scratch=(
            pltpu.VMEM((2, 4, 2, SUB, cols), F32),
            pltpu.SemaphoreType.DMA((10,)),
        ),
        size=2**20,
    )(*(pltpu.with_memory_space_constraint(block, pltpu.HBM) for block in blocks))

    def pairs(count, start):
        some = [(i, i + 1) for i in range(start, count - 1, 2)]
        return some + [(j, i) for i, j in some]

    cross = lax.ppermute(cross, "gx", pairs(gx_count, 1))
    near = lax.ppermute(near, "gx", pairs(gx_count, 0))

    packed = shape(ext_rows - SUB, LANES)
    channels = mon_x.shape[0]
    cross_cols, near_cols, base, src, src_edge, place, place_edge = call(
        lambda *refs: prep_kernel(capacity, *refs),
        (
            packed,
            packed,
            shape(4 + STEPS, ext_rows, LANES),
            shape(STEPS, 2, ext_rows, cols),
            shape(STEPS, ext_rows, LANES),
            shape(owners * capacity, tiles, dtype=BF16),
            shape(owners * capacity, 4 * SUB, dtype=BF16),
        ),
        8,
        flops=16 * ext_rows * (cols + LANES) * 3 * channels,
        size=64 * cells,
    )(
        *blocks,
        mon_x.reshape(1, channels),
        mon_y.reshape(1, channels),
        mon_amp,
        design_mask.reshape(1, tiles),
        tile_owner.reshape(1, tiles),
    )
    cross_cols, near_cols = call(
        corners_kernel, (packed, packed), 4, flops=cells, size=8 * ext_rows * LANES
    )(cross_cols, near_cols, cross, near)
    cross_cols = lax.ppermute(cross_cols, "gy", pairs(gy_count, 1))
    near_cols = lax.ppermute(near_cols, "gy", pairs(gy_count, 0))

    plane = (2, n_lanes, ext_rows, LANES)
    last, slots, base = call(
        inner_kernel,
        (
            shape(3, 2, n_lanes, rows, LANES),
            shape(owners * capacity, width),
            shape(4 + STEPS, ext_rows, LANES),
        ),
        9,
        scratch=(
            pltpu.VMEM((1 + STEPS,) + plane, F32),
            pltpu.VMEM(plane, F32),
            pltpu.VMEM(plane, F32),
            pltpu.VMEM(plane, F32),
            pltpu.VMEM((2, ext_rows // PIX, LANES), F32),
        ),
        flops=200 * cells,
        size=96 * cells,
    )(*blocks, cross, near, src, pool_matrices(), base, place)

    plane = (ext_rows, LANES)
    (base,) = call(
        edge_cross_kernel, (shape(4 + STEPS, *plane),), 2, flops=10 * cells, size=8 * cells
    )(base, cross_cols)
    edge_last, outgoing = call(
        edge_kernel,
        (shape(3, rows, LANES), pltpu.VMEM((owners * capacity, width), F32)),
        5,
        scratch=(
            pltpu.VMEM((1 + STEPS,) + plane, F32),
            pltpu.VMEM((2,) + plane, F32),
            pltpu.VMEM(plane, F32),
            pltpu.VMEM(plane, F32),
            pltpu.VMEM((STEPS,) + plane, F32),
            pltpu.VMEM(plane, F32),
            pltpu.VMEM((2, SUB, LANES), F32),
        ),
        flops=50 * cells,
        size=16 * cells,
    )(slots, base, near_cols, src_edge, place_edge)

    outgoing = outgoing.reshape(owners, capacity, width)
    incoming = lax.all_to_all(outgoing, ("gx", "gy"), split_axis=0, concat_axis=0, tiled=True)
    anywhere = pl.BlockSpec(memory_space=pl.ANY)
    return call(
        deliver_kernel,
        (shape(3, 2, rows, cols), shape(1, *incoming.shape)),
        3,
        out_specs=(anywhere, anywhere),
        scratch=(pltpu.VMEM((3, 2, rows, cols), F32), pltpu.SemaphoreType.DMA((7,))),
        flops=20 * cells,
        size=48 * cells,
    )(last, edge_last, pltpu.with_memory_space_constraint(incoming, pltpu.VMEM))


def solution(mesh):
    placed = (
        P(None, None, ("parts", "gx"), "gy"),
        P(None, ("parts", "gx"), "gy"),
        P(None, None, ("parts", "gx"), "gy"),
        P("parts"),
        P("parts"),
        P(None, "parts"),
        P(("parts", "gx"), "gy", None),
        P(("parts", "gx"), "gy", None, None),
    )
    return jax.shard_map(
        on_device,
        mesh=mesh,
        in_specs=placed,
        out_specs=(
            P(None, None, ("parts", "gx"), "gy"),
            P(("parts", "gx", "gy"), None, None, None),
        ),
        check_vma=False,
    )
```

```python
import jax
import jax.numpy as jnp
import ml_dtypes
import numpy as np
from jax import lax
from jax.experimental import pallas as pl
from jax.experimental.pallas import tpu as pltpu
from jax.sharding import PartitionSpec as P

STEPS = 4
PIX = 2
TS = 16
RADIUS = 4
COURANT = 0.6
COUPLING = 0.25

LANES = 128
SUB = 8
FAR = STEPS + PIX * (RADIUS - 1)
NEAR = PIX * (RADIUS - 1)
LEFT_OVER = FAR - SUB
PAD = 2 * SUB
HALF = LANES // 2
SIDE = HALF // 2
OUT = SIDE // 2
KEEP = 8
F32 = jnp.float32
BF16 = jnp.bfloat16
WIDTHS = (FAR,) * 4 + (NEAR,) * STEPS
FIRST = tuple(sum(WIDTHS[:k]) for k in range(len(WIDTHS)))
assert sum(WIDTHS) <= HALF and FAR <= OUT and STEPS + KEEP <= OUT


def cone_weights(radius):
    reach_cells = radius - 1
    offsets = np.arange(-reach_cells, reach_cells + 1)
    distance = np.sqrt(offsets[:, None] * offsets[:, None] + offsets[None, :] * offsets[None, :])
    weights = np.maximum(radius - distance, 0.0)
    return weights / weights.sum()


def pool_matrices():
    inner = np.zeros((2, LANES, LANES), np.float32)
    for j in range(KEEP, 2 * LANES - KEEP):
        inner[j // LANES, j % LANES, j // PIX] = 1.0
    return inner.astype(ml_dtypes.bfloat16)


def split2(value):
    high = value.astype(BF16)
    return high, (value - high.astype(F32)).astype(BF16)


def split3(value):
    high = value.astype(BF16)
    rest = value - high.astype(F32)
    mid = rest.astype(BF16)
    return high, mid, (rest - mid.astype(F32)).astype(BF16)


def dot(a, b):
    return jnp.dot(a, b, preferred_element_type=F32)


def turn(value, shift, axis):
    size = value.shape[axis]
    return pltpu.roll(value, shift % size, axis) if shift % size else value


def lanes():
    return lax.broadcasted_iota(jnp.int32, (SUB, LANES), 1)


def subs():
    return lax.broadcasted_iota(jnp.int32, (SUB, LANES), 0)


def lane_tile(k):
    return pl.ds(k * LANES, LANES)


def is_odd(axis):
    return ((subs() * 0 + lax.axis_index(axis)) & 1) == 1


def rows_kernel(fields, eps, fwd, cross, near, hold, sems):
    rows, cols = fields.shape[2], fields.shape[3]
    sub = subs()
    odd = lax.axis_index("gx") & 1
    parts = []
    for n, (out, at_end) in enumerate(((cross, odd), (near, 1 - odd))):
        at = pl.ds(pl.multiple_of(at_end * (rows - SUB), SUB), SUB)
        rest = pl.ds(pl.multiple_of(SUB + at_end * (rows - 3 * SUB), SUB), SUB)
        pairs = (
            (fields.at[:, :, rest, :], hold.at[n, pl.ds(0, 3)]),
            (eps.at[:, rest, :], hold.at[n, 3]),
            (fwd.at[:, :, at, :], out.at[pl.ds(4, STEPS)]),
            (fields.at[:, :, at, :], out.at[pl.ds(0, 3)]),
            (eps.at[:, at, :], out.at[3]),
        )
        copies = [
            pltpu.make_async_copy(src, dst, sems.at[len(pairs) * n + m])
            for m, (src, dst) in enumerate(pairs)
        ]
        parts.append((n, out, at_end, copies))
    for group in (slice(0, 3), slice(3, 5)):
        for part in parts:
            for copy in part[3][group]:
                copy.start()
    for n, out, at_end, copies in parts:
        for copy in copies[:3]:
            copy.wait()
        low = (1 - at_end) * NEAR
        rest = (sub >= low) & (sub < low + LEFT_OVER)
        shift = NEAR + at_end * (LEFT_OVER - NEAR)
        for kind in range(4):
            for layer in range(2):
                values = []
                for k in range(cols // LANES):
                    moved = pltpu.roll(hold[n, kind, layer, :, lane_tile(k)], shift, 0)
                    values.append(jnp.where(rest, moved, out[4 + kind, layer, :, lane_tile(k)]))
                for k, value in enumerate(values):
                    out[4 + kind, layer, :, lane_tile(k)] = value
    for part in parts:
        for copy in part[3][3:]:
            copy.wait()


def halo_tile(cross, near, odd, tile, kind, layer, at):
    is_above = tile < 2
    outer = tile in (0, 3)
    if outer and kind >= 4:
        return None
    plane = kind + (4 if outer else 0)
    a, b = near[plane, layer, :, at], cross[plane, layer, :, at]
    value = jnp.where(odd, a, b) if is_above else jnp.where(odd, b, a)
    if outer:
        value = turn(value, -LEFT_OVER if is_above else LEFT_OVER, 0)
    return value


def core_tile(fields, eps, fwd, at, kind, layer, cols):
    if kind < 3:
        return fields[kind, layer, at, cols]
    if kind == 3:
        return eps[layer, at, cols]
    return fwd[kind - 4, layer, at, cols]


def pack_tile(load, lane, right):
    total = jnp.zeros((SUB, LANES), F32)
    for kind, width in enumerate(WIDTHS):
        for layer in range(2):
            value = load(kind, layer)
            if value is None:
                continue
            first = FIRST[kind] + HALF * layer
            value = turn(value, first + width if right else first, 1)
            total = jnp.where((lane >= first) & (lane < first + width), value, total)
    return total


def edge_tile(load, kind, lane, n_lanes):
    spot = lane & (HALF - 1)
    total = None
    for layer in range(2):
        low = turn(load(kind, layer, 0), HALF * layer + OUT, 1)
        high = turn(load(kind, layer, n_lanes - 1), HALF * layer + SIDE + OUT, 1)
        value = jnp.where(spot < SIDE, low, high)
        total = value if total is None else jnp.where(lane < HALF, total, value)
    return total


def cols_kernel(fields, eps, fwd, cross, near, base):
    rows, cols = fields.shape[2], fields.shape[3]
    n_lanes = cols // LANES
    lane, odd = lanes(), is_odd("gy")

    def tile(t, carry):
        at = pl.ds(pl.multiple_of(t * SUB, SUB), SUB)
        out_at = pl.ds(pl.multiple_of(t * SUB + PAD, SUB), SUB)

        def load(kind, layer, k):
            return core_tile(fields, eps, fwd, at, kind, layer, lane_tile(k))

        left = pack_tile(lambda kind, layer: load(kind, layer, 0), lane, False)
        right = pack_tile(lambda kind, layer: load(kind, layer, n_lanes - 1), lane, True)
        cross[out_at, :] = jnp.where(odd, right, left)
        near[out_at, :] = jnp.where(odd, left, right)
        for kind in range(4 + STEPS):
            base[kind, out_at, :] = edge_tile(load, kind, lane, n_lanes)
        return carry

    lax.fori_loop(0, rows // SUB, tile, 0, unroll=4)
    zero = jnp.zeros((SUB, LANES), F32)
    for out in (cross, near):
        for at in (0, SUB, PAD + rows):
            out[pl.ds(at, SUB), :] = zero


def packed_at(t, n_tiles):
    return pl.ds((t if t < n_tiles - 1 else 0) * SUB, SUB)


def corners_kernel(cross_in, near_in, cross_rows, near_rows, cross, near):
    rows, cols = cross.shape[0] - 3 * SUB, cross_rows.shape[3]
    lane, odd, odd_col = lanes(), is_odd("gx"), is_odd("gy")
    is_first = subs() >= SUB - LEFT_OVER
    core = pl.ds(PAD, rows)
    cross[core, :] = cross_in[core, :]
    near[core, :] = near_in[core, :]
    for base, tiles in ((0, (0, 3)), (SUB, (1,)), (PAD + rows, (2,))):
        at = pl.ds(base, SUB)
        packs = []
        for lo, is_right in ((0, False), (cols - LANES, True)):

            def load(kind, layer):
                values = [
                    halo_tile(cross_rows, near_rows, odd, tile, kind, layer, pl.ds(lo, LANES))
                    for tile in tiles
                ]
                if len(values) == 1 or values[0] is None:
                    return values[0]
                return jnp.where(is_first, values[0], values[1])

            packs.append(pack_tile(load, lane, is_right))
        left, right = packs
        cross[at, :] = jnp.where(odd_col, right, left)
        near[at, :] = jnp.where(odd_col, left, right)


def prep_kernel(
    capacity, fields, eps, fwd, mon_x, mon_y, amp, mask, owner, cross, near, base, src, src_edge, place, place_edge
):
    cols_kernel(fields, eps, fwd, cross, near, base)
    side_kernel(capacity, fields.shape[2], mon_x, mon_y, amp, mask, owner, src, src_edge, place, place_edge)


def side_kernel(capacity, rows, mon_x, mon_y, amp, mask, owner, src, src_edge, place, place_edge):
    _, _, ext_rows, cols = src.shape
    channels = mon_x.shape[1]
    row = mon_x[...] - lax.axis_index("gx") * rows + PAD
    col = mon_y[...] - lax.axis_index("gy") * cols
    in_left = (col >= -OUT) & (col < OUT)
    in_right = (col >= cols - OUT) & (col < cols + OUT)
    edge = jnp.where(in_left, col + OUT, jnp.where(in_right, col - cols + OUT + SIDE, -LANES))
    layer = lax.broadcasted_iota(jnp.int32, (1, channels), 1) & 1
    edge = edge + HALF * layer
    inside = jnp.where((col >= 0) & (col < cols), col, -1)
    one_y = lax.broadcasted_iota(jnp.int32, (cols, channels), 0) == inside
    one_e = lax.broadcasted_iota(jnp.int32, (LANES, channels), 0) == edge
    one_y = jnp.where(one_y, 1.0, 0.0).astype(BF16)
    one_e = jnp.where(one_e, 1.0, 0.0).astype(BF16)
    one_y = jnp.concatenate([one_y] * 3, axis=1)
    one_e = jnp.concatenate([one_e] * 3, axis=1)
    one_x = lax.broadcasted_iota(jnp.int32, (ext_rows, channels), 0) == row
    one_x = jnp.where(one_x, 1.0, 0.0).astype(F32)
    nt = (((1,), (1,)), ((), ()))
    for step in range(STEPS):
        parts = [part.astype(F32) for part in split3(amp[pl.ds(step, 1), :])]
        lhs = jnp.concatenate([one_x * part for part in parts], axis=1)
        src_edge[step] = lax.dot_general(lhs.astype(BF16), one_e, nt, preferred_element_type=F32)
        layer_wide = jnp.concatenate([layer] * 3, axis=1)
        for which in range(2):
            some = jnp.where(layer_wide == which, lhs, 0.0).astype(BF16)
            src[step, which] = lax.dot_general(some, one_y, nt, preferred_element_type=F32)
    tiles = owner.shape[1]
    own = owner[...].astype(F32)
    own_wide = jnp.broadcast_to(own, (tiles, tiles))
    earlier = lax.broadcasted_iota(jnp.int32, (tiles, tiles), 0) < lax.broadcasted_iota(
        jnp.int32, (tiles, tiles), 1
    )
    same = (own_wide.T == own_wide) & earlier
    slot = jnp.sum(jnp.where(same, 1.0, 0.0), axis=0, keepdims=True)
    dest = owner[...] * capacity + slot.astype(jnp.int32)
    dest = jnp.where(mask[...] != 0, dest, -1)
    hit = lax.broadcasted_iota(jnp.int32, place.shape, 0) == dest
    hit = jnp.where(hit, 1.0, 0.0).astype(BF16)
    place[...] = hit
    tile_cols = cols // TS
    column = lax.broadcasted_iota(jnp.int32, (tiles, 4 * SUB), 1)
    wanted = (column % SUB) * tile_cols + ((column // SUB) & 1) * (tile_cols - 1)
    picked = lax.broadcasted_iota(jnp.int32, (tiles, 4 * SUB), 0) == wanted
    place_edge[...] = dot(hit, jnp.where(picked, 1.0, 0.0).astype(BF16)).astype(BF16)


class Shifts:
    def __init__(self, next_col, prev_col):
        self.next_col, self.prev_col = next_col, prev_col
        self.bottom, self.top = subs() == SUB - 1, subs() == 0

    def up(self, tile):
        return {key: turn(value, -1, 0) for key, value in tile.items()}

    def down(self, tile):
        return {key: turn(value, 1, 0) for key, value in tile.items()}

    def below(self, up_here, up_next):
        return {key: jnp.where(self.bottom, up_next[key], up_here[key]) for key in up_here}

    def above(self, down_here, down_before):
        return {key: jnp.where(self.top, down_before[key], down_here[key]) for key in down_here}


def tile_at(t):
    return (pl.ds(t * SUB, SUB), slice(None))


def first_curl(n_tiles, shifts, load_hx, load_hy, curl):
    before = None
    for t in range(n_tiles):
        hx, hy = load_hx(t), load_hy(t)
        down = shifts.down(hy)
        over = shifts.above(down, before if t else down)
        left = shifts.prev_col(hx)
        for key in hx:
            curl[key + tile_at(t)] = (hy[key] - over[key]) - (hx[key] - left[key])
        before = down


def steps(n_tiles, keys, shifts, e, curl, eps_of, src_of, other):
    no_above = shifts.top & ((lax.axis_index("gx") + subs() * 0) == 0)
    for step in range(STEPS):
        low, high = (0, n_tiles) if step == 0 else (1, n_tiles - 1)

        def load(t):
            return {key: e[(step,) + key + tile_at(t)] for key in keys}

        here = load(low)
        up = shifts.up(here)
        down_before = shifts.down(load(max(low - 1, 0)))
        for t in range(low, high):
            after = load(min(t + 1, n_tiles - 1))
            up_next, down = shifts.up(after), shifts.down(here)
            below, above = shifts.below(up, up_next), shifts.above(down, down_before)
            right, left = shifts.next_col(here), shifts.prev_col(here)
            for key in keys:
                center, over = here[key], above[key]
                if t == PAD // SUB:
                    over = jnp.where(no_above, center, over)
                ring = (below[key] + over) + (right[key] + left[key]) - 4.0 * center
                change = curl[key + tile_at(t)] - COURANT * ring
                if step < STEPS - 1:
                    curl[key + tile_at(t)] = change
                change = change + COUPLING * (other(here, key) - center)
                e[(step + 1,) + key + tile_at(t)] = (
                    center - eps_of(key, t) * change + src_of(step, key, t)
                )
            here, up, down_before = after, up_next, down


def gradient(keys, t, e, change_of):
    result = {}
    for key in keys:
        total = None
        for step in range(STEPS):
            term = e[(step + 1,) + key + tile_at(t)] * change_of(step, key, t)
            total = term if total is None else total + term
        result[key] = -total
    return result


def last_fields(tiles, keys, shifts, e, load_hx, load_hy, store):
    def total(t):
        result = {}
        for key in keys:
            parts = [e[(step,) + key + tile_at(t)] for step in range(STEPS)]
            result[key] = (parts[0] + parts[1]) + (parts[2] + parts[3])
        return result

    here = total(tiles[0])
    up = shifts.up(here)
    for t in tiles:
        after = total(t + 1)
        up_next = shifts.up(after)
        below, right = shifts.below(up, up_next), shifts.next_col(here)
        hx, hy = load_hx(t), load_hy(t)
        for key in keys:
            store(
                key, t, e[(STEPS,) + key + tile_at(t)],
                hx[key] + COURANT * (right[key] - here[key]),
                hy[key] - COURANT * (below[key] - here[key]),
            )
        here, up = after, up_next


def row_pairs(ref, lead, count):
    even = ref[lead + (pl.ds(0, count, stride=PIX), slice(None))]
    return even + ref[lead + (pl.ds(1, count, stride=PIX), slice(None))]


def inner_kernel(
    fields, eps, fwd, cross, near, src, mats, base_in, place, last, slots, base, e, curl, eps_c, g, pooled
):
    rows, cols = fields.shape[2], fields.shape[3]
    n_tiles = (rows + 2 * PAD) // SUB
    n_lanes = cols // LANES
    lane, odd = lanes(), is_odd("gx")
    halo_of = {0: 0, 1: 1, n_tiles - 2: 2, n_tiles - 1: 3}
    keys = [(layer, k) for layer in range(2) for k in range(n_lanes)]

    def load(kind, layer, t, k):
        if t in halo_of:
            return halo_tile(cross, near, odd, halo_of[t], kind, layer, lane_tile(k))
        return core_tile(fields, eps, fwd, pl.ds(t * SUB - PAD, SUB), kind, layer, lane_tile(k))

    def load_all(kind, t):
        return {key: load(kind, key[0], t, key[1]) for key in keys}

    at_end, at_start = lane == LANES - 1, lane == 0

    def next_col(values):
        moved = {key: turn(value, -1, 1) for key, value in values.items()}
        return {
            (l, k): jnp.where(at_end, moved[l, (k + 1) % n_lanes], moved[l, k]) for l, k in keys
        }

    def prev_col(values):
        moved = {key: turn(value, 1, 1) for key, value in values.items()}
        return {
            (l, k): jnp.where(at_start, moved[l, (k - 1) % n_lanes], moved[l, k]) for l, k in keys
        }

    shifts = Shifts(next_col, prev_col)
    for t in range(n_tiles):
        for key in keys:
            e[(0,) + key + tile_at(t)] = load(0, key[0], t, key[1])
            eps_c[key + tile_at(t)] = COURANT * load(3, key[0], t, key[1])
    first_curl(n_tiles, shifts, lambda t: load_all(1, t), lambda t: load_all(2, t), curl)
    steps(
        n_tiles, keys, shifts, e, curl,
        lambda key, t: eps_c[key + tile_at(t)],
        lambda step, key, t: src[step, key[0], pl.ds(t * SUB, SUB), lane_tile(key[1])],
        lambda values, key: values[1 - key[0], key[1]],
    )
    for t in range(1, n_tiles - 1):
        values = gradient(keys, t, e, lambda step, key, t: load(4 + step, key[0], t, key[1]))
        for key in keys:
            g[key + tile_at(t)] = values[key]

    def store(key, t, *values):
        for kind, value in enumerate(values):
            last[(kind,) + key + (pl.ds(t * SUB - PAD, SUB), slice(None))] = value

    last_fields(
        range(PAD // SUB, n_tiles - PAD // SUB), keys, shifts, e,
        lambda t: load_all(1, t), lambda t: load_all(2, t), store,
    )
    for layer in range(2):
        total = None
        for k in range(n_lanes):
            for part in split2(row_pairs(g, (layer, k), n_tiles * SUB // PIX)):
                term = dot(part, mats[k])
                total = term if total is None else total + term
        pooled[layer] = total

    vals = by_tile([cone_filter(pooled.at[layer], rows // PIX, PAD // PIX) for layer in range(2)])
    high, low = split2(vals)
    slots[...] = dot(place[...], high) + dot(place[...], low)

    for t in range(n_tiles):
        for kind in range(4 + STEPS):
            at = pl.ds(t * SUB, SUB)
            if t not in halo_of:
                base[kind, at, :] = base_in[kind, at, :]
            elif kind < 4 or t not in (0, n_tiles - 1):
                base[kind, at, :] = edge_tile(
                    lambda kind, layer, k: load(kind, layer, t, k), kind, lane, n_lanes
                )


def cone_filter(pooled, out_pix, first):
    weights = cone_weights(RADIUS)
    reach = RADIUS - 1
    lane = lax.broadcasted_iota(jnp.int32, (out_pix, LANES), 1)
    at = [pooled[pl.ds(first + s, out_pix), :] for s in range(-reach, reach + 1)]
    sums = [at[reach]] + [at[reach + s] + at[reach - s] for s in range(1, reach + 1)]
    total = None
    for shift in range(reach + 1):
        mixed = None
        for s in range(reach + 1):
            weight = float(weights[reach + s, reach + shift])
            if weight > 0.0:
                term = weight * sums[s]
                mixed = term if mixed is None else mixed + term
        if shift == 0:
            total = mixed
        else:
            total = total + turn(jnp.where(lane < shift, 0.0, mixed), -shift, 1)
            total = total + turn(jnp.where(lane >= LANES - shift, 0.0, mixed), shift, 1)
    return total


def by_tile(blocks):
    span = TS // PIX
    tile_rows = blocks[0].shape[0] // span
    x = jnp.stack([block.reshape(tile_rows, span, LANES) for block in blocks], axis=1)
    x = x.reshape(tile_rows * 2, span, LANES)
    group = lax.broadcasted_iota(jnp.int32, x.shape, 2) // span
    row = lax.broadcasted_iota(jnp.int32, x.shape, 1)
    for bit in (1, 2, 4):
        row_on, lane_on = (row & bit) != 0, (group & bit) != 0
        ahead = turn(turn(x, -bit, 1), bit * span, 2)
        behind = turn(turn(x, bit, 1), -bit * span, 2)
        x = jnp.where(row_on == lane_on, x, jnp.where(lane_on, ahead, behind))
    x = x.reshape(tile_rows, 2, span, LANES)
    even, odd = x[:, 0], x[:, 1]
    upper = lax.broadcasted_iota(jnp.int32, even.shape, 2) >= HALF
    new_even = jnp.where(upper, turn(odd, HALF, 2), even)
    new_odd = jnp.where(upper, odd, turn(even, HALF, 2))
    return jnp.stack([new_even, new_odd], axis=1).reshape(tile_rows * 2 * span, LANES)


def from_partner(is_cross, lane):
    next_one = (lax.axis_index("gy") + (0 if is_cross else 1)) & 1
    spot = lane & (HALF - 1)
    start = next_one * (HALF - OUT)
    mine = (spot >= start) & (spot < start + OUT)
    shifts = []
    for kind, width in enumerate(WIDTHS):
        left, right = (OUT - width - FIRST[kind]) % LANES, (HALF - OUT - FIRST[kind]) % LANES
        shifts.append(left + next_one * (right - left))
    return mine, shifts


def edge_cross_kernel(base, cross, result):
    n_tiles = base.shape[1] // SUB
    mine, shifts = from_partner(True, lanes())
    for t in range(n_tiles):
        at = pl.ds(t * SUB, SUB)
        strip = cross[packed_at(t, n_tiles), :]
        kinds = range(4 if t in (0, n_tiles - 1) else 4 + STEPS)
        values = [
            jnp.where(mine, pltpu.roll(strip, shifts[kind], 1), base[kind, at, :])
            for kind in kinds
        ]
        for kind in kinds:
            result[kind, at, :] = values[kind]


def edge_kernel(
    slots_in, base, near, src, place, edge_last, slots, e, first, curl, eps_c, d, g, merged
):
    ext_rows = base.shape[1]
    rows = ext_rows - 2 * PAD
    n_tiles = ext_rows // SUB
    lane = lanes()
    spot = lane & (HALF - 1)
    mine, moves = from_partner(False, lane)

    for t in range(n_tiles):
        at = pl.ds(t * SUB, SUB)
        strip = near[packed_at(t, n_tiles), :]
        for kind in range(4 if t in (0, n_tiles - 1) else 4 + STEPS):
            value = jnp.where(mine, pltpu.roll(strip, moves[kind], 1), base[kind, at, :])
            if kind == 0:
                e[0, at, :] = value
            elif kind < 3:
                first[kind - 1, at, :] = value
            elif kind == 3:
                eps_c[at, :] = COURANT * value
            else:
                d[kind - 4, at, :] = value

    no_left = (spot == OUT) & ((lax.axis_index("gy") + lane * 0) == 0)
    shifts = Shifts(
        lambda values: {(): turn(values[()], -1, 1)},
        lambda values: {(): turn(values[()], 1, 1)},
    )

    def load_hx(t):
        return {(): first[0, pl.ds(t * SUB, SUB), :]}

    def load_hy(t):
        return {(): first[1, pl.ds(t * SUB, SUB), :]}

    first_curl(n_tiles, shifts, load_hx, load_hy, curl)
    shifts.prev_col = lambda values: {(): jnp.where(no_left, values[()], turn(values[()], 1, 1))}
    steps(
        n_tiles, [()], shifts, e, curl,
        lambda key, t: eps_c[pl.ds(t * SUB, SUB), :],
        lambda step, key, t: src[step, pl.ds(t * SUB, SUB), :],
        lambda values, key: turn(values[()], HALF, 1),
    )
    inside = (spot >= OUT - NEAR) & (spot < OUT + KEEP)
    inside = inside | ((spot >= HALF - OUT - KEEP) & (spot < HALF - OUT + NEAR))
    for t in range(1, n_tiles - 1):
        value = gradient([()], t, e, lambda step, key, t: d[step, pl.ds(t * SUB, SUB), :])[()]
        g[pl.ds(t * SUB, SUB), :] = jnp.where(inside, value, 0.0)

    def store(key, t, *values):
        for kind, value in enumerate(values):
            edge_last[kind, pl.ds(t * SUB - PAD, SUB), :] = value

    last_fields(
        range(PAD // SUB, n_tiles - PAD // SUB), [()], shifts, e, load_hx, load_hy, store
    )
    edge_filter(g, merged)
    edge_slots(merged, slots_in, place, slots)


def edge_filter(g, merged):
    lane = lanes()
    span, reach = TS // PIX, RADIUS - 1
    pixel = {}
    for j in range(-reach, span + reach):
        value = g[pl.ds(PAD + PIX * j, SUB, stride=TS), :]
        pixel[j] = value + g[pl.ds(PAD + PIX * j + 1, SUB, stride=TS), :]

    weights = cone_weights(RADIUS)
    spans = []
    for row in range(span):
        sums = [pixel[row]] + [pixel[row + s] + pixel[row - s] for s in range(1, reach + 1)]
        move = (row & 1) + SIDE * ((row >> 1) & 1)
        total = None
        for shift in range(reach + 1):
            mixed = None
            for s in range(reach + 1):
                weight = float(weights[reach + s, reach + shift])
                if weight > 0.0:
                    term = weight * sums[s]
                    mixed = term if mixed is None else mixed + term
            for place in {PIX * shift, -PIX * shift}:
                term = turn(mixed, move + place, 1) + turn(mixed, move + place - 1, 1)
                total = term if total is None else total + term
        spans.append(total)
    even = (lane & 1) == 0
    window = ((lane - OUT) & (HALF - 1)) < SIDE
    for n in range(2):
        a, b, c, d = spans[4 * n : 4 * n + 4]
        merged[n] = jnp.where(window, jnp.where(even, a, b), jnp.where(even, c, d))


def edge_slots(merged, slots_in, place, slots):
    lane = lanes()
    span = TS // PIX
    row, pixel = lane // span % span, lane % span
    start = (lane & HALF) + OUT + PIX * pixel + (row & 1) + SIDE * ((row >> 1) & 1)
    edge = []
    for side in range(2):
        index = (start + OUT * side) & (LANES - 1)
        low, high = (jnp.take_along_axis(merged[n], index, axis=1) for n in range(2))
        edge.append(jnp.where(row < span // 2, low, high))
    parts = split2(jnp.concatenate(edge, axis=0))
    slots[...] = slots_in[...] + dot(place[...], jnp.concatenate(parts, axis=0))


def deliver_kernel(last, edge_last, slots, out_fields, out_slots, merged, sems):
    rows, cols = merged.shape[2], merged.shape[3]
    n_lanes = cols // LANES
    lane = lanes()
    copies = [pltpu.make_async_copy(slots, out_slots.at[0], sems.at[6])]
    copies[0].start()
    for kind in range(3):
        for layer in range(2):
            for t in range(rows // SUB):
                at = pl.ds(t * SUB, SUB)
                edge = edge_last[kind, at, :]
                for k in range(n_lanes):
                    value = last[kind, layer, k, at, :]
                    if k == 0:
                        value = jnp.where(lane < KEEP, turn(edge, -HALF * layer - OUT, 1), value)
                    if k == n_lanes - 1:
                        value = jnp.where(
                            lane >= LANES - KEEP, turn(edge, -HALF * layer - SIDE - OUT, 1), value
                        )
                    merged[kind, layer, at, lane_tile(k)] = value
            copies.append(
                pltpu.make_async_copy(
                    merged.at[kind, layer], out_fields.at[kind, layer], sems.at[2 * kind + layer]
                )
            )
            copies[-1].start()
    for copy in copies:
        copy.wait()


def vmem():
    return pl.BlockSpec(memory_space=pltpu.VMEM)


def shape(*dims, dtype=F32):
    return jax.ShapeDtypeStruct(dims, dtype)


def call(kernel, outs, n_in, *, in_space=pltpu.VMEM, out_specs=None, scratch=(), flops=0, size=0):
    return pl.pallas_call(
        kernel,
        out_shape=outs,
        in_specs=[pl.BlockSpec(memory_space=in_space)] * n_in,
        out_specs=out_specs or tuple(vmem() for _ in outs),
        scratch_shapes=list(scratch),
        compiler_params=pltpu.CompilerParams(vmem_limit_bytes=40 * 1024 * 1024),
        cost_estimate=pl.CostEstimate(flops=flops, bytes_accessed=size, transcendentals=0),
    )


def on_device(adj_fields, inv_eps, fwd_diff, mon_x, mon_y, mon_amp, design_mask, tile_owner):
    rows, cols = adj_fields.shape[2], adj_fields.shape[3]
    assert cols == 2 * LANES and rows % TS == 0
    gx_count, gy_count = lax.axis_size("gx"), lax.axis_size("gy")
    owners = gx_count * gy_count
    tiles = (rows // TS) * (cols // TS)
    width = 2 * (TS // PIX) ** 2
    assert width == LANES
    capacity = max(8, 2 * tiles // owners)
    assert rows == TS * SUB and cols == 2 * TS * SUB
    ext_rows = rows + 2 * PAD
    n_lanes = cols // LANES
    cells = rows * cols
    blocks = (adj_fields, inv_eps, fwd_diff)


    strip = shape(4 + STEPS, 2, SUB, cols)
    cross, near = call(
        rows_kernel, (strip, strip), 3, in_space=pltpu.HBM,
        scratch=(
            pltpu.VMEM((2, 4, 2, SUB, cols), F32),
            pltpu.SemaphoreType.DMA((10,)),
        ),
        size=2**20,
    )(*(pltpu.with_memory_space_constraint(block, pltpu.HBM) for block in blocks))

    def pairs(count, start):
        some = [(i, i + 1) for i in range(start, count - 1, 2)]
        return some + [(j, i) for i, j in some]

    cross = lax.ppermute(cross, "gx", pairs(gx_count, 1))
    near = lax.ppermute(near, "gx", pairs(gx_count, 0))

    packed = shape(ext_rows - SUB, LANES)
    channels = mon_x.shape[0]
    cross_cols, near_cols, base, src, src_edge, place, place_edge = call(
        lambda *refs: prep_kernel(capacity, *refs),
        (
            packed,
            packed,
            shape(4 + STEPS, ext_rows, LANES),
            shape(STEPS, 2, ext_rows, cols),
            shape(STEPS, ext_rows, LANES),
            shape(owners * capacity, tiles, dtype=BF16),
            shape(owners * capacity, 4 * SUB, dtype=BF16),
        ),
        8,
        flops=16 * ext_rows * (cols + LANES) * 3 * channels,
        size=64 * cells,
    )(
        *blocks,
        mon_x.reshape(1, channels),
        mon_y.reshape(1, channels),
        mon_amp,
        design_mask.reshape(1, tiles),
        tile_owner.reshape(1, tiles),
    )
    cross_cols, near_cols = call(
        corners_kernel, (packed, packed), 4, flops=cells, size=8 * ext_rows * LANES
    )(cross_cols, near_cols, cross, near)
    cross_cols = lax.ppermute(cross_cols, "gy", pairs(gy_count, 1))
    near_cols = lax.ppermute(near_cols, "gy", pairs(gy_count, 0))

    plane = (2, n_lanes, ext_rows, LANES)
    last, slots, base = call(
        inner_kernel,
        (
            shape(3, 2, n_lanes, rows, LANES),
            shape(owners * capacity, width),
            shape(4 + STEPS, ext_rows, LANES),
        ),
        9,
        scratch=(
            pltpu.VMEM((1 + STEPS,) + plane, F32),
            pltpu.VMEM(plane, F32),
            pltpu.VMEM(plane, F32),
            pltpu.VMEM(plane, F32),
            pltpu.VMEM((2, ext_rows // PIX, LANES), F32),
        ),
        flops=200 * cells,
        size=96 * cells,
    )(*blocks, cross, near, src, pool_matrices(), base, place)

    plane = (ext_rows, LANES)
    (base,) = call(
        edge_cross_kernel, (shape(4 + STEPS, *plane),), 2, flops=10 * cells, size=8 * cells
    )(base, cross_cols)
    edge_last, outgoing = call(
        edge_kernel,
        (shape(3, rows, LANES), pltpu.VMEM((owners * capacity, width), F32)),
        5,
        scratch=(
            pltpu.VMEM((1 + STEPS,) + plane, F32),
            pltpu.VMEM((2,) + plane, F32),
            pltpu.VMEM(plane, F32),
            pltpu.VMEM(plane, F32),
            pltpu.VMEM((STEPS,) + plane, F32),
            pltpu.VMEM(plane, F32),
            pltpu.VMEM((2, SUB, LANES), F32),
        ),
        flops=50 * cells,
        size=16 * cells,
    )(slots, base, near_cols, src_edge, place_edge)

    outgoing = outgoing.reshape(owners, capacity, width)
    incoming = lax.all_to_all(outgoing, ("gx", "gy"), split_axis=0, concat_axis=0, tiled=True)
    anywhere = pl.BlockSpec(memory_space=pl.ANY)
    return call(
        deliver_kernel,
        (shape(3, 2, rows, cols), shape(1, *incoming.shape)),
        3,
        out_specs=(anywhere, anywhere),
        scratch=(pltpu.VMEM((3, 2, rows, cols), F32), pltpu.SemaphoreType.DMA((7,))),
        flops=20 * cells,
        size=48 * cells,
    )(last, edge_last, pltpu.with_memory_space_constraint(incoming, pltpu.VMEM))


def solution(mesh):
    placed = (
        P(None, None, ("parts", "gx"), "gy"),
        P(None, ("parts", "gx"), "gy"),
        P(None, None, ("parts", "gx"), "gy"),
        P("parts"),
        P("parts"),
        P(None, "parts"),
        P(("parts", "gx"), "gy", None),
        P(("parts", "gx"), "gy", None, None),
    )
    return jax.shard_map(
        on_device,
        mesh=mesh,
        in_specs=placed,
        out_specs=(
            P(None, None, ("parts", "gx"), "gy"),
            P(("parts", "gx", "gy"), None, None, None),
        ),
        check_vma=False,
    )
```

```python
import jax
import jax.numpy as jnp
import ml_dtypes
import numpy as np
from jax import lax
from jax.experimental import pallas as pl
from jax.experimental.pallas import tpu as pltpu
from jax.sharding import PartitionSpec as P

STEPS = 4
PIX = 2
TS = 16
RADIUS = 4
COURANT = 0.6
COUPLING = 0.25

LANES = 128
SUB = 8
FAR = STEPS + PIX * (RADIUS - 1)
NEAR = PIX * (RADIUS - 1)
LEFT_OVER = FAR - SUB
PAD = 2 * SUB
HALF = LANES // 2
SIDE = HALF // 2
OUT = SIDE // 2
KEEP = 8
F32 = jnp.float32
BF16 = jnp.bfloat16
WIDTHS = (FAR,) * 4 + (NEAR,) * STEPS
FIRST = tuple(sum(WIDTHS[:k]) for k in range(len(WIDTHS)))
assert sum(WIDTHS) <= HALF and FAR <= OUT and STEPS + KEEP <= OUT


def cone_weights(radius):
    reach_cells = radius - 1
    offsets = np.arange(-reach_cells, reach_cells + 1)
    distance = np.sqrt(offsets[:, None] * offsets[:, None] + offsets[None, :] * offsets[None, :])
    weights = np.maximum(radius - distance, 0.0)
    return weights / weights.sum()


def pool_matrices():
    inner = np.zeros((2, LANES, LANES), np.float32)
    for j in range(KEEP, 2 * LANES - KEEP):
        inner[j // LANES, j % LANES, j // PIX] = 1.0
    return inner.astype(ml_dtypes.bfloat16)


def split2(value):
    high = value.astype(BF16)
    return high, (value - high.astype(F32)).astype(BF16)


def split3(value):
    high = value.astype(BF16)
    rest = value - high.astype(F32)
    mid = rest.astype(BF16)
    return high, mid, (rest - mid.astype(F32)).astype(BF16)


def dot(a, b):
    return jnp.dot(a, b, preferred_element_type=F32)


def turn(value, shift, axis):
    size = value.shape[axis]
    return pltpu.roll(value, shift % size, axis) if shift % size else value


def lanes():
    return lax.broadcasted_iota(jnp.int32, (SUB, LANES), 1)


def subs():
    return lax.broadcasted_iota(jnp.int32, (SUB, LANES), 0)


def lane_tile(k):
    return pl.ds(k * LANES, LANES)


def is_odd(axis):
    return ((subs() * 0 + lax.axis_index(axis)) & 1) == 1


def rows_kernel(fields, eps, fwd, cross, near, hold, sems):
    rows, cols = fields.shape[2], fields.shape[3]
    sub = subs()
    odd = lax.axis_index("gx") & 1
    parts = []
    for n, (out, at_end) in enumerate(((cross, odd), (near, 1 - odd))):
        at = pl.ds(pl.multiple_of(at_end * (rows - SUB), SUB), SUB)
        rest = pl.ds(pl.multiple_of(SUB + at_end * (rows - 3 * SUB), SUB), SUB)
        pairs = (
            (fields.at[:, :, rest, :], hold.at[n, pl.ds(0, 3)]),
            (eps.at[:, rest, :], hold.at[n, 3]),
            (fwd.at[:, :, at, :], out.at[pl.ds(4, STEPS)]),
            (fields.at[:, :, at, :], out.at[pl.ds(0, 3)]),
            (eps.at[:, at, :], out.at[3]),
        )
        copies = [
            pltpu.make_async_copy(src, dst, sems.at[len(pairs) * n + m])
            for m, (src, dst) in enumerate(pairs)
        ]
        parts.append((n, out, at_end, copies))
    for group in (slice(0, 3), slice(3, 5)):
        for part in parts:
            for copy in part[3][group]:
                copy.start()
    for n, out, at_end, copies in parts:
        for copy in copies[:3]:
            copy.wait()
        low = (1 - at_end) * NEAR
        rest = (sub >= low) & (sub < low + LEFT_OVER)
        shift = NEAR + at_end * (LEFT_OVER - NEAR)
        for kind in range(4):
            for layer in range(2):
                values = []
                for k in range(cols // LANES):
                    moved = pltpu.roll(hold[n, kind, layer, :, lane_tile(k)], shift, 0)
                    values.append(jnp.where(rest, moved, out[4 + kind, layer, :, lane_tile(k)]))
                for k, value in enumerate(values):
                    out[4 + kind, layer, :, lane_tile(k)] = value
    for part in parts:
        for copy in part[3][3:]:
            copy.wait()


def halo_tile(cross, near, odd, tile, kind, layer, at):
    is_above = tile < 2
    outer = tile in (0, 3)
    if outer and kind >= 4:
        return None
    plane = kind + (4 if outer else 0)
    a, b = near[plane, layer, :, at], cross[plane, layer, :, at]
    value = jnp.where(odd, a, b) if is_above else jnp.where(odd, b, a)
    if outer:
        value = turn(value, -LEFT_OVER if is_above else LEFT_OVER, 0)
    return value


def core_tile(fields, eps, fwd, at, kind, layer, cols):
    if kind < 3:
        return fields[kind, layer, at, cols]
    if kind == 3:
        return eps[layer, at, cols]
    return fwd[kind - 4, layer, at, cols]


def pack_tile(load, lane, right):
    total = jnp.zeros((SUB, LANES), F32)
    for kind, width in enumerate(WIDTHS):
        for layer in range(2):
            value = load(kind, layer)
            if value is None:
                continue
            first = FIRST[kind] + HALF * layer
            value = turn(value, first + width if right else first, 1)
            total = jnp.where((lane >= first) & (lane < first + width), value, total)
    return total


def edge_tile(load, kind, lane, n_lanes):
    spot = lane & (HALF - 1)
    total = None
    for layer in range(2):
        low = turn(load(kind, layer, 0), HALF * layer + OUT, 1)
        high = turn(load(kind, layer, n_lanes - 1), HALF * layer + SIDE + OUT, 1)
        value = jnp.where(spot < SIDE, low, high)
        total = value if total is None else jnp.where(lane < HALF, total, value)
    return total


def cols_kernel(fields, eps, fwd, cross, near, base):
    rows, cols = fields.shape[2], fields.shape[3]
    n_lanes = cols // LANES
    lane, odd = lanes(), is_odd("gy")

    def tile(t, carry):
        at = pl.ds(pl.multiple_of(t * SUB, SUB), SUB)
        out_at = pl.ds(pl.multiple_of(t * SUB + PAD, SUB), SUB)

        def load(kind, layer, k):
            return core_tile(fields, eps, fwd, at, kind, layer, lane_tile(k))

        left = pack_tile(lambda kind, layer: load(kind, layer, 0), lane, False)
        right = pack_tile(lambda kind, layer: load(kind, layer, n_lanes - 1), lane, True)
        cross[out_at, :] = jnp.where(odd, right, left)
        near[out_at, :] = jnp.where(odd, left, right)
        for kind in range(4 + STEPS):
            base[kind, out_at, :] = edge_tile(load, kind, lane, n_lanes)
        return carry

    lax.fori_loop(0, rows // SUB, tile, 0, unroll=4)
    zero = jnp.zeros((SUB, LANES), F32)
    for out in (cross, near):
        for at in (0, SUB, PAD + rows):
            out[pl.ds(at, SUB), :] = zero


def packed_at(t, n_tiles):
    return pl.ds((t if t < n_tiles - 1 else 0) * SUB, SUB)


def corners_kernel(cross_in, near_in, cross_rows, near_rows, cross, near):
    rows, cols = cross.shape[0] - 3 * SUB, cross_rows.shape[3]
    lane, odd, odd_col = lanes(), is_odd("gx"), is_odd("gy")
    is_first = subs() >= SUB - LEFT_OVER
    core = pl.ds(PAD, rows)
    cross[core, :] = cross_in[core, :]
    near[core, :] = near_in[core, :]
    for base, tiles in ((0, (0, 3)), (SUB, (1,)), (PAD + rows, (2,))):
        at = pl.ds(base, SUB)
        packs = []
        for lo, is_right in ((0, False), (cols - LANES, True)):

            def load(kind, layer):
                values = [
                    halo_tile(cross_rows, near_rows, odd, tile, kind, layer, pl.ds(lo, LANES))
                    for tile in tiles
                ]
                if len(values) == 1 or values[0] is None:
                    return values[0]
                return jnp.where(is_first, values[0], values[1])

            packs.append(pack_tile(load, lane, is_right))
        left, right = packs
        cross[at, :] = jnp.where(odd_col, right, left)
        near[at, :] = jnp.where(odd_col, left, right)


def prep_kernel(
    capacity, fields, eps, fwd, mon_x, mon_y, amp, mask, owner, cross, near, base, src, src_edge, place, place_edge
):
    cols_kernel(fields, eps, fwd, cross, near, base)
    side_kernel(capacity, fields.shape[2], mon_x, mon_y, amp, mask, owner, src, src_edge, place, place_edge)


def side_kernel(capacity, rows, mon_x, mon_y, amp, mask, owner, src, src_edge, place, place_edge):
    _, _, ext_rows, cols = src.shape
    channels = mon_x.shape[1]
    row = mon_x[...] - lax.axis_index("gx") * rows + PAD
    col = mon_y[...] - lax.axis_index("gy") * cols
    in_left = (col >= -OUT) & (col < OUT)
    in_right = (col >= cols - OUT) & (col < cols + OUT)
    edge = jnp.where(in_left, col + OUT, jnp.where(in_right, col - cols + OUT + SIDE, -LANES))
    layer = lax.broadcasted_iota(jnp.int32, (1, channels), 1) & 1
    edge = edge + HALF * layer
    inside = jnp.where((col >= 0) & (col < cols), col, -1)
    one_y = lax.broadcasted_iota(jnp.int32, (cols, channels), 0) == inside
    one_e = lax.broadcasted_iota(jnp.int32, (LANES, channels), 0) == edge
    one_y = jnp.where(one_y, 1.0, 0.0).astype(BF16)
    one_e = jnp.where(one_e, 1.0, 0.0).astype(BF16)
    one_y = jnp.concatenate([one_y] * 3, axis=1)
    one_e = jnp.concatenate([one_e] * 3, axis=1)
    one_x = lax.broadcasted_iota(jnp.int32, (ext_rows, channels), 0) == row
    one_x = jnp.where(one_x, 1.0, 0.0).astype(F32)
    nt = (((1,), (1,)), ((), ()))
    for step in range(STEPS):
        parts = [part.astype(F32) for part in split3(amp[pl.ds(step, 1), :])]
        lhs = jnp.concatenate([one_x * part for part in parts], axis=1)
        src_edge[step] = lax.dot_general(lhs.astype(BF16), one_e, nt, preferred_element_type=F32)
        layer_wide = jnp.concatenate([layer] * 3, axis=1)
        for which in range(2):
            some = jnp.where(layer_wide == which, lhs, 0.0).astype(BF16)
            src[step, which] = lax.dot_general(some, one_y, nt, preferred_element_type=F32)
    tiles = owner.shape[1]
    own = owner[...].astype(F32)
    own_wide = jnp.broadcast_to(own, (tiles, tiles))
    earlier = lax.broadcasted_iota(jnp.int32, (tiles, tiles), 0) < lax.broadcasted_iota(
        jnp.int32, (tiles, tiles), 1
    )
    same = (own_wide.T == own_wide) & earlier
    slot = jnp.sum(jnp.where(same, 1.0, 0.0), axis=0, keepdims=True)
    dest = owner[...] * capacity + slot.astype(jnp.int32)
    dest = jnp.where(mask[...] != 0, dest, -1)
    hit = lax.broadcasted_iota(jnp.int32, place.shape, 0) == dest
    hit = jnp.where(hit, 1.0, 0.0).astype(BF16)
    place[...] = hit
    tile_cols = cols // TS
    column = lax.broadcasted_iota(jnp.int32, (tiles, 4 * SUB), 1)
    wanted = (column % SUB) * tile_cols + ((column // SUB) & 1) * (tile_cols - 1)
    picked = lax.broadcasted_iota(jnp.int32, (tiles, 4 * SUB), 0) == wanted
    place_edge[...] = dot(hit, jnp.where(picked, 1.0, 0.0).astype(BF16)).astype(BF16)


class Shifts:
    def __init__(self, next_col, prev_col):
        self.next_col, self.prev_col = next_col, prev_col
        self.bottom, self.top = subs() == SUB - 1, subs() == 0

    def up(self, tile):
        return {key: turn(value, -1, 0) for key, value in tile.items()}

    def down(self, tile):
        return {key: turn(value, 1, 0) for key, value in tile.items()}

    def below(self, up_here, up_next):
        return {key: jnp.where(self.bottom, up_next[key], up_here[key]) for key in up_here}

    def above(self, down_here, down_before):
        return {key: jnp.where(self.top, down_before[key], down_here[key]) for key in down_here}


def tile_at(t):
    return (pl.ds(t * SUB, SUB), slice(None))


def first_curl(n_tiles, shifts, load_hx, load_hy, curl):
    before = None
    for t in range(n_tiles):
        hx, hy = load_hx(t), load_hy(t)
        down = shifts.down(hy)
        over = shifts.above(down, before if t else down)
        left = shifts.prev_col(hx)
        for key in hx:
            curl[key + tile_at(t)] = (hy[key] - over[key]) - (hx[key] - left[key])
        before = down


def steps(n_tiles, keys, shifts, e, curl, eps_of, src_of, other):
    no_above = shifts.top & ((lax.axis_index("gx") + subs() * 0) == 0)
    for step in range(STEPS):
        low, high = (0, n_tiles) if step == 0 else (1, n_tiles - 1)

        def load(t):
            return {key: e[(step,) + key + tile_at(t)] for key in keys}

        here = load(low)
        up = shifts.up(here)
        down_before = shifts.down(load(max(low - 1, 0)))
        for t in range(low, high):
            after = load(min(t + 1, n_tiles - 1))
            up_next, down = shifts.up(after), shifts.down(here)
            below, above = shifts.below(up, up_next), shifts.above(down, down_before)
            right, left = shifts.next_col(here), shifts.prev_col(here)
            for key in keys:
                center, over = here[key], above[key]
                if t == PAD // SUB:
                    over = jnp.where(no_above, center, over)
                ring = (below[key] + over) + (right[key] + left[key]) - 4.0 * center
                change = curl[key + tile_at(t)] - COURANT * ring
                if step < STEPS - 1:
                    curl[key + tile_at(t)] = change
                change = change + COUPLING * (other(here, key) - center)
                e[(step + 1,) + key + tile_at(t)] = (
                    center - eps_of(key, t) * change + src_of(step, key, t)
                )
            here, up, down_before = after, up_next, down


def gradient(keys, t, e, change_of):
    result = {}
    for key in keys:
        total = None
        for step in range(STEPS):
            term = e[(step + 1,) + key + tile_at(t)] * change_of(step, key, t)
            total = term if total is None else total + term
        result[key] = -total
    return result


def last_fields(tiles, keys, shifts, e, load_hx, load_hy, store):
    def total(t):
        result = {}
        for key in keys:
            parts = [e[(step,) + key + tile_at(t)] for step in range(STEPS)]
            result[key] = (parts[0] + parts[1]) + (parts[2] + parts[3])
        return result

    here = total(tiles[0])
    up = shifts.up(here)
    for t in tiles:
        after = total(t + 1)
        up_next = shifts.up(after)
        below, right = shifts.below(up, up_next), shifts.next_col(here)
        hx, hy = load_hx(t), load_hy(t)
        for key in keys:
            store(
                key, t, e[(STEPS,) + key + tile_at(t)],
                hx[key] + COURANT * (right[key] - here[key]),
                hy[key] - COURANT * (below[key] - here[key]),
            )
        here, up = after, up_next


def row_pairs(ref, lead, count):
    even = ref[lead + (pl.ds(0, count, stride=PIX), slice(None))]
    return even + ref[lead + (pl.ds(1, count, stride=PIX), slice(None))]


def inner_kernel(
    fields, eps, fwd, cross, near, src, mats, base_in, place, last, slots, base, e, curl, eps_c, g, pooled
):
    rows, cols = fields.shape[2], fields.shape[3]
    n_tiles = (rows + 2 * PAD) // SUB
    n_lanes = cols // LANES
    lane, odd = lanes(), is_odd("gx")
    halo_of = {0: 0, 1: 1, n_tiles - 2: 2, n_tiles - 1: 3}
    keys = [(layer, k) for layer in range(2) for k in range(n_lanes)]

    def load(kind, layer, t, k):
        if t in halo_of:
            return halo_tile(cross, near, odd, halo_of[t], kind, layer, lane_tile(k))
        return core_tile(fields, eps, fwd, pl.ds(t * SUB - PAD, SUB), kind, layer, lane_tile(k))

    def load_all(kind, t):
        return {key: load(kind, key[0], t, key[1]) for key in keys}

    at_end, at_start = lane == LANES - 1, lane == 0

    def next_col(values):
        moved = {key: turn(value, -1, 1) for key, value in values.items()}
        return {
            (l, k): jnp.where(at_end, moved[l, (k + 1) % n_lanes], moved[l, k]) for l, k in keys
        }

    def prev_col(values):
        moved = {key: turn(value, 1, 1) for key, value in values.items()}
        return {
            (l, k): jnp.where(at_start, moved[l, (k - 1) % n_lanes], moved[l, k]) for l, k in keys
        }

    shifts = Shifts(next_col, prev_col)
    for t in range(n_tiles):
        for key in keys:
            e[(0,) + key + tile_at(t)] = load(0, key[0], t, key[1])
            eps_c[key + tile_at(t)] = COURANT * load(3, key[0], t, key[1])
    first_curl(n_tiles, shifts, lambda t: load_all(1, t), lambda t: load_all(2, t), curl)
    steps(
        n_tiles, keys, shifts, e, curl,
        lambda key, t: eps_c[key + tile_at(t)],
        lambda step, key, t: src[step, key[0], pl.ds(t * SUB, SUB), lane_tile(key[1])],
        lambda values, key: values[1 - key[0], key[1]],
    )
    for t in range(1, n_tiles - 1):
        values = gradient(keys, t, e, lambda step, key, t: load(4 + step, key[0], t, key[1]))
        for key in keys:
            g[key + tile_at(t)] = values[key]

    def store(key, t, *values):
        for kind, value in enumerate(values):
            last[(kind,) + key + (pl.ds(t * SUB - PAD, SUB), slice(None))] = value

    last_fields(
        range(PAD // SUB, n_tiles - PAD // SUB), keys, shifts, e,
        lambda t: load_all(1, t), lambda t: load_all(2, t), store,
    )
    for layer in range(2):
        total = None
        for k in range(n_lanes):
            for part in split2(row_pairs(g, (layer, k), n_tiles * SUB // PIX)):
                term = dot(part, mats[k])
                total = term if total is None else total + term
        pooled[layer] = total

    vals = by_tile([cone_filter(pooled.at[layer], rows // PIX, PAD // PIX) for layer in range(2)])
    high, low = split2(vals)
    slots[...] = dot(place[...], high) + dot(place[...], low)

    for t in range(n_tiles):
        for kind in range(4 + STEPS):
            at = pl.ds(t * SUB, SUB)
            if t not in halo_of:
                base[kind, at, :] = base_in[kind, at, :]
            elif kind < 4 or t not in (0, n_tiles - 1):
                base[kind, at, :] = edge_tile(
                    lambda kind, layer, k: load(kind, layer, t, k), kind, lane, n_lanes
                )


def cone_filter(pooled, out_pix, first):
    weights = cone_weights(RADIUS)
    reach = RADIUS - 1
    lane = lax.broadcasted_iota(jnp.int32, (out_pix, LANES), 1)
    at = [pooled[pl.ds(first + s, out_pix), :] for s in range(-reach, reach + 1)]
    sums = [at[reach]] + [at[reach + s] + at[reach - s] for s in range(1, reach + 1)]
    total = None
    for shift in range(reach + 1):
        mixed = None
        for s in range(reach + 1):
            weight = float(weights[reach + s, reach + shift])
            if weight > 0.0:
                term = weight * sums[s]
                mixed = term if mixed is None else mixed + term
        if shift == 0:
            total = mixed
        else:
            total = total + turn(jnp.where(lane < shift, 0.0, mixed), -shift, 1)
            total = total + turn(jnp.where(lane >= LANES - shift, 0.0, mixed), shift, 1)
    return total


def by_tile(blocks):
    span = TS // PIX
    tile_rows = blocks[0].shape[0] // span
    x = jnp.stack([block.reshape(tile_rows, span, LANES) for block in blocks], axis=1)
    x = x.reshape(tile_rows * 2, span, LANES)
    group = lax.broadcasted_iota(jnp.int32, x.shape, 2) // span
    row = lax.broadcasted_iota(jnp.int32, x.shape, 1)
    for bit in (1, 2, 4):
        row_on, lane_on = (row & bit) != 0, (group & bit) != 0
        ahead = turn(turn(x, -bit, 1), bit * span, 2)
        behind = turn(turn(x, bit, 1), -bit * span, 2)
        x = jnp.where(row_on == lane_on, x, jnp.where(lane_on, ahead, behind))
    x = x.reshape(tile_rows, 2, span, LANES)
    even, odd = x[:, 0], x[:, 1]
    upper = lax.broadcasted_iota(jnp.int32, even.shape, 2) >= HALF
    new_even = jnp.where(upper, turn(odd, HALF, 2), even)
    new_odd = jnp.where(upper, odd, turn(even, HALF, 2))
    return jnp.stack([new_even, new_odd], axis=1).reshape(tile_rows * 2 * span, LANES)


def from_partner(is_cross, lane):
    next_one = (lax.axis_index("gy") + (0 if is_cross else 1)) & 1
    spot = lane & (HALF - 1)
    start = next_one * (HALF - OUT)
    mine = (spot >= start) & (spot < start + OUT)
    shifts = []
    for kind, width in enumerate(WIDTHS):
        left, right = (OUT - width - FIRST[kind]) % LANES, (HALF - OUT - FIRST[kind]) % LANES
        shifts.append(left + next_one * (right - left))
    return mine, shifts


def edge_cross_kernel(base, cross, result):
    n_tiles = base.shape[1] // SUB
    mine, shifts = from_partner(False, lanes())
    for t in range(n_tiles):
        at = pl.ds(t * SUB, SUB)
        strip = cross[packed_at(t, n_tiles), :]
        kinds = range(4 if t in (0, n_tiles - 1) else 4 + STEPS)
        values = [
            jnp.where(mine, pltpu.roll(strip, shifts[kind], 1), base[kind, at, :])
            for kind in kinds
        ]
        for kind in kinds:
            result[kind, at, :] = values[kind]


def edge_kernel(
    slots_in, base, near, src, place, edge_last, slots, e, first, curl, eps_c, d, g, merged
):
    ext_rows = base.shape[1]
    rows = ext_rows - 2 * PAD
    n_tiles = ext_rows // SUB
    lane = lanes()
    spot = lane & (HALF - 1)
    mine, moves = from_partner(True, lane)

    for t in range(n_tiles):
        at = pl.ds(t * SUB, SUB)
        strip = near[packed_at(t, n_tiles), :]
        for kind in range(4 if t in (0, n_tiles - 1) else 4 + STEPS):
            value = jnp.where(mine, pltpu.roll(strip, moves[kind], 1), base[kind, at, :])
            if kind == 0:
                e[0, at, :] = value
            elif kind < 3:
                first[kind - 1, at, :] = value
            elif kind == 3:
                eps_c[at, :] = COURANT * value
            else:
                d[kind - 4, at, :] = value

    no_left = (spot == OUT) & ((lax.axis_index("gy") + lane * 0) == 0)
    shifts = Shifts(
        lambda values: {(): turn(values[()], -1, 1)},
        lambda values: {(): turn(values[()], 1, 1)},
    )

    def load_hx(t):
        return {(): first[0, pl.ds(t * SUB, SUB), :]}

    def load_hy(t):
        return {(): first[1, pl.ds(t * SUB, SUB), :]}

    first_curl(n_tiles, shifts, load_hx, load_hy, curl)
    shifts.prev_col = lambda values: {(): jnp.where(no_left, values[()], turn(values[()], 1, 1))}
    steps(
        n_tiles, [()], shifts, e, curl,
        lambda key, t: eps_c[pl.ds(t * SUB, SUB), :],
        lambda step, key, t: src[step, pl.ds(t * SUB, SUB), :],
        lambda values, key: turn(values[()], HALF, 1),
    )
    inside = (spot >= OUT - NEAR) & (spot < OUT + KEEP)
    inside = inside | ((spot >= HALF - OUT - KEEP) & (spot < HALF - OUT + NEAR))
    for t in range(1, n_tiles - 1):
        value = gradient([()], t, e, lambda step, key, t: d[step, pl.ds(t * SUB, SUB), :])[()]
        g[pl.ds(t * SUB, SUB), :] = jnp.where(inside, value, 0.0)

    def store(key, t, *values):
        for kind, value in enumerate(values):
            edge_last[kind, pl.ds(t * SUB - PAD, SUB), :] = value

    edge_filter(g, merged)
    edge_slots(merged, slots_in, place, slots)
    last_fields(
        range(PAD // SUB, n_tiles - PAD // SUB), [()], shifts, e, load_hx, load_hy, store
    )


def edge_filter(g, merged):
    lane = lanes()
    span, reach = TS // PIX, RADIUS - 1
    pixel = {}
    for j in range(-reach, span + reach):
        value = g[pl.ds(PAD + PIX * j, SUB, stride=TS), :]
        pixel[j] = value + g[pl.ds(PAD + PIX * j + 1, SUB, stride=TS), :]

    weights = cone_weights(RADIUS)
    spans = []
    for row in range(span):
        sums = [pixel[row]] + [pixel[row + s] + pixel[row - s] for s in range(1, reach + 1)]
        move = (row & 1) + SIDE * ((row >> 1) & 1)
        total = None
        for shift in range(reach + 1):
            mixed = None
            for s in range(reach + 1):
                weight = float(weights[reach + s, reach + shift])
                if weight > 0.0:
                    term = weight * sums[s]
                    mixed = term if mixed is None else mixed + term
            for place in {PIX * shift, -PIX * shift}:
                term = turn(mixed, move + place, 1) + turn(mixed, move + place - 1, 1)
                total = term if total is None else total + term
        spans.append(total)
    even = (lane & 1) == 0
    window = ((lane - OUT) & (HALF - 1)) < SIDE
    for n in range(2):
        a, b, c, d = spans[4 * n : 4 * n + 4]
        merged[n] = jnp.where(window, jnp.where(even, a, b), jnp.where(even, c, d))


def edge_slots(merged, slots_in, place, slots):
    lane = lanes()
    span = TS // PIX
    row, pixel = lane // span % span, lane % span
    start = (lane & HALF) + OUT + PIX * pixel + (row & 1) + SIDE * ((row >> 1) & 1)
    edge = []
    for side in range(2):
        index = (start + OUT * side) & (LANES - 1)
        low, high = (jnp.take_along_axis(merged[n], index, axis=1) for n in range(2))
        edge.append(jnp.where(row < span // 2, low, high))
    parts = split2(jnp.concatenate(edge, axis=0))
    slots[...] = slots_in[...] + dot(place[...], jnp.concatenate(parts, axis=0))


def deliver_kernel(last, edge_last, slots, out_fields, out_slots, merged, sems):
    rows, cols = merged.shape[2], merged.shape[3]
    n_lanes = cols // LANES
    lane = lanes()
    copies = [pltpu.make_async_copy(slots, out_slots.at[0], sems.at[6])]
    copies[0].start()
    for kind in range(3):
        for layer in range(2):
            for t in range(rows // SUB):
                at = pl.ds(t * SUB, SUB)
                edge = edge_last[kind, at, :]
                for k in range(n_lanes):
                    value = last[kind, layer, k, at, :]
                    if k == 0:
                        value = jnp.where(lane < KEEP, turn(edge, -HALF * layer - OUT, 1), value)
                    if k == n_lanes - 1:
                        value = jnp.where(
                            lane >= LANES - KEEP, turn(edge, -HALF * layer - SIDE - OUT, 1), value
                        )
                    merged[kind, layer, at, lane_tile(k)] = value
            copies.append(
                pltpu.make_async_copy(
                    merged.at[kind, layer], out_fields.at[kind, layer], sems.at[2 * kind + layer]
                )
            )
            copies[-1].start()
    for copy in copies:
        copy.wait()


def vmem():
    return pl.BlockSpec(memory_space=pltpu.VMEM)


def shape(*dims, dtype=F32):
    return jax.ShapeDtypeStruct(dims, dtype)


def call(kernel, outs, n_in, *, in_space=pltpu.VMEM, out_specs=None, scratch=(), flops=0, size=0):
    return pl.pallas_call(
        kernel,
        out_shape=outs,
        in_specs=[pl.BlockSpec(memory_space=in_space)] * n_in,
        out_specs=out_specs or tuple(vmem() for _ in outs),
        scratch_shapes=list(scratch),
        compiler_params=pltpu.CompilerParams(vmem_limit_bytes=40 * 1024 * 1024),
        cost_estimate=pl.CostEstimate(flops=flops, bytes_accessed=size, transcendentals=0),
    )


def on_device(adj_fields, inv_eps, fwd_diff, mon_x, mon_y, mon_amp, design_mask, tile_owner):
    rows, cols = adj_fields.shape[2], adj_fields.shape[3]
    assert cols == 2 * LANES and rows % TS == 0
    gx_count, gy_count = lax.axis_size("gx"), lax.axis_size("gy")
    owners = gx_count * gy_count
    tiles = (rows // TS) * (cols // TS)
    width = 2 * (TS // PIX) ** 2
    assert width == LANES
    capacity = max(8, 2 * tiles // owners)
    assert rows == TS * SUB and cols == 2 * TS * SUB
    ext_rows = rows + 2 * PAD
    n_lanes = cols // LANES
    cells = rows * cols
    blocks = (adj_fields, inv_eps, fwd_diff)


    strip = shape(4 + STEPS, 2, SUB, cols)
    cross, near = call(
        rows_kernel, (strip, strip), 3, in_space=pltpu.HBM,
        scratch=(
            pltpu.VMEM((2, 4, 2, SUB, cols), F32),
            pltpu.SemaphoreType.DMA((10,)),
        ),
        size=2**20,
    )(*(pltpu.with_memory_space_constraint(block, pltpu.HBM) for block in blocks))

    def pairs(count, start):
        some = [(i, i + 1) for i in range(start, count - 1, 2)]
        return some + [(j, i) for i, j in some]

    cross = lax.ppermute(cross, "gx", pairs(gx_count, 1))
    near = lax.ppermute(near, "gx", pairs(gx_count, 0))

    packed = shape(ext_rows - SUB, LANES)
    channels = mon_x.shape[0]
    cross_cols, near_cols, base, src, src_edge, place, place_edge = call(
        lambda *refs: prep_kernel(capacity, *refs),
        (
            packed,
            packed,
            shape(4 + STEPS, ext_rows, LANES),
            shape(STEPS, 2, ext_rows, cols),
            shape(STEPS, ext_rows, LANES),
            shape(owners * capacity, tiles, dtype=BF16),
            shape(owners * capacity, 4 * SUB, dtype=BF16),
        ),
        8,
        flops=16 * ext_rows * (cols + LANES) * 3 * channels,
        size=64 * cells,
    )(
        *blocks,
        mon_x.reshape(1, channels),
        mon_y.reshape(1, channels),
        mon_amp,
        design_mask.reshape(1, tiles),
        tile_owner.reshape(1, tiles),
    )
    cross_cols, near_cols = call(
        corners_kernel, (packed, packed), 4, flops=cells, size=8 * ext_rows * LANES
    )(cross_cols, near_cols, cross, near)
    near_cols = lax.ppermute(near_cols, "gy", pairs(gy_count, 0))
    cross_cols = lax.ppermute(cross_cols, "gy", pairs(gy_count, 1))

    plane = (2, n_lanes, ext_rows, LANES)
    last, slots, base = call(
        inner_kernel,
        (
            shape(3, 2, n_lanes, rows, LANES),
            shape(owners * capacity, width),
            shape(4 + STEPS, ext_rows, LANES),
        ),
        9,
        scratch=(
            pltpu.VMEM((1 + STEPS,) + plane, F32),
            pltpu.VMEM(plane, F32),
            pltpu.VMEM(plane, F32),
            pltpu.VMEM(plane, F32),
            pltpu.VMEM((2, ext_rows // PIX, LANES), F32),
        ),
        flops=200 * cells,
        size=96 * cells,
    )(*blocks, cross, near, src, pool_matrices(), base, place)

    plane = (ext_rows, LANES)
    (base,) = call(
        edge_cross_kernel, (shape(4 + STEPS, *plane),), 2, flops=10 * cells, size=8 * cells
    )(base, near_cols)
    edge_last, outgoing = call(
        edge_kernel,
        (shape(3, rows, LANES), pltpu.VMEM((owners * capacity, width), F32)),
        5,
        scratch=(
            pltpu.VMEM((1 + STEPS,) + plane, F32),
            pltpu.VMEM((2,) + plane, F32),
            pltpu.VMEM(plane, F32),
            pltpu.VMEM(plane, F32),
            pltpu.VMEM((STEPS,) + plane, F32),
            pltpu.VMEM(plane, F32),
            pltpu.VMEM((2, SUB, LANES), F32),
        ),
        flops=50 * cells,
        size=16 * cells,
    )(slots, base, cross_cols, src_edge, place_edge)

    outgoing = outgoing.reshape(owners, capacity, width)
    incoming = lax.all_to_all(outgoing, ("gx", "gy"), split_axis=0, concat_axis=0, tiled=True)
    anywhere = pl.BlockSpec(memory_space=pl.ANY)
    return call(
        deliver_kernel,
        (shape(3, 2, rows, cols), shape(1, *incoming.shape)),
        3,
        out_specs=(anywhere, anywhere),
        scratch=(pltpu.VMEM((3, 2, rows, cols), F32), pltpu.SemaphoreType.DMA((7,))),
        flops=20 * cells,
        size=48 * cells,
    )(last, edge_last, pltpu.with_memory_space_constraint(incoming, pltpu.VMEM))


def solution(mesh):
    placed = (
        P(None, None, ("parts", "gx"), "gy"),
        P(None, ("parts", "gx"), "gy"),
        P(None, None, ("parts", "gx"), "gy"),
        P("parts"),
        P("parts"),
        P(None, "parts"),
        P(("parts", "gx"), "gy", None),
        P(("parts", "gx"), "gy", None, None),
    )
    return jax.shard_map(
        on_device,
        mesh=mesh,
        in_specs=placed,
        out_specs=(
            P(None, None, ("parts", "gx"), "gy"),
            P(("parts", "gx", "gy"), None, None, None),
        ),
        check_vma=False,
    )
```
